32 devices in a mesh: dp: 8 (over y, x, core), tensor: 4 (over z).
Axes of the slice: x: 2, y: 2, z: 4, core: 2. Of those that a mesh axis runs over, the one named last changes fastest.
Arguments:
- layer_in: bfloat16 [16, 1024, 1024], P('dp', 'tensor'), may hold values from -6 to 6
- seq_lengths: int32 [16], P('dp'), may hold values from 256 to 1024, as said below
- out_grad: bfloat16 [16, 1024, 1024], P('dp', 'tensor'), may hold values from -6 to 6
- norm_gain: float32 [1024], replicated, may hold values from 0.5 to 1.5
- mixer_weight: bfloat16 [1024, 2, 1536], P('dp', None, 'tensor'), may hold values from -0.1875 to 0.1875
- step_weight: bfloat16 [1024, 24], P('dp', 'tensor'), may hold values from -0.09375 to 0.09375
- state_weight: bfloat16 [1024, 2, 128], P('dp'), may hold values from -0.1875 to 0.1875
- query_weight: bfloat16 [1024, 512], P('dp', 'tensor'), may hold values from -0.1875 to 0.1875
- key_value_weight: bfloat16 [1024, 2, 128], P('dp'), may hold values from -0.1875 to 0.1875
- conv_channels: float32 [4, 1536], P(None, 'tensor'), may hold values from -3 to 3
- conv_states: float32 [4, 2, 128], replicated, may hold values from -3 to 3
- step_bias: float32 [24], P('tensor'), may hold values from -7 to -3
- decay_log: float32 [24], P('tensor'), may hold values from 0 to 1.5
- skip_scale: float32 [24], P('tensor'), may hold values from 0.5 to 1.5
- group_gain: float32 [1536], P('tensor'), may hold values from 0.5 to 1.5
- mamba_proj: bfloat16 [1536, 1024], P('tensor', 'dp'), may hold values from -0.15625 to 0.15625
- attn_proj: bfloat16 [512, 1024], P('tensor', 'dp'), may hold values from -1 to 1
- ffn_gain: float32 [1024], replicated, may hold values from 0.5 to 1.5
- ffn_weight: bfloat16 [1024, 2, 2048], P('dp', None, 'tensor'), may hold values from -0.1875 to 0.1875
- ffn_down: bfloat16 [2048, 1024], P('tensor', 'dp'), may hold values from -0.125 to 0.125
Outputs:
- layer_out: bfloat16 [16, 1024, 1024], P('dp', 'tensor')
- input_grad: bfloat16 [16, 1024, 1024], P('dp', 'tensor')
- grad_norm_gain: float32 [1024], replicated
- grad_mixer_weight: float32 [1024, 2, 1536], P('dp', None, 'tensor')
- grad_step_weight: float32 [1024, 24], P('dp', 'tensor')
- grad_state_weight: float32 [1024, 2, 128], P('dp')
- grad_query_weight: float32 [1024, 512], P('dp', 'tensor')
- grad_keyval_weight: float32 [1024, 2, 128], P('dp')
- grad_conv_channels: float32 [4, 1536], P(None, 'tensor')
- grad_conv_states: float32 [4, 2, 128], replicated
- grad_step_bias: float32 [24], P('tensor')
- grad_decay_log: float32 [24], P('tensor')
- grad_skip_scale: float32 [24], P('tensor')
- grad_group_gain: float32 [1536], P('tensor')
- grad_mamba_proj: float32 [1536, 1024], P('tensor', 'dp')
- grad_attn_proj: float32 [512, 1024], P('tensor', 'dp')
- grad_ffn_gain: float32 [1024], replicated
- grad_ffn_weight: float32 [1024, 2, 2048], P('dp', None, 'tensor')
- grad_ffn_down: float32 [2048, 1024], P('tensor', 'dp')
The draws below stay inside these ranges and needn't reach their ends.
Inputs may be any that keep to these rules, and one draw needn't show every extreme that they name: `seq_lengths`: among the 2 sequences of each index of dp, one has the full length 1024.
All inputs are finite; a program needn't handle non-finite values.
Results may differ from the reference program's by a relative error of at most 0.018.
Values may be sent and summed in bfloat16 or wider, within the bound.
A program may use at most 192 MiB of HBM per device.

```python
import jax
import jax.numpy as jnp
from jax import lax

MODEL_WIDTH = 1024
H = 24
HEAD_SIZE = 64
N = 128
KCONV = 4
QUERY_HEADS = 8
KEY_VALUE_HEADS = 2
F = 2048
GH = 6
LEN = 1024
SEQ_DEV = 2
DI = 1536
SEQS = 16
N_TENSOR = 4


def draw_seq_lengths(key, part):
    key = jax.random.fold_in(key, 7)
    first_key, second_key, third_key = jax.random.split(key, 3)
    row_count = SEQS // SEQ_DEV
    lengths = jax.random.randint(first_key, (row_count, SEQ_DEV), LEN // 4, LEN + 1)
    full_at = jax.random.randint(second_key, (row_count, 1), 0, SEQ_DEV)
    slots = jnp.arange(SEQ_DEV, dtype=jnp.int32)[None, :]
    lengths = jnp.where(slots == full_at, LEN, lengths)
    short_row = jax.random.randint(third_key, (), 0, row_count)
    row_ids = jnp.arange(row_count, dtype=jnp.int32)[:, None]
    short_at = (full_at + 1) % SEQ_DEV
    lengths = jnp.where((row_ids == short_row) & (slots == short_at), LEN // 4, lengths)
    return lengths.reshape(SEQS).astype(jnp.int32)


def block_scale(own_key, extent, pieces, least, largest):
    def one(position, parts):
        steps = jax.random.uniform(jax.random.fold_in(jax.random.fold_in(own_key, 6), position), (parts,), jnp.float32, least / len(pieces), largest / len(pieces))
        return jnp.repeat(jnp.exp(steps), extent[position] // parts).reshape((-1,) + (1,) * (len(extent) - position - 1))

    factor_of = one(*pieces[0])
    for cut in pieces[1:]:
        factor_of = factor_of * one(*cut)
    return factor_of


def bell_draw(stream_key, dims, width, limit, cuts=(), held_as=jnp.bfloat16):
    result = jax.random.normal(stream_key, dims, jnp.float32) * width
    if len(cuts) > 0:
        result = block_scale(stream_key, dims, cuts, -0.22, 0.18) * result
    return jnp.clip(result, min=-limit, max=limit).astype(held_as)


def setup_inputs(seed: int = 0) -> dict:
    arg_keys = jax.random.split(jax.random.key(seed), 21)
    return {
        "layer_in": bell_draw(arg_keys[0], (SEQS, LEN, MODEL_WIDTH), 1.0, 6.0, ((0, 8), (1, 4))),
        "seq_lengths": draw_seq_lengths(jax.random.fold_in(arg_keys[20], 71), 0),
        "out_grad": bell_draw(arg_keys[2], (SEQS, LEN, MODEL_WIDTH), 1.0, 6.0, ((0, 8), (1, 4))),
        "norm_gain": jnp.clip(1.0 + 0.1 * jax.random.normal(arg_keys[3], (MODEL_WIDTH,), jnp.float32), 0.5, 1.5),
        "mixer_weight": bell_draw(arg_keys[4], (MODEL_WIDTH, 2, DI), MODEL_WIDTH ** -0.5, 0.1875, ((0, 8), (2, 4))),
        "step_weight": bell_draw(arg_keys[5], (MODEL_WIDTH, H), (4 * MODEL_WIDTH) ** -0.5, 0.09375, ((0, 8), (1, 4))),
        "state_weight": bell_draw(arg_keys[6], (MODEL_WIDTH, 2, N), MODEL_WIDTH ** -0.5, 0.1875, ((0, 8),)),
        "query_weight": bell_draw(arg_keys[7], (MODEL_WIDTH, QUERY_HEADS * HEAD_SIZE), MODEL_WIDTH ** -0.5, 0.1875, ((0, 8), (1, 4))),
        "key_value_weight": bell_draw(arg_keys[8], (MODEL_WIDTH, 2, KEY_VALUE_HEADS * HEAD_SIZE), MODEL_WIDTH ** -0.5, 0.1875, ((0, 8),)),
        "conv_channels": bell_draw(arg_keys[9], (KCONV, DI), KCONV ** -0.5, 3.0, ((1, 4),), jnp.float32),
        "conv_states": bell_draw(arg_keys[10], (KCONV, 2, N), KCONV ** -0.5, 3.0, (), jnp.float32),
        "step_bias": jnp.clip(-7.0 + 4.0 * jax.random.uniform(arg_keys[11], (H,), jnp.float32) ** block_scale(arg_keys[11], (H,), ((0, 4),), -0.2, 0.2), -7.0, -3.0),
        "decay_log": jnp.clip(1.5 * jax.random.uniform(arg_keys[12], (H,), jnp.float32) ** block_scale(arg_keys[12], (H,), ((0, 4),), -0.2, 0.2), 0.0, 1.5),
        "skip_scale": jnp.clip(0.5 + 1.0 * jax.random.uniform(arg_keys[13], (H,), jnp.float32) ** block_scale(arg_keys[13], (H,), ((0, 4),), -0.2, 0.2), 0.5, 1.5),
        "group_gain": jnp.clip(1.0 + 0.1 * jax.random.normal(arg_keys[14], (DI,), jnp.float32), 0.5, 1.5),
        "mamba_proj": bell_draw(arg_keys[15], (DI, MODEL_WIDTH), DI ** -0.5, 0.15625, ((0, 4), (1, 8))),
        "attn_proj": bell_draw(arg_keys[16], (QUERY_HEADS * HEAD_SIZE, MODEL_WIDTH), (QUERY_HEADS * HEAD_SIZE // 16) ** -0.5, 1.0, ((0, 4), (1, 8))),
        "ffn_gain": jnp.clip(1.0 + 0.1 * jax.random.normal(arg_keys[17], (MODEL_WIDTH,), jnp.float32), 0.5, 1.5),
        "ffn_weight": bell_draw(arg_keys[18], (MODEL_WIDTH, 2, F), MODEL_WIDTH ** -0.5, 0.1875, ((0, 8), (2, 4))),
        "ffn_down": bell_draw(arg_keys[19], (F, MODEL_WIDTH), F ** -0.5, 0.125, ((0, 4), (1, 8))),
    }


EPS = 1e-05
THETA = 10000.0
MASKED = -1e+30

@jax.custom_vjp
def low(v):
    return lax.optimization_barrier(v.astype(jnp.bfloat16)).astype(jnp.float32)

@jax.custom_vjp
def low_back(v):
    return v

def low_keep(v):
    return (low(v), None)

def low_pass(kept, grad):
    return (grad,)

def back_keep(v):
    return (v, None)

def back_low(kept, grad):
    return (low(grad),)
low.defvjp(low_keep, low_pass)
low_back.defvjp(back_keep, back_low)

def product(left, right):
    return jnp.dot(left, right, precision=lax.Precision.HIGHEST, preferred_element_type=jnp.float32)

def silu_act(values):
    return values / (1.0 + jnp.exp(-values))

def softplus(values):
    return jnp.log1p(jnp.exp(-jnp.abs(values))) + jnp.maximum(values, 0.0)

def rms_norm(values, gain_vec):
    return values * lax.rsqrt(lax.optimization_barrier(jnp.mean(values * values, axis=-1, keepdims=True)) + EPS) * gain_vec

def causal_conv(values, kernel):
    seq_count = values.shape[0]
    padded = jnp.concatenate([jnp.zeros((KCONV - 1, values.shape[1]), values.dtype), values], axis=0)
    summed = jnp.zeros_like(values)
    for offset in range(KCONV):
        summed = summed + padded[offset:offset + seq_count] * kernel[offset]
    return summed

def rotary(values):
    seq_count = values.shape[0]
    head_count = values.shape[1] // HEAD_SIZE
    half_dim = HEAD_SIZE // 2
    freqs = THETA ** (-jnp.arange(half_dim, dtype=jnp.float32) * 2.0 / HEAD_SIZE)
    angles = jnp.arange(seq_count, dtype=jnp.float32)[:, None] * freqs[None, :]
    cosine = jnp.cos(angles)[:, None, :]
    sine = jnp.sin(angles)[:, None, :]
    shaped = values.reshape(seq_count, head_count, HEAD_SIZE)
    first_half = shaped[..., :half_dim]
    second_half = shaped[..., half_dim:]
    turned = jnp.concatenate([first_half * cosine - second_half * sine, second_half * cosine + first_half * sine], axis=-1)
    return turned.reshape(seq_count, head_count * HEAD_SIZE)

def attention_front(query_proj, key_part):
    return (rotary(query_proj) * HEAD_SIZE ** (-0.5), rotary(key_part))

def mamba_front(chan_in, state_in, step_in, conv_chan, conv_state, bias_vec, decay_vec):
    chan_act = silu_act(causal_conv(chan_in, conv_chan))
    state_act = silu_act(causal_conv(state_in, conv_state))
    step_act = softplus(step_in + bias_vec)
    cumul = jnp.cumsum(-jnp.exp(decay_vec) * step_act, axis=0)
    return (chan_act, state_act, step_act, cumul)

def head_mix(gram_mat, cumul_head, step_head, chan_head):
    seq_count = gram_mat.shape[0]
    causal = jnp.arange(seq_count)[:, None] >= jnp.arange(seq_count)[None, :]
    spread = jnp.where(causal, cumul_head[:, None] - cumul_head[None, :], 0.0)
    mixing = jnp.where(causal, gram_mat * jnp.exp(spread), 0.0)
    return (mixing, chan_head * step_head[:, None])

def mamba_tail(state_out, chan_act, gate_val, skip_vec, gain_vec):
    seq_count, columns = chan_act.shape
    skipped = state_out + chan_act * jnp.repeat(skip_vec, HEAD_SIZE)
    gated = skipped * silu_act(gate_val)
    grouped = gated.reshape(seq_count, columns // (GH * HEAD_SIZE), GH * HEAD_SIZE)
    normed = grouped * lax.rsqrt(lax.optimization_barrier(jnp.mean(grouped * grouped, axis=-1, keepdims=True)) + EPS)
    return normed.reshape(seq_count, columns) * gain_vec

def swiglu(gate_up):
    half_cols = gate_up.shape[1] // 2
    return silu_act(gate_up[:, :half_cols]) * gate_up[:, half_cols:]

def layer(x_value, seq_len, params):
    norm_gain, mixer_w, step_w, state_w, query_w, keyval_w, conv_chan, conv_state, step_bias, decay_log, skip_scale, group_gain, mamba_w, attn_w, ffn_gain, ffn_w, down_w = params
    positions = jnp.arange(LEN, dtype=jnp.int32)
    valid_rows = (positions < seq_len).astype(jnp.float32)[:, None]
    allowed = (positions[None, :] <= positions[:, None]) & (positions[None, :] < seq_len)
    normed = low(rms_norm(x_value, norm_gain))
    heads_dev = H // N_TENSOR
    chans = heads_dev * HEAD_SIZE
    query_head_count = QUERY_HEADS // N_TENSOR
    queries_per_group = QUERY_HEADS // KEY_VALUE_HEADS
    mixed = jnp.zeros((LEN, MODEL_WIDTH), jnp.float32)
    for group_idx in range(N_TENSOR):
        chan_cols = slice(group_idx * chans, (group_idx + 1) * chans)
        head_cols = slice(group_idx * heads_dev, (group_idx + 1) * heads_dev)
        query_cols = slice(group_idx * query_head_count * HEAD_SIZE, (group_idx + 1) * query_head_count * HEAD_SIZE)
        key_value_head = group_idx * query_head_count // queries_per_group
        gate_chan = low_back(product(normed, mixer_w[:, :, chan_cols].reshape(MODEL_WIDTH, 2 * chans)))
        step_in = low_back(product(normed, step_w[:, head_cols]))
        state_in = low_back(product(normed, state_w.reshape(MODEL_WIDTH, 2 * N)))
        chan_act, state_act, step_act, cumul = mamba_front(gate_chan[:, chans:], state_in, step_in, conv_chan[:, chan_cols], conv_state.reshape(KCONV, 2 * N), step_bias[head_cols], decay_log[head_cols])
        gram_mat = low_back(product(low(state_act[:, N:]), low(state_act[:, :N]).T))
        mixing, inputs = jax.vmap(head_mix, in_axes=(None, 1, 1, 1))(gram_mat, cumul, step_act, chan_act.reshape(LEN, heads_dev, HEAD_SIZE))
        state_out = jnp.einsum('hts,hsp->thp', low(mixing), low(inputs), precision=lax.Precision.HIGHEST)
        state_out = low_back(state_out.reshape(LEN, chans))
        tail_val = low(mamba_tail(state_out, chan_act, gate_chan[:, :chans], skip_scale[head_cols], group_gain[chan_cols]))
        mixed = mixed + product(tail_val, mamba_w[chan_cols, :])
        query_proj = low_back(product(normed, query_w[:, query_cols]))
        keyval_proj = low_back(product(normed, keyval_w[:, :, key_value_head * HEAD_SIZE:(key_value_head + 1) * HEAD_SIZE].reshape(MODEL_WIDTH, 2 * HEAD_SIZE)))
        query_rot, key_rot = attention_front(query_proj, keyval_proj[:, :HEAD_SIZE])
        query_rot = low(query_rot)
        key_rot = low(key_rot)
        value_low = low(keyval_proj[:, HEAD_SIZE:])
        head_outs = []
        for head_idx in range(query_head_count):
            scores = low_back(product(query_rot[:, head_idx * HEAD_SIZE:(head_idx + 1) * HEAD_SIZE], key_rot.T))
            scores = jnp.where(allowed, scores, MASKED)
            row_peak = lax.optimization_barrier(jnp.max(scores, axis=-1, keepdims=True))
            exp_scores = jnp.exp(scores - row_peak)
            probs = exp_scores / lax.optimization_barrier(jnp.sum(exp_scores, axis=-1, keepdims=True))
            head_outs.append(product(low(probs), value_low))
        attn_val = low(low_back(jnp.concatenate(head_outs, axis=1)))
        mixed = mixed + product(attn_val, attn_w[query_cols, :])
    mixed = low_back(mixed)
    hidden = x_value + mixed
    normed_two = low(rms_norm(hidden, ffn_gain))
    gate_up = low_back(product(normed_two, ffn_w.reshape(MODEL_WIDTH, 2 * F)))
    act_val = low(swiglu(gate_up))
    ffn_out = low_back(product(act_val, down_w))
    return valid_rows * (hidden + ffn_out)

def reference(layer_in, seq_lengths, out_grad, norm_gain, mixer_weight, step_weight, state_weight, query_weight, key_value_weight, conv_channels, conv_states, step_bias, decay_log, skip_scale, group_gain, mamba_proj, attn_proj, ffn_gain, ffn_weight, ffn_down):
    params = tuple((item.astype(jnp.float32) for item in (norm_gain, mixer_weight, step_weight, state_weight, query_weight, key_value_weight, conv_channels, conv_states, step_bias, decay_log, skip_scale, group_gain, mamba_proj, attn_proj, ffn_gain, ffn_weight, ffn_down)))
    zero_grads = tuple((jnp.zeros(item.shape, jnp.float32) for item in params))

    def one_sequence(totals, items):
        seq_in, seq_len, seq_grad = items

        def forward(x_value, weights):
            return layer(x_value, seq_len, weights)
        seq_out, pull = jax.vjp(forward, seq_in.astype(jnp.float32), params)
        grad_x, grad_params = pull(seq_grad.astype(jnp.float32))
        totals = tuple((left + right for left, right in zip(totals, grad_params)))
        return (totals, (seq_out.astype(jnp.bfloat16), grad_x.astype(jnp.bfloat16)))
    totals, outputs = lax.scan(one_sequence, zero_grads, (layer_in, seq_lengths, out_grad))
    return (outputs[0], outputs[1], totals[0], totals[1], totals[2], totals[3], totals[4], totals[5], totals[6], totals[7], totals[8], totals[9], totals[10], totals[11], totals[12], totals[13], totals[14], totals[15], totals[16])
```

```python
import jax
import jax.numpy as jnp
from jax import lax
from jax.experimental import pallas as pl
from jax.experimental.pallas import tpu as pltpu
from jax.sharding import Mesh
from jax.sharding import PartitionSpec as P

HEAD_SIZE = 64
N = 128
KCONV = 4
GH = 6
EPS = 1e-05
THETA = 10000.0
MASKED = -1e30
SWAP = [(0, 1), (1, 0)]


def low(values):
    return values.astype(jnp.bfloat16)


def wide(values):
    return values.astype(jnp.float32)


def dot(left, right):
    return jnp.dot(left, right, preferred_element_type=jnp.float32)


def dot_nt(left, right):
    return lax.dot_general(
        left, right, (((1,), (1,)), ((), ())), preferred_element_type=jnp.float32
    )


def dot_tn(left, right):
    return lax.dot_general(
        left, right, (((0,), (0,)), ((), ())), preferred_element_type=jnp.float32
    )


def dot_fine(left, right):
    high = low(right)
    rest = right - wide(high)
    mid = low(rest)
    last = low(rest - wide(mid))
    return dot(left, high) + dot(left, mid) + dot(left, last)


def dot_by(left, right):
    high = low(left)
    rest = left - wide(high)
    mid = low(rest)
    last = low(rest - wide(mid))
    return dot(high, right) + dot(mid, right) + dot(last, right)


def sigmoid(values):
    return 1.0 / (1.0 + jnp.exp(-values))


def turn(values, cosine, sine):
    lane = lax.broadcasted_iota(jnp.int32, values.shape, 1)
    half = HEAD_SIZE // 2
    up = pltpu.roll(values, 128 - half, 1)
    down = pltpu.roll(values, half, 1)
    return values * cosine + jnp.where(lane % HEAD_SIZE < half, up, down) * sine


def turn_back(values, cosine, sine):
    lane = lax.broadcasted_iota(jnp.int32, values.shape, 1)
    half = HEAD_SIZE // 2
    turned = values * sine
    up = pltpu.roll(turned, 128 - half, 1)
    down = pltpu.roll(turned, half, 1)
    return values * cosine + jnp.where(lane % HEAD_SIZE < half, up, down)


SCALE = HEAD_SIZE ** (-0.5)
ROWS = 256


def key_value_parts(kv, cosine, sine):
    lane = lax.broadcasted_iota(jnp.int32, kv.shape, 1)
    key = jnp.where(lane < HEAD_SIZE, turn(kv, cosine, sine), 0.0)
    value = jnp.where(lane < HEAD_SIZE, 0.0, kv)
    keys = (low(key), low(pltpu.roll(key, HEAD_SIZE, 1)))
    values = (low(pltpu.roll(value, HEAD_SIZE, 1)), low(value))
    return keys, values


def block_scores(query, keys, begin, seq_len):
    scores = dot_nt(query, keys)
    row = lax.broadcasted_iota(jnp.int32, (scores.shape[0], 1), 0) + begin
    col = lax.broadcasted_iota(jnp.int32, scores.shape, 1)
    return jnp.where(col < jnp.minimum(row + 1, seq_len), scores, MASKED)


def attention_forward_kernel(len_ref, q_ref, kv_ref, cos_ref, sin_ref, out_ref, sum_ref):
    seq_len = len_ref[0]
    cosine, sine = cos_ref[...], sin_ref[...]
    keys, values = key_value_parts(kv_ref[...], cosine, sine)
    query = low(turn(q_ref[...], cosine, sine) * SCALE)
    rows = query.shape[0]
    lane = lax.broadcasted_iota(jnp.int32, (ROWS, 128), 1)
    for begin in range(0, rows, ROWS):
        end = begin + ROWS
        outs, sums = [], []
        for head in range(2):
            scores = block_scores(query[begin:end], keys[head][:end], begin, seq_len)
            peak = jnp.max(scores, axis=1, keepdims=True)
            exps = jnp.exp(scores - peak)
            total = jnp.sum(exps, axis=1, keepdims=True)
            probs = low(exps * (1.0 / total))
            outs.append(dot(probs, values[head][:end]))
            sums.append(peak + jnp.log(total))
        out_ref[begin:end, :] = low(outs[0] + outs[1])
        sum_ref[begin:end, :] = jnp.where(lane < HEAD_SIZE, sums[0], sums[1])


def attention_backward_kernel(
    len_ref, q_ref, kv_ref, cos_ref, sin_ref, sum_ref, grad_ref, dq_ref, dkv_ref, dk_acc, dv_acc
):
    seq_len = len_ref[0]
    cosine, sine = cos_ref[...], sin_ref[...]
    keys, values = key_value_parts(kv_ref[...], cosine, sine)
    query = low(turn(q_ref[...], cosine, sine) * SCALE)
    query_t = query.T
    rows = query.shape[0]
    group = pl.program_id(0)
    grad = low(grad_ref[...])
    grad_t = grad.T

    @pl.when(group == 0)
    def _():
        dk_acc[...] = jnp.zeros_like(dk_acc)
        dv_acc[...] = jnp.zeros_like(dv_acc)

    for begin in range(0, rows, ROWS):
        end = begin + ROWS
        dq = jnp.zeros((ROWS, 128), jnp.float32)
        for head in range(2):
            lanes = slice(head * HEAD_SIZE, (head + 1) * HEAD_SIZE)
            scores = block_scores(query[begin:end], keys[head][:end], begin, seq_len)
            at = head * HEAD_SIZE
            probs = jnp.exp(scores - sum_ref[begin:end, at : at + 1])
            dv_acc[:, :end] += dot(grad_t[lanes, begin:end], low(probs))
            dp = dot_nt(grad[begin:end], values[head][:end])
            inner = jnp.sum(probs * dp, axis=1, keepdims=True)
            ds = low(probs * (dp - inner))
            dq = dq + dot(ds, keys[head][:end])
            dk_acc[:, :end] += dot(query_t[lanes, begin:end], ds)
        dq = turn_back(dq * SCALE, cosine[begin:end], sine[begin:end])
        dq_ref[begin:end, :] = low(dq)

    @pl.when(group == pl.num_programs(0) - 1)
    def _():
        both = jnp.concatenate([dk_acc[...], dv_acc[...]], axis=0).T
        lane = lax.broadcasted_iota(jnp.int32, both.shape, 1)
        dkv_ref[...] = low(jnp.where(lane < HEAD_SIZE, turn_back(both, cosine, sine), both))


def attention_specs(rows, group_cols):
    whole = pl.BlockSpec((rows, 128), lambda g: (0, 0))
    return [
        pl.BlockSpec(memory_space=pltpu.SMEM),
        pl.BlockSpec((rows, 128), lambda g: (0, g * (group_cols // 128) + 6)),
        pl.BlockSpec((rows, 128), lambda g: (0, 2 * (group_cols // 128) + 2)),
        whole,
        whole,
    ]


BIG = 60 * 1024 * 1024


def attention_forward(seq_len, proj, cosine, sine, group_cols):
    rows = proj.shape[0]
    pairs = pl.BlockSpec((rows, 128), lambda g: (0, g))
    return pl.pallas_call(
        attention_forward_kernel,
        grid=(2,),
        in_specs=attention_specs(rows, group_cols),
        out_specs=[pairs, pairs],
        out_shape=[
            jax.ShapeDtypeStruct((rows, 256), jnp.bfloat16),
            jax.ShapeDtypeStruct((rows, 256), jnp.float32),
        ],
        compiler_params=pltpu.CompilerParams(vmem_limit_bytes=BIG),
        name="attention_forward",
    )(seq_len, proj, proj, cosine, sine)


def attention_backward(seq_len, proj, cosine, sine, sums, grad, group_cols, grad_at):
    rows = proj.shape[0]
    pairs = pl.BlockSpec((rows, 128), lambda g: (0, g))
    return pl.pallas_call(
        attention_backward_kernel,
        grid=(2,),
        in_specs=attention_specs(rows, group_cols)
        + [pairs, pl.BlockSpec((rows, 128), lambda g: (0, grad_at + g))],
        out_specs=[pairs, pl.BlockSpec((rows, 128), lambda g: (0, 0))],
        out_shape=[
            jax.ShapeDtypeStruct((rows, 256), jnp.bfloat16),
            jax.ShapeDtypeStruct((rows, 128), jnp.bfloat16),
        ],
        scratch_shapes=[
            pltpu.VMEM((HEAD_SIZE, rows), jnp.float32),
            pltpu.VMEM((HEAD_SIZE, rows), jnp.float32),
        ],
        compiler_params=pltpu.CompilerParams(vmem_limit_bytes=BIG),
        name="attention_backward",
    )(seq_len, proj, proj, cosine, sine, sums, grad)


CHUNK = 128
GROUP = GH * HEAD_SIZE
PAIRS = GH // 2
CONV = 2 * GROUP + 2 * N
SHARED = 2048


def triangle():
    row = lax.broadcasted_iota(jnp.int32, (CHUNK, CHUNK), 0)
    col = lax.broadcasted_iota(jnp.int32, (CHUNK, CHUNK), 1)
    return col <= row


def pair_lanes(values, pair):
    lane = lax.broadcasted_iota(jnp.int32, (values.shape[0], 128), 1)
    at = 2 * pair
    return jnp.where(lane < HEAD_SIZE, values[:, at : at + 1], values[:, at + 1 : at + 2])


def split_pair(values):
    lane = lax.broadcasted_iota(jnp.int32, values.shape, 1)
    empty = jnp.zeros_like(values)
    return jnp.concatenate(
        [jnp.where(lane < HEAD_SIZE, values, empty), jnp.where(lane < HEAD_SIZE, empty, values)],
        axis=0,
    )


def conv_pre(buf_ref, taps_ref, begin, size):
    total = buf_ref[5 : 5 + CHUNK, begin : begin + size] * taps_ref[0:1, begin : begin + size]
    for tap in range(1, KCONV):
        total = total + (
            buf_ref[5 + tap : 5 + tap + CHUNK, begin : begin + size]
            * taps_ref[tap : tap + 1, begin : begin + size]
        )
    return total


def load_conv(buf_ref, proj_ref):
    for group in range(2):
        at = group * 1024 + GROUP
        buf_ref[8:, group * GROUP : (group + 1) * GROUP] = proj_ref[:, at : at + GROUP]
    buf_ref[8:, 2 * GROUP :] = proj_ref[:, SHARED : SHARED + 2 * N]


def group_steps(proj_ref, bias_ref, decay_ref, group, lower):
    at = group * 1024 + 896
    raw = proj_ref[:, at : at + 128] + bias_ref[group : group + 1, :]
    step = jnp.log1p(jnp.exp(-jnp.abs(raw))) + jnp.maximum(raw, 0.0)
    rate = -jnp.exp(decay_ref[group : group + 1, :])
    cumul = dot_fine(lower, rate * step)
    return raw, step, rate, cumul


def head_decay(cumul, cumul_t, head, mask):
    spread = cumul[:, head : head + 1] - cumul_t[head : head + 1, :]
    return jnp.exp(jnp.where(mask, spread, MASKED))


def mamba_forward_kernel(
    proj_ref,
    attn_ref,
    taps_ref,
    bias_ref,
    decay_ref,
    skip_ref,
    gain_ref,
    both_ref,
    out_ref,
    states_ref,
    buf_ref,
    state_ref,
):
    chunk = pl.program_id(0)

    @pl.when(chunk == 0)
    def _():
        buf_ref[0:8, :] = jnp.zeros((8, CONV), jnp.float32)
        state_ref[...] = jnp.zeros_like(state_ref)

    load_conv(buf_ref, proj_ref)
    mask = triangle()
    lower = mask.astype(jnp.bfloat16)
    pre = conv_pre(buf_ref, taps_ref, 2 * GROUP, 2 * N)
    state_act = low(pre * sigmoid(pre))
    b_rows, c_rows = state_act[:, :N], state_act[:, N:]
    gram = dot_nt(c_rows, b_rows)
    b_cols = b_rows.T
    for group in range(2):
        cols = slice(group * GROUP, (group + 1) * GROUP)
        _, step, _, cumul = group_steps(proj_ref, bias_ref, decay_ref, group, lower)
        cumul_t = cumul.T
        last = cumul[CHUNK - 1 : CHUNK, :]
        state = state_ref[:, cols]
        states_ref[0, :, cols] = state
        from_state = dot(c_rows, low(state))
        gated = []
        for pair in range(PAIRS):
            at = group * GROUP + pair * 128
            pre = conv_pre(buf_ref, taps_ref, at, 128)
            chan = pre * sigmoid(pre)
            inputs = low(chan * pair_lanes(step, pair))
            mixing = jnp.concatenate(
                [
                    low(gram * head_decay(cumul, cumul_t, 2 * pair + side, mask))
                    for side in range(2)
                ],
                axis=1,
            )
            lanes = slice(pair * 128, (pair + 1) * 128)
            inner = pair_lanes(cumul, pair)
            out = dot(mixing, split_pair(inputs)) + jnp.exp(inner) * from_state[:, lanes]
            out_ref[:, at : at + 128] = out
            last_lanes = pair_lanes(last, pair)
            x_end = low(jnp.exp(last_lanes - inner) * wide(inputs))
            state_ref[:, at : at + 128] = jnp.exp(last_lanes) * state[:, lanes] + dot(
                b_cols, x_end
            )
            gate = proj_ref[:, group * 1024 + pair * 128 : group * 1024 + pair * 128 + 128]
            skipped = out + chan * skip_ref[:, at : at + 128]
            gated.append(skipped * (gate * sigmoid(gate)))
        square = sum(jnp.sum(part * part, axis=1, keepdims=True) for part in gated)
        scale = lax.rsqrt(square * (1.0 / GROUP) + EPS)
        for pair in range(PAIRS):
            at = group * GROUP + pair * 128
            to = group * 512 + pair * 128
            both_ref[:, to : to + 128] = low(gated[pair] * scale * gain_ref[:, at : at + 128])
        to = group * 512 + GROUP
        both_ref[:, to : to + 128] = attn_ref[:, group * 128 : (group + 1) * 128]
    buf_ref[0:8, :] = buf_ref[CHUNK : CHUNK + 8, :]


def mamba_forward(proj, attn, taps, bias, decay, skip, gain):
    rows, columns = proj.shape
    chunks = rows // CHUNK

    def whole(value):
        return pl.BlockSpec(value.shape, lambda k: (0, 0))

    return pl.pallas_call(
        mamba_forward_kernel,
        grid=(chunks,),
        in_specs=[
            pl.BlockSpec((CHUNK, columns), lambda k: (k, 0)),
            pl.BlockSpec((CHUNK, 256), lambda k: (k, 0)),
        ]
        + [whole(value) for value in (taps, bias, decay, skip, gain)],
        out_specs=[
            pl.BlockSpec((CHUNK, 1024), lambda k: (k, 0)),
            pl.BlockSpec((CHUNK, 2 * GROUP), lambda k: (k, 0)),
            pl.BlockSpec((1, N, 2 * GROUP), lambda k: (k, 0, 0)),
        ],
        out_shape=[
            jax.ShapeDtypeStruct((rows, 1024), jnp.bfloat16),
            jax.ShapeDtypeStruct((rows, 2 * GROUP), jnp.float32),
            jax.ShapeDtypeStruct((chunks, N, 2 * GROUP), jnp.float32),
        ],
        scratch_shapes=[
            pltpu.VMEM((CHUNK + 8, CONV), jnp.float32),
            pltpu.VMEM((N, 2 * GROUP), jnp.float32),
        ],
        compiler_params=pltpu.CompilerParams(vmem_limit_bytes=BIG),
        name="mamba_forward",
    )(proj, attn, taps, bias, decay, skip, gain)


def silu_slope(values, sig):
    return sig * (1.0 + values * (1.0 - sig))


def mamba_backward_kernel(
    proj_ref,
    before_ref,
    out_ref,
    states_ref,
    back_ref,
    dq_ref,
    dkv_ref,
    taps_ref,
    bias_ref,
    decay_ref,
    skip_ref,
    gain_ref,
    dproj_ref,
    dtaps_ref,
    dgain_ref,
    dskip_ref,
    dbias_ref,
    ddecay_ref,
    buf_ref,
    grad_buf,
    after_ref,
    flow_ref,
):
    step_at = pl.program_id(0)

    @pl.when(step_at == 0)
    def _():
        for ref in (dtaps_ref, dgain_ref, dskip_ref, dbias_ref, ddecay_ref, after_ref, flow_ref):
            ref[...] = jnp.zeros_like(ref)
        grad_buf[CHUNK:, :] = jnp.zeros((8, CONV), jnp.float32)

    inside = jnp.where(step_at == pl.num_programs(0) - 1, 0.0, 1.0)
    for group in range(2):
        at = group * 1024 + GROUP
        buf_ref[0:8, group * GROUP : (group + 1) * GROUP] = before_ref[:, at : at + GROUP] * inside
    buf_ref[0:8, 2 * GROUP :] = before_ref[:, SHARED : SHARED + 2 * N] * inside
    load_conv(buf_ref, proj_ref)
    mask = triangle()
    lower = mask.astype(jnp.bfloat16)
    row = lax.broadcasted_iota(jnp.int32, (CHUNK, CHUNK), 0)
    col = lax.broadcasted_iota(jnp.int32, (CHUNK, CHUNK), 1)
    upper = (row <= col).astype(jnp.bfloat16)
    pre_state = conv_pre(buf_ref, taps_ref, 2 * GROUP, 2 * N)
    sig_state = sigmoid(pre_state)
    state_act = low(pre_state * sig_state)
    b_rows, c_rows = state_act[:, :N], state_act[:, N:]
    gram = dot_nt(c_rows, b_rows)
    c_cols = c_rows.T
    dgram = jnp.zeros((CHUNK, CHUNK), jnp.float32)
    d_c = jnp.zeros((CHUNK, N), jnp.float32)
    d_b = jnp.zeros((CHUNK, N), jnp.float32)
    for group in range(2):
        raw, step, rate, cumul = group_steps(proj_ref, bias_ref, decay_ref, group, lower)
        cumul_t = cumul.T
        last = cumul[CHUNK - 1 : CHUNK, :]
        pres, sigs, chans, gates, gate_sigs, skips, gated = [], [], [], [], [], [], []
        for pair in range(PAIRS):
            at = group * GROUP + pair * 128
            pre = conv_pre(buf_ref, taps_ref, at, 128)
            sig = sigmoid(pre)
            chan = pre * sig
            gate = proj_ref[:, group * 1024 + pair * 128 : group * 1024 + pair * 128 + 128]
            gate_sig = sigmoid(gate)
            skipped = out_ref[:, at : at + 128] + chan * skip_ref[:, at : at + 128]
            pres.append(pre)
            sigs.append(sig)
            chans.append(chan)
            gates.append(gate)
            gate_sigs.append(gate_sig)
            skips.append(skipped)
            gated.append(skipped * (gate * gate_sig))
        square = sum(jnp.sum(part * part, axis=1, keepdims=True) for part in gated)
        scale = lax.rsqrt(square * (1.0 / GROUP) + EPS)
        grads = []
        cross = jnp.zeros((CHUNK, 1), jnp.float32)
        for pair in range(PAIRS):
            at = group * GROUP + pair * 128
            grad = back_ref[:, group * 512 + pair * 128 : group * 512 + pair * 128 + 128]
            dgain_ref[:, at : at + 128] += jnp.sum(grad * gated[pair] * scale, axis=0, keepdims=True)
            grad = grad * gain_ref[:, at : at + 128]
            cross = cross + jnp.sum(gated[pair] * grad, axis=1, keepdims=True)
            grads.append(grad)
        cross = cross * (1.0 / GROUP) * scale * scale * scale
        dstep = jnp.zeros((CHUNK, 128), jnp.float32)
        flow = jnp.zeros((CHUNK, 128), jnp.float32)
        flow_end = flow_ref[group : group + 1, :]
        flow_next = jnp.zeros((1, 128), jnp.float32)
        for pair in range(PAIRS):
            at = group * GROUP + pair * 128
            head_of_lane = lax.broadcasted_iota(jnp.int32, (128, 128), 0) // HEAD_SIZE + 2 * pair
            lane = lax.broadcasted_iota(jnp.int32, (128, 128), 1)
            pick = (head_of_lane == lane).astype(jnp.bfloat16)
            chan = chans[pair]
            grad = scale * grads[pair] - gated[pair] * cross
            gate, gate_sig = gates[pair], gate_sigs[pair]
            dgate = grad * skips[pair] * silu_slope(gate, gate_sig)
            to = group * 1024 + pair * 128
            dproj_ref[:, to : to + 128] = low(dgate)
            grad = grad * (gate * gate_sig)
            dskip_ref[:, at : at + 128] += jnp.sum(grad * chan, axis=0, keepdims=True)
            dchan = grad * skip_ref[:, at : at + 128]
            dout = low(grad)
            step_lanes = pair_lanes(step, pair)
            inputs = low(chan * step_lanes)
            halves = split_pair(inputs)
            decays = [head_decay(cumul, cumul_t, 2 * pair + side, mask) for side in range(2)]
            mixing = jnp.concatenate([low(gram * decay) for decay in decays], axis=1)
            dmix = dot_nt(dout, halves)
            dgram = dgram + dmix[:, :CHUNK] * decays[0] + dmix[:, CHUNK:] * decays[1]
            dinputs = dot_tn(mixing, dout)
            lane = lax.broadcasted_iota(jnp.int32, (CHUNK, 128), 1)
            dinputs = jnp.where(lane < HEAD_SIZE, dinputs[:CHUNK], dinputs[CHUNK:])
            inner = pair_lanes(cumul, pair)
            last_lanes = pair_lanes(last, pair)
            to_end = jnp.exp(last_lanes - inner)
            after = after_ref[:, at : at + 128]
            after_low = low(after)
            dinputs = dinputs + to_end * dot(b_rows, after_low)
            x_end = low(to_end * wide(inputs))
            g_start = low(jnp.exp(inner) * wide(dout))
            state = states_ref[0, :, at : at + 128]
            d_c = d_c + dot_nt(g_start, low(state))
            d_b = d_b + dot_nt(x_end, after_low)
            after = jnp.exp(last_lanes) * after + dot(c_cols, g_start)
            after_ref[:, at : at + 128] = after
            through = jnp.sum(after * state, axis=0, keepdims=True)
            flow_next = flow_next + dot_by(jnp.broadcast_to(through, (8, 128)), pick)[0:1]
            flow = flow + dot_by(
                wide(dout) * out_ref[:, at : at + 128] - wide(inputs) * dinputs, pick
            )
            dstep = dstep + dot_by(dinputs * chan, pick)
            dchan = dchan + dinputs * step_lanes
            grad_buf[0:CHUNK, at : at + 128] = dchan * silu_slope(pres[pair], sigs[pair])
        dcumul = dot_fine(upper, flow) + flow_end
        flow_ref[group : group + 1, :] = flow_next
        dstep = dstep + rate * dcumul
        ddecay_ref[group : group + 1, :] += jnp.sum(rate * step * dcumul, axis=0, keepdims=True)
        draw = dstep * sigmoid(raw)
        dbias_ref[group : group + 1, :] += jnp.sum(draw, axis=0, keepdims=True)
        to = group * 1024 + 896
        lane = lax.broadcasted_iota(jnp.int32, (CHUNK, 128), 1)
        dproj_ref[:, to : to + 128] = low(jnp.where(lane < GH, draw, 0.0))
        to = group * 1024 + 2 * GROUP
        dproj_ref[:, to : to + 128] = dq_ref[:, group * 128 : (group + 1) * 128]
    dgram_low = low(dgram)
    d_c = d_c + dot(dgram_low, b_rows)
    d_b = d_b + dot_tn(dgram_low, c_rows)
    slope = silu_slope(pre_state, sig_state)
    grad_buf[0:CHUNK, 2 * GROUP : 2 * GROUP + N] = d_b * slope[:, :N]
    grad_buf[0:CHUNK, 2 * GROUP + N :] = d_c * slope[:, N:]
    for at in range(0, CONV, 128):
        grad = jnp.zeros((CHUNK, 128), jnp.float32)
        here = grad_buf[0:CHUNK, at : at + 128]
        for tap in range(KCONV):
            shift = KCONV - 1 - tap
            grad = grad + (
                grad_buf[shift : shift + CHUNK, at : at + 128] * taps_ref[tap : tap + 1, at : at + 128]
            )
            dtaps_ref[tap : tap + 1, at : at + 128] += jnp.sum(
                here * buf_ref[5 + tap : 5 + tap + CHUNK, at : at + 128], axis=0, keepdims=True
            )
        if at < 2 * GROUP:
            to = (at // GROUP) * 1024 + GROUP + at % GROUP
        else:
            to = SHARED + at - 2 * GROUP
        dproj_ref[:, to : to + 128] = low(grad)
    dproj_ref[:, SHARED + 2 * N :] = dkv_ref[...]
    grad_buf[CHUNK:, :] = grad_buf[0:8, :]


def mamba_backward(proj, out, states, back, dq, dkv, taps, bias, decay, skip, gain):
    rows, columns = proj.shape
    chunks = rows // CHUNK

    def whole(value):
        return pl.BlockSpec(value.shape, lambda k: (0, 0))

    def rows_of(width):
        return pl.BlockSpec((CHUNK, width), lambda k: (chunks - 1 - k, 0))

    params = (taps, bias, decay, skip, gain)
    return pl.pallas_call(
        mamba_backward_kernel,
        grid=(chunks,),
        in_specs=[
            rows_of(columns),
            pl.BlockSpec(
                (8, columns),
                lambda k: (jnp.maximum((chunks - 1 - k) * (CHUNK // 8) - 1, 0), 0),
            ),
            rows_of(2 * GROUP),
            pl.BlockSpec((1, N, 2 * GROUP), lambda k: (chunks - 1 - k, 0, 0)),
            rows_of(1024),
            rows_of(256),
            rows_of(128),
        ]
        + [whole(value) for value in params],
        out_specs=[rows_of(columns)]
        + [whole(value) for value in (taps, gain, skip, bias, decay)],
        out_shape=[jax.ShapeDtypeStruct((rows, columns), jnp.bfloat16)]
        + [
            jax.ShapeDtypeStruct(value.shape, jnp.float32)
            for value in (taps, gain, skip, bias, decay)
        ],
        scratch_shapes=[
            pltpu.VMEM((CHUNK + 8, CONV), jnp.float32),
            pltpu.VMEM((CHUNK + 8, CONV), jnp.float32),
            pltpu.VMEM((N, 2 * GROUP), jnp.float32),
            pltpu.VMEM((8, 128), jnp.float32),
        ],
        compiler_params=pltpu.CompilerParams(vmem_limit_bytes=BIG),
        name="mamba_backward",
    )(proj, proj, out, states, back, dq, dkv, *params)


def rms_norm(values, gain_vec):
    return values * lax.rsqrt(jnp.mean(values * values, axis=-1, keepdims=True) + EPS) * gain_vec


def turn_tables(seq_count, head_count):
    half_dim = HEAD_SIZE // 2
    freqs = THETA ** (-jnp.arange(half_dim, dtype=jnp.float32) * 2.0 / HEAD_SIZE)
    angles = jnp.arange(seq_count, dtype=jnp.float32)[:, None] * freqs[None, :]
    cosine, sine = jnp.cos(angles), jnp.sin(angles)
    return (
        jnp.tile(jnp.concatenate([cosine, cosine], axis=1), (1, head_count)),
        jnp.tile(jnp.concatenate([-sine, sine], axis=1), (1, head_count)),
    )


def swiglu(gate_up):
    half_cols = gate_up.shape[1] // 2
    gate = gate_up[:, :half_cols]
    return gate * sigmoid(gate) * gate_up[:, half_cols:]


def swapped(values):
    return lax.ppermute(values, "core", SWAP)


def body(
    layer_in,
    seq_lengths,
    out_grad,
    norm_gain,
    mixer_weight,
    step_weight,
    state_weight,
    query_weight,
    key_value_weight,
    conv_channels,
    conv_states,
    step_bias,
    decay_log,
    skip_scale,
    group_gain,
    mamba_proj,
    attn_proj,
    ffn_gain,
    ffn_weight,
    ffn_down,
):
    core = lax.axis_index("core")
    place = lax.axis_index("tensor")
    first = core == 0
    seq_dev, rows_dev, model_dim = layer_in.shape
    groups = lax.axis_size("tensor")
    seq_total = rows_dev * groups
    half_rows = rows_dev // 2
    share = mixer_weight.shape[0]
    chans_dev = mixer_weight.shape[2]
    heads_dev = step_weight.shape[1]
    query_dev = query_weight.shape[1]
    hidden_dev = ffn_weight.shape[2]
    held = groups // 2
    step_pad = 128

    def mine(values):
        return lax.dynamic_slice_in_dim(values, core * held, held, 0)

    def other(values):
        return lax.dynamic_slice_in_dim(values, (1 - core) * held, held, 0)

    def in_order(own, others, axis):
        return jnp.where(
            first,
            jnp.concatenate([own, others], axis=axis),
            jnp.concatenate([others, own], axis=axis),
        )

    def flat(values):
        return values.transpose(1, 0, 2).reshape(values.shape[1], -1)

    def positions_in(values):
        shaped = values.reshape(seq_dev, 2, half_rows, model_dim)
        keep = lax.dynamic_index_in_dim(shaped, core, 1, False)
        send = lax.dynamic_index_in_dim(shaped, 1 - core, 1, False)
        four = in_order(keep, swapped(send), 0)
        own = lax.all_to_all(four, "tensor", 0, 0, tiled=True)
        both = in_order(own[:, None], swapped(own)[:, None], 1)
        return both.reshape(seq_total, model_dim)

    def positions_out(own):
        four = lax.all_to_all(own, "tensor", 0, 0, tiled=True)
        keep = lax.dynamic_slice_in_dim(four, core * seq_dev, seq_dev, 0)
        send = lax.dynamic_slice_in_dim(four, (1 - core) * seq_dev, seq_dev, 0)
        both = in_order(keep[:, None], swapped(send)[:, None], 1)
        return both.reshape(seq_dev, rows_dev, model_dim)

    def own_half(values):
        shaped = values.reshape(groups, 2, half_rows, -1)
        return lax.dynamic_index_in_dim(shaped, core, 1, False)

    def other_half(values):
        shaped = values.reshape(groups, 2, half_rows, -1)
        return lax.dynamic_index_in_dim(shaped, 1 - core, 1, False)

    x_low = positions_in(layer_in)
    pack_one = jnp.concatenate(
        [
            mixer_weight.reshape(share, 2 * chans_dev),
            query_weight,
            jnp.pad(step_weight, ((0, 0), (0, step_pad - heads_dev))),
        ],
        axis=1,
    )
    all_one = lax.all_gather(pack_one, "tensor", axis=0)
    kv_heads = key_value_weight.reshape(share, 2, 2, HEAD_SIZE)

    def lay_one(pack, at):
        return jnp.concatenate(
            [
                flat(pack),
                state_weight.reshape(share, 2 * N),
                lax.dynamic_index_in_dim(kv_heads, at, 2, False).reshape(share, 2 * HEAD_SIZE),
            ],
            axis=1,
        )

    own_one = lay_one(mine(all_one), core)
    their_one = lay_one(other(all_one), 1 - core)
    weight_one = lax.all_gather(
        in_order(own_one, swapped(their_one), 0), "plane", axis=0, tiled=True
    )

    pack_two = jnp.concatenate(
        [mamba_proj.T, attn_proj.T, ffn_weight.reshape(share, 2 * hidden_dev), ffn_down.T], axis=1
    )
    all_two = lax.all_gather(pack_two, "tensor", axis=0)
    out_dev = chans_dev + query_dev

    def lay_two(pack):
        cut = out_dev + hidden_dev
        return jnp.concatenate(
            [
                flat(pack[:, :, :out_dev]),
                flat(pack[:, :, out_dev:cut]),
                flat(pack[:, :, cut : cut + hidden_dev]),
                flat(pack[:, :, cut + hidden_dev :]),
            ],
            axis=1,
        )

    rows_two = in_order(lay_two(mine(all_two)), swapped(lay_two(other(all_two))), 0)
    edges = (0, held * out_dev, held * (out_dev + 2 * hidden_dev), held * (out_dev + 3 * hidden_dev))
    weight_two, gate_up_weight, down_weight = (
        lax.all_gather(rows_two[:, begin:end], "plane", axis=0, tiled=True)
        for begin, end in zip(edges[:-1], edges[1:])
    )

    small_in = jnp.concatenate(
        [conv_channels.reshape(-1), step_bias, decay_log, skip_scale, group_gain]
    )
    small_mine = mine(lax.all_gather(small_in, "tensor", axis=0))
    cuts = []
    at = 0
    for size in (KCONV * chans_dev, heads_dev, heads_dev, heads_dev, chans_dev):
        cuts.append(small_mine[:, at : at + size])
        at += size
    taps = cuts[0].reshape(held, KCONV, chans_dev).transpose(1, 0, 2).reshape(KCONV, -1)
    taps = jnp.concatenate([taps, conv_states.reshape(KCONV, 2 * N)], axis=1)
    bias = jnp.pad(cuts[1], ((0, 0), (0, step_pad - heads_dev)))
    decay = jnp.pad(cuts[2], ((0, 0), (0, step_pad - heads_dev)))
    skip = jnp.repeat(cuts[3].reshape(1, -1), HEAD_SIZE, axis=1)
    gain = cuts[4].reshape(1, -1)

    lengths = lax.all_gather(seq_lengths, "core", axis=0).reshape(-1)
    seq_len = lengths[place]
    len_one = seq_len.reshape(1)
    valid_rows = (jnp.arange(seq_total, dtype=jnp.int32) < seq_len).astype(jnp.float32)[:, None]

    x_rows = wide(x_low)
    normed = low(rms_norm(x_rows, norm_gain))
    proj = dot(normed, weight_one)
    group_cols = 2 * chans_dev + query_dev + step_pad
    cosine, sine = turn_tables(seq_total, 2)
    attn, log_sums = attention_forward(len_one, proj, cosine, sine, group_cols)
    both_low, state_out, states = mamba_forward(proj, attn, taps, bias, decay, skip, gain)

    mixed_part = low(dot_nt(both_low, weight_two))
    mixed = wide(mixed_part) + wide(swapped(mixed_part))
    hidden = x_rows + mixed
    normed_two = low(rms_norm(hidden, ffn_gain))
    gate_up = dot(normed_two, gate_up_weight)
    act, act_pull = jax.vjp(swiglu, gate_up)
    act_low = low(act)
    ffn_part = low(dot_nt(act_low, down_weight))
    ffn_own = wide(own_half(ffn_part)) + wide(swapped(other_half(ffn_part)))
    out_own = own_half(valid_rows) * (own_half(hidden) + ffn_own)
    layer_out = positions_out(low(out_own))

    grad_rows = valid_rows * wide(positions_in(out_grad))
    grad_low = low(grad_rows)
    grad_down = low(dot_tn(grad_low, act_low))
    (grad_gate_up,) = act_pull(dot(grad_low, down_weight))
    gate_up_low = low(grad_gate_up)
    grad_gate_up_weight = low(dot_tn(normed_two, gate_up_low))
    grad_two_part = low(dot_nt(gate_up_low, gate_up_weight))
    grad_two = wide(grad_two_part) + wide(swapped(grad_two_part))
    r_two = lax.rsqrt(jnp.mean(hidden * hidden, axis=-1, keepdims=True) + EPS)
    scaled = grad_two * ffn_gain
    grad_hidden = (
        grad_rows
        + r_two * scaled
        - hidden * (r_two**3 * jnp.mean(hidden * scaled, axis=-1, keepdims=True))
    )
    grad_ffn_gain = jnp.sum(own_half(hidden * r_two * grad_two), axis=(0, 1))
    grad_mixed = low(grad_hidden)

    def scatter(values):
        part = lax.psum_scatter(values, "plane", scatter_dimension=0, tiled=True)
        part = part.reshape(2, share, -1)
        return (
            lax.dynamic_index_in_dim(part, core, 0, False),
            lax.dynamic_index_in_dim(part, 1 - core, 0, False),
        )

    def by_group(values, widths):
        pieces = []
        at = 0
        for width in widths:
            piece = values[:, at : at + held * width]
            pieces.append(piece.reshape(share, held, width).transpose(1, 0, 2))
            at += held * width
        return jnp.concatenate(pieces, axis=2)

    def to_groups(own, theirs):
        whole = in_order(own, theirs, 0)
        return lax.psum_scatter(whole, "tensor", scatter_dimension=0, tiled=True)[0]

    def sum_rest(parts, widths):
        both = [scatter(part) for part in parts]
        own = by_group(jnp.concatenate([pair[0] for pair in both], axis=1), widths)
        theirs = by_group(jnp.concatenate([pair[1] for pair in both], axis=1), widths)
        return to_groups(own, swapped(theirs))

    sum_three = sum_rest((grad_gate_up_weight, grad_down), (hidden_dev,) * 3)
    grad_both = low(dot_tn(grad_mixed, both_low))
    sum_two = sum_rest((grad_both,), (out_dev,))

    back = dot(grad_mixed, weight_two)
    attn_back = jnp.concatenate(
        [low(back[:, chans_dev:out_dev]), low(back[:, out_dev + chans_dev :])], axis=1
    )
    grad_q, grad_kv = attention_backward(
        len_one, proj, cosine, sine, log_sums, attn_back, group_cols, 0
    )
    proj_grad, grad_taps, grad_gain, grad_skip_cols, grad_bias, grad_decay = mamba_backward(
        proj, state_out, states, back, grad_q, grad_kv, taps, bias, decay, skip, gain
    )
    grad_one = low(dot_tn(normed, proj_grad))
    own_grad, their_grad = scatter(grad_one)
    their_grad = swapped(their_grad)
    edge = held * group_cols
    shared_own = wide(own_grad[:, edge : edge + 2 * N]) + wide(their_grad[:, edge : edge + 2 * N])
    kv_both = in_order(
        own_grad[:, None, edge + 2 * N :], their_grad[:, None, edge + 2 * N :], 1
    )
    kv_both = kv_both.reshape(share, 2, 2, HEAD_SIZE).transpose(0, 2, 1, 3)
    shared_low = jnp.concatenate([low(shared_own), kv_both.reshape(share, -1)], axis=1)
    shared_sum = jnp.sum(wide(lax.all_gather(shared_low, "tensor", axis=0)), axis=0)
    sum_one = to_groups(
        by_group(own_grad[:, :edge], (group_cols,)), by_group(their_grad[:, :edge], (group_cols,))
    )

    grad_norm_part = low(dot_nt(proj_grad, weight_one))
    grad_norm_own = wide(own_half(grad_norm_part)) + wide(swapped(other_half(grad_norm_part)))
    x_own = wide(own_half(x_low))
    r_one = lax.rsqrt(jnp.mean(x_own * x_own, axis=-1, keepdims=True) + EPS)
    scaled = grad_norm_own * norm_gain
    grad_x = (
        own_half(grad_hidden)
        + r_one * scaled
        - x_own * (r_one**3 * jnp.mean(x_own * scaled, axis=-1, keepdims=True))
    )
    grad_norm_gain = jnp.sum(x_own * r_one * grad_norm_own, axis=(0, 1))
    input_grad = positions_out(low(grad_x))

    grad_skip = jnp.sum(grad_skip_cols.reshape(held, heads_dev, HEAD_SIZE), axis=-1)
    chan_taps = grad_taps[:, : held * chans_dev].reshape(KCONV, held, chans_dev)
    group_small = jnp.concatenate(
        [
            chan_taps.transpose(1, 0, 2).reshape(held, -1),
            grad_bias[:, :heads_dev],
            grad_decay[:, :heads_dev],
            grad_skip,
            grad_gain.reshape(held, -1),
        ],
        axis=1,
    )
    small_groups = in_order(group_small, jnp.zeros_like(group_small), 0)
    small_out = jnp.concatenate(
        [
            grad_norm_gain,
            grad_ffn_gain,
            grad_taps[:, held * chans_dev :].reshape(-1),
            small_groups.reshape(-1),
        ]
    )
    small_sum = lax.psum(small_out, ("plane", "core", "tensor"))
    group_sum = lax.dynamic_index_in_dim(
        small_sum[2 * model_dim + KCONV * 2 * N :].reshape(groups, -1), place, 0, False
    )
    pieces = []
    at = 0
    for size in (KCONV * chans_dev, heads_dev, heads_dev, heads_dev, chans_dev):
        pieces.append(group_sum[at : at + size])
        at += size

    one, two, three = wide(sum_one), wide(sum_two), wide(sum_three)
    return (
        layer_out,
        input_grad,
        small_sum[:model_dim],
        one[:, : 2 * chans_dev].reshape(share, 2, chans_dev),
        one[:, 2 * chans_dev + query_dev :][:, :heads_dev],
        shared_sum[:, : 2 * N].reshape(share, 2, N),
        one[:, 2 * chans_dev : 2 * chans_dev + query_dev],
        shared_sum[:, 2 * N :].reshape(share, 2, 2 * HEAD_SIZE),
        pieces[0].reshape(KCONV, chans_dev),
        small_sum[2 * model_dim : 2 * model_dim + KCONV * 2 * N].reshape(KCONV, 2, N),
        pieces[1],
        pieces[2],
        pieces[3],
        pieces[4],
        two[:, :chans_dev].T,
        two[:, chans_dev:].T,
        small_sum[model_dim : 2 * model_dim],
        three[:, : 2 * hidden_dev].reshape(share, 2, hidden_dev),
        three[:, 2 * hidden_dev :].T,
    )


def solution(mesh):
    rows, columns = mesh.devices.shape
    fine = Mesh(mesh.devices.reshape(rows // 2, 2, columns), ("plane", "core", "tensor"))
    dp = ("plane", "core")
    return jax.shard_map(
        body,
        mesh=fine,
        in_specs=(
            P(dp, "tensor", None),
            P(dp),
            P(dp, "tensor", None),
            P(),
            P(dp, None, "tensor"),
            P(dp, "tensor"),
            P(dp, None, None),
            P(dp, "tensor"),
            P(dp, None, None),
            P(None, "tensor"),
            P(),
            P("tensor"),
            P("tensor"),
            P("tensor"),
            P("tensor"),
            P("tensor", dp),
            P("tensor", dp),
            P(),
            P(dp, None, "tensor"),
            P("tensor", dp),
        ),
        out_specs=(
            P(dp, "tensor", None),
            P(dp, "tensor", None),
            P(),
            P(dp, None, "tensor"),
            P(dp, "tensor"),
            P(dp, None, None),
            P(dp, "tensor"),
            P(dp, None, None),
            P(None, "tensor"),
            P(),
            P("tensor"),
            P("tensor"),
            P("tensor"),
            P("tensor"),
            P("tensor", dp),
            P("tensor", dp),
            P(),
            P(dp, None, "tensor"),
            P("tensor", dp),
        ),
        check_vma=False,
    )
```

```python
import jax
import jax.numpy as jnp
from jax import lax
from jax.experimental import pallas as pl
from jax.experimental.pallas import tpu as pltpu
from jax.sharding import Mesh
from jax.sharding import PartitionSpec as P

HEAD_SIZE = 64
N = 128
KCONV = 4
GH = 6
EPS = 1e-05
THETA = 10000.0
MASKED = -1e30
SWAP = [(0, 1), (1, 0)]


def low(values):
    return values.astype(jnp.bfloat16)


def wide(values):
    return values.astype(jnp.float32)


def dot(left, right):
    return jnp.dot(left, right, preferred_element_type=jnp.float32)


def dot_nt(left, right):
    return lax.dot_general(
        left, right, (((1,), (1,)), ((), ())), preferred_element_type=jnp.float32
    )


def dot_tn(left, right):
    return lax.dot_general(
        left, right, (((0,), (0,)), ((), ())), preferred_element_type=jnp.float32
    )


def dot_fine(left, right):
    high = low(right)
    rest = right - wide(high)
    mid = low(rest)
    last = low(rest - wide(mid))
    return dot(left, high) + dot(left, mid) + dot(left, last)


def dot_by(left, right):
    high = low(left)
    rest = left - wide(high)
    mid = low(rest)
    last = low(rest - wide(mid))
    return dot(high, right) + dot(mid, right) + dot(last, right)


def sigmoid(values):
    return 1.0 / (1.0 + jnp.exp(-values))


def turn(values, cosine, sine):
    lane = lax.broadcasted_iota(jnp.int32, values.shape, 1)
    half = HEAD_SIZE // 2
    up = pltpu.roll(values, 128 - half, 1)
    down = pltpu.roll(values, half, 1)
    return values * cosine + jnp.where(lane % HEAD_SIZE < half, up, down) * sine


def turn_back(values, cosine, sine):
    lane = lax.broadcasted_iota(jnp.int32, values.shape, 1)
    half = HEAD_SIZE // 2
    turned = values * sine
    up = pltpu.roll(turned, 128 - half, 1)
    down = pltpu.roll(turned, half, 1)
    return values * cosine + jnp.where(lane % HEAD_SIZE < half, up, down)


SCALE = HEAD_SIZE ** (-0.5)
ROWS = 256


def key_value_parts(kv, cosine, sine):
    lane = lax.broadcasted_iota(jnp.int32, kv.shape, 1)
    key = jnp.where(lane < HEAD_SIZE, turn(kv, cosine, sine), 0.0)
    value = jnp.where(lane < HEAD_SIZE, 0.0, kv)
    keys = (low(key), low(pltpu.roll(key, HEAD_SIZE, 1)))
    values = (low(pltpu.roll(value, HEAD_SIZE, 1)), low(value))
    return keys, values


def block_scores(query, keys, begin, seq_len):
    scores = dot_nt(query, keys)
    row = lax.broadcasted_iota(jnp.int32, (scores.shape[0], 1), 0) + begin
    col = lax.broadcasted_iota(jnp.int32, scores.shape, 1)
    return jnp.where(col < jnp.minimum(row + 1, seq_len), scores, MASKED)


def attention_forward_kernel(len_ref, q_ref, kv_ref, cos_ref, sin_ref, out_ref, sum_ref):
    seq_len = len_ref[0]
    cosine, sine = cos_ref[...], sin_ref[...]
    keys, values = key_value_parts(kv_ref[...], cosine, sine)
    query = low(turn(q_ref[...], cosine, sine) * SCALE)
    rows = query.shape[0]
    lane = lax.broadcasted_iota(jnp.int32, (ROWS, 128), 1)
    for begin in range(0, rows, ROWS):
        end = begin + ROWS
        outs, sums = [], []
        for head in range(2):
            scores = block_scores(query[begin:end], keys[head][:end], begin, seq_len)
            peak = jnp.max(scores, axis=1, keepdims=True)
            exps = jnp.exp(scores - peak)
            total = jnp.sum(exps, axis=1, keepdims=True)
            probs = low(exps * (1.0 / total))
            outs.append(dot(probs, values[head][:end]))
            sums.append(peak + jnp.log(total))
        out_ref[begin:end, :] = low(outs[0] + outs[1])
        sum_ref[begin:end, :] = jnp.where(lane < HEAD_SIZE, sums[0], sums[1])


def attention_backward_kernel(
    len_ref, q_ref, kv_ref, cos_ref, sin_ref, sum_ref, grad_ref, dq_ref, dkv_ref, dk_acc, dv_acc
):
    seq_len = len_ref[0]
    cosine, sine = cos_ref[...], sin_ref[...]
    keys, values = key_value_parts(kv_ref[...], cosine, sine)
    query = low(turn(q_ref[...], cosine, sine) * SCALE)
    query_t = query.T
    rows = query.shape[0]
    group = pl.program_id(0)
    grad = low(grad_ref[...])
    grad_t = grad.T

    @pl.when(group == 0)
    def _():
        dk_acc[...] = jnp.zeros_like(dk_acc)
        dv_acc[...] = jnp.zeros_like(dv_acc)

    for begin in range(0, rows, ROWS):
        end = begin + ROWS
        dq = jnp.zeros((ROWS, 128), jnp.float32)
        for head in range(2):
            lanes = slice(head * HEAD_SIZE, (head + 1) * HEAD_SIZE)
            scores = block_scores(query[begin:end], keys[head][:end], begin, seq_len)
            at = head * HEAD_SIZE
            probs = jnp.exp(scores - sum_ref[begin:end, at : at + 1])
            dv_acc[:, :end] += dot(grad_t[lanes, begin:end], low(probs))
            dp = dot_nt(grad[begin:end], values[head][:end])
            inner = jnp.sum(probs * dp, axis=1, keepdims=True)
            ds = low(probs * (dp - inner))
            dq = dq + dot(ds, keys[head][:end])
            dk_acc[:, :end] += dot(query_t[lanes, begin:end], ds)
        dq = turn_back(dq * SCALE, cosine[begin:end], sine[begin:end])
        dq_ref[begin:end, :] = low(dq)

    @pl.when(group == pl.num_programs(0) - 1)
    def _():
        both = jnp.concatenate([dk_acc[...], dv_acc[...]], axis=0).T
        lane = lax.broadcasted_iota(jnp.int32, both.shape, 1)
        dkv_ref[...] = low(jnp.where(lane < HEAD_SIZE, turn_back(both, cosine, sine), both))


def attention_specs(rows, group_cols):
    whole = pl.BlockSpec((rows, 128), lambda g: (0, 0))
    return [
        pl.BlockSpec(memory_space=pltpu.SMEM),
        pl.BlockSpec((rows, 128), lambda g: (0, g * (group_cols // 128) + 6)),
        pl.BlockSpec((rows, 128), lambda g: (0, 2 * (group_cols // 128) + 2)),
        whole,
        whole,
    ]


BIG = 60 * 1024 * 1024


def attention_forward(seq_len, proj, cosine, sine, group_cols):
    rows = proj.shape[0]
    pairs = pl.BlockSpec((rows, 128), lambda g: (0, g))
    return pl.pallas_call(
        attention_forward_kernel,
        grid=(2,),
        in_specs=attention_specs(rows, group_cols),
        out_specs=[pairs, pairs],
        out_shape=[
            jax.ShapeDtypeStruct((rows, 256), jnp.bfloat16),
            jax.ShapeDtypeStruct((rows, 256), jnp.float32),
        ],
        compiler_params=pltpu.CompilerParams(vmem_limit_bytes=BIG),
        name="attention_forward",
    )(seq_len, proj, proj, cosine, sine)


def attention_backward(seq_len, proj, cosine, sine, sums, grad, group_cols, grad_at):
    rows = proj.shape[0]
    pairs = pl.BlockSpec((rows, 128), lambda g: (0, g))
    return pl.pallas_call(
        attention_backward_kernel,
        grid=(2,),
        in_specs=attention_specs(rows, group_cols)
        + [pairs, pl.BlockSpec((rows, 128), lambda g: (0, grad_at + g))],
        out_specs=[pairs, pl.BlockSpec((rows, 128), lambda g: (0, 0))],
        out_shape=[
            jax.ShapeDtypeStruct((rows, 256), jnp.bfloat16),
            jax.ShapeDtypeStruct((rows, 128), jnp.bfloat16),
        ],
        scratch_shapes=[
            pltpu.VMEM((HEAD_SIZE, rows), jnp.float32),
            pltpu.VMEM((HEAD_SIZE, rows), jnp.float32),
        ],
        compiler_params=pltpu.CompilerParams(vmem_limit_bytes=BIG),
        name="attention_backward",
    )(seq_len, proj, proj, cosine, sine, sums, grad)


CHUNK = 128
GROUP = GH * HEAD_SIZE
PAIRS = GH // 2
CONV = 2 * GROUP + 2 * N
SHARED = 2048


def triangle():
    row = lax.broadcasted_iota(jnp.int32, (CHUNK, CHUNK), 0)
    col = lax.broadcasted_iota(jnp.int32, (CHUNK, CHUNK), 1)
    return col <= row


def pair_lanes(values, pair):
    lane = lax.broadcasted_iota(jnp.int32, (values.shape[0], 128), 1)
    at = 2 * pair
    return jnp.where(lane < HEAD_SIZE, values[:, at : at + 1], values[:, at + 1 : at + 2])


def split_pair(values):
    lane = lax.broadcasted_iota(jnp.int32, values.shape, 1)
    empty = jnp.zeros_like(values)
    return jnp.concatenate(
        [jnp.where(lane < HEAD_SIZE, values, empty), jnp.where(lane < HEAD_SIZE, empty, values)],
        axis=0,
    )


def conv_pre(buf_ref, taps_ref, begin, size):
    total = buf_ref[5 : 5 + CHUNK, begin : begin + size] * taps_ref[0:1, begin : begin + size]
    for tap in range(1, KCONV):
        total = total + (
            buf_ref[5 + tap : 5 + tap + CHUNK, begin : begin + size]
            * taps_ref[tap : tap + 1, begin : begin + size]
        )
    return total


def load_conv(buf_ref, proj_ref):
    for group in range(2):
        at = group * 1024 + GROUP
        buf_ref[8:, group * GROUP : (group + 1) * GROUP] = proj_ref[:, at : at + GROUP]
    buf_ref[8:, 2 * GROUP :] = proj_ref[:, SHARED : SHARED + 2 * N]


def group_steps(proj_ref, bias_ref, decay_ref, group, lower):
    at = group * 1024 + 896
    raw = proj_ref[:, at : at + 128] + bias_ref[group : group + 1, :]
    step = jnp.log1p(jnp.exp(-jnp.abs(raw))) + jnp.maximum(raw, 0.0)
    rate = -jnp.exp(decay_ref[group : group + 1, :])
    cumul = dot_fine(lower, rate * step)
    return raw, step, rate, cumul


def head_decay(cumul, cumul_t, head, mask):
    spread = cumul[:, head : head + 1] - cumul_t[head : head + 1, :]
    return jnp.exp(jnp.where(mask, spread, MASKED))


def mamba_forward_kernel(
    proj_ref,
    attn_ref,
    taps_ref,
    bias_ref,
    decay_ref,
    skip_ref,
    gain_ref,
    both_ref,
    out_ref,
    states_ref,
    buf_ref,
    state_ref,
):
    chunk = pl.program_id(0)

    @pl.when(chunk == 0)
    def _():
        buf_ref[0:8, :] = jnp.zeros((8, CONV), jnp.float32)
        state_ref[...] = jnp.zeros_like(state_ref)

    load_conv(buf_ref, proj_ref)
    mask = triangle()
    lower = mask.astype(jnp.bfloat16)
    pre = conv_pre(buf_ref, taps_ref, 2 * GROUP, 2 * N)
    state_act = low(pre * sigmoid(pre))
    b_rows, c_rows = state_act[:, :N], state_act[:, N:]
    gram = dot_nt(c_rows, b_rows)
    b_cols = b_rows.T
    for group in range(2):
        cols = slice(group * GROUP, (group + 1) * GROUP)
        _, step, _, cumul = group_steps(proj_ref, bias_ref, decay_ref, group, lower)
        cumul_t = cumul.T
        last = cumul[CHUNK - 1 : CHUNK, :]
        state = state_ref[:, cols]
        states_ref[0, :, cols] = state
        from_state = dot(c_rows, low(state))
        gated = []
        for pair in range(PAIRS):
            at = group * GROUP + pair * 128
            pre = conv_pre(buf_ref, taps_ref, at, 128)
            chan = pre * sigmoid(pre)
            inputs = low(chan * pair_lanes(step, pair))
            mixing = jnp.concatenate(
                [
                    low(gram * head_decay(cumul, cumul_t, 2 * pair + side, mask))
                    for side in range(2)
                ],
                axis=1,
            )
            lanes = slice(pair * 128, (pair + 1) * 128)
            inner = pair_lanes(cumul, pair)
            out = dot(mixing, split_pair(inputs)) + jnp.exp(inner) * from_state[:, lanes]
            out_ref[:, at : at + 128] = out
            last_lanes = pair_lanes(last, pair)
            x_end = low(jnp.exp(last_lanes - inner) * wide(inputs))
            state_ref[:, at : at + 128] = jnp.exp(last_lanes) * state[:, lanes] + dot(
                b_cols, x_end
            )
            gate = proj_ref[:, group * 1024 + pair * 128 : group * 1024 + pair * 128 + 128]
            skipped = out + chan * skip_ref[:, at : at + 128]
            gated.append(skipped * (gate * sigmoid(gate)))
        square = sum(jnp.sum(part * part, axis=1, keepdims=True) for part in gated)
        scale = lax.rsqrt(square * (1.0 / GROUP) + EPS)
        for pair in range(PAIRS):
            at = group * GROUP + pair * 128
            to = group * 512 + pair * 128
            both_ref[:, to : to + 128] = low(gated[pair] * scale * gain_ref[:, at : at + 128])
        to = group * 512 + GROUP
        both_ref[:, to : to + 128] = attn_ref[:, group * 128 : (group + 1) * 128]
    buf_ref[0:8, :] = buf_ref[CHUNK : CHUNK + 8, :]


def mamba_forward(proj, attn, taps, bias, decay, skip, gain):
    rows, columns = proj.shape
    chunks = rows // CHUNK

    def whole(value):
        return pl.BlockSpec(value.shape, lambda k: (0, 0))

    return pl.pallas_call(
        mamba_forward_kernel,
        grid=(chunks,),
        in_specs=[
            pl.BlockSpec((CHUNK, columns), lambda k: (k, 0)),
            pl.BlockSpec((CHUNK, 256), lambda k: (k, 0)),
        ]
        + [whole(value) for value in (taps, bias, decay, skip, gain)],
        out_specs=[
            pl.BlockSpec((CHUNK, 1024), lambda k: (k, 0)),
            pl.BlockSpec((CHUNK, 2 * GROUP), lambda k: (k, 0)),
            pl.BlockSpec((1, N, 2 * GROUP), lambda k: (k, 0, 0)),
        ],
        out_shape=[
            jax.ShapeDtypeStruct((rows, 1024), jnp.bfloat16),
            jax.ShapeDtypeStruct((rows, 2 * GROUP), jnp.float32),
            jax.ShapeDtypeStruct((chunks, N, 2 * GROUP), jnp.float32),
        ],
        scratch_shapes=[
            pltpu.VMEM((CHUNK + 8, CONV), jnp.float32),
            pltpu.VMEM((N, 2 * GROUP), jnp.float32),
        ],
        compiler_params=pltpu.CompilerParams(vmem_limit_bytes=BIG),
        name="mamba_forward",
    )(proj, attn, taps, bias, decay, skip, gain)


def silu_slope(values, sig):
    return sig * (1.0 + values * (1.0 - sig))


def mamba_backward_kernel(
    proj_ref,
    before_ref,
    out_ref,
    states_ref,
    back_ref,
    dq_ref,
    dkv_ref,
    taps_ref,
    bias_ref,
    decay_ref,
    skip_ref,
    gain_ref,
    dproj_ref,
    dtaps_ref,
    dgain_ref,
    dskip_ref,
    dbias_ref,
    ddecay_ref,
    buf_ref,
    grad_buf,
    after_ref,
    flow_ref,
):
    step_at = pl.program_id(0)

    @pl.when(step_at == 0)
    def _():
        for ref in (dtaps_ref, dgain_ref, dskip_ref, dbias_ref, ddecay_ref, after_ref, flow_ref):
            ref[...] = jnp.zeros_like(ref)
        grad_buf[CHUNK:, :] = jnp.zeros((8, CONV), jnp.float32)

    inside = jnp.where(step_at == pl.num_programs(0) - 1, 0.0, 1.0)
    for group in range(2):
        at = group * 1024 + GROUP
        buf_ref[0:8, group * GROUP : (group + 1) * GROUP] = before_ref[:, at : at + GROUP] * inside
    buf_ref[0:8, 2 * GROUP :] = before_ref[:, SHARED : SHARED + 2 * N] * inside
    load_conv(buf_ref, proj_ref)
    mask = triangle()
    lower = mask.astype(jnp.bfloat16)
    row = lax.broadcasted_iota(jnp.int32, (CHUNK, CHUNK), 0)
    col = lax.broadcasted_iota(jnp.int32, (CHUNK, CHUNK), 1)
    upper = (row <= col).astype(jnp.bfloat16)
    pre_state = conv_pre(buf_ref, taps_ref, 2 * GROUP, 2 * N)
    sig_state = sigmoid(pre_state)
    state_act = low(pre_state * sig_state)
    b_rows, c_rows = state_act[:, :N], state_act[:, N:]
    gram = dot_nt(c_rows, b_rows)
    c_cols = c_rows.T
    dgram = jnp.zeros((CHUNK, CHUNK), jnp.float32)
    d_c = jnp.zeros((CHUNK, N), jnp.float32)
    d_b = jnp.zeros((CHUNK, N), jnp.float32)
    for group in range(2):
        raw, step, rate, cumul = group_steps(proj_ref, bias_ref, decay_ref, group, lower)
        cumul_t = cumul.T
        last = cumul[CHUNK - 1 : CHUNK, :]
        pres, sigs, chans, gates, gate_sigs, skips, gated = [], [], [], [], [], [], []
        for pair in range(PAIRS):
            at = group * GROUP + pair * 128
            pre = conv_pre(buf_ref, taps_ref, at, 128)
            sig = sigmoid(pre)
            chan = pre * sig
            gate = proj_ref[:, group * 1024 + pair * 128 : group * 1024 + pair * 128 + 128]
            gate_sig = sigmoid(gate)
            skipped = out_ref[:, at : at + 128] + chan * skip_ref[:, at : at + 128]
            pres.append(pre)
            sigs.append(sig)
            chans.append(chan)
            gates.append(gate)
            gate_sigs.append(gate_sig)
            skips.append(skipped)
            gated.append(skipped * (gate * gate_sig))
        square = sum(jnp.sum(part * part, axis=1, keepdims=True) for part in gated)
        scale = lax.rsqrt(square * (1.0 / GROUP) + EPS)
        grads = []
        cross = jnp.zeros((CHUNK, 1), jnp.float32)
        for pair in range(PAIRS):
            at = group * GROUP + pair * 128
            grad = back_ref[:, group * 512 + pair * 128 : group * 512 + pair * 128 + 128]
            dgain_ref[:, at : at + 128] += jnp.sum(grad * gated[pair] * scale, axis=0, keepdims=True)
            grad = grad * gain_ref[:, at : at + 128]
            cross = cross + jnp.sum(gated[pair] * grad, axis=1, keepdims=True)
            grads.append(grad)
        cross = cross * (1.0 / GROUP) * scale * scale * scale
        dstep = jnp.zeros((CHUNK, 128), jnp.float32)
        flow = jnp.zeros((CHUNK, 128), jnp.float32)
        flow_end = flow_ref[group : group + 1, :]
        flow_next = jnp.zeros((1, 128), jnp.float32)
        for pair in range(PAIRS):
            at = group * GROUP + pair * 128
            head_of_lane = lax.broadcasted_iota(jnp.int32, (128, 128), 0) // HEAD_SIZE + 2 * pair
            lane = lax.broadcasted_iota(jnp.int32, (128, 128), 1)
            pick = (head_of_lane == lane).astype(jnp.bfloat16)
            chan = chans[pair]
            grad = scale * grads[pair] - gated[pair] * cross
            gate, gate_sig = gates[pair], gate_sigs[pair]
            dgate = grad * skips[pair] * silu_slope(gate, gate_sig)
            to = group * 1024 + pair * 128
            dproj_ref[:, to : to + 128] = low(dgate)
            grad = grad * (gate * gate_sig)
            dskip_ref[:, at : at + 128] += jnp.sum(grad * chan, axis=0, keepdims=True)
            dchan = grad * skip_ref[:, at : at + 128]
            dout = low(grad)
            step_lanes = pair_lanes(step, pair)
            inputs = low(chan * step_lanes)
            halves = split_pair(inputs)
            decays = [head_decay(cumul, cumul_t, 2 * pair + side, mask) for side in range(2)]
            mixing = jnp.concatenate([low(gram * decay) for decay in decays], axis=1)
            dmix = dot_nt(dout, halves)
            dgram = dgram + dmix[:, :CHUNK] * decays[0] + dmix[:, CHUNK:] * decays[1]
            dinputs = dot_tn(mixing, dout)
            lane = lax.broadcasted_iota(jnp.int32, (CHUNK, 128), 1)
            dinputs = jnp.where(lane < HEAD_SIZE, dinputs[:CHUNK], dinputs[CHUNK:])
            inner = pair_lanes(cumul, pair)
            last_lanes = pair_lanes(last, pair)
            to_end = jnp.exp(last_lanes - inner)
            after = after_ref[:, at : at + 128]
            after_low = low(after)
            dinputs = dinputs + to_end * dot(b_rows, after_low)
            x_end = low(to_end * wide(inputs))
            g_start = low(jnp.exp(inner) * wide(dout))
            state = states_ref[0, :, at : at + 128]
            d_c = d_c + dot_nt(g_start, low(state))
            d_b = d_b + dot_nt(x_end, after_low)
            after = jnp.exp(last_lanes) * after + dot(c_cols, g_start)
            after_ref[:, at : at + 128] = after
            through = jnp.sum(after * state, axis=0, keepdims=True)
            flow_next = flow_next + dot_by(jnp.broadcast_to(through, (8, 128)), pick)[0:1]
            flow = flow + dot_by(
                wide(dout) * out_ref[:, at : at + 128] - wide(inputs) * dinputs, pick
            )
            dstep = dstep + dot_by(dinputs * chan, pick)
            dchan = dchan + dinputs * step_lanes
            grad_buf[0:CHUNK, at : at + 128] = dchan * silu_slope(pres[pair], sigs[pair])
        dcumul = dot_fine(upper, flow) + flow_end
        flow_ref[group : group + 1, :] = flow_next
        dstep = dstep + rate * dcumul
        ddecay_ref[group : group + 1, :] += jnp.sum(rate * step * dcumul, axis=0, keepdims=True)
        draw = dstep * sigmoid(raw)
        dbias_ref[group : group + 1, :] += jnp.sum(draw, axis=0, keepdims=True)
        to = group * 1024 + 896
        lane = lax.broadcasted_iota(jnp.int32, (CHUNK, 128), 1)
        dproj_ref[:, to : to + 128] = low(jnp.where(lane < GH, draw, 0.0))
        to = group * 1024 + 2 * GROUP
        dproj_ref[:, to : to + 128] = dq_ref[:, group * 128 : (group + 1) * 128]
    dgram_low = low(dgram)
    d_c = d_c + dot(dgram_low, b_rows)
    d_b = d_b + dot_tn(dgram_low, c_rows)
    slope = silu_slope(pre_state, sig_state)
    grad_buf[0:CHUNK, 2 * GROUP : 2 * GROUP + N] = d_b * slope[:, :N]
    grad_buf[0:CHUNK, 2 * GROUP + N :] = d_c * slope[:, N:]
    for at in range(0, CONV, 128):
        grad = jnp.zeros((CHUNK, 128), jnp.float32)
        here = grad_buf[0:CHUNK, at : at + 128]
        for tap in range(KCONV):
            shift = KCONV - 1 - tap
            grad = grad + (
                grad_buf[shift : shift + CHUNK, at : at + 128] * taps_ref[tap : tap + 1, at : at + 128]
            )
            dtaps_ref[tap : tap + 1, at : at + 128] += jnp.sum(
                here * buf_ref[5 + tap : 5 + tap + CHUNK, at : at + 128], axis=0, keepdims=True
            )
        if at < 2 * GROUP:
            to = (at // GROUP) * 1024 + GROUP + at % GROUP
        else:
            to = SHARED + at - 2 * GROUP
        dproj_ref[:, to : to + 128] = low(grad)
    dproj_ref[:, SHARED + 2 * N :] = dkv_ref[...]
    grad_buf[CHUNK:, :] = grad_buf[0:8, :]


def mamba_backward(proj, out, states, back, dq, dkv, taps, bias, decay, skip, gain):
    rows, columns = proj.shape
    chunks = rows // CHUNK

    def whole(value):
        return pl.BlockSpec(value.shape, lambda k: (0, 0))

    def rows_of(width):
        return pl.BlockSpec((CHUNK, width), lambda k: (chunks - 1 - k, 0))

    params = (taps, bias, decay, skip, gain)
    return pl.pallas_call(
        mamba_backward_kernel,
        grid=(chunks,),
        in_specs=[
            rows_of(columns),
            pl.BlockSpec(
                (8, columns),
                lambda k: (jnp.maximum((chunks - 1 - k) * (CHUNK // 8) - 1, 0), 0),
            ),
            rows_of(2 * GROUP),
            pl.BlockSpec((1, N, 2 * GROUP), lambda k: (chunks - 1 - k, 0, 0)),
            rows_of(1024),
            rows_of(256),
            rows_of(128),
        ]
        + [whole(value) for value in params],
        out_specs=[rows_of(columns)]
        + [whole(value) for value in (taps, gain, skip, bias, decay)],
        out_shape=[jax.ShapeDtypeStruct((rows, columns), jnp.bfloat16)]
        + [
            jax.ShapeDtypeStruct(value.shape, jnp.float32)
            for value in (taps, gain, skip, bias, decay)
        ],
        scratch_shapes=[
            pltpu.VMEM((CHUNK + 8, CONV), jnp.float32),
            pltpu.VMEM((CHUNK + 8, CONV), jnp.float32),
            pltpu.VMEM((N, 2 * GROUP), jnp.float32),
            pltpu.VMEM((8, 128), jnp.float32),
        ],
        compiler_params=pltpu.CompilerParams(vmem_limit_bytes=BIG),
        name="mamba_backward",
    )(proj, proj, out, states, back, dq, dkv, *params)


MESH = pl.DeviceIdType.MESH


def landed(ref, sem):
    pltpu.make_async_copy(ref, ref, sem).wait()


def spread_kernel(
    pack_ref,
    next_ref,
    shared_ref,
    x_ref,
    small_ref,
    w_ref,
    v_ref,
    full_ref,
    params_ref,
    near_sem,
    out_sem,
    part_sem,
    fromx_sem,
    fromy_sem,
    overx_sem,
    overy_sem,
    tox_sem,
    toy_sem,
    relx_sem,
    rely_sem,
    row_sem,
    row_out,
    pair_sem,
    pair_out,
    param_sem,
    param_out,
):
    plane = lax.axis_index("plane")
    core = lax.axis_index("core")
    place = lax.axis_index("tensor")
    xside = plane + 1 - 2 * (plane % 2)
    yside = plane + 2 - 4 * (plane // 2)
    across = xside + 2 - 4 * (xside // 2)
    target = place // 2
    column = place % 2
    share, width = pack_ref.shape
    narrow = next_ref.shape[1]
    rest = shared_ref.shape[2]
    half = share
    rows_dev = x_ref.shape[1]

    barrier = pltpu.get_barrier_semaphore()
    for step in range(4):
        for side in range(2):
            if step or side:
                pl.semaphore_signal(
                    barrier,
                    inc=1,
                    device_id={"core": (core + side) % 2, "tensor": (place + step) % 4},
                    device_id_type=MESH,
                )
    for neighbour in (xside, yside):
        pl.semaphore_signal(
            barrier, inc=1, device_id={"plane": neighbour}, device_id_type=MESH
        )
    pl.semaphore_wait(barrier, 9)

    def block(at, part):
        return pl.ds(pl.multiple_of(at * 2 * share + part * share, share), share)

    def piece(at, part, col):
        return w_ref.at[block(at, part), pl.ds(pl.multiple_of(col * width, width), width)]

    def next_piece(at, part, col):
        return v_ref.at[block(at, part), pl.ds(pl.multiple_of(col * narrow, narrow), narrow)]

    def rest_piece(at, part):
        return w_ref.at[block(at, part), pl.ds(2 * width, rest)]

    started = []

    def send(src, dst, send_sem, recv_sem, device):
        copy = pltpu.make_async_remote_copy(
            src_ref=src,
            dst_ref=dst,
            send_sem=send_sem,
            recv_sem=recv_sem,
            device_id=device,
            device_id_type=MESH,
        )
        copy.start()
        started.append((src, send_sem))

    mine = piece(plane, core, column)
    slot = core * 2 + column
    mine_next = next_piece(plane, core, column)

    def send_parts(src, dst, at, recv_sem):
        for step in (2, 1, 3):
            send(
                src,
                dst,
                out_sem.at[at + step],
                recv_sem,
                {"core": target, "tensor": (place + step) % 4},
            )

    send_parts(pack_ref, mine, 0, part_sem.at[slot])

    params = params_ref.at[column]

    @pl.when(target == core)
    def _():
        pltpu.make_async_copy(pack_ref, mine, part_sem.at[slot]).start()
        pltpu.make_async_copy(next_ref, mine_next, part_sem.at[6 + slot]).start()
        pltpu.make_async_copy(small_ref, params, param_sem.at[column]).start()
        for step in range(1, 4):
            pltpu.make_async_remote_copy(
                src_ref=small_ref,
                dst_ref=params,
                send_sem=param_out.at[step],
                recv_sem=param_sem.at[column],
                device_id={"tensor": (place + step) % 4},
                device_id_type=MESH,
            ).start()

    @pl.when(target != core)
    def _():
        pltpu.make_async_remote_copy(
            src_ref=pack_ref,
            dst_ref=mine,
            send_sem=out_sem.at[0],
            recv_sem=part_sem.at[slot],
            device_id={"core": 1 - core},
            device_id_type=MESH,
        ).start()
        pltpu.make_async_remote_copy(
            src_ref=next_ref,
            dst_ref=mine_next,
            send_sem=out_sem.at[4],
            recv_sem=part_sem.at[6 + slot],
            device_id={"core": 1 - core},
            device_id_type=MESH,
        ).start()

    own_rest = rest_piece(plane, core)
    near = pltpu.make_async_copy(shared_ref.at[core], own_rest, part_sem.at[4 + core])
    near.start()
    send(
        shared_ref.at[1 - core],
        own_rest,
        near_sem.at[0],
        part_sem.at[4 + core],
        {"core": 1 - core},
    )

    def rows_at(at, side):
        return full_ref.at[pl.ds(pl.multiple_of(at * rows_dev + side * half, half), half)]

    for seq in range(2):
        for side in range(2):
            goal = 2 * core + seq
            src = x_ref.at[seq, pl.ds(side * half, half)]
            dst = rows_at(place, side)
            here = jnp.logical_and(core == side, goal == place)

            @pl.when(here)
            def _():
                pltpu.make_async_copy(src, dst, row_sem.at[place]).start()

            @pl.when(jnp.logical_not(here))
            def _():
                pltpu.make_async_remote_copy(
                    src_ref=src,
                    dst_ref=dst,
                    send_sem=row_out.at[seq * 2 + side],
                    recv_sem=row_sem.at[place],
                    device_id={"core": side, "tensor": goal},
                    device_id_type=MESH,
                ).start()

    send_parts(next_ref, mine_next, 4, part_sem.at[6 + slot])

    first_col = jnp.where(place // 2 == core, place % 2, 1 - core)
    order = [(0, None, 0), (0, None, 1)]
    for kind in (1, 2):
        for turn in range(2):
            for part in range(2):
                order.append((kind, (first_col + turn) % 2, part))

    def at_piece(at, item):
        kind, col, part = item
        if kind == 0:
            return rest_piece(at, part)
        return piece(at, part, col) if kind == 1 else next_piece(at, part, col)

    def index(item):
        kind, col, part = item
        return 4 + part if kind == 0 else (kind - 1) * 6 + part * 2 + col

    def relay(item):
        at = index(item)
        if item[2] == 0:
            landed(at_piece(xside, item), fromx_sem.at[at])
            ref = at_piece(xside, item)
            send(ref, ref, rely_sem.at[at], overy_sem.at[at], {"plane": yside})
        else:
            landed(at_piece(yside, item), fromy_sem.at[at])
            ref = at_piece(yside, item)
            send(ref, ref, relx_sem.at[at], overx_sem.at[at], {"plane": xside})

    for number, item in enumerate(order):
        at = index(item)
        ref = at_piece(plane, item)
        landed(ref, part_sem.at[at])
        send(ref, ref, tox_sem.at[at], fromx_sem.at[at], {"plane": xside})
        send(ref, ref, toy_sem.at[at], fromy_sem.at[at], {"plane": yside})
        if number >= 2:
            relay(order[number - 2])
        if number == 5:
            for step in range(4):
                at = (place + step) % 4
                ref = rows_at(at, core)
                landed(ref, row_sem.at[at])
                send(ref, ref, pair_out.at[at], pair_sem.at[at], {"core": 1 - core})
    for item in order[-2:]:
        relay(item)
    for step in range(4):
        at = (place + step) % 4
        landed(rows_at(at, 1 - core), pair_sem.at[at])
    for item in order:
        at = index(item)
        if item[2] == 0:
            landed(at_piece(yside, item), fromy_sem.at[at])
            landed(at_piece(across, item), overy_sem.at[at])
        else:
            landed(at_piece(xside, item), fromx_sem.at[at])
            landed(at_piece(across, item), overx_sem.at[at])

    for src, sem in started:
        landed(src, sem)

    for at in range(2):
        landed(params_ref.at[at], param_sem.at[at])

    @pl.when(target == core)
    def _():
        for step in range(1, 4):
            landed(small_ref, param_out.at[step])

    @pl.when(target != core)
    def _():
        landed(pack_ref, out_sem.at[0])
        landed(next_ref, out_sem.at[4])

    for seq in range(2):
        for side in range(2):
            here = jnp.logical_and(core == side, 2 * core + seq == place)

            @pl.when(jnp.logical_not(here))
            def _():
                landed(x_ref.at[seq, pl.ds(side * half, half)], row_out.at[seq * 2 + side])


def spread(pack, following, shared, x_rows, small):
    share, width = pack.shape
    narrow = following.shape[1]
    rest = shared.shape[2]
    rows = x_rows.shape[1] * 4
    dma = pltpu.SemaphoreType.DMA
    any_space = pl.BlockSpec(memory_space=pl.ANY)
    return pl.pallas_call(
        spread_kernel,
        in_specs=[any_space] * 5,
        out_specs=[any_space] * 4,
        out_shape=[
            jax.ShapeDtypeStruct((8 * share, 2 * width + rest), pack.dtype),
            jax.ShapeDtypeStruct((8 * share, 2 * narrow), pack.dtype),
            jax.ShapeDtypeStruct((rows, x_rows.shape[2]), x_rows.dtype),
            jax.ShapeDtypeStruct((2,) + small.shape, small.dtype),
        ],
        scratch_shapes=[dma((1,)), dma((8,))] + [dma((10,))] * 9 + [dma((4,))] * 6,
        compiler_params=pltpu.CompilerParams(collective_id=1, has_side_effects=True),
        name="spread",
    )(pack, following, shared, x_rows, small)


def rms_norm(values, gain_vec):
    return values * lax.rsqrt(jnp.mean(values * values, axis=-1, keepdims=True) + EPS) * gain_vec


def turn_tables(seq_count, head_count):
    half_dim = HEAD_SIZE // 2
    freqs = THETA ** (-jnp.arange(half_dim, dtype=jnp.float32) * 2.0 / HEAD_SIZE)
    angles = jnp.arange(seq_count, dtype=jnp.float32)[:, None] * freqs[None, :]
    cosine, sine = jnp.cos(angles), jnp.sin(angles)
    return (
        jnp.tile(jnp.concatenate([cosine, cosine], axis=1), (1, head_count)),
        jnp.tile(jnp.concatenate([-sine, sine], axis=1), (1, head_count)),
    )


def swiglu(gate_up):
    half_cols = gate_up.shape[1] // 2
    gate = gate_up[:, :half_cols]
    return gate * sigmoid(gate) * gate_up[:, half_cols:]


def swapped(values):
    return lax.ppermute(values, "core", SWAP)


def body(
    layer_in,
    seq_lengths,
    out_grad,
    norm_gain,
    mixer_weight,
    step_weight,
    state_weight,
    query_weight,
    key_value_weight,
    conv_channels,
    conv_states,
    step_bias,
    decay_log,
    skip_scale,
    group_gain,
    mamba_proj,
    attn_proj,
    ffn_gain,
    ffn_weight,
    ffn_down,
):
    core = lax.axis_index("core")
    place = lax.axis_index("tensor")
    first = core == 0
    seq_dev, rows_dev, model_dim = layer_in.shape
    groups = lax.axis_size("tensor")
    seq_total = rows_dev * groups
    half_rows = rows_dev // 2
    share = mixer_weight.shape[0]
    chans_dev = mixer_weight.shape[2]
    heads_dev = step_weight.shape[1]
    query_dev = query_weight.shape[1]
    hidden_dev = ffn_weight.shape[2]
    held = groups // 2
    step_pad = 128

    def mine(values):
        return lax.dynamic_slice_in_dim(values, core * held, held, 0)

    def other(values):
        return lax.dynamic_slice_in_dim(values, (1 - core) * held, held, 0)

    def in_order(own, others, axis):
        return jnp.where(
            first,
            jnp.concatenate([own, others], axis=axis),
            jnp.concatenate([others, own], axis=axis),
        )

    def flat(values):
        return values.transpose(1, 0, 2).reshape(values.shape[1], -1)

    def positions_in(values):
        shaped = values.reshape(seq_dev, 2, half_rows, model_dim)
        keep = lax.dynamic_index_in_dim(shaped, core, 1, False)
        send = lax.dynamic_index_in_dim(shaped, 1 - core, 1, False)
        four = in_order(keep, swapped(send), 0)
        own = lax.all_to_all(four, "tensor", 0, 0, tiled=True)
        both = in_order(own[:, None], swapped(own)[:, None], 1)
        return both.reshape(seq_total, model_dim)

    def positions_out(own):
        four = lax.all_to_all(own, "tensor", 0, 0, tiled=True)
        keep = lax.dynamic_slice_in_dim(four, core * seq_dev, seq_dev, 0)
        send = lax.dynamic_slice_in_dim(four, (1 - core) * seq_dev, seq_dev, 0)
        both = in_order(keep[:, None], swapped(send)[:, None], 1)
        return both.reshape(seq_dev, rows_dev, model_dim)

    def own_half(values):
        shaped = values.reshape(groups, 2, half_rows, -1)
        return lax.dynamic_index_in_dim(shaped, core, 1, False)

    def other_half(values):
        shaped = values.reshape(groups, 2, half_rows, -1)
        return lax.dynamic_index_in_dim(shaped, 1 - core, 1, False)

    out_dev = chans_dev + query_dev
    pack_two = jnp.concatenate([mamba_proj.T, attn_proj.T], axis=1)
    pack_one = jnp.concatenate(
        [
            mixer_weight.reshape(share, 2 * chans_dev),
            query_weight,
            jnp.pad(step_weight, ((0, 0), (0, step_pad - heads_dev))),
        ],
        axis=1,
    )
    kv_heads = key_value_weight.reshape(share, 2, 2, HEAD_SIZE)

    def shared_for(at):
        return jnp.concatenate(
            [
                state_weight.reshape(share, 2 * N),
                lax.dynamic_index_in_dim(kv_heads, at, 2, False).reshape(share, 2 * HEAD_SIZE),
            ],
            axis=1,
        )

    small_in = jnp.concatenate(
        [conv_channels.reshape(-1), step_bias, decay_log, skip_scale, group_gain]
    )
    small_pad = -(-small_in.shape[0] // 1024) * 1024
    small_in = jnp.pad(small_in, (0, small_pad - small_in.shape[0])).reshape(-1, 128)
    if lax.axis_size("plane") == 4 and groups == 4 and share % 16 == 0:
        shared = jnp.stack([shared_for(0), shared_for(1)])
        weight_one, weight_two, x_low, small_mine = spread(
            pack_one, pack_two, shared, layer_in, small_in
        )
    else:
        x_low = positions_in(layer_in)
        all_one = lax.all_gather(pack_one, "tensor", axis=0)
        own_one = jnp.concatenate([flat(mine(all_one)), shared_for(core)], axis=1)
        their_one = jnp.concatenate([flat(other(all_one)), shared_for(1 - core)], axis=1)
        weight_one = lax.all_gather(
            in_order(own_one, swapped(their_one), 0), "plane", axis=0, tiled=True
        )
        all_two = lax.all_gather(pack_two, "tensor", axis=0)
        weight_two = lax.all_gather(
            in_order(flat(mine(all_two)), swapped(flat(other(all_two))), 0),
            "plane",
            axis=0,
            tiled=True,
        )
        small_mine = mine(lax.all_gather(small_in, "tensor", axis=0))
    small_mine = small_mine.reshape(held, -1)

    pack_three = jnp.concatenate([ffn_weight.reshape(share, 2 * hidden_dev), ffn_down.T], axis=1)
    all_three = lax.all_gather(pack_three, "tensor", axis=0)
    all_three, weight_one = lax.optimization_barrier((all_three, weight_one))

    def lay_three(pack):
        cuts = [pack[:, :, at * hidden_dev : (at + 1) * hidden_dev] for at in range(3)]
        return jnp.concatenate([flat(cut) for cut in cuts], axis=1)

    rows_three = in_order(lay_three(mine(all_three)), swapped(lay_three(other(all_three))), 0)
    weight_three = lax.all_gather(rows_three, "plane", axis=0, tiled=True)
    gate_up_weight = weight_three[:, : 2 * held * hidden_dev]
    down_weight = weight_three[:, 2 * held * hidden_dev :]

    cuts = []
    at = 0
    for size in (KCONV * chans_dev, heads_dev, heads_dev, heads_dev, chans_dev):
        cuts.append(small_mine[:, at : at + size])
        at += size
    taps = cuts[0].reshape(held, KCONV, chans_dev).transpose(1, 0, 2).reshape(KCONV, -1)
    taps = jnp.concatenate([taps, conv_states.reshape(KCONV, 2 * N)], axis=1)
    bias = jnp.pad(cuts[1], ((0, 0), (0, step_pad - heads_dev)))
    decay = jnp.pad(cuts[2], ((0, 0), (0, step_pad - heads_dev)))
    skip = jnp.repeat(cuts[3].reshape(1, -1), HEAD_SIZE, axis=1)
    gain = cuts[4].reshape(1, -1)

    lengths = in_order(seq_lengths, swapped(seq_lengths), 0)
    seq_len = lengths[place]
    len_one = seq_len.reshape(1)
    valid_rows = (jnp.arange(seq_total, dtype=jnp.int32) < seq_len).astype(jnp.float32)[:, None]

    x_rows = wide(x_low)
    normed = low(rms_norm(x_rows, norm_gain))
    proj = dot(normed, weight_one)
    group_cols = 2 * chans_dev + query_dev + step_pad
    cosine, sine = turn_tables(seq_total, 2)
    attn, log_sums = attention_forward(len_one, proj, cosine, sine, group_cols)
    both_low, state_out, states = mamba_forward(proj, attn, taps, bias, decay, skip, gain)

    mixed_part = low(dot_nt(both_low, weight_two))
    mixed = wide(mixed_part) + wide(swapped(mixed_part))
    hidden = x_rows + mixed
    normed_two = low(rms_norm(hidden, ffn_gain))
    gate_up = dot(normed_two, gate_up_weight)
    act, act_pull = jax.vjp(swiglu, gate_up)
    act_low = low(act)
    ffn_part = low(dot_nt(act_low, down_weight))
    ffn_own = wide(own_half(ffn_part)) + wide(swapped(other_half(ffn_part)))
    out_own = own_half(valid_rows) * (own_half(hidden) + ffn_own)
    layer_out = positions_out(low(out_own))

    grad_rows = valid_rows * wide(positions_in(out_grad))
    grad_low = low(grad_rows)
    grad_down = low(dot_tn(grad_low, act_low))
    (grad_gate_up,) = act_pull(dot(grad_low, down_weight))
    gate_up_low = low(grad_gate_up)
    grad_gate_up_weight = low(dot_tn(normed_two, gate_up_low))
    grad_two_part = low(dot_nt(gate_up_low, gate_up_weight))
    grad_two = wide(grad_two_part) + wide(swapped(grad_two_part))
    r_two = lax.rsqrt(jnp.mean(hidden * hidden, axis=-1, keepdims=True) + EPS)
    scaled = grad_two * ffn_gain
    grad_hidden = (
        grad_rows
        + r_two * scaled
        - hidden * (r_two**3 * jnp.mean(hidden * scaled, axis=-1, keepdims=True))
    )
    grad_ffn_gain = jnp.sum(own_half(hidden * r_two * grad_two), axis=(0, 1))
    grad_mixed = low(grad_hidden)

    def scatter(values):
        part = lax.psum_scatter(values, "plane", scatter_dimension=0, tiled=True)
        part = part.reshape(2, share, -1)
        return (
            lax.dynamic_index_in_dim(part, core, 0, False),
            lax.dynamic_index_in_dim(part, 1 - core, 0, False),
        )

    def by_group(values, widths):
        pieces = []
        at = 0
        for width in widths:
            piece = values[:, at : at + held * width]
            pieces.append(piece.reshape(share, held, width).transpose(1, 0, 2))
            at += held * width
        return jnp.concatenate(pieces, axis=2)

    def to_groups(own, theirs):
        whole = in_order(own, theirs, 0)
        return lax.psum_scatter(whole, "tensor", scatter_dimension=0, tiled=True)[0]

    def sum_rest(parts, widths):
        both = [scatter(part) for part in parts]
        own = by_group(jnp.concatenate([pair[0] for pair in both], axis=1), widths)
        theirs = by_group(jnp.concatenate([pair[1] for pair in both], axis=1), widths)
        return to_groups(own, swapped(theirs))

    sum_three = sum_rest((grad_gate_up_weight, grad_down), (hidden_dev,) * 3)
    grad_both = low(dot_tn(grad_mixed, both_low))
    sum_two = sum_rest((grad_both,), (out_dev,))

    back = dot(grad_mixed, weight_two)
    attn_back = jnp.concatenate(
        [low(back[:, chans_dev:out_dev]), low(back[:, out_dev + chans_dev :])], axis=1
    )
    grad_q, grad_kv = attention_backward(
        len_one, proj, cosine, sine, log_sums, attn_back, group_cols, 0
    )
    proj_grad, grad_taps, grad_gain, grad_skip_cols, grad_bias, grad_decay = mamba_backward(
        proj, state_out, states, back, grad_q, grad_kv, taps, bias, decay, skip, gain
    )
    grad_one = low(dot_tn(normed, proj_grad))
    own_grad, their_grad = scatter(grad_one)
    their_grad = swapped(their_grad)
    edge = held * group_cols
    shared_own = wide(own_grad[:, edge : edge + 2 * N]) + wide(their_grad[:, edge : edge + 2 * N])
    kv_both = in_order(
        own_grad[:, None, edge + 2 * N :], their_grad[:, None, edge + 2 * N :], 1
    )
    kv_both = kv_both.reshape(share, 2, 2, HEAD_SIZE).transpose(0, 2, 1, 3)
    shared_low = jnp.concatenate([low(shared_own), kv_both.reshape(share, -1)], axis=1)
    shared_sum = jnp.sum(wide(lax.all_gather(shared_low, "tensor", axis=0)), axis=0)
    sum_one = to_groups(
        by_group(own_grad[:, :edge], (group_cols,)), by_group(their_grad[:, :edge], (group_cols,))
    )

    grad_norm_part = low(dot_nt(proj_grad, weight_one))
    grad_norm_own = wide(own_half(grad_norm_part)) + wide(swapped(other_half(grad_norm_part)))
    x_own = wide(own_half(x_low))
    r_one = lax.rsqrt(jnp.mean(x_own * x_own, axis=-1, keepdims=True) + EPS)
    scaled = grad_norm_own * norm_gain
    grad_x = (
        own_half(grad_hidden)
        + r_one * scaled
        - x_own * (r_one**3 * jnp.mean(x_own * scaled, axis=-1, keepdims=True))
    )
    grad_norm_gain = jnp.sum(x_own * r_one * grad_norm_own, axis=(0, 1))
    input_grad = positions_out(low(grad_x))

    grad_skip = jnp.sum(grad_skip_cols.reshape(held, heads_dev, HEAD_SIZE), axis=-1)
    chan_taps = grad_taps[:, : held * chans_dev].reshape(KCONV, held, chans_dev)
    group_small = jnp.concatenate(
        [
            chan_taps.transpose(1, 0, 2).reshape(held, -1),
            grad_bias[:, :heads_dev],
            grad_decay[:, :heads_dev],
            grad_skip,
            grad_gain.reshape(held, -1),
        ],
        axis=1,
    )
    small_groups = in_order(group_small, jnp.zeros_like(group_small), 0)
    small_out = jnp.concatenate(
        [
            grad_norm_gain,
            grad_ffn_gain,
            grad_taps[:, held * chans_dev :].reshape(-1),
            small_groups.reshape(-1),
        ]
    )
    small_sum = lax.psum(small_out, ("plane", "core", "tensor"))
    group_sum = lax.dynamic_index_in_dim(
        small_sum[2 * model_dim + KCONV * 2 * N :].reshape(groups, -1), place, 0, False
    )
    pieces = []
    at = 0
    for size in (KCONV * chans_dev, heads_dev, heads_dev, heads_dev, chans_dev):
        pieces.append(group_sum[at : at + size])
        at += size

    one, two, three = wide(sum_one), wide(sum_two), wide(sum_three)
    return (
        layer_out,
        input_grad,
        small_sum[:model_dim],
        one[:, : 2 * chans_dev].reshape(share, 2, chans_dev),
        one[:, 2 * chans_dev + query_dev :][:, :heads_dev],
        shared_sum[:, : 2 * N].reshape(share, 2, N),
        one[:, 2 * chans_dev : 2 * chans_dev + query_dev],
        shared_sum[:, 2 * N :].reshape(share, 2, 2 * HEAD_SIZE),
        pieces[0].reshape(KCONV, chans_dev),
        small_sum[2 * model_dim : 2 * model_dim + KCONV * 2 * N].reshape(KCONV, 2, N),
        pieces[1],
        pieces[2],
        pieces[3],
        pieces[4],
        two[:, :chans_dev].T,
        two[:, chans_dev:].T,
        small_sum[model_dim : 2 * model_dim],
        three[:, : 2 * hidden_dev].reshape(share, 2, hidden_dev),
        three[:, 2 * hidden_dev :].T,
    )


def solution(mesh):
    rows, columns = mesh.devices.shape
    fine = Mesh(mesh.devices.reshape(rows // 2, 2, columns), ("plane", "core", "tensor"))
    dp = ("plane", "core")
    return jax.shard_map(
        body,
        mesh=fine,
        in_specs=(
            P(dp, "tensor", None),
            P(dp),
            P(dp, "tensor", None),
            P(),
            P(dp, None, "tensor"),
            P(dp, "tensor"),
            P(dp, None, None),
            P(dp, "tensor"),
            P(dp, None, None),
            P(None, "tensor"),
            P(),
            P("tensor"),
            P("tensor"),
            P("tensor"),
            P("tensor"),
            P("tensor", dp),
            P("tensor", dp),
            P(),
            P(dp, None, "tensor"),
            P("tensor", dp),
        ),
        out_specs=(
            P(dp, "tensor", None),
            P(dp, "tensor", None),
            P(),
            P(dp, None, "tensor"),
            P(dp, "tensor"),
            P(dp, None, None),
            P(dp, "tensor"),
            P(dp, None, None),
            P(None, "tensor"),
            P(),
            P("tensor"),
            P("tensor"),
            P("tensor"),
            P("tensor"),
            P("tensor", dp),
            P("tensor", dp),
            P(),
            P(dp, None, "tensor"),
            P("tensor", dp),
        ),
        check_vma=False,
    )
```

```python
import jax
import jax.numpy as jnp
from jax import lax
from jax.experimental import pallas as pl
from jax.experimental.pallas import tpu as pltpu
from jax.sharding import Mesh
from jax.sharding import PartitionSpec as P

HEAD_SIZE = 64
N = 128
KCONV = 4
GH = 6
EPS = 1e-05
THETA = 10000.0
MASKED = -1e30
SWAP = [(0, 1), (1, 0)]


def low(values):
    return values.astype(jnp.bfloat16)


def wide(values):
    return values.astype(jnp.float32)


def dot(left, right):
    return jnp.dot(left, right, preferred_element_type=jnp.float32)


def dot_nt(left, right):
    return lax.dot_general(
        left, right, (((1,), (1,)), ((), ())), preferred_element_type=jnp.float32
    )


def dot_tn(left, right):
    return lax.dot_general(
        left, right, (((0,), (0,)), ((), ())), preferred_element_type=jnp.float32
    )


def dot_fine(left, right):
    high = low(right)
    rest = right - wide(high)
    mid = low(rest)
    last = low(rest - wide(mid))
    return dot(left, high) + dot(left, mid) + dot(left, last)


def dot_by(left, right):
    high = low(left)
    rest = left - wide(high)
    mid = low(rest)
    last = low(rest - wide(mid))
    return dot(high, right) + dot(mid, right) + dot(last, right)


def sigmoid(values):
    return 1.0 / (1.0 + jnp.exp(-values))


def turn(values, cosine, sine):
    lane = lax.broadcasted_iota(jnp.int32, values.shape, 1)
    half = HEAD_SIZE // 2
    up = pltpu.roll(values, 128 - half, 1)
    down = pltpu.roll(values, half, 1)
    return values * cosine + jnp.where(lane % HEAD_SIZE < half, up, down) * sine


def turn_back(values, cosine, sine):
    lane = lax.broadcasted_iota(jnp.int32, values.shape, 1)
    half = HEAD_SIZE // 2
    turned = values * sine
    up = pltpu.roll(turned, 128 - half, 1)
    down = pltpu.roll(turned, half, 1)
    return values * cosine + jnp.where(lane % HEAD_SIZE < half, up, down)


SCALE = HEAD_SIZE ** (-0.5)
ROWS = 256


def key_value_parts(kv, cosine, sine):
    lane = lax.broadcasted_iota(jnp.int32, kv.shape, 1)
    key = jnp.where(lane < HEAD_SIZE, turn(kv, cosine, sine), 0.0)
    value = jnp.where(lane < HEAD_SIZE, 0.0, kv)
    keys = (low(key), low(pltpu.roll(key, HEAD_SIZE, 1)))
    values = (low(pltpu.roll(value, HEAD_SIZE, 1)), low(value))
    return keys, values


def block_scores(query, keys, begin, seq_len):
    scores = dot_nt(query, keys)
    row = lax.broadcasted_iota(jnp.int32, (scores.shape[0], 1), 0) + begin
    col = lax.broadcasted_iota(jnp.int32, scores.shape, 1)
    return jnp.where(col < jnp.minimum(row + 1, seq_len), scores, MASKED)


def attention_forward_kernel(len_ref, q_ref, kv_ref, cos_ref, sin_ref, out_ref, sum_ref):
    seq_len = len_ref[0]
    cosine, sine = cos_ref[...], sin_ref[...]
    keys, values = key_value_parts(kv_ref[...], cosine, sine)
    query = low(turn(q_ref[...], cosine, sine) * SCALE)
    rows = query.shape[0]
    lane = lax.broadcasted_iota(jnp.int32, (ROWS, 128), 1)
    for begin in range(0, rows, ROWS):
        end = begin + ROWS
        outs, sums = [], []
        for head in range(2):
            scores = block_scores(query[begin:end], keys[head][:end], begin, seq_len)
            peak = jnp.max(scores, axis=1, keepdims=True)
            exps = jnp.exp(scores - peak)
            total = jnp.sum(exps, axis=1, keepdims=True)
            probs = low(exps * (1.0 / total))
            outs.append(dot(probs, values[head][:end]))
            sums.append(peak + jnp.log(total))
        out_ref[begin:end, :] = low(outs[0] + outs[1])
        sum_ref[begin:end, :] = jnp.where(lane < HEAD_SIZE, sums[0], sums[1])


def attention_backward_kernel(
    len_ref, q_ref, kv_ref, cos_ref, sin_ref, sum_ref, grad_ref, dq_ref, dkv_ref, dk_acc, dv_acc
):
    seq_len = len_ref[0]
    cosine, sine = cos_ref[...], sin_ref[...]
    keys, values = key_value_parts(kv_ref[...], cosine, sine)
    query = low(turn(q_ref[...], cosine, sine) * SCALE)
    query_t = query.T
    rows = query.shape[0]
    group = pl.program_id(0)
    grad = low(grad_ref[...])
    grad_t = grad.T

    @pl.when(group == 0)
    def _():
        dk_acc[...] = jnp.zeros_like(dk_acc)
        dv_acc[...] = jnp.zeros_like(dv_acc)

    for begin in range(0, rows, ROWS):
        end = begin + ROWS
        dq = jnp.zeros((ROWS, 128), jnp.float32)
        for head in range(2):
            lanes = slice(head * HEAD_SIZE, (head + 1) * HEAD_SIZE)
            scores = block_scores(query[begin:end], keys[head][:end], begin, seq_len)
            at = head * HEAD_SIZE
            probs = jnp.exp(scores - sum_ref[begin:end, at : at + 1])
            dv_acc[:, :end] += dot(grad_t[lanes, begin:end], low(probs))
            dp = dot_nt(grad[begin:end], values[head][:end])
            inner = jnp.sum(probs * dp, axis=1, keepdims=True)
            ds = low(probs * (dp - inner))
            dq = dq + dot(ds, keys[head][:end])
            dk_acc[:, :end] += dot(query_t[lanes, begin:end], ds)
        dq = turn_back(dq * SCALE, cosine[begin:end], sine[begin:end])
        dq_ref[begin:end, :] = low(dq)

    @pl.when(group == pl.num_programs(0) - 1)
    def _():
        both = jnp.concatenate([dk_acc[...], dv_acc[...]], axis=0).T
        lane = lax.broadcasted_iota(jnp.int32, both.shape, 1)
        dkv_ref[...] = low(jnp.where(lane < HEAD_SIZE, turn_back(both, cosine, sine), both))


def attention_specs(rows, group_cols):
    whole = pl.BlockSpec((rows, 128), lambda g: (0, 0))
    return [
        pl.BlockSpec(memory_space=pltpu.SMEM),
        pl.BlockSpec((rows, 128), lambda g: (0, g * (group_cols // 128) + 6)),
        pl.BlockSpec((rows, 128), lambda g: (0, 2 * (group_cols // 128) + 2)),
        whole,
        whole,
    ]


BIG = 60 * 1024 * 1024


def attention_forward(seq_len, proj, cosine, sine, group_cols):
    rows = proj.shape[0]
    pairs = pl.BlockSpec((rows, 128), lambda g: (0, g))
    return pl.pallas_call(
        attention_forward_kernel,
        grid=(2,),
        in_specs=attention_specs(rows, group_cols),
        out_specs=[pairs, pairs],
        out_shape=[
            jax.ShapeDtypeStruct((rows, 256), jnp.bfloat16),
            jax.ShapeDtypeStruct((rows, 256), jnp.float32),
        ],
        compiler_params=pltpu.CompilerParams(vmem_limit_bytes=BIG),
        name="attention_forward",
    )(seq_len, proj, proj, cosine, sine)


def attention_backward(seq_len, proj, cosine, sine, sums, grad, group_cols, grad_at):
    rows = proj.shape[0]
    pairs = pl.BlockSpec((rows, 128), lambda g: (0, g))
    return pl.pallas_call(
        attention_backward_kernel,
        grid=(2,),
        in_specs=attention_specs(rows, group_cols)
        + [pairs, pl.BlockSpec((rows, 128), lambda g: (0, grad_at + g))],
        out_specs=[pairs, pl.BlockSpec((rows, 128), lambda g: (0, 0))],
        out_shape=[
            jax.ShapeDtypeStruct((rows, 256), jnp.bfloat16),
            jax.ShapeDtypeStruct((rows, 128), jnp.bfloat16),
        ],
        scratch_shapes=[
            pltpu.VMEM((HEAD_SIZE, rows), jnp.float32),
            pltpu.VMEM((HEAD_SIZE, rows), jnp.float32),
        ],
        compiler_params=pltpu.CompilerParams(vmem_limit_bytes=BIG),
        name="attention_backward",
    )(seq_len, proj, proj, cosine, sine, sums, grad)


CHUNK = 128
GROUP = GH * HEAD_SIZE
PAIRS = GH // 2
CONV = 2 * GROUP + 2 * N
SHARED = 2048


def triangle():
    row = lax.broadcasted_iota(jnp.int32, (CHUNK, CHUNK), 0)
    col = lax.broadcasted_iota(jnp.int32, (CHUNK, CHUNK), 1)
    return col <= row


def pair_lanes(values, pair):
    lane = lax.broadcasted_iota(jnp.int32, (values.shape[0], 128), 1)
    at = 2 * pair
    return jnp.where(lane < HEAD_SIZE, values[:, at : at + 1], values[:, at + 1 : at + 2])


def split_pair(values):
    lane = lax.broadcasted_iota(jnp.int32, values.shape, 1)
    empty = jnp.zeros_like(values)
    return jnp.concatenate(
        [jnp.where(lane < HEAD_SIZE, values, empty), jnp.where(lane < HEAD_SIZE, empty, values)],
        axis=0,
    )


def conv_pre(buf_ref, taps_ref, begin, size):
    total = buf_ref[5 : 5 + CHUNK, begin : begin + size] * taps_ref[0:1, begin : begin + size]
    for tap in range(1, KCONV):
        total = total + (
            buf_ref[5 + tap : 5 + tap + CHUNK, begin : begin + size]
            * taps_ref[tap : tap + 1, begin : begin + size]
        )
    return total


def load_conv(buf_ref, proj_ref):
    for group in range(2):
        at = group * 1024 + GROUP
        buf_ref[8:, group * GROUP : (group + 1) * GROUP] = proj_ref[:, at : at + GROUP]
    buf_ref[8:, 2 * GROUP :] = proj_ref[:, SHARED : SHARED + 2 * N]


def group_steps(proj_ref, bias_ref, decay_ref, group, lower):
    at = group * 1024 + 896
    raw = proj_ref[:, at : at + 128] + bias_ref[group : group + 1, :]
    step = jnp.log1p(jnp.exp(-jnp.abs(raw))) + jnp.maximum(raw, 0.0)
    rate = -jnp.exp(decay_ref[group : group + 1, :])
    cumul = dot_fine(lower, rate * step)
    return raw, step, rate, cumul


def head_decay(cumul, cumul_t, head, mask):
    spread = cumul[:, head : head + 1] - cumul_t[head : head + 1, :]
    return jnp.exp(jnp.where(mask, spread, MASKED))


def mamba_forward_kernel(
    proj_ref,
    attn_ref,
    taps_ref,
    bias_ref,
    decay_ref,
    skip_ref,
    gain_ref,
    both_ref,
    out_ref,
    states_ref,
    buf_ref,
    state_ref,
):
    chunk = pl.program_id(0)

    @pl.when(chunk == 0)
    def _():
        buf_ref[0:8, :] = jnp.zeros((8, CONV), jnp.float32)
        state_ref[...] = jnp.zeros_like(state_ref)

    load_conv(buf_ref, proj_ref)
    mask = triangle()
    lower = mask.astype(jnp.bfloat16)
    pre = conv_pre(buf_ref, taps_ref, 2 * GROUP, 2 * N)
    state_act = low(pre * sigmoid(pre))
    b_rows, c_rows = state_act[:, :N], state_act[:, N:]
    gram = dot_nt(c_rows, b_rows)
    b_cols = b_rows.T
    for group in range(2):
        cols = slice(group * GROUP, (group + 1) * GROUP)
        _, step, _, cumul = group_steps(proj_ref, bias_ref, decay_ref, group, lower)
        cumul_t = cumul.T
        last = cumul[CHUNK - 1 : CHUNK, :]
        state = state_ref[:, cols]
        states_ref[0, :, cols] = state
        from_state = dot(c_rows, low(state))
        gated = []
        for pair in range(PAIRS):
            at = group * GROUP + pair * 128
            pre = conv_pre(buf_ref, taps_ref, at, 128)
            chan = pre * sigmoid(pre)
            inputs = low(chan * pair_lanes(step, pair))
            mixing = jnp.concatenate(
                [
                    low(gram * head_decay(cumul, cumul_t, 2 * pair + side, mask))
                    for side in range(2)
                ],
                axis=1,
            )
            lanes = slice(pair * 128, (pair + 1) * 128)
            inner = pair_lanes(cumul, pair)
            out = dot(mixing, split_pair(inputs)) + jnp.exp(inner) * from_state[:, lanes]
            out_ref[:, at : at + 128] = out
            last_lanes = pair_lanes(last, pair)
            x_end = low(jnp.exp(last_lanes - inner) * wide(inputs))
            state_ref[:, at : at + 128] = jnp.exp(last_lanes) * state[:, lanes] + dot(
                b_cols, x_end
            )
            gate = proj_ref[:, group * 1024 + pair * 128 : group * 1024 + pair * 128 + 128]
            skipped = out + chan * skip_ref[:, at : at + 128]
            gated.append(skipped * (gate * sigmoid(gate)))
        square = sum(jnp.sum(part * part, axis=1, keepdims=True) for part in gated)
        scale = lax.rsqrt(square * (1.0 / GROUP) + EPS)
        for pair in range(PAIRS):
            at = group * GROUP + pair * 128
            to = group * 512 + pair * 128
            both_ref[:, to : to + 128] = low(gated[pair] * scale * gain_ref[:, at : at + 128])
        to = group * 512 + GROUP
        both_ref[:, to : to + 128] = attn_ref[:, group * 128 : (group + 1) * 128]
    buf_ref[0:8, :] = buf_ref[CHUNK : CHUNK + 8, :]


def mamba_forward(proj, attn, taps, bias, decay, skip, gain):
    rows, columns = proj.shape
    chunks = rows // CHUNK

    def whole(value):
        return pl.BlockSpec(value.shape, lambda k: (0, 0))

    return pl.pallas_call(
        mamba_forward_kernel,
        grid=(chunks,),
        in_specs=[
            pl.BlockSpec((CHUNK, columns), lambda k: (k, 0)),
            pl.BlockSpec((CHUNK, 256), lambda k: (k, 0)),
        ]
        + [whole(value) for value in (taps, bias, decay, skip, gain)],
        out_specs=[
            pl.BlockSpec((CHUNK, 1024), lambda k: (k, 0)),
            pl.BlockSpec((CHUNK, 2 * GROUP), lambda k: (k, 0)),
            pl.BlockSpec((1, N, 2 * GROUP), lambda k: (k, 0, 0)),
        ],
        out_shape=[
            jax.ShapeDtypeStruct((rows, 1024), jnp.bfloat16),
            jax.ShapeDtypeStruct((rows, 2 * GROUP), jnp.float32),
            jax.ShapeDtypeStruct((chunks, N, 2 * GROUP), jnp.float32),
        ],
        scratch_shapes=[
            pltpu.VMEM((CHUNK + 8, CONV), jnp.float32),
            pltpu.VMEM((N, 2 * GROUP), jnp.float32),
        ],
        compiler_params=pltpu.CompilerParams(vmem_limit_bytes=BIG),
        name="mamba_forward",
    )(proj, attn, taps, bias, decay, skip, gain)


def silu_slope(values, sig):
    return sig * (1.0 + values * (1.0 - sig))


def mamba_backward_kernel(
    proj_ref,
    before_ref,
    out_ref,
    states_ref,
    back_ref,
    dq_ref,
    dkv_ref,
    taps_ref,
    bias_ref,
    decay_ref,
    skip_ref,
    gain_ref,
    dproj_ref,
    dtaps_ref,
    dgain_ref,
    dskip_ref,
    dbias_ref,
    ddecay_ref,
    buf_ref,
    grad_buf,
    after_ref,
    flow_ref,
):
    step_at = pl.program_id(0)

    @pl.when(step_at == 0)
    def _():
        for ref in (dtaps_ref, dgain_ref, dskip_ref, dbias_ref, ddecay_ref, after_ref, flow_ref):
            ref[...] = jnp.zeros_like(ref)
        grad_buf[CHUNK:, :] = jnp.zeros((8, CONV), jnp.float32)

    inside = jnp.where(step_at == pl.num_programs(0) - 1, 0.0, 1.0)
    for group in range(2):
        at = group * 1024 + GROUP
        buf_ref[0:8, group * GROUP : (group + 1) * GROUP] = before_ref[:, at : at + GROUP] * inside
    buf_ref[0:8, 2 * GROUP :] = before_ref[:, SHARED : SHARED + 2 * N] * inside
    load_conv(buf_ref, proj_ref)
    mask = triangle()
    lower = mask.astype(jnp.bfloat16)
    row = lax.broadcasted_iota(jnp.int32, (CHUNK, CHUNK), 0)
    col = lax.broadcasted_iota(jnp.int32, (CHUNK, CHUNK), 1)
    upper = (row <= col).astype(jnp.bfloat16)
    pre_state = conv_pre(buf_ref, taps_ref, 2 * GROUP, 2 * N)
    sig_state = sigmoid(pre_state)
    state_act = low(pre_state * sig_state)
    b_rows, c_rows = state_act[:, :N], state_act[:, N:]
    gram = dot_nt(c_rows, b_rows)
    c_cols = c_rows.T
    dgram = jnp.zeros((CHUNK, CHUNK), jnp.float32)
    d_c = jnp.zeros((CHUNK, N), jnp.float32)
    d_b = jnp.zeros((CHUNK, N), jnp.float32)
    for group in range(2):
        raw, step, rate, cumul = group_steps(proj_ref, bias_ref, decay_ref, group, lower)
        cumul_t = cumul.T
        last = cumul[CHUNK - 1 : CHUNK, :]
        pres, sigs, chans, gates, gate_sigs, skips, gated = [], [], [], [], [], [], []
        for pair in range(PAIRS):
            at = group * GROUP + pair * 128
            pre = conv_pre(buf_ref, taps_ref, at, 128)
            sig = sigmoid(pre)
            chan = pre * sig
            gate = proj_ref[:, group * 1024 + pair * 128 : group * 1024 + pair * 128 + 128]
            gate_sig = sigmoid(gate)
            skipped = out_ref[:, at : at + 128] + chan * skip_ref[:, at : at + 128]
            pres.append(pre)
            sigs.append(sig)
            chans.append(chan)
            gates.append(gate)
            gate_sigs.append(gate_sig)
            skips.append(skipped)
            gated.append(skipped * (gate * gate_sig))
        square = sum(jnp.sum(part * part, axis=1, keepdims=True) for part in gated)
        scale = lax.rsqrt(square * (1.0 / GROUP) + EPS)
        grads = []
        cross = jnp.zeros((CHUNK, 1), jnp.float32)
        for pair in range(PAIRS):
            at = group * GROUP + pair * 128
            grad = back_ref[:, group * 512 + pair * 128 : group * 512 + pair * 128 + 128]
            dgain_ref[:, at : at + 128] += jnp.sum(grad * gated[pair] * scale, axis=0, keepdims=True)
            grad = grad * gain_ref[:, at : at + 128]
            cross = cross + jnp.sum(gated[pair] * grad, axis=1, keepdims=True)
            grads.append(grad)
        cross = cross * (1.0 / GROUP) * scale * scale * scale
        dstep = jnp.zeros((CHUNK, 128), jnp.float32)
        flow = jnp.zeros((CHUNK, 128), jnp.float32)
        flow_end = flow_ref[group : group + 1, :]
        flow_next = jnp.zeros((1, 128), jnp.float32)
        for pair in range(PAIRS):
            at = group * GROUP + pair * 128
            head_of_lane = lax.broadcasted_iota(jnp.int32, (128, 128), 0) // HEAD_SIZE + 2 * pair
            lane = lax.broadcasted_iota(jnp.int32, (128, 128), 1)
            pick = (head_of_lane == lane).astype(jnp.bfloat16)
            chan = chans[pair]
            grad = scale * grads[pair] - gated[pair] * cross
            gate, gate_sig = gates[pair], gate_sigs[pair]
            dgate = grad * skips[pair] * silu_slope(gate, gate_sig)
            to = group * 1024 + pair * 128
            dproj_ref[:, to : to + 128] = low(dgate)
            grad = grad * (gate * gate_sig)
            dskip_ref[:, at : at + 128] += jnp.sum(grad * chan, axis=0, keepdims=True)
            dchan = grad * skip_ref[:, at : at + 128]
            dout = low(grad)
            step_lanes = pair_lanes(step, pair)
            inputs = low(chan * step_lanes)
            halves = split_pair(inputs)
            decays = [head_decay(cumul, cumul_t, 2 * pair + side, mask) for side in range(2)]
            mixing = jnp.concatenate([low(gram * decay) for decay in decays], axis=1)
            dmix = dot_nt(dout, halves)
            dgram = dgram + dmix[:, :CHUNK] * decays[0] + dmix[:, CHUNK:] * decays[1]
            dinputs = dot_tn(mixing, dout)
            lane = lax.broadcasted_iota(jnp.int32, (CHUNK, 128), 1)
            dinputs = jnp.where(lane < HEAD_SIZE, dinputs[:CHUNK], dinputs[CHUNK:])
            inner = pair_lanes(cumul, pair)
            last_lanes = pair_lanes(last, pair)
            to_end = jnp.exp(last_lanes - inner)
            after = after_ref[:, at : at + 128]
            after_low = low(after)
            dinputs = dinputs + to_end * dot(b_rows, after_low)
            x_end = low(to_end * wide(inputs))
            g_start = low(jnp.exp(inner) * wide(dout))
            state = states_ref[0, :, at : at + 128]
            d_c = d_c + dot_nt(g_start, low(state))
            d_b = d_b + dot_nt(x_end, after_low)
            after = jnp.exp(last_lanes) * after + dot(c_cols, g_start)
            after_ref[:, at : at + 128] = after
            through = jnp.sum(after * state, axis=0, keepdims=True)
            flow_next = flow_next + dot_by(jnp.broadcast_to(through, (8, 128)), pick)[0:1]
            flow = flow + dot_by(
                wide(dout) * out_ref[:, at : at + 128] - wide(inputs) * dinputs, pick
            )
            dstep = dstep + dot_by(dinputs * chan, pick)
            dchan = dchan + dinputs * step_lanes
            grad_buf[0:CHUNK, at : at + 128] = dchan * silu_slope(pres[pair], sigs[pair])
        dcumul = dot_fine(upper, flow) + flow_end
        flow_ref[group : group + 1, :] = flow_next
        dstep = dstep + rate * dcumul
        ddecay_ref[group : group + 1, :] += jnp.sum(rate * step * dcumul, axis=0, keepdims=True)
        draw = dstep * sigmoid(raw)
        dbias_ref[group : group + 1, :] += jnp.sum(draw, axis=0, keepdims=True)
        to = group * 1024 + 896
        lane = lax.broadcasted_iota(jnp.int32, (CHUNK, 128), 1)
        dproj_ref[:, to : to + 128] = low(jnp.where(lane < GH, draw, 0.0))
        to = group * 1024 + 2 * GROUP
        dproj_ref[:, to : to + 128] = dq_ref[:, group * 128 : (group + 1) * 128]
    dgram_low = low(dgram)
    d_c = d_c + dot(dgram_low, b_rows)
    d_b = d_b + dot_tn(dgram_low, c_rows)
    slope = silu_slope(pre_state, sig_state)
    grad_buf[0:CHUNK, 2 * GROUP : 2 * GROUP + N] = d_b * slope[:, :N]
    grad_buf[0:CHUNK, 2 * GROUP + N :] = d_c * slope[:, N:]
    for at in range(0, CONV, 128):
        grad = jnp.zeros((CHUNK, 128), jnp.float32)
        here = grad_buf[0:CHUNK, at : at + 128]
        for tap in range(KCONV):
            shift = KCONV - 1 - tap
            grad = grad + (
                grad_buf[shift : shift + CHUNK, at : at + 128] * taps_ref[tap : tap + 1, at : at + 128]
            )
            dtaps_ref[tap : tap + 1, at : at + 128] += jnp.sum(
                here * buf_ref[5 + tap : 5 + tap + CHUNK, at : at + 128], axis=0, keepdims=True
            )
        if at < 2 * GROUP:
            to = (at // GROUP) * 1024 + GROUP + at % GROUP
        else:
            to = SHARED + at - 2 * GROUP
        dproj_ref[:, to : to + 128] = low(grad)
    dproj_ref[:, SHARED + 2 * N :] = dkv_ref[...]
    grad_buf[CHUNK:, :] = grad_buf[0:8, :]


def mamba_backward(proj, out, states, back, dq, dkv, taps, bias, decay, skip, gain):
    rows, columns = proj.shape
    chunks = rows // CHUNK

    def whole(value):
        return pl.BlockSpec(value.shape, lambda k: (0, 0))

    def rows_of(width):
        return pl.BlockSpec((CHUNK, width), lambda k: (chunks - 1 - k, 0))

    params = (taps, bias, decay, skip, gain)
    return pl.pallas_call(
        mamba_backward_kernel,
        grid=(chunks,),
        in_specs=[
            rows_of(columns),
            pl.BlockSpec(
                (8, columns),
                lambda k: (jnp.maximum((chunks - 1 - k) * (CHUNK // 8) - 1, 0), 0),
            ),
            rows_of(2 * GROUP),
            pl.BlockSpec((1, N, 2 * GROUP), lambda k: (chunks - 1 - k, 0, 0)),
            rows_of(1024),
            rows_of(256),
            rows_of(128),
        ]
        + [whole(value) for value in params],
        out_specs=[rows_of(columns)]
        + [whole(value) for value in (taps, gain, skip, bias, decay)],
        out_shape=[jax.ShapeDtypeStruct((rows, columns), jnp.bfloat16)]
        + [
            jax.ShapeDtypeStruct(value.shape, jnp.float32)
            for value in (taps, gain, skip, bias, decay)
        ],
        scratch_shapes=[
            pltpu.VMEM((CHUNK + 8, CONV), jnp.float32),
            pltpu.VMEM((CHUNK + 8, CONV), jnp.float32),
            pltpu.VMEM((N, 2 * GROUP), jnp.float32),
            pltpu.VMEM((8, 128), jnp.float32),
        ],
        compiler_params=pltpu.CompilerParams(vmem_limit_bytes=BIG),
        name="mamba_backward",
    )(proj, proj, out, states, back, dq, dkv, *params)


MESH = pl.DeviceIdType.MESH


def landed(ref, sem):
    pltpu.make_async_copy(ref, ref, sem).wait()


def spread_kernel(
    pack_ref,
    next_ref,
    ups_ref,
    downs_ref,
    shared_ref,
    x_ref,
    small_ref,
    w_ref,
    v_ref,
    up_rows,
    down_rows,
    full_ref,
    params_ref,
    near_sem,
    out_sem,
    part_sem,
    fromx_sem,
    fromy_sem,
    overx_sem,
    overy_sem,
    tox_sem,
    toy_sem,
    relx_sem,
    rely_sem,
    row_sem,
    row_out,
    pair_sem,
    pair_out,
    param_sem,
    param_out,
    ffn_sem,
    ffn_out,
):
    plane = lax.axis_index("plane")
    core = lax.axis_index("core")
    place = lax.axis_index("tensor")
    xside = plane + 1 - 2 * (plane % 2)
    yside = plane + 2 - 4 * (plane // 2)
    across = xside + 2 - 4 * (xside // 2)
    target = place // 2
    column = place % 2
    share, width = pack_ref.shape
    narrow = next_ref.shape[1]
    rest = shared_ref.shape[2]
    half = share
    rows_dev = x_ref.shape[1]

    barrier = pltpu.get_barrier_semaphore()
    for step in range(4):
        for side in range(2):
            if step or side:
                pl.semaphore_signal(
                    barrier,
                    inc=1,
                    device_id={"core": (core + side) % 2, "tensor": (place + step) % 4},
                    device_id_type=MESH,
                )
    for neighbour in (xside, yside):
        pl.semaphore_signal(
            barrier, inc=1, device_id={"plane": neighbour}, device_id_type=MESH
        )
    pl.semaphore_wait(barrier, 9)

    def block(at, part):
        return pl.ds(pl.multiple_of(at * 2 * share + part * share, share), share)

    def piece(at, part, col):
        return w_ref.at[block(at, part), pl.ds(pl.multiple_of(col * width, width), width)]

    def next_piece(at, part, col):
        return v_ref.at[block(at, part), pl.ds(pl.multiple_of(col * narrow, narrow), narrow)]

    def rest_piece(at, part):
        return w_ref.at[block(at, part), pl.ds(2 * width, rest)]

    started = []

    def send(src, dst, send_sem, recv_sem, device):
        copy = pltpu.make_async_remote_copy(
            src_ref=src,
            dst_ref=dst,
            send_sem=send_sem,
            recv_sem=recv_sem,
            device_id=device,
            device_id_type=MESH,
        )
        copy.start()
        started.append((src, send_sem))

    mine = piece(plane, core, column)
    slot = core * 2 + column
    mine_next = next_piece(plane, core, column)

    def send_parts(src, dst, at, recv_sem):
        for step in (2, 1, 3):
            send(
                src,
                dst,
                out_sem.at[at + step],
                recv_sem,
                {"core": target, "tensor": (place + step) % 4},
            )

    send_parts(pack_ref, mine, 0, part_sem.at[slot])
    send_parts(next_ref, mine_next, 4, part_sem.at[6 + slot])

    params = params_ref.at[column]

    @pl.when(target == core)
    def _():
        pltpu.make_async_copy(pack_ref, mine, part_sem.at[slot]).start()
        pltpu.make_async_copy(next_ref, mine_next, part_sem.at[6 + slot]).start()
        pltpu.make_async_copy(small_ref, params, param_sem.at[column]).start()
        for step in range(1, 4):
            pltpu.make_async_remote_copy(
                src_ref=small_ref,
                dst_ref=params,
                send_sem=param_out.at[step],
                recv_sem=param_sem.at[column],
                device_id={"tensor": (place + step) % 4},
                device_id_type=MESH,
            ).start()

    @pl.when(target != core)
    def _():
        pltpu.make_async_remote_copy(
            src_ref=pack_ref,
            dst_ref=mine,
            send_sem=out_sem.at[0],
            recv_sem=part_sem.at[slot],
            device_id={"core": 1 - core},
            device_id_type=MESH,
        ).start()
        pltpu.make_async_remote_copy(
            src_ref=next_ref,
            dst_ref=mine_next,
            send_sem=out_sem.at[4],
            recv_sem=part_sem.at[6 + slot],
            device_id={"core": 1 - core},
            device_id_type=MESH,
        ).start()

    own_rest = rest_piece(plane, core)
    near = pltpu.make_async_copy(shared_ref.at[core], own_rest, part_sem.at[4 + core])
    near.start()
    send(
        shared_ref.at[1 - core],
        own_rest,
        near_sem.at[0],
        part_sem.at[4 + core],
        {"core": 1 - core},
    )

    def rows_at(at, side):
        return full_ref.at[pl.ds(pl.multiple_of(at * rows_dev + side * half, half), half)]

    for seq in range(2):
        for side in range(2):
            goal = 2 * core + seq
            src = x_ref.at[seq, pl.ds(side * half, half)]
            dst = rows_at(place, side)
            here = jnp.logical_and(core == side, goal == place)

            @pl.when(here)
            def _():
                pltpu.make_async_copy(src, dst, row_sem.at[place]).start()

            @pl.when(jnp.logical_not(here))
            def _():
                pltpu.make_async_remote_copy(
                    src_ref=src,
                    dst_ref=dst,
                    send_sem=row_out.at[seq * 2 + side],
                    recv_sem=row_sem.at[place],
                    device_id={"core": side, "tensor": goal},
                    device_id_type=MESH,
                ).start()

    wide_up, wide_down = ups_ref.shape[2], downs_ref.shape[2]
    ffn_parts = []
    for number, (src, dst, size) in enumerate(
        ((ups_ref, up_rows, wide_up), (downs_ref, down_rows, wide_down))
    ):
        goal_ref = dst.at[
            pl.ds(pl.multiple_of(core * share, share), share),
            pl.ds(pl.multiple_of(place * size, size), size),
        ]
        for step in (2, 1, 3):
            for side in range(2):
                send(
                    src.at[side],
                    goal_ref,
                    ffn_out.at[number, 2 * step + side],
                    ffn_sem.at[number, 2 * place + core],
                    {"core": side, "tensor": (place + step) % 4},
                )
        send(
            src.at[1 - core],
            goal_ref,
            ffn_out.at[number, 0],
            ffn_sem.at[number, 2 * place + core],
            {"core": 1 - core},
        )
        pltpu.make_async_copy(src.at[core], goal_ref, ffn_sem.at[number, 2 * place + core]).start()
        for at in range(4):
            for part in range(2):
                ffn_parts.append(
                    (
                        dst.at[pl.ds(part * share, share), pl.ds(at * size, size)],
                        ffn_sem.at[number, 2 * at + part],
                    )
                )

    first_col = jnp.where(place // 2 == core, place % 2, 1 - core)
    order = [(0, None, 0), (0, None, 1)]
    for kind in (1, 2):
        for turn in range(2):
            for part in range(2):
                order.append((kind, (first_col + turn) % 2, part))

    def at_piece(at, item):
        kind, col, part = item
        if kind == 0:
            return rest_piece(at, part)
        return piece(at, part, col) if kind == 1 else next_piece(at, part, col)

    def index(item):
        kind, col, part = item
        return 4 + part if kind == 0 else (kind - 1) * 6 + part * 2 + col

    def relay(item):
        at = index(item)
        if item[2] == 0:
            landed(at_piece(xside, item), fromx_sem.at[at])
            ref = at_piece(xside, item)
            send(ref, ref, rely_sem.at[at], overy_sem.at[at], {"plane": yside})
        else:
            landed(at_piece(yside, item), fromy_sem.at[at])
            ref = at_piece(yside, item)
            send(ref, ref, relx_sem.at[at], overx_sem.at[at], {"plane": xside})

    for number, item in enumerate(order):
        at = index(item)
        ref = at_piece(plane, item)
        landed(ref, part_sem.at[at])
        send(ref, ref, tox_sem.at[at], fromx_sem.at[at], {"plane": xside})
        send(ref, ref, toy_sem.at[at], fromy_sem.at[at], {"plane": yside})
        if number >= 2:
            relay(order[number - 2])
        if number == 9:
            for step in range(4):
                at = (place + step) % 4
                ref = rows_at(at, core)
                landed(ref, row_sem.at[at])
                send(ref, ref, pair_out.at[at], pair_sem.at[at], {"core": 1 - core})
    for item in order[-2:]:
        relay(item)
    for step in range(4):
        at = (place + step) % 4
        landed(rows_at(at, 1 - core), pair_sem.at[at])
    for item in order:
        at = index(item)
        if item[2] == 0:
            landed(at_piece(yside, item), fromy_sem.at[at])
            landed(at_piece(across, item), overy_sem.at[at])
        else:
            landed(at_piece(xside, item), fromx_sem.at[at])
            landed(at_piece(across, item), overx_sem.at[at])

    for src, sem in started:
        landed(src, sem)

    for at in range(2):
        landed(params_ref.at[at], param_sem.at[at])
    for ref, sem in ffn_parts:
        landed(ref, sem)

    @pl.when(target == core)
    def _():
        for step in range(1, 4):
            landed(small_ref, param_out.at[step])

    @pl.when(target != core)
    def _():
        landed(pack_ref, out_sem.at[0])
        landed(next_ref, out_sem.at[4])

    for seq in range(2):
        for side in range(2):
            here = jnp.logical_and(core == side, 2 * core + seq == place)

            @pl.when(jnp.logical_not(here))
            def _():
                landed(x_ref.at[seq, pl.ds(side * half, half)], row_out.at[seq * 2 + side])


def spread(pack, following, ups, downs, shared, x_rows, small):
    share, width = pack.shape
    narrow = following.shape[1]
    rest = shared.shape[2]
    rows = x_rows.shape[1] * 4
    dma = pltpu.SemaphoreType.DMA
    any_space = pl.BlockSpec(memory_space=pl.ANY)
    return pl.pallas_call(
        spread_kernel,
        in_specs=[any_space] * 7,
        out_specs=[any_space] * 6,
        out_shape=[
            jax.ShapeDtypeStruct((8 * share, 2 * width + rest), pack.dtype),
            jax.ShapeDtypeStruct((8 * share, 2 * narrow), pack.dtype),
            jax.ShapeDtypeStruct((2 * share, 4 * ups.shape[2]), pack.dtype),
            jax.ShapeDtypeStruct((2 * share, 4 * downs.shape[2]), pack.dtype),
            jax.ShapeDtypeStruct((rows, x_rows.shape[2]), x_rows.dtype),
            jax.ShapeDtypeStruct((2,) + small.shape, small.dtype),
        ],
        scratch_shapes=[dma((1,)), dma((8,))] + [dma((10,))] * 9 + [dma((4,))] * 6 + [dma((2, 8))] * 2,
        compiler_params=pltpu.CompilerParams(collective_id=1, has_side_effects=True),
        name="spread",
    )(pack, following, ups, downs, shared, x_rows, small)


def collect_kernel(
    grad_ref,
    next_ref,
    small_ref,
    rows_ref,
    one_ref,
    shared_ref,
    total_ref,
    back_ref,
    mamba_out,
    attn_out,
    in_ref,
    next_in,
    sum_ref,
    next_sum,
    piece_ref,
    next_buf,
    pair_ref,
    mix_ref,
    near_ref,
    far_ref,
    in_sem,
    out_sem,
    piece_sem,
    piece_out,
    pair_sem,
    mix_sem,
    mix_out,
    near_sem,
    near_out,
    far_sem,
    far_out,
    row_sem,
    row_out,
):
    plane = lax.axis_index("plane")
    core = lax.axis_index("core")
    place = lax.axis_index("tensor")
    xside = plane + 1 - 2 * (plane % 2)
    yside = plane + 2 - 4 * (plane // 2)
    across = xside + 2 - 4 * (xside // 2)
    share, width = one_ref.shape
    rest = grad_ref.shape[1] - 2 * width

    barrier = pltpu.get_barrier_semaphore()
    for step in range(4):
        for side in range(2):
            if step or side:
                pl.semaphore_signal(
                    barrier,
                    inc=1,
                    device_id={"core": (core + side) % 2, "tensor": (place + step) % 4},
                    device_id_type=MESH,
                )
    for neighbour in (xside, yside):
        pl.semaphore_signal(
            barrier, inc=1, device_id={"plane": neighbour}, device_id_type=MESH
        )
    pl.semaphore_wait(barrier, 9)

    started = []

    def send(src, dst, send_sem, recv_sem, device):
        pltpu.make_async_remote_copy(
            src_ref=src,
            dst_ref=dst,
            send_sem=send_sem,
            recv_sem=recv_sem,
            device_id=device,
            device_id_type=MESH,
        ).start()
        started.append((src, send_sem))

    narrow = next_ref.shape[1] // 2
    spans = [(0, 2 * width, rest), (0, 0, width), (0, width, width)]
    spans += [(1, 0, narrow), (1, narrow, narrow)]

    def block(at, part, span):
        rows = pl.ds(pl.multiple_of(at * 2 * share + part * share, share), share)
        return (grad_ref, next_ref)[span[0]].at[rows, pl.ds(*span[1:])]

    def held(slot, span):
        return (in_ref, next_in)[span[0]].at[slot, :, pl.ds(*span[1:])]

    def summed(part, span):
        return (sum_ref, next_sum)[span[0]].at[part, :, pl.ds(*span[1:])]

    def begin(number):
        span = spans[number]
        send(
            block(across, 0, span),
            held(0, span),
            out_sem.at[0, number],
            in_sem.at[0, number],
            {"plane": xside},
        )
        send(
            block(across, 1, span),
            held(1, span),
            out_sem.at[1, number],
            in_sem.at[1, number],
            {"plane": yside},
        )
        send(
            block(xside, 0, span),
            held(2, span),
            out_sem.at[2, number],
            in_sem.at[2, number],
            {"plane": xside},
        )
        send(
            block(yside, 1, span),
            held(3, span),
            out_sem.at[3, number],
            in_sem.at[3, number],
            {"plane": yside},
        )

    send(small_ref, near_ref.at[0], near_out.at[0], near_sem.at[0], {"plane": xside})
    begin(0)
    begin(1)

    seq = place % 2
    owner = place // 2
    dst_rows = back_ref.at[seq, pl.ds(pl.multiple_of(core * share, share), share)]
    for step in (2, 1, 3):
        at = (place + step) % 4
        send(
            rows_ref.at[at],
            dst_rows,
            row_out.at[step],
            row_sem.at[seq * 2 + core],
            {"core": owner, "tensor": at},
        )

    @pl.when(owner == core)
    def _():
        pltpu.make_async_copy(rows_ref.at[place], dst_rows, row_sem.at[seq * 2 + core]).start()

    @pl.when(owner != core)
    def _():
        pltpu.make_async_remote_copy(
            src_ref=rows_ref.at[place],
            dst_ref=dst_rows,
            send_sem=row_out.at[0],
            recv_sem=row_sem.at[seq * 2 + core],
            device_id={"core": 1 - core},
            device_id_type=MESH,
        ).start()

    def pass_on(number):
        span = spans[number]
        landed(held(0, span), in_sem.at[0, number])
        held(0, span)[...] = low(wide(held(0, span)[...]) + wide(block(yside, 0, span)[...]))
        send(
            held(0, span),
            held(5, span),
            out_sem.at[4, number],
            in_sem.at[5, number],
            {"plane": yside},
        )
        landed(held(1, span), in_sem.at[1, number])
        held(1, span)[...] = low(wide(held(1, span)[...]) + wide(block(xside, 1, span)[...]))
        send(
            held(1, span),
            held(4, span),
            out_sem.at[5, number],
            in_sem.at[4, number],
            {"plane": xside},
        )

    def finish(number):
        span = spans[number]
        landed(held(2, span), in_sem.at[2, number])
        landed(held(5, span), in_sem.at[5, number])
        summed(0, span)[...] = low(
            wide(block(plane, 0, span)[...]) + wide(held(2, span)[...]) + wide(held(5, span)[...])
        )
        landed(held(3, span), in_sem.at[3, number])
        landed(held(4, span), in_sem.at[4, number])
        summed(1, span)[...] = low(
            wide(block(plane, 1, span)[...]) + wide(held(3, span)[...]) + wide(held(4, span)[...])
        )

    def send_pieces(number):
        span = spans[number]
        kind, col = span[0], span[1] // span[2]
        buf = (piece_ref, next_buf)[kind]
        goal = 2 * core + col
        for part in range(2):
            src = summed(part, span)
            here = jnp.logical_and(core == part, goal == place)

            @pl.when(here)
            def _():
                pltpu.make_async_copy(src, buf.at[place], piece_sem.at[kind, place]).start()

            @pl.when(jnp.logical_not(here))
            def _():
                pltpu.make_async_remote_copy(
                    src_ref=src,
                    dst_ref=buf.at[place],
                    send_sem=piece_out.at[kind, 2 * col + part],
                    recv_sem=piece_sem.at[kind, place],
                    device_id={"core": part, "tensor": goal},
                    device_id_type=MESH,
                ).start()

    rest_cols = pl.ds(2 * width, rest)
    state = rest * 2 // 3
    pass_on(0)
    landed(near_ref.at[0], near_sem.at[0])
    near_ref[3] = small_ref[...] + near_ref[0]
    send(near_ref.at[3], near_ref.at[1], near_out.at[1], near_sem.at[1], {"plane": yside})
    begin(2)
    finish(0)
    send(
        sum_ref.at[1 - core, :, rest_cols],
        pair_ref,
        pair_sem.at[0],
        pair_sem.at[1],
        {"core": 1 - core},
    )
    pass_on(1)
    begin(3)
    landed(near_ref.at[1], near_sem.at[1])
    near_ref[4] = near_ref[3] + near_ref[1]
    send(near_ref.at[4], near_ref.at[2], near_out.at[2], near_sem.at[2], {"core": 1 - core})
    landed(pair_ref, pair_sem.at[1])
    mine = sum_ref[core, :, rest_cols]
    mix_ref[place, :, 0:state] = low(wide(mine[:, :state]) + wide(pair_ref[:, :state]))
    first = core == 0
    mix_ref[place, :, state:rest] = jnp.where(first, mine[:, state:], pair_ref[:, state:])
    mix_ref[place, :, rest:] = jnp.where(first, pair_ref[:, state:], mine[:, state:])
    own_mix = mix_ref.at[place]
    for step in (2, 1, 3):
        send(
            own_mix,
            own_mix,
            mix_out.at[step],
            mix_sem.at[place],
            {"tensor": (place + step) % 4},
        )
    finish(1)
    send_pieces(1)
    pass_on(2)
    begin(4)
    landed(near_ref.at[2], near_sem.at[2])
    far_ref[place] = near_ref[4] + near_ref[2]
    own_far = far_ref.at[place]
    for step in (2, 1, 3):
        send(
            own_far,
            own_far,
            far_out.at[step],
            far_sem.at[place],
            {"tensor": (place + step) % 4},
        )
    finish(2)
    send_pieces(2)
    pass_on(3)
    finish(3)
    send_pieces(3)
    pass_on(4)
    finish(4)
    send_pieces(4)

    for step in (1, 2, 3):
        at = (place + step) % 4
        landed(mix_ref.at[at], mix_sem.at[at])
        landed(far_ref.at[at], far_sem.at[at])
    shared_ref[...] = (
        wide(mix_ref[0]) + wide(mix_ref[1]) + wide(mix_ref[2]) + wide(mix_ref[3])
    )
    total_ref[...] = (far_ref[0] + far_ref[1]) + (far_ref[2] + far_ref[3])
    def gathered(buf, kind):
        for at in range(4):
            landed(buf.at[at], piece_sem.at[kind, at])
        return wide(buf[0]) + wide(buf[1]) + wide(buf[2]) + wide(buf[3])

    one_ref[...] = gathered(piece_ref, 0)
    both = gathered(next_buf, 1).T
    mamba_out[...] = both[: mamba_out.shape[0]]
    attn_out[...] = both[mamba_out.shape[0] :]
    for at in range(4):
        landed(dst_rows, row_sem.at[at])
    for src, sem in started:
        landed(src, sem)

    @pl.when(owner != core)
    def _():
        landed(rows_ref.at[place], row_out.at[0])

    for span in spans[1:]:
        col = span[1] // span[2]
        for part in range(2):
            here = jnp.logical_and(core == part, 2 * core + col == place)

            @pl.when(jnp.logical_not(here))
            def _():
                landed(summed(part, span), piece_out.at[span[0], 2 * col + part])


def collect(grad, following, small, rows, width, mamba_cols):
    share = grad.shape[0] // 8
    rest = grad.shape[1] - 2 * width
    narrow = following.shape[1] // 2
    dma = pltpu.SemaphoreType.DMA
    any_space = pl.BlockSpec(memory_space=pl.ANY)
    near = pl.BlockSpec(memory_space=pltpu.VMEM)
    model = rows.shape[2]
    shared_cols = rest + rest // 3
    bf16, f32 = jnp.bfloat16, jnp.float32
    return pl.pallas_call(
        collect_kernel,
        in_specs=[near, near, near, any_space],
        out_specs=[near, near, near, any_space, near, near],
        out_shape=[
            jax.ShapeDtypeStruct((share, width), f32),
            jax.ShapeDtypeStruct((share, shared_cols), f32),
            jax.ShapeDtypeStruct(small.shape, f32),
            jax.ShapeDtypeStruct((2, 2 * rows.shape[1], model), rows.dtype),
            jax.ShapeDtypeStruct((mamba_cols, share), f32),
            jax.ShapeDtypeStruct((narrow - mamba_cols, share), f32),
        ],
        scratch_shapes=[
            pltpu.VMEM((6, share, grad.shape[1]), bf16),
            pltpu.VMEM((6, share, following.shape[1]), bf16),
            pltpu.VMEM((2, share, grad.shape[1]), bf16),
            pltpu.VMEM((2, share, following.shape[1]), bf16),
            pltpu.VMEM((4, share, width), bf16),
            pltpu.VMEM((4, share, narrow), bf16),
            pltpu.VMEM((share, rest), bf16),
            pltpu.VMEM((4, share, shared_cols), bf16),
            pltpu.VMEM((5,) + small.shape, f32),
            pltpu.VMEM((4,) + small.shape, f32),
            dma((6, 5)),
            dma((6, 5)),
            dma((2, 4)),
            dma((2, 4)),
            dma((2,)),
            dma((4,)),
            dma((4,)),
            dma((3,)),
            dma((3,)),
            dma((4,)),
            dma((4,)),
            dma((4,)),
            dma((4,)),
        ],
        compiler_params=pltpu.CompilerParams(
            collective_id=2, has_side_effects=True, vmem_limit_bytes=BIG
        ),
        name="collect",
    )(grad, following, small, rows)


def rms_norm(values, gain_vec):
    return values * lax.rsqrt(jnp.mean(values * values, axis=-1, keepdims=True) + EPS) * gain_vec


def turn_tables(seq_count, head_count):
    half_dim = HEAD_SIZE // 2
    freqs = THETA ** (-jnp.arange(half_dim, dtype=jnp.float32) * 2.0 / HEAD_SIZE)
    angles = jnp.arange(seq_count, dtype=jnp.float32)[:, None] * freqs[None, :]
    cosine, sine = jnp.cos(angles), jnp.sin(angles)
    return (
        jnp.tile(jnp.concatenate([cosine, cosine], axis=1), (1, head_count)),
        jnp.tile(jnp.concatenate([-sine, sine], axis=1), (1, head_count)),
    )


def swiglu(gate_up):
    rows, columns = gate_up.shape
    units = columns // 8
    parts = []
    for at in range(0, columns, 2 * units):
        gate, up = gate_up[:, at : at + units], gate_up[:, at + units : at + 2 * units]
        parts.append(gate * sigmoid(gate) * up)
    return jnp.concatenate(parts, axis=1)


def pairs_split(step):
    return [
        (core * 4 + place, (goal // 2) * 4 + 2 * core + goal % 2)
        for core in range(2)
        for place in range(4)
        for goal in [(place + step) % 4]
    ]


def pairs_join(step):
    return [
        (core * 4 + place, (place // 2) * 4 + (2 * core + place % 2 + step) % 4)
        for core in range(2)
        for place in range(4)
    ]


def exchange(piece_at, mine, yours, pairs):
    moved = [
        lax.ppermute(piece_at((mine + step) % 4), ("core", "tensor"), pairs(step))
        for step in range(4)
    ]
    stacked = jnp.stack(moved)
    return [
        lax.dynamic_index_in_dim(stacked, (yours - source) % 4, 0, False) for source in range(4)
    ]


def swapped(values):
    return lax.ppermute(values, "core", SWAP)


def body(
    layer_in,
    seq_lengths,
    out_grad,
    norm_gain,
    mixer_weight,
    step_weight,
    state_weight,
    query_weight,
    key_value_weight,
    conv_channels,
    conv_states,
    step_bias,
    decay_log,
    skip_scale,
    group_gain,
    mamba_proj,
    attn_proj,
    ffn_gain,
    ffn_weight,
    ffn_down,
):
    core = lax.axis_index("core")
    place = lax.axis_index("tensor")
    first = core == 0
    seq_dev, rows_dev, model_dim = layer_in.shape
    groups = lax.axis_size("tensor")
    seq_total = rows_dev * groups
    half_rows = rows_dev // 2
    share = mixer_weight.shape[0]
    chans_dev = mixer_weight.shape[2]
    heads_dev = step_weight.shape[1]
    query_dev = query_weight.shape[1]
    hidden_dev = ffn_weight.shape[2]
    held = groups // 2
    step_pad = 128

    def mine(values):
        return lax.dynamic_slice_in_dim(values, core * held, held, 0)

    def other(values):
        return lax.dynamic_slice_in_dim(values, (1 - core) * held, held, 0)

    def in_order(own, others, axis):
        return jnp.where(
            first,
            jnp.concatenate([own, others], axis=axis),
            jnp.concatenate([others, own], axis=axis),
        )

    def flat(values):
        return values.transpose(1, 0, 2).reshape(values.shape[1], -1)

    spot = 2 * core + place % 2

    def positions_in(values):
        shaped = values.reshape(seq_dev, 2, half_rows, model_dim)
        keep = lax.dynamic_index_in_dim(shaped, core, 1, False)
        send = lax.dynamic_index_in_dim(shaped, 1 - core, 1, False)
        return lax.all_to_all(in_order(keep, swapped(send), 0), "tensor", 0, 0, tiled=True)

    def both_halves(own):
        both = in_order(own[:, None], swapped(own)[:, None], 1)
        return both.reshape(seq_total, model_dim)

    def positions_out(own):
        four = lax.all_to_all(own, "tensor", 0, 0, tiled=True)
        keep = lax.dynamic_slice_in_dim(four, core * seq_dev, seq_dev, 0)
        send = lax.dynamic_slice_in_dim(four, (1 - core) * seq_dev, seq_dev, 0)
        both = in_order(keep[:, None], swapped(send)[:, None], 1)
        return both.reshape(seq_dev, rows_dev, model_dim)

    def own_half(values):
        shaped = values.reshape(groups, 2, half_rows, -1)
        return lax.dynamic_index_in_dim(shaped, core, 1, False)

    def other_half(values):
        shaped = values.reshape(groups, 2, half_rows, -1)
        return lax.dynamic_index_in_dim(shaped, 1 - core, 1, False)

    out_dev = chans_dev + query_dev
    pack_two = jnp.concatenate([mamba_proj.T, attn_proj.T], axis=1)
    own_units = hidden_dev // 2
    pack_ups = ffn_weight.reshape(share, 2, 2, own_units).transpose(2, 0, 1, 3)
    pack_ups = pack_ups.reshape(2, share, hidden_dev)
    pack_downs = ffn_down.reshape(2, own_units, share).transpose(0, 2, 1)
    out_dev = chans_dev + query_dev
    pack_two = jnp.concatenate([mamba_proj.T, attn_proj.T], axis=1)
    pack_one = jnp.concatenate(
        [
            mixer_weight.reshape(share, 2 * chans_dev),
            query_weight,
            jnp.pad(step_weight, ((0, 0), (0, step_pad - heads_dev))),
        ],
        axis=1,
    )
    kv_heads = key_value_weight.reshape(share, 2, 2, HEAD_SIZE)

    def shared_for(at):
        return jnp.concatenate(
            [
                state_weight.reshape(share, 2 * N),
                lax.dynamic_index_in_dim(kv_heads, at, 2, False).reshape(share, 2 * HEAD_SIZE),
            ],
            axis=1,
        )

    small_in = jnp.concatenate(
        [conv_channels.reshape(-1), step_bias, decay_log, skip_scale, group_gain]
    )
    small_pad = -(-small_in.shape[0] // 1024) * 1024
    small_in = jnp.pad(small_in, (0, small_pad - small_in.shape[0])).reshape(-1, 128)
    quad = lax.axis_size("plane") == 4 and groups == 4 and share % 16 == 0
    quad = quad and share == half_rows
    if quad:
        shared = jnp.stack([shared_for(0), shared_for(1)])
        weight_one, weight_two, rows_up, rows_down, x_low, small_mine = spread(
            pack_one, pack_two, pack_ups, pack_downs, shared, layer_in, small_in
        )
    else:
        x_low = both_halves(positions_in(layer_in))
        all_one = lax.all_gather(pack_one, "tensor", axis=0)
        own_one = jnp.concatenate([flat(mine(all_one)), shared_for(core)], axis=1)
        their_one = jnp.concatenate([flat(other(all_one)), shared_for(1 - core)], axis=1)
        weight_one = lax.all_gather(
            in_order(own_one, swapped(their_one), 0), "plane", axis=0, tiled=True
        )
        all_two = lax.all_gather(pack_two, "tensor", axis=0)
        weight_two = lax.all_gather(
            in_order(flat(mine(all_two)), swapped(flat(other(all_two))), 0),
            "plane",
            axis=0,
            tiled=True,
        )
        rows_up, rows_down = (
            in_order(
                lax.dynamic_index_in_dim(pack, core, 0, False),
                swapped(lax.dynamic_index_in_dim(pack, 1 - core, 0, False)),
                0,
            )
            for pack in (pack_ups, pack_downs)
        )
        rows_up, rows_down = (
            lax.all_gather(rows, "tensor", axis=1, tiled=True) for rows in (rows_up, rows_down)
        )
        small_mine = mine(lax.all_gather(small_in, "tensor", axis=0))
    small_mine = small_mine.reshape(held, -1)

    gate_up_weight = lax.all_gather(rows_up, "plane", axis=0, tiled=True)
    down_weight = lax.all_gather(rows_down, "plane", axis=0, tiled=True)

    cuts = []
    at = 0
    for size in (KCONV * chans_dev, heads_dev, heads_dev, heads_dev, chans_dev):
        cuts.append(small_mine[:, at : at + size])
        at += size
    taps = cuts[0].reshape(held, KCONV, chans_dev).transpose(1, 0, 2).reshape(KCONV, -1)
    taps = jnp.concatenate([taps, conv_states.reshape(KCONV, 2 * N)], axis=1)
    bias = jnp.pad(cuts[1], ((0, 0), (0, step_pad - heads_dev)))
    decay = jnp.pad(cuts[2], ((0, 0), (0, step_pad - heads_dev)))
    skip = jnp.repeat(cuts[3].reshape(1, -1), HEAD_SIZE, axis=1)
    gain = cuts[4].reshape(1, -1)

    lengths = in_order(seq_lengths, swapped(seq_lengths), 0)
    seq_len = lengths[place]
    len_one = seq_len.reshape(1)
    valid_rows = (jnp.arange(seq_total, dtype=jnp.int32) < seq_len).astype(jnp.float32)[:, None]

    x_rows = wide(x_low)
    normed = low(rms_norm(x_rows, norm_gain))
    proj = dot(normed, weight_one)
    group_cols = 2 * chans_dev + query_dev + step_pad
    cosine, sine = turn_tables(seq_total, 2)
    attn, log_sums = attention_forward(len_one, proj, cosine, sine, group_cols)
    both_low, state_out, states = mamba_forward(proj, attn, taps, bias, decay, skip, gain)

    grad_own = positions_in(lax.optimization_barrier((out_grad, proj))[0])
    grad_own, both_low = lax.optimization_barrier((grad_own, both_low))
    mixed_part = low(dot_nt(both_low, weight_two))
    mixed = wide(mixed_part) + wide(swapped(mixed_part))
    hidden = x_rows + mixed
    normed_two = low(rms_norm(hidden, ffn_gain))
    gate_up = dot(normed_two, gate_up_weight)
    act, act_pull = jax.vjp(swiglu, gate_up)
    act_low = low(act)
    ffn_part = low(dot_nt(act_low, down_weight))
    ffn_own = wide(own_half(ffn_part)) + wide(swapped(other_half(ffn_part)))
    out_own = own_half(valid_rows) * (own_half(hidden) + ffn_own)
    layer_out = positions_out(low(out_own))

    grad_rows = valid_rows * wide(both_halves(grad_own))
    grad_low = low(grad_rows)
    grad_down = low(dot_tn(grad_low, act_low))
    (grad_gate_up,) = act_pull(dot(grad_low, down_weight))
    gate_up_low = low(grad_gate_up)
    grad_gate_up_weight = low(dot_tn(normed_two, gate_up_low))
    grad_two_part = low(dot_nt(gate_up_low, gate_up_weight))
    grad_n2 = wide(grad_two_part) + wide(swapped(grad_two_part))
    r_two = lax.rsqrt(jnp.mean(hidden * hidden, axis=-1, keepdims=True) + EPS)
    scaled = grad_n2 * ffn_gain
    grad_hidden = (
        grad_rows
        + r_two * scaled
        - hidden * (r_two**3 * jnp.mean(hidden * scaled, axis=-1, keepdims=True))
    )
    grad_ffn_gain = jnp.sum(own_half(hidden * r_two * grad_n2), axis=(0, 1))
    grad_mixed = low(grad_hidden)

    def scatter(values):
        return lax.psum_scatter(values, "plane", scatter_dimension=0, tiled=True)

    def to_groups(values):
        rows, columns = values.shape

        def piece_at(goal):
            return lax.dynamic_slice(
                values,
                ((goal // 2) * (rows // 2), (goal % 2) * (columns // 2)),
                (rows // 2, columns // 2),
            )

        parts = exchange(piece_at, place, spot, pairs_split)
        return wide(parts[0]) + wide(parts[1]) + wide(parts[2]) + wide(parts[3])

    def to_units(values):
        part = lax.psum_scatter(values, "tensor", scatter_dimension=1, tiled=True)
        by_part = part.reshape(2, share, -1)
        own = lax.dynamic_index_in_dim(by_part, core, 0, False)
        theirs = swapped(lax.dynamic_index_in_dim(by_part, 1 - core, 0, False))
        return wide(in_order(own[None], theirs[None], 0))

    units_down = to_units(scatter(grad_down))
    units_up = to_units(scatter(grad_gate_up_weight))
    sum_down = units_down.transpose(0, 2, 1).reshape(hidden_dev, share)
    sum_up = units_up.reshape(2, share, 2, own_units).transpose(1, 2, 0, 3)
    grad_two = low(dot_tn(grad_mixed, both_low))

    back = dot(grad_mixed, weight_two)
    attn_back = jnp.concatenate(
        [low(back[:, chans_dev:out_dev]), low(back[:, out_dev + chans_dev :])], axis=1
    )
    grad_q, grad_kv = attention_backward(
        len_one, proj, cosine, sine, log_sums, attn_back, group_cols, 0
    )
    proj_grad, grad_taps, grad_gain, grad_skip_cols, grad_bias, grad_decay = mamba_backward(
        proj, state_out, states, back, grad_q, grad_kv, taps, bias, decay, skip, gain
    )
    grad_one = low(dot_tn(normed, proj_grad))
    edge = held * group_cols
    grad_norm_part = low(dot_nt(proj_grad, weight_one))
    grad_norm_own = wide(own_half(grad_norm_part)) + wide(swapped(other_half(grad_norm_part)))
    x_own = wide(own_half(x_low))
    r_one = lax.rsqrt(jnp.mean(x_own * x_own, axis=-1, keepdims=True) + EPS)
    scaled = grad_norm_own * norm_gain
    grad_x = low(
        own_half(grad_hidden)
        + r_one * scaled
        - x_own * (r_one**3 * jnp.mean(x_own * scaled, axis=-1, keepdims=True))
    )
    grad_norm_gain = jnp.sum(x_own * r_one * grad_norm_own, axis=(0, 1))

    grad_skip = jnp.sum(grad_skip_cols.reshape(held, heads_dev, HEAD_SIZE), axis=-1)
    chan_taps = grad_taps[:, : held * chans_dev].reshape(KCONV, held, chans_dev)
    group_small = jnp.concatenate(
        [
            chan_taps.transpose(1, 0, 2).reshape(held, -1),
            grad_bias[:, :heads_dev],
            grad_decay[:, :heads_dev],
            grad_skip,
            grad_gain.reshape(held, -1),
        ],
        axis=1,
    )
    small_groups = in_order(group_small, jnp.zeros_like(group_small), 0)
    small_out = jnp.concatenate(
        [
            grad_norm_gain,
            grad_ffn_gain,
            grad_taps[:, held * chans_dev :].reshape(-1),
            small_groups.reshape(-1),
        ]
    )
    if quad:
        small_size = small_out.shape[0]
        small_room = -(-small_size // 1024) * 1024
        sum_one, shared_sum, small_sum, input_grad, sum_mamba, sum_attn = collect(
            grad_one,
            grad_two,
            jnp.pad(small_out, (0, small_room - small_size)).reshape(-1, 128),
            grad_x,
            group_cols,
            chans_dev,
        )
        small_sum = small_sum.reshape(-1)[:small_size]
    else:
        part_one = scatter(grad_one)
        both_parts = part_one[:, edge:].reshape(2, share, -1)
        own_rest = lax.dynamic_index_in_dim(both_parts, core, 0, False)
        their_rest = swapped(lax.dynamic_index_in_dim(both_parts, 1 - core, 0, False))
        shared_own = wide(own_rest[:, : 2 * N]) + wide(their_rest[:, : 2 * N])
        kv_both = in_order(own_rest[:, 2 * N :], their_rest[:, 2 * N :], 1)
        shared_low = jnp.concatenate([low(shared_own), kv_both], axis=1)
        shared_sum = jnp.sum(wide(lax.all_gather(shared_low, "tensor", axis=0)), axis=0)
        sum_one = to_groups(part_one[:, :edge])
        sum_two = to_groups(scatter(grad_two)).T
        sum_mamba, sum_attn = sum_two[:chans_dev], sum_two[chans_dev:]
        input_grad = positions_out(grad_x)
        small_sum = lax.psum(small_out, ("plane", "core", "tensor"))
    kv_sum = shared_sum[:, 2 * N :].reshape(share, 2, 2, HEAD_SIZE).transpose(0, 2, 1, 3)
    group_sum = lax.dynamic_index_in_dim(
        small_sum[2 * model_dim + KCONV * 2 * N :].reshape(groups, -1), place, 0, False
    )
    pieces = []
    at = 0
    for size in (KCONV * chans_dev, heads_dev, heads_dev, heads_dev, chans_dev):
        pieces.append(group_sum[at : at + size])
        at += size

    one = sum_one
    return (
        layer_out,
        input_grad,
        small_sum[:model_dim],
        one[:, : 2 * chans_dev].reshape(share, 2, chans_dev),
        one[:, 2 * chans_dev + query_dev :][:, :heads_dev],
        shared_sum[:, : 2 * N].reshape(share, 2, N),
        one[:, 2 * chans_dev : 2 * chans_dev + query_dev],
        kv_sum.reshape(share, 2, 2 * HEAD_SIZE),
        pieces[0].reshape(KCONV, chans_dev),
        small_sum[2 * model_dim : 2 * model_dim + KCONV * 2 * N].reshape(KCONV, 2, N),
        pieces[1],
        pieces[2],
        pieces[3],
        pieces[4],
        sum_mamba,
        sum_attn,
        small_sum[model_dim : 2 * model_dim],
        sum_up.reshape(share, 2, hidden_dev),
        sum_down,
    )


def solution(mesh):
    rows, columns = mesh.devices.shape
    fine = Mesh(mesh.devices.reshape(rows // 2, 2, columns), ("plane", "core", "tensor"))
    dp = ("plane", "core")
    return jax.shard_map(
        body,
        mesh=fine,
        in_specs=(
            P(dp, "tensor", None),
            P(dp),
            P(dp, "tensor", None),
            P(),
            P(dp, None, "tensor"),
            P(dp, "tensor"),
            P(dp, None, None),
            P(dp, "tensor"),
            P(dp, None, None),
            P(None, "tensor"),
            P(),
            P("tensor"),
            P("tensor"),
            P("tensor"),
            P("tensor"),
            P("tensor", dp),
            P("tensor", dp),
            P(),
            P(dp, None, "tensor"),
            P("tensor", dp),
        ),
        out_specs=(
            P(dp, "tensor", None),
            P(dp, "tensor", None),
            P(),
            P(dp, None, "tensor"),
            P(dp, "tensor"),
            P(dp, None, None),
            P(dp, "tensor"),
            P(dp, None, None),
            P(None, "tensor"),
            P(),
            P("tensor"),
            P("tensor"),
            P("tensor"),
            P("tensor"),
            P("tensor", dp),
            P("tensor", dp),
            P(),
            P(dp, None, "tensor"),
            P("tensor", dp),
        ),
        check_vma=False,
    )
```

```python
import jax
import jax.numpy as jnp
import numpy as np
from jax import lax
from jax.experimental import pallas as pl
from jax.experimental.pallas import tpu as pltpu
from jax.sharding import Mesh
from jax.sharding import PartitionSpec as P

HEAD_SIZE = 64
N = 128
KCONV = 4
GH = 6
EPS = 1e-05
THETA = 10000.0
MASKED = -1e30
SWAP = [(0, 1), (1, 0)]


def low(values):
    return values.astype(jnp.bfloat16)


def wide(values):
    return values.astype(jnp.float32)


def dot(left, right):
    return jnp.dot(left, right, preferred_element_type=jnp.float32)


def dot_nt(left, right):
    return lax.dot_general(
        left, right, (((1,), (1,)), ((), ())), preferred_element_type=jnp.float32
    )


def dot_tn(left, right):
    return lax.dot_general(
        left, right, (((0,), (0,)), ((), ())), preferred_element_type=jnp.float32
    )


def dot_fine(left, right):
    high = low(right)
    rest = right - wide(high)
    mid = low(rest)
    last = low(rest - wide(mid))
    return dot(left, high) + dot(left, mid) + dot(left, last)


def dot_by(left, right):
    high = low(left)
    rest = left - wide(high)
    mid = low(rest)
    last = low(rest - wide(mid))
    return dot(high, right) + dot(mid, right) + dot(last, right)


def sigmoid(values):
    return 1.0 / (1.0 + jnp.exp(-values))


def turn(values, cosine, sine):
    lane = lax.broadcasted_iota(jnp.int32, values.shape, 1)
    half = HEAD_SIZE // 2
    up = pltpu.roll(values, 128 - half, 1)
    down = pltpu.roll(values, half, 1)
    return values * cosine + jnp.where(lane % HEAD_SIZE < half, up, down) * sine


def turn_back(values, cosine, sine):
    lane = lax.broadcasted_iota(jnp.int32, values.shape, 1)
    half = HEAD_SIZE // 2
    turned = values * sine
    up = pltpu.roll(turned, 128 - half, 1)
    down = pltpu.roll(turned, half, 1)
    return values * cosine + jnp.where(lane % HEAD_SIZE < half, up, down)


def cost(micros):
    return pl.CostEstimate(flops=int(micros * 1e9), bytes_accessed=0, transcendentals=0)


SCALE = HEAD_SIZE ** (-0.5)
ROWS = 256


def key_value_parts(kv, cosine, sine):
    lane = lax.broadcasted_iota(jnp.int32, kv.shape, 1)
    key = jnp.where(lane < HEAD_SIZE, turn(kv, cosine, sine), 0.0)
    value = jnp.where(lane < HEAD_SIZE, 0.0, kv)
    keys = (low(key), low(pltpu.roll(key, HEAD_SIZE, 1)))
    values = (low(pltpu.roll(value, HEAD_SIZE, 1)), low(value))
    return keys, values


def block_scores(query, keys, begin, seq_len):
    scores = dot_nt(query, keys)
    row = lax.broadcasted_iota(jnp.int32, (scores.shape[0], 1), 0) + begin
    col = lax.broadcasted_iota(jnp.int32, scores.shape, 1)
    return jnp.where(col < jnp.minimum(row + 1, seq_len), scores, MASKED)


def attention_forward_kernel(len_ref, q_ref, kv_ref, cos_ref, sin_ref, out_ref, sum_ref):
    seq_len = len_ref[0]
    cosine, sine = cos_ref[...], sin_ref[...]
    keys, values = key_value_parts(kv_ref[...], cosine, sine)
    query = low(turn(q_ref[...], cosine, sine) * SCALE)
    rows = query.shape[0]
    lane = lax.broadcasted_iota(jnp.int32, (ROWS, 128), 1)
    for begin in range(0, rows, ROWS):
        end = begin + ROWS
        outs, sums = [], []
        for head in range(2):
            scores = block_scores(query[begin:end], keys[head][:end], begin, seq_len)
            peak = jnp.max(scores, axis=1, keepdims=True)
            exps = jnp.exp(scores - peak)
            total = jnp.sum(exps, axis=1, keepdims=True)
            probs = low(exps * (1.0 / total))
            outs.append(dot(probs, values[head][:end]))
            sums.append(peak + jnp.log(total))
        out_ref[begin:end, :] = low(outs[0] + outs[1])
        sum_ref[begin:end, :] = jnp.where(lane < HEAD_SIZE, sums[0], sums[1])


def attention_backward_kernel(
    len_ref, q_ref, kv_ref, cos_ref, sin_ref, sum_ref, grad_ref, dq_ref, dkv_ref, dk_acc, dv_acc
):
    seq_len = len_ref[0]
    cosine, sine = cos_ref[...], sin_ref[...]
    keys, values = key_value_parts(kv_ref[...], cosine, sine)
    query = low(turn(q_ref[...], cosine, sine) * SCALE)
    query_t = query.T
    rows = query.shape[0]
    group = pl.program_id(0)
    grad = low(grad_ref[...])
    grad_t = grad.T

    @pl.when(group == 0)
    def _():
        dk_acc[...] = jnp.zeros_like(dk_acc)
        dv_acc[...] = jnp.zeros_like(dv_acc)

    for begin in range(0, rows, ROWS):
        end = begin + ROWS
        dq = jnp.zeros((ROWS, 128), jnp.float32)
        for head in range(2):
            lanes = slice(head * HEAD_SIZE, (head + 1) * HEAD_SIZE)
            scores = block_scores(query[begin:end], keys[head][:end], begin, seq_len)
            at = head * HEAD_SIZE
            probs = jnp.exp(scores - sum_ref[begin:end, at : at + 1])
            dv_acc[:, :end] += dot(grad_t[lanes, begin:end], low(probs))
            dp = dot_nt(grad[begin:end], values[head][:end])
            inner = jnp.sum(probs * dp, axis=1, keepdims=True)
            ds = low(probs * (dp - inner))
            dq = dq + dot(ds, keys[head][:end])
            dk_acc[:, :end] += dot(query_t[lanes, begin:end], ds)
        dq = turn_back(dq * SCALE, cosine[begin:end], sine[begin:end])
        dq_ref[begin:end, :] = low(dq)

    @pl.when(group == pl.num_programs(0) - 1)
    def _():
        both = jnp.concatenate([dk_acc[...], dv_acc[...]], axis=0).T
        lane = lax.broadcasted_iota(jnp.int32, both.shape, 1)
        dkv_ref[...] = low(jnp.where(lane < HEAD_SIZE, turn_back(both, cosine, sine), both))


def attention_specs(rows, group_cols):
    whole = pl.BlockSpec((rows, 128), lambda g: (0, 0))
    return [
        pl.BlockSpec(memory_space=pltpu.SMEM),
        pl.BlockSpec((rows, 128), lambda g: (0, g * (group_cols // 128) + 6)),
        pl.BlockSpec((rows, 128), lambda g: (0, 2 * (group_cols // 128) + 2)),
        whole,
        whole,
    ]


BIG = 60 * 1024 * 1024


def attention_forward(seq_len, proj, cosine, sine, group_cols):
    rows = proj.shape[0]
    pairs = pl.BlockSpec((rows, 128), lambda g: (0, g))
    return pl.pallas_call(
        attention_forward_kernel,
        grid=(2,),
        in_specs=attention_specs(rows, group_cols),
        out_specs=[pairs, pairs],
        out_shape=[
            jax.ShapeDtypeStruct((rows, 256), jnp.bfloat16),
            jax.ShapeDtypeStruct((rows, 256), jnp.float32),
        ],
        compiler_params=pltpu.CompilerParams(vmem_limit_bytes=BIG),
        cost_estimate=cost(11),
        name="attention_forward",
    )(seq_len, proj, proj, cosine, sine)


def attention_backward(seq_len, proj, cosine, sine, sums, grad, group_cols, grad_at):
    rows = proj.shape[0]
    pairs = pl.BlockSpec((rows, 128), lambda g: (0, g))
    return pl.pallas_call(
        attention_backward_kernel,
        grid=(2,),
        in_specs=attention_specs(rows, group_cols)
        + [pairs, pl.BlockSpec((rows, 128), lambda g: (0, grad_at + g))],
        out_specs=[pairs, pl.BlockSpec((rows, 128), lambda g: (0, 0))],
        out_shape=[
            jax.ShapeDtypeStruct((rows, 256), jnp.bfloat16),
            jax.ShapeDtypeStruct((rows, 128), jnp.bfloat16),
        ],
        scratch_shapes=[
            pltpu.VMEM((HEAD_SIZE, rows), jnp.float32),
            pltpu.VMEM((HEAD_SIZE, rows), jnp.float32),
        ],
        compiler_params=pltpu.CompilerParams(vmem_limit_bytes=BIG),
        cost_estimate=cost(18),
        name="attention_backward",
    )(seq_len, proj, proj, cosine, sine, sums, grad)


CHUNK = 128
GROUP = GH * HEAD_SIZE
PAIRS = GH // 2
CONV = 2 * GROUP + 2 * N
SHARED = 2048


def triangle():
    row = lax.broadcasted_iota(jnp.int32, (CHUNK, CHUNK), 0)
    col = lax.broadcasted_iota(jnp.int32, (CHUNK, CHUNK), 1)
    return col <= row


def pair_lanes(values, pair):
    lane = lax.broadcasted_iota(jnp.int32, (values.shape[0], 128), 1)
    at = 2 * pair
    return jnp.where(lane < HEAD_SIZE, values[:, at : at + 1], values[:, at + 1 : at + 2])


def split_pair(values):
    lane = lax.broadcasted_iota(jnp.int32, values.shape, 1)
    empty = jnp.zeros_like(values)
    return jnp.concatenate(
        [jnp.where(lane < HEAD_SIZE, values, empty), jnp.where(lane < HEAD_SIZE, empty, values)],
        axis=0,
    )


def conv_pre(buf_ref, taps_ref, begin, size):
    total = buf_ref[5 : 5 + CHUNK, begin : begin + size] * taps_ref[0:1, begin : begin + size]
    for tap in range(1, KCONV):
        total = total + (
            buf_ref[5 + tap : 5 + tap + CHUNK, begin : begin + size]
            * taps_ref[tap : tap + 1, begin : begin + size]
        )
    return total


def load_conv(buf_ref, proj_ref):
    for group in range(2):
        at = group * 1024 + GROUP
        buf_ref[8:, group * GROUP : (group + 1) * GROUP] = proj_ref[:, at : at + GROUP]
    buf_ref[8:, 2 * GROUP :] = proj_ref[:, SHARED : SHARED + 2 * N]


def group_steps(proj_ref, bias_ref, decay_ref, group, lower):
    at = group * 1024 + 896
    raw = proj_ref[:, at : at + 128] + bias_ref[group : group + 1, :]
    step = jnp.log1p(jnp.exp(-jnp.abs(raw))) + jnp.maximum(raw, 0.0)
    rate = -jnp.exp(decay_ref[group : group + 1, :])
    cumul = dot_fine(lower, rate * step)
    return raw, step, rate, cumul


def head_decay(cumul, cumul_t, head, mask):
    spread = cumul[:, head : head + 1] - cumul_t[head : head + 1, :]
    return jnp.exp(jnp.where(mask, spread, MASKED))


def mamba_forward_kernel(
    proj_ref,
    attn_ref,
    taps_ref,
    bias_ref,
    decay_ref,
    skip_ref,
    gain_ref,
    both_ref,
    out_ref,
    states_ref,
    buf_ref,
    state_ref,
):
    chunk = pl.program_id(0)

    @pl.when(chunk == 0)
    def _():
        buf_ref[0:8, :] = jnp.zeros((8, CONV), jnp.float32)
        state_ref[...] = jnp.zeros_like(state_ref)

    load_conv(buf_ref, proj_ref)
    mask = triangle()
    lower = mask.astype(jnp.bfloat16)
    pre = conv_pre(buf_ref, taps_ref, 2 * GROUP, 2 * N)
    state_act = low(pre * sigmoid(pre))
    b_rows, c_rows = state_act[:, :N], state_act[:, N:]
    gram = dot_nt(c_rows, b_rows)
    b_cols = b_rows.T
    for group in range(2):
        cols = slice(group * GROUP, (group + 1) * GROUP)
        _, step, _, cumul = group_steps(proj_ref, bias_ref, decay_ref, group, lower)
        cumul_t = cumul.T
        last = cumul[CHUNK - 1 : CHUNK, :]
        state = state_ref[:, cols]
        states_ref[0, :, cols] = state
        from_state = dot(c_rows, low(state))
        gated = []
        for pair in range(PAIRS):
            at = group * GROUP + pair * 128
            pre = conv_pre(buf_ref, taps_ref, at, 128)
            chan = pre * sigmoid(pre)
            inputs = low(chan * pair_lanes(step, pair))
            mixing = jnp.concatenate(
                [
                    low(gram * head_decay(cumul, cumul_t, 2 * pair + side, mask))
                    for side in range(2)
                ],
                axis=1,
            )
            lanes = slice(pair * 128, (pair + 1) * 128)
            inner = pair_lanes(cumul, pair)
            out = dot(mixing, split_pair(inputs)) + jnp.exp(inner) * from_state[:, lanes]
            out_ref[:, at : at + 128] = out
            last_lanes = pair_lanes(last, pair)
            x_end = low(jnp.exp(last_lanes - inner) * wide(inputs))
            state_ref[:, at : at + 128] = jnp.exp(last_lanes) * state[:, lanes] + dot(
                b_cols, x_end
            )
            gate = proj_ref[:, group * 1024 + pair * 128 : group * 1024 + pair * 128 + 128]
            skipped = out + chan * skip_ref[:, at : at + 128]
            gated.append(skipped * (gate * sigmoid(gate)))
        square = sum(jnp.sum(part * part, axis=1, keepdims=True) for part in gated)
        scale = lax.rsqrt(square * (1.0 / GROUP) + EPS)
        for pair in range(PAIRS):
            at = group * GROUP + pair * 128
            to = group * 512 + pair * 128
            both_ref[:, to : to + 128] = low(gated[pair] * scale * gain_ref[:, at : at + 128])
        to = group * 512 + GROUP
        both_ref[:, to : to + 128] = attn_ref[:, group * 128 : (group + 1) * 128]
    buf_ref[0:8, :] = buf_ref[CHUNK : CHUNK + 8, :]


def mamba_forward(proj, attn, taps, bias, decay, skip, gain):
    rows, columns = proj.shape
    chunks = rows // CHUNK

    def whole(value):
        return pl.BlockSpec(value.shape, lambda k: (0, 0))

    return pl.pallas_call(
        mamba_forward_kernel,
        grid=(chunks,),
        in_specs=[
            pl.BlockSpec((CHUNK, columns), lambda k: (k, 0)),
            pl.BlockSpec((CHUNK, 256), lambda k: (k, 0)),
        ]
        + [whole(value) for value in (taps, bias, decay, skip, gain)],
        out_specs=[
            pl.BlockSpec((CHUNK, 1024), lambda k: (k, 0)),
            pl.BlockSpec((CHUNK, 2 * GROUP), lambda k: (k, 0)),
            pl.BlockSpec((1, N, 2 * GROUP), lambda k: (k, 0, 0)),
        ],
        out_shape=[
            jax.ShapeDtypeStruct((rows, 1024), jnp.bfloat16),
            jax.ShapeDtypeStruct((rows, 2 * GROUP), jnp.float32),
            jax.ShapeDtypeStruct((chunks, N, 2 * GROUP), jnp.float32),
        ],
        scratch_shapes=[
            pltpu.VMEM((CHUNK + 8, CONV), jnp.float32),
            pltpu.VMEM((N, 2 * GROUP), jnp.float32),
        ],
        compiler_params=pltpu.CompilerParams(vmem_limit_bytes=BIG),
        cost_estimate=cost(14),
        name="mamba_forward",
    )(proj, attn, taps, bias, decay, skip, gain)


def silu_slope(values, sig):
    return sig * (1.0 + values * (1.0 - sig))


def mamba_backward_kernel(
    proj_ref,
    before_ref,
    out_ref,
    states_ref,
    back_ref,
    dq_ref,
    dkv_ref,
    taps_ref,
    bias_ref,
    decay_ref,
    skip_ref,
    gain_ref,
    dproj_ref,
    dtaps_ref,
    dgain_ref,
    dskip_ref,
    dbias_ref,
    ddecay_ref,
    buf_ref,
    grad_buf,
    after_ref,
    flow_ref,
):
    step_at = pl.program_id(0)

    @pl.when(step_at == 0)
    def _():
        for ref in (dtaps_ref, dgain_ref, dskip_ref, dbias_ref, ddecay_ref, after_ref, flow_ref):
            ref[...] = jnp.zeros_like(ref)
        grad_buf[CHUNK:, :] = jnp.zeros((8, CONV), jnp.float32)

    inside = jnp.where(step_at == pl.num_programs(0) - 1, 0.0, 1.0)
    for group in range(2):
        at = group * 1024 + GROUP
        buf_ref[0:8, group * GROUP : (group + 1) * GROUP] = before_ref[:, at : at + GROUP] * inside
    buf_ref[0:8, 2 * GROUP :] = before_ref[:, SHARED : SHARED + 2 * N] * inside
    load_conv(buf_ref, proj_ref)
    mask = triangle()
    lower = mask.astype(jnp.bfloat16)
    row = lax.broadcasted_iota(jnp.int32, (CHUNK, CHUNK), 0)
    col = lax.broadcasted_iota(jnp.int32, (CHUNK, CHUNK), 1)
    upper = (row <= col).astype(jnp.bfloat16)
    pre_state = conv_pre(buf_ref, taps_ref, 2 * GROUP, 2 * N)
    sig_state = sigmoid(pre_state)
    state_act = low(pre_state * sig_state)
    b_rows, c_rows = state_act[:, :N], state_act[:, N:]
    gram = dot_nt(c_rows, b_rows)
    c_cols = c_rows.T
    dgram = jnp.zeros((CHUNK, CHUNK), jnp.float32)
    d_c = jnp.zeros((CHUNK, N), jnp.float32)
    d_b = jnp.zeros((CHUNK, N), jnp.float32)
    for group in range(2):
        raw, step, rate, cumul = group_steps(proj_ref, bias_ref, decay_ref, group, lower)
        cumul_t = cumul.T
        last = cumul[CHUNK - 1 : CHUNK, :]
        pres, sigs, chans, gates, gate_sigs, skips, gated = [], [], [], [], [], [], []
        for pair in range(PAIRS):
            at = group * GROUP + pair * 128
            pre = conv_pre(buf_ref, taps_ref, at, 128)
            sig = sigmoid(pre)
            chan = pre * sig
            gate = proj_ref[:, group * 1024 + pair * 128 : group * 1024 + pair * 128 + 128]
            gate_sig = sigmoid(gate)
            skipped = out_ref[:, at : at + 128] + chan * skip_ref[:, at : at + 128]
            pres.append(pre)
            sigs.append(sig)
            chans.append(chan)
            gates.append(gate)
            gate_sigs.append(gate_sig)
            skips.append(skipped)
            gated.append(skipped * (gate * gate_sig))
        square = sum(jnp.sum(part * part, axis=1, keepdims=True) for part in gated)
        scale = lax.rsqrt(square * (1.0 / GROUP) + EPS)
        grads = []
        cross = jnp.zeros((CHUNK, 1), jnp.float32)
        for pair in range(PAIRS):
            at = group * GROUP + pair * 128
            grad = back_ref[:, group * 512 + pair * 128 : group * 512 + pair * 128 + 128]
            dgain_ref[:, at : at + 128] += jnp.sum(grad * gated[pair] * scale, axis=0, keepdims=True)
            grad = grad * gain_ref[:, at : at + 128]
            cross = cross + jnp.sum(gated[pair] * grad, axis=1, keepdims=True)
            grads.append(grad)
        cross = cross * (1.0 / GROUP) * scale * scale * scale
        dstep = jnp.zeros((CHUNK, 128), jnp.float32)
        flow = jnp.zeros((CHUNK, 128), jnp.float32)
        flow_end = flow_ref[group : group + 1, :]
        flow_next = jnp.zeros((1, 128), jnp.float32)
        for pair in range(PAIRS):
            at = group * GROUP + pair * 128
            head_of_lane = lax.broadcasted_iota(jnp.int32, (128, 128), 0) // HEAD_SIZE + 2 * pair
            lane = lax.broadcasted_iota(jnp.int32, (128, 128), 1)
            pick = (head_of_lane == lane).astype(jnp.bfloat16)
            chan = chans[pair]
            grad = scale * grads[pair] - gated[pair] * cross
            gate, gate_sig = gates[pair], gate_sigs[pair]
            dgate = grad * skips[pair] * silu_slope(gate, gate_sig)
            to = group * 1024 + pair * 128
            dproj_ref[:, to : to + 128] = low(dgate)
            grad = grad * (gate * gate_sig)
            dskip_ref[:, at : at + 128] += jnp.sum(grad * chan, axis=0, keepdims=True)
            dchan = grad * skip_ref[:, at : at + 128]
            dout = low(grad)
            step_lanes = pair_lanes(step, pair)
            inputs = low(chan * step_lanes)
            halves = split_pair(inputs)
            decays = [head_decay(cumul, cumul_t, 2 * pair + side, mask) for side in range(2)]
            mixing = jnp.concatenate([low(gram * decay) for decay in decays], axis=1)
            dmix = dot_nt(dout, halves)
            dgram = dgram + dmix[:, :CHUNK] * decays[0] + dmix[:, CHUNK:] * decays[1]
            dinputs = dot_tn(mixing, dout)
            lane = lax.broadcasted_iota(jnp.int32, (CHUNK, 128), 1)
            dinputs = jnp.where(lane < HEAD_SIZE, dinputs[:CHUNK], dinputs[CHUNK:])
            inner = pair_lanes(cumul, pair)
            last_lanes = pair_lanes(last, pair)
            to_end = jnp.exp(last_lanes - inner)
            after = after_ref[:, at : at + 128]
            after_low = low(after)
            dinputs = dinputs + to_end * dot(b_rows, after_low)
            x_end = low(to_end * wide(inputs))
            g_start = low(jnp.exp(inner) * wide(dout))
            state = states_ref[0, :, at : at + 128]
            d_c = d_c + dot_nt(g_start, low(state))
            d_b = d_b + dot_nt(x_end, after_low)
            after = jnp.exp(last_lanes) * after + dot(c_cols, g_start)
            after_ref[:, at : at + 128] = after
            through = jnp.sum(after * state, axis=0, keepdims=True)
            flow_next = flow_next + dot_by(jnp.broadcast_to(through, (8, 128)), pick)[0:1]
            flow = flow + dot_by(
                wide(dout) * out_ref[:, at : at + 128] - wide(inputs) * dinputs, pick
            )
            dstep = dstep + dot_by(dinputs * chan, pick)
            dchan = dchan + dinputs * step_lanes
            grad_buf[0:CHUNK, at : at + 128] = dchan * silu_slope(pres[pair], sigs[pair])
        dcumul = dot_fine(upper, flow) + flow_end
        flow_ref[group : group + 1, :] = flow_next
        dstep = dstep + rate * dcumul
        ddecay_ref[group : group + 1, :] += jnp.sum(rate * step * dcumul, axis=0, keepdims=True)
        draw = dstep * sigmoid(raw)
        dbias_ref[group : group + 1, :] += jnp.sum(draw, axis=0, keepdims=True)
        to = group * 1024 + 896
        lane = lax.broadcasted_iota(jnp.int32, (CHUNK, 128), 1)
        dproj_ref[:, to : to + 128] = low(jnp.where(lane < GH, draw, 0.0))
        to = group * 1024 + 2 * GROUP
        dproj_ref[:, to : to + 128] = dq_ref[:, group * 128 : (group + 1) * 128]
    dgram_low = low(dgram)
    d_c = d_c + dot(dgram_low, b_rows)
    d_b = d_b + dot_tn(dgram_low, c_rows)
    slope = silu_slope(pre_state, sig_state)
    grad_buf[0:CHUNK, 2 * GROUP : 2 * GROUP + N] = d_b * slope[:, :N]
    grad_buf[0:CHUNK, 2 * GROUP + N :] = d_c * slope[:, N:]
    for at in range(0, CONV, 128):
        grad = jnp.zeros((CHUNK, 128), jnp.float32)
        here = grad_buf[0:CHUNK, at : at + 128]
        for tap in range(KCONV):
            shift = KCONV - 1 - tap
            grad = grad + (
                grad_buf[shift : shift + CHUNK, at : at + 128] * taps_ref[tap : tap + 1, at : at + 128]
            )
            dtaps_ref[tap : tap + 1, at : at + 128] += jnp.sum(
                here * buf_ref[5 + tap : 5 + tap + CHUNK, at : at + 128], axis=0, keepdims=True
            )
        if at < 2 * GROUP:
            to = (at // GROUP) * 1024 + GROUP + at % GROUP
        else:
            to = SHARED + at - 2 * GROUP
        dproj_ref[:, to : to + 128] = low(grad)
    dproj_ref[:, SHARED + 2 * N :] = dkv_ref[...]
    grad_buf[CHUNK:, :] = grad_buf[0:8, :]


def mamba_backward(proj, out, states, back, dq, dkv, taps, bias, decay, skip, gain):
    rows, columns = proj.shape
    chunks = rows // CHUNK

    def whole(value):
        return pl.BlockSpec(value.shape, lambda k: (0, 0))

    def rows_of(width):
        return pl.BlockSpec((CHUNK, width), lambda k: (chunks - 1 - k, 0))

    params = (taps, bias, decay, skip, gain)
    return pl.pallas_call(
        mamba_backward_kernel,
        grid=(chunks,),
        in_specs=[
            rows_of(columns),
            pl.BlockSpec(
                (8, columns),
                lambda k: (jnp.maximum((chunks - 1 - k) * (CHUNK // 8) - 1, 0), 0),
            ),
            rows_of(2 * GROUP),
            pl.BlockSpec((1, N, 2 * GROUP), lambda k: (chunks - 1 - k, 0, 0)),
            rows_of(1024),
            rows_of(256),
            rows_of(128),
        ]
        + [whole(value) for value in params],
        out_specs=[rows_of(columns)]
        + [whole(value) for value in (taps, gain, skip, bias, decay)],
        out_shape=[jax.ShapeDtypeStruct((rows, columns), jnp.bfloat16)]
        + [
            jax.ShapeDtypeStruct(value.shape, jnp.float32)
            for value in (taps, gain, skip, bias, decay)
        ],
        scratch_shapes=[
            pltpu.VMEM((CHUNK + 8, CONV), jnp.float32),
            pltpu.VMEM((CHUNK + 8, CONV), jnp.float32),
            pltpu.VMEM((N, 2 * GROUP), jnp.float32),
            pltpu.VMEM((8, 128), jnp.float32),
        ],
        compiler_params=pltpu.CompilerParams(vmem_limit_bytes=BIG),
        cost_estimate=cost(36),
        name="mamba_backward",
    )(proj, proj, out, states, back, dq, dkv, *params)


MESH = pl.DeviceIdType.MESH


def landed(ref, sem):
    pltpu.make_async_copy(ref, ref, sem).wait()


def spread_kernel(
    pack_ref,
    next_ref,
    ups_ref,
    downs_ref,
    shared_ref,
    x_ref,
    small_ref,
    w_ref,
    v_ref,
    up_rows,
    d_ref,
    full_ref,
    params_ref,
    near_sem,
    out_sem,
    part_sem,
    fromx_sem,
    fromy_sem,
    overx_sem,
    overy_sem,
    tox_sem,
    toy_sem,
    relx_sem,
    rely_sem,
    row_sem,
    row_out,
    pair_sem,
    pair_out,
    param_sem,
    param_out,
    ffn_sem,
    ffn_out,
):
    plane = lax.axis_index("plane")
    core = lax.axis_index("core")
    place = lax.axis_index("tensor")
    xside = plane + 1 - 2 * (plane % 2)
    yside = plane + 2 - 4 * (plane // 2)
    across = xside + 2 - 4 * (xside // 2)
    target = place // 2
    column = place % 2
    share, width = pack_ref.shape
    narrow = next_ref.shape[1]
    rest = shared_ref.shape[2]
    half = share
    rows_dev = x_ref.shape[1]

    barrier = pltpu.get_barrier_semaphore()
    for step in range(4):
        for side in range(2):
            if step or side:
                pl.semaphore_signal(
                    barrier,
                    inc=1,
                    device_id={"core": (core + side) % 2, "tensor": (place + step) % 4},
                    device_id_type=MESH,
                )
    for neighbour in (xside, yside):
        pl.semaphore_signal(
            barrier, inc=1, device_id={"plane": neighbour}, device_id_type=MESH
        )
    pl.semaphore_wait(barrier, 9)

    def block(at, part):
        return pl.ds(pl.multiple_of(at * 2 * share + part * share, share), share)

    def piece(at, part, col):
        return w_ref.at[block(at, part), pl.ds(pl.multiple_of(col * width, width), width)]

    def next_piece(at, part, col):
        return v_ref.at[block(at, part), pl.ds(pl.multiple_of(col * narrow, narrow), narrow)]

    def rest_piece(at, part):
        return w_ref.at[block(at, part), pl.ds(2 * width, rest)]

    started = []

    def send(src, dst, send_sem, recv_sem, device):
        copy = pltpu.make_async_remote_copy(
            src_ref=src,
            dst_ref=dst,
            send_sem=send_sem,
            recv_sem=recv_sem,
            device_id=device,
            device_id_type=MESH,
        )
        copy.start()
        started.append((src, send_sem))

    mine = piece(plane, core, column)
    slot = core * 2 + column
    mine_next = next_piece(plane, core, column)

    def send_parts(src, dst, at, recv_sem):
        for step in (2, 1, 3):
            send(
                src,
                dst,
                out_sem.at[at + step],
                recv_sem,
                {"core": target, "tensor": (place + step) % 4},
            )

    send_parts(pack_ref, mine, 0, part_sem.at[slot])
    send_parts(next_ref, mine_next, 4, part_sem.at[6 + slot])

    params = params_ref.at[column]

    @pl.when(target == core)
    def _():
        pltpu.make_async_copy(pack_ref, mine, part_sem.at[slot]).start()
        pltpu.make_async_copy(next_ref, mine_next, part_sem.at[6 + slot]).start()
        pltpu.make_async_copy(small_ref, params, param_sem.at[column]).start()
        for step in range(1, 4):
            pltpu.make_async_remote_copy(
                src_ref=small_ref,
                dst_ref=params,
                send_sem=param_out.at[step],
                recv_sem=param_sem.at[column],
                device_id={"tensor": (place + step) % 4},
                device_id_type=MESH,
            ).start()

    @pl.when(target != core)
    def _():
        pltpu.make_async_remote_copy(
            src_ref=pack_ref,
            dst_ref=mine,
            send_sem=out_sem.at[0],
            recv_sem=part_sem.at[slot],
            device_id={"core": 1 - core},
            device_id_type=MESH,
        ).start()
        pltpu.make_async_remote_copy(
            src_ref=next_ref,
            dst_ref=mine_next,
            send_sem=out_sem.at[4],
            recv_sem=part_sem.at[6 + slot],
            device_id={"core": 1 - core},
            device_id_type=MESH,
        ).start()

    own_rest = rest_piece(plane, core)
    near = pltpu.make_async_copy(shared_ref.at[core], own_rest, part_sem.at[4 + core])
    near.start()
    send(
        shared_ref.at[1 - core],
        own_rest,
        near_sem.at[0],
        part_sem.at[4 + core],
        {"core": 1 - core},
    )

    def rows_at(at, side):
        return full_ref.at[pl.ds(pl.multiple_of(at * rows_dev + side * half, half), half)]

    wide_up, wide_down = ups_ref.shape[2], downs_ref.shape[2]

    def down_piece(at, part, place_at):
        cols = pl.ds(pl.multiple_of(place_at * wide_down, wide_down), wide_down)
        return d_ref.at[block(at, part), cols]

    def up_piece(part, place_at):
        return up_rows.at[
            pl.ds(pl.multiple_of(part * share, share), share),
            pl.ds(pl.multiple_of(place_at * wide_up, wide_up), wide_up),
        ]

    def send_halves(number, src, goal_ref, recv_sem):
        for step in (2, 1, 3):
            for side in range(2):
                send(
                    src.at[side],
                    goal_ref,
                    ffn_out.at[number, 2 * step + side],
                    recv_sem,
                    {"core": side, "tensor": (place + step) % 4},
                )
        send(
            src.at[1 - core], goal_ref, ffn_out.at[number, 0], recv_sem, {"core": 1 - core}
        )
        pltpu.make_async_copy(src.at[core], goal_ref, recv_sem).start()

    send_halves(
        0, downs_ref, down_piece(plane, core, place), part_sem.at[10 + 2 * place + core]
    )

    for seq in range(2):
        for side in range(2):
            goal = 2 * core + seq
            src = x_ref.at[seq, pl.ds(side * half, half)]
            dst = rows_at(place, side)
            here = jnp.logical_and(core == side, goal == place)

            @pl.when(here)
            def _():
                pltpu.make_async_copy(src, dst, row_sem.at[place]).start()

            @pl.when(jnp.logical_not(here))
            def _():
                pltpu.make_async_remote_copy(
                    src_ref=src,
                    dst_ref=dst,
                    send_sem=row_out.at[seq * 2 + side],
                    recv_sem=row_sem.at[place],
                    device_id={"core": side, "tensor": goal},
                    device_id_type=MESH,
                ).start()

    send_halves(1, ups_ref, up_piece(core, place), ffn_sem.at[2 * place + core])

    first_col = jnp.where(place // 2 == core, place % 2, 1 - core)
    order = [(0, None, 0), (0, None, 1)]
    for kind in (1, 2):
        for turn in range(2):
            for part in range(2):
                order.append((kind, (first_col + turn) % 2, part))

    for step in (0, 1, 3, 2):
        for part in range(2):
            order.append((3, (place + step) % 4, part))

    def at_piece(at, item):
        kind, col, part = item
        if kind == 3:
            return down_piece(at, part, col)
        if kind == 0:
            return rest_piece(at, part)
        return piece(at, part, col) if kind == 1 else next_piece(at, part, col)

    def index(item):
        kind, col, part = item
        if kind == 3:
            return 10 + 2 * col + part
        return 4 + part if kind == 0 else (kind - 1) * 6 + part * 2 + col

    def relay(item):
        at = index(item)
        if item[2] == 0:
            landed(at_piece(xside, item), fromx_sem.at[at])
            ref = at_piece(xside, item)
            send(ref, ref, rely_sem.at[at], overy_sem.at[at], {"plane": yside})
        else:
            landed(at_piece(yside, item), fromy_sem.at[at])
            ref = at_piece(yside, item)
            send(ref, ref, relx_sem.at[at], overx_sem.at[at], {"plane": xside})

    for number, item in enumerate(order):
        at = index(item)
        ref = at_piece(plane, item)
        landed(ref, part_sem.at[at])
        send(ref, ref, tox_sem.at[at], fromx_sem.at[at], {"plane": xside})
        send(ref, ref, toy_sem.at[at], fromy_sem.at[at], {"plane": yside})
        if number >= 2:
            relay(order[number - 2])
        if number == 13:
            for step in range(4):
                at = (place + step) % 4
                ref = rows_at(at, core)
                landed(ref, row_sem.at[at])
                send(ref, ref, pair_out.at[at], pair_sem.at[at], {"core": 1 - core})
    for item in order[-2:]:
        relay(item)
    for step in range(4):
        at = (place + step) % 4
        landed(rows_at(at, 1 - core), pair_sem.at[at])
    for item in order:
        at = index(item)
        if item[2] == 0:
            landed(at_piece(yside, item), fromy_sem.at[at])
            landed(at_piece(across, item), overy_sem.at[at])
        else:
            landed(at_piece(xside, item), fromx_sem.at[at])
            landed(at_piece(across, item), overx_sem.at[at])

    for src, sem in started:
        landed(src, sem)

    for at in range(2):
        landed(params_ref.at[at], param_sem.at[at])
    for at in range(4):
        for part in range(2):
            landed(up_piece(part, at), ffn_sem.at[2 * at + part])

    @pl.when(target == core)
    def _():
        for step in range(1, 4):
            landed(small_ref, param_out.at[step])

    @pl.when(target != core)
    def _():
        landed(pack_ref, out_sem.at[0])
        landed(next_ref, out_sem.at[4])

    for seq in range(2):
        for side in range(2):
            here = jnp.logical_and(core == side, 2 * core + seq == place)

            @pl.when(jnp.logical_not(here))
            def _():
                landed(x_ref.at[seq, pl.ds(side * half, half)], row_out.at[seq * 2 + side])


def spread(pack, following, ups, downs, shared, x_rows, small):
    share, width = pack.shape
    narrow = following.shape[1]
    rest = shared.shape[2]
    rows = x_rows.shape[1] * 4
    dma = pltpu.SemaphoreType.DMA
    any_space = pl.BlockSpec(memory_space=pl.ANY)
    return pl.pallas_call(
        spread_kernel,
        in_specs=[any_space] * 7,
        out_specs=[any_space] * 6,
        out_shape=[
            jax.ShapeDtypeStruct((8 * share, 2 * width + rest), pack.dtype),
            jax.ShapeDtypeStruct((8 * share, 2 * narrow), pack.dtype),
            jax.ShapeDtypeStruct((2 * share, 4 * ups.shape[2]), pack.dtype),
            jax.ShapeDtypeStruct((8 * share, 4 * downs.shape[2]), pack.dtype),
            jax.ShapeDtypeStruct((rows, x_rows.shape[2]), x_rows.dtype),
            jax.ShapeDtypeStruct((2,) + small.shape, small.dtype),
        ],
        scratch_shapes=[dma((1,)), dma((8,))] + [dma((18,))] * 9 + [dma((4,))] * 6 + [dma((8,)), dma((2, 8))],
        compiler_params=pltpu.CompilerParams(collective_id=1, has_side_effects=True),
        cost_estimate=cost(80),
        name="spread",
    )(pack, following, ups, downs, shared, x_rows, small)


def collect_kernel(*refs):
    (mixed_ref, both_ref, normed_hbm, dproj_hbm, weight_hbm, x_hbm, hidden_hbm) = refs[:7]
    (gain_ref, small_ref) = refs[7:9]
    (mixer_out, query_out, step_out, shared_ref, total_ref, back_ref) = refs[9:15]
    (mamba_out, attn_out) = refs[15:17]
    (normed_ref, dproj_ref, weight_ref, x_ref, hidden_ref, grad_ref, next_ref) = refs[17:24]
    (norm_ref, norm_in, rows_ref, in_ref, next_in, sum_ref, next_sum) = refs[24:31]
    (piece_ref, next_buf, pair_ref, mix_ref, near_ref, far_ref) = refs[31:37]
    (in_sem, out_sem, piece_sem, piece_out, pair_sem, mix_sem, mix_out) = refs[37:44]
    (near_sem, near_out, far_sem, far_out, row_sem, row_out, load_sem, norm_sem) = refs[44:]
    plane = lax.axis_index("plane")
    core = lax.axis_index("core")
    place = lax.axis_index("tensor")
    xside = plane + 1 - 2 * (plane % 2)
    yside = plane + 2 - 4 * (plane // 2)
    across = xside + 2 - 4 * (xside // 2)
    share = pair_ref.shape[0]
    width = piece_ref.shape[2]
    rest = grad_ref.shape[1] - 2 * width

    loads = [
        (dproj_hbm, dproj_ref),
        (weight_hbm, weight_ref),
        (normed_hbm, normed_ref),
        (x_hbm.at[:, core], x_ref),
        (hidden_hbm.at[:, core], hidden_ref),
    ]
    for number, (src, dst) in enumerate(loads):
        pltpu.make_async_copy(src, dst, load_sem.at[number]).start()

    def loaded(number):
        src, dst = loads[number]
        pltpu.make_async_copy(src, dst, load_sem.at[number]).wait()

    barrier = pltpu.get_barrier_semaphore()
    for step in range(4):
        for side in range(2):
            if step or side:
                pl.semaphore_signal(
                    barrier,
                    inc=1,
                    device_id={"core": (core + side) % 2, "tensor": (place + step) % 4},
                    device_id_type=MESH,
                )
    for neighbour in (xside, yside):
        pl.semaphore_signal(
            barrier, inc=1, device_id={"plane": neighbour}, device_id_type=MESH
        )
    pl.semaphore_wait(barrier, 9)

    started = []

    def send(src, dst, send_sem, recv_sem, device):
        pltpu.make_async_remote_copy(
            src_ref=src,
            dst_ref=dst,
            send_sem=send_sem,
            recv_sem=recv_sem,
            device_id=device,
            device_id_type=MESH,
        ).start()
        started.append((src, send_sem))

    narrow = next_ref.shape[1] // 2
    spans = [(0, 2 * width, rest), (0, 0, width), (0, width, width)]
    spans += [(1, 0, narrow), (1, narrow, narrow)]

    def block(at, part, span):
        rows = pl.ds(pl.multiple_of(at * 2 * share + part * share, share), share)
        return (grad_ref, next_ref)[span[0]].at[rows, pl.ds(*span[1:])]

    def held(slot, span):
        return (in_ref, next_in)[span[0]].at[slot, :, pl.ds(*span[1:])]

    def summed(part, span):
        return (sum_ref, next_sum)[span[0]].at[part, :, pl.ds(*span[1:])]

    def begin(number):
        span = spans[number]
        send(
            block(across, 0, span),
            held(0, span),
            out_sem.at[0, number],
            in_sem.at[0, number],
            {"plane": xside},
        )
        send(
            block(across, 1, span),
            held(1, span),
            out_sem.at[1, number],
            in_sem.at[1, number],
            {"plane": yside},
        )
        send(
            block(xside, 0, span),
            held(2, span),
            out_sem.at[2, number],
            in_sem.at[2, number],
            {"plane": xside},
        )
        send(
            block(yside, 1, span),
            held(3, span),
            out_sem.at[3, number],
            in_sem.at[3, number],
            {"plane": yside},
        )

    def work(number):
        kind, begin_at, size = spans[number]
        left = (normed_ref, mixed_ref)[kind]
        right = (dproj_ref, both_ref)[kind]
        result = (grad_ref, next_ref)[kind]
        tile = 256 if size % 256 == 0 else size

        @pl.loop(0, size // tile)
        def _(at):
            cols = pl.ds(pl.multiple_of(begin_at + at * tile, 128), tile)
            result[:, cols] = low(dot_tn(left[...], right[:, cols]))

    seq = place % 2
    owner = place // 2
    dst_rows = back_ref.at[seq, pl.ds(pl.multiple_of(core * share, share), share)]

    def send_back():
        for step in (2, 1, 3):
            at = (place + step) % 4
            send(
                rows_ref.at[at],
                dst_rows,
                row_out.at[step],
                row_sem.at[seq * 2 + core],
                {"core": owner, "tensor": at},
            )

        @pl.when(owner == core)
        def _():
            pltpu.make_async_copy(
                rows_ref.at[place], dst_rows, row_sem.at[seq * 2 + core]
            ).start()

        @pl.when(owner != core)
        def _():
            pltpu.make_async_remote_copy(
                src_ref=rows_ref.at[place],
                dst_ref=dst_rows,
                send_sem=row_out.at[0],
                recv_sem=row_sem.at[seq * 2 + core],
                device_id={"core": 1 - core},
                device_id_type=MESH,
            ).start()

    def norm_product():
        loaded(0)
        loaded(1)
        for at in range(4):
            rows = pl.ds(at * 2 * share, 2 * share)
            part = low(dot_nt(dproj_ref[rows, :], weight_ref[...]))
            norm_ref[at, 0] = part[:share]
            norm_ref[at, 1] = part[share:]
        send(
            norm_ref.at[:, 1 - core],
            norm_in,
            norm_sem.at[0],
            norm_sem.at[1],
            {"core": 1 - core},
        )

    def norm_back():
        loaded(3)
        loaded(4)
        landed(norm_in, norm_sem.at[1])
        gain_total = jnp.zeros((1, x_ref.shape[2]), jnp.float32)
        for at in range(4):
            grad = wide(norm_ref[at, core]) + wide(norm_in[at])
            values = wide(x_ref[at])
            size = 1.0 / values.shape[1]
            root = lax.rsqrt(jnp.sum(values * values, axis=1, keepdims=True) * size + EPS)
            scaled = grad * gain_ref[...]
            inner = jnp.sum(values * scaled, axis=1, keepdims=True) * size
            rows_ref[at] = low(
                hidden_ref[at] + root * scaled - values * (root * root * root * inner)
            )
            gain_total = gain_total + jnp.sum(values * root * grad, axis=0, keepdims=True)
        near_ref[5] = small_ref[...]
        for at in range(gain_total.shape[1] // 128):
            near_ref[5, at : at + 1, :] = gain_total[:, at * 128 : (at + 1) * 128]

    def pass_on(number):
        span = spans[number]
        landed(held(0, span), in_sem.at[0, number])
        held(0, span)[...] = low(wide(held(0, span)[...]) + wide(block(yside, 0, span)[...]))
        send(
            held(0, span),
            held(5, span),
            out_sem.at[4, number],
            in_sem.at[5, number],
            {"plane": yside},
        )
        landed(held(1, span), in_sem.at[1, number])
        held(1, span)[...] = low(wide(held(1, span)[...]) + wide(block(xside, 1, span)[...]))
        send(
            held(1, span),
            held(4, span),
            out_sem.at[5, number],
            in_sem.at[4, number],
            {"plane": xside},
        )

    def finish(number):
        span = spans[number]
        landed(held(2, span), in_sem.at[2, number])
        landed(held(5, span), in_sem.at[5, number])
        summed(0, span)[...] = low(
            wide(block(plane, 0, span)[...]) + wide(held(2, span)[...]) + wide(held(5, span)[...])
        )
        landed(held(3, span), in_sem.at[3, number])
        landed(held(4, span), in_sem.at[4, number])
        summed(1, span)[...] = low(
            wide(block(plane, 1, span)[...]) + wide(held(3, span)[...]) + wide(held(4, span)[...])
        )

    def send_pieces(number):
        span = spans[number]
        kind, col = span[0], span[1] // span[2]
        buf = (piece_ref, next_buf)[kind]
        goal = 2 * core + col
        for part in range(2):
            src = summed(part, span)
            here = jnp.logical_and(core == part, goal == place)

            @pl.when(here)
            def _():
                pltpu.make_async_copy(src, buf.at[place], piece_sem.at[kind, place]).start()

            @pl.when(jnp.logical_not(here))
            def _():
                pltpu.make_async_remote_copy(
                    src_ref=src,
                    dst_ref=buf.at[place],
                    send_sem=piece_out.at[kind, 2 * col + part],
                    recv_sem=piece_sem.at[kind, place],
                    device_id={"core": part, "tensor": goal},
                    device_id_type=MESH,
                ).start()

    rest_cols = pl.ds(2 * width, rest)
    state = rest * 2 // 3

    def pair_up():
        send(
            sum_ref.at[1 - core, :, rest_cols],
            pair_ref,
            pair_sem.at[0],
            pair_sem.at[1],
            {"core": 1 - core},
        )

    def mix():
        landed(pair_ref, pair_sem.at[1])
        mine = sum_ref[core, :, rest_cols]
        mix_ref[place, :, 0:state] = low(wide(mine[:, :state]) + wide(pair_ref[:, :state]))
        first = core == 0
        mix_ref[place, :, state:rest] = jnp.where(first, mine[:, state:], pair_ref[:, state:])
        mix_ref[place, :, rest:] = jnp.where(first, pair_ref[:, state:], mine[:, state:])
        own_mix = mix_ref.at[place]
        for step in (2, 1, 3):
            send(
                own_mix,
                own_mix,
                mix_out.at[step],
                mix_sem.at[place],
                {"tensor": (place + step) % 4},
            )

    work(3)
    begin(3)
    work(4)
    begin(4)
    norm_product()
    pass_on(3)
    loaded(2)
    work(0)
    begin(0)
    finish(3)
    send_pieces(3)
    pass_on(4)
    norm_back()
    send_back()
    send(near_ref.at[5], near_ref.at[0], near_out.at[0], near_sem.at[0], {"plane": xside})
    work(1)
    begin(1)
    finish(4)
    send_pieces(4)
    pass_on(0)
    work(2)
    landed(near_ref.at[0], near_sem.at[0])
    near_ref[3] = near_ref[5] + near_ref[0]
    send(near_ref.at[3], near_ref.at[1], near_out.at[1], near_sem.at[1], {"plane": yside})
    finish(0)
    pair_up()
    pass_on(1)
    begin(2)
    landed(near_ref.at[1], near_sem.at[1])
    near_ref[4] = near_ref[3] + near_ref[1]
    send(near_ref.at[4], near_ref.at[2], near_out.at[2], near_sem.at[2], {"core": 1 - core})
    mix()
    finish(1)
    send_pieces(1)
    landed(near_ref.at[2], near_sem.at[2])
    far_ref[place] = near_ref[4] + near_ref[2]
    own_far = far_ref.at[place]
    for step in (2, 1, 3):
        send(
            own_far,
            own_far,
            far_out.at[step],
            far_sem.at[place],
            {"tensor": (place + step) % 4},
        )
    pass_on(2)
    finish(2)
    send_pieces(2)

    for step in (1, 2, 3):
        at = (place + step) % 4
        landed(mix_ref.at[at], mix_sem.at[at])
        landed(far_ref.at[at], far_sem.at[at])
    shared_ref[...] = (
        wide(mix_ref[0]) + wide(mix_ref[1]) + wide(mix_ref[2]) + wide(mix_ref[3])
    )
    total_ref[...] = (far_ref[0] + far_ref[1]) + (far_ref[2] + far_ref[3])
    def gathered(buf, kind):
        for at in range(4):
            landed(buf.at[at], piece_sem.at[kind, at])
        return wide(buf[0]) + wide(buf[1]) + wide(buf[2]) + wide(buf[3])

    one = gathered(piece_ref, 0)
    cut = mixer_out.shape[1]
    mixer_out[...] = one[:, :cut]
    query_out[...] = one[:, cut : cut + query_out.shape[1]]
    step_out[...] = one[:, cut + query_out.shape[1] :]
    both = gathered(next_buf, 1).T
    mamba_out[...] = both[: mamba_out.shape[0]]
    attn_out[...] = both[mamba_out.shape[0] :]
    for at in range(4):
        landed(dst_rows, row_sem.at[at])
    for src, sem in started:
        landed(src, sem)

    @pl.when(owner != core)
    def _():
        landed(rows_ref.at[place], row_out.at[0])

    for span in spans[1:]:
        col = span[1] // span[2]
        for part in range(2):
            here = jnp.logical_and(core == part, 2 * core + col == place)

            @pl.when(jnp.logical_not(here))
            def _():
                landed(summed(part, span), piece_out.at[span[0], 2 * col + part])


def collect(normed, dproj, weight, mixed, both, x_rows, hidden, gain, small, sizes):
    chans, queries, width = sizes
    share = weight.shape[0] // 8
    model = weight.shape[0]
    columns = weight.shape[1]
    rest = columns - 2 * width
    narrow = both.shape[1] // 2
    dma = pltpu.SemaphoreType.DMA
    any_space = pl.BlockSpec(memory_space=pl.ANY)
    near = pl.BlockSpec(memory_space=pltpu.VMEM)
    shared_cols = rest + rest // 3
    bf16, f32 = jnp.bfloat16, jnp.float32
    split = (4, 2, x_rows.shape[0] // 8, model)
    half = (4, x_rows.shape[0] // 8, model)
    return pl.pallas_call(
        collect_kernel,
        in_specs=[near, near] + [any_space] * 5 + [near, near],
        out_specs=[near] * 5 + [any_space] + [near] * 2,
        out_shape=[
            jax.ShapeDtypeStruct((share, 2 * chans), f32),
            jax.ShapeDtypeStruct((share, queries), f32),
            jax.ShapeDtypeStruct((share, width - 2 * chans - queries), f32),
            jax.ShapeDtypeStruct((share, shared_cols), f32),
            jax.ShapeDtypeStruct(small.shape, f32),
            jax.ShapeDtypeStruct((2, 2 * half[1], model), bf16),
            jax.ShapeDtypeStruct((chans, share), f32),
            jax.ShapeDtypeStruct((narrow - chans, share), f32),
        ],
        scratch_shapes=[
            pltpu.VMEM(normed.shape, bf16),
            pltpu.VMEM(dproj.shape, bf16),
            pltpu.VMEM(weight.shape, bf16),
            pltpu.VMEM(half, bf16),
            pltpu.VMEM(half, f32),
            pltpu.VMEM((model, columns), bf16),
            pltpu.VMEM((model, 2 * narrow), bf16),
            pltpu.VMEM(split, bf16),
            pltpu.VMEM(half, bf16),
            pltpu.VMEM(half, bf16),
            pltpu.VMEM((6, share, columns), bf16),
            pltpu.VMEM((6, share, 2 * narrow), bf16),
            pltpu.VMEM((2, share, columns), bf16),
            pltpu.VMEM((2, share, 2 * narrow), bf16),
            pltpu.VMEM((4, share, width), bf16),
            pltpu.VMEM((4, share, narrow), bf16),
            pltpu.VMEM((share, rest), bf16),
            pltpu.VMEM((4, share, shared_cols), bf16),
            pltpu.VMEM((6,) + small.shape, f32),
            pltpu.VMEM((4,) + small.shape, f32),
            dma((6, 5)),
            dma((6, 5)),
            dma((2, 4)),
            dma((2, 4)),
            dma((2,)),
            dma((4,)),
            dma((4,)),
            dma((3,)),
            dma((3,)),
            dma((4,)),
            dma((4,)),
            dma((4,)),
            dma((4,)),
            dma((5,)),
            dma((2,)),
        ],
        compiler_params=pltpu.CompilerParams(
            collective_id=2, has_side_effects=True, vmem_limit_bytes=BIG
        ),
        cost_estimate=cost(80),
        name="collect",
    )(
        mixed,
        both,
        normed,
        dproj,
        weight,
        x_rows.reshape(split),
        hidden.reshape(split),
        gain.reshape(1, -1),
        small,
    )


def rms_norm(values, gain_vec):
    return values * lax.rsqrt(jnp.mean(values * values, axis=-1, keepdims=True) + EPS) * gain_vec


def turn_tables(seq_count, head_count):
    half_dim = HEAD_SIZE // 2
    freqs = np.float32(THETA) ** (-np.arange(half_dim, dtype=np.float32) * 2.0 / HEAD_SIZE)
    angles = np.arange(seq_count, dtype=np.float32)[:, None] * freqs.astype(np.float32)[None, :]
    cosine, sine = np.cos(angles), np.sin(angles)
    return (
        jnp.asarray(np.tile(np.concatenate([cosine, cosine], axis=1), (1, head_count))),
        jnp.asarray(np.tile(np.concatenate([-sine, sine], axis=1), (1, head_count))),
    )


def swiglu(gate_up):
    rows, columns = gate_up.shape
    units = columns // 8
    parts = []
    for at in range(0, columns, 2 * units):
        gate, up = gate_up[:, at : at + units], gate_up[:, at + units : at + 2 * units]
        parts.append(gate * sigmoid(gate) * up)
    return jnp.concatenate(parts, axis=1)


def swapped(values):
    return lax.ppermute(values, "core", SWAP)


def body(
    layer_in,
    seq_lengths,
    out_grad,
    norm_gain,
    mixer_weight,
    step_weight,
    state_weight,
    query_weight,
    key_value_weight,
    conv_channels,
    conv_states,
    step_bias,
    decay_log,
    skip_scale,
    group_gain,
    mamba_proj,
    attn_proj,
    ffn_gain,
    ffn_weight,
    ffn_down,
):
    core = lax.axis_index("core")
    place = lax.axis_index("tensor")
    first = core == 0
    seq_dev, rows_dev, model_dim = layer_in.shape
    groups = lax.axis_size("tensor")
    seq_total = rows_dev * groups
    half_rows = rows_dev // 2
    share = mixer_weight.shape[0]
    chans_dev = mixer_weight.shape[2]
    heads_dev = step_weight.shape[1]
    query_dev = query_weight.shape[1]
    hidden_dev = ffn_weight.shape[2]
    held = groups // 2
    step_pad = 128

    def mine(values):
        return lax.dynamic_slice_in_dim(values, core * held, held, 0)

    def other(values):
        return lax.dynamic_slice_in_dim(values, (1 - core) * held, held, 0)

    def in_order(own, others, axis):
        return jnp.where(
            first,
            jnp.concatenate([own, others], axis=axis),
            jnp.concatenate([others, own], axis=axis),
        )

    def flat(values):
        return values.transpose(1, 0, 2).reshape(values.shape[1], -1)

    spot = 2 * core + place % 2

    def positions_in(values):
        shaped = values.reshape(seq_dev, 2, half_rows, model_dim)
        keep = lax.dynamic_index_in_dim(shaped, core, 1, False)
        send = lax.dynamic_index_in_dim(shaped, 1 - core, 1, False)
        return lax.all_to_all(in_order(keep, swapped(send), 0), "tensor", 0, 0, tiled=True)

    def both_halves(own):
        both = in_order(own[:, None], swapped(own)[:, None], 1)
        return both.reshape(seq_total, model_dim)

    def positions_out(own):
        four = lax.all_to_all(own, "tensor", 0, 0, tiled=True)
        keep = lax.dynamic_slice_in_dim(four, core * seq_dev, seq_dev, 0)
        send = lax.dynamic_slice_in_dim(four, (1 - core) * seq_dev, seq_dev, 0)
        both = in_order(keep[:, None], swapped(send)[:, None], 1)
        return both.reshape(seq_dev, rows_dev, model_dim)

    def own_half(values):
        shaped = values.reshape(groups, 2, half_rows, -1)
        return lax.dynamic_index_in_dim(shaped, core, 1, False)

    def other_half(values):
        shaped = values.reshape(groups, 2, half_rows, -1)
        return lax.dynamic_index_in_dim(shaped, 1 - core, 1, False)

    out_dev = chans_dev + query_dev
    pack_two = jnp.concatenate([mamba_proj.T, attn_proj.T], axis=1)
    own_units = hidden_dev // 2
    pack_ups = ffn_weight.reshape(share, 2, 2, own_units).transpose(2, 0, 1, 3)
    pack_ups = pack_ups.reshape(2, share, hidden_dev)
    pack_downs = ffn_down.reshape(2, own_units, share).transpose(0, 2, 1)
    out_dev = chans_dev + query_dev
    pack_two = jnp.concatenate([mamba_proj.T, attn_proj.T], axis=1)
    pack_one = jnp.concatenate(
        [
            mixer_weight.reshape(share, 2 * chans_dev),
            query_weight,
            jnp.pad(step_weight, ((0, 0), (0, step_pad - heads_dev))),
        ],
        axis=1,
    )
    kv_heads = key_value_weight.reshape(share, 2, 2, HEAD_SIZE)

    def shared_for(at):
        return jnp.concatenate(
            [
                state_weight.reshape(share, 2 * N),
                lax.dynamic_index_in_dim(kv_heads, at, 2, False).reshape(share, 2 * HEAD_SIZE),
            ],
            axis=1,
        )

    small_in = jnp.concatenate(
        [conv_channels.reshape(-1), step_bias, decay_log, skip_scale, group_gain]
    )
    small_pad = -(-small_in.shape[0] // 1024) * 1024
    small_in = jnp.pad(small_in, (0, small_pad - small_in.shape[0])).reshape(-1, 128)
    quad = lax.axis_size("plane") == 4 and groups == 4 and share % 16 == 0
    quad = quad and share == half_rows
    if quad:
        shared = jnp.stack([shared_for(0), shared_for(1)])
        weight_one, weight_two, rows_up, down_weight, x_low, small_mine = spread(
            pack_one, pack_two, pack_ups, pack_downs, shared, layer_in, small_in
        )
    else:
        x_low = both_halves(positions_in(layer_in))
        all_one = lax.all_gather(pack_one, "tensor", axis=0)
        own_one = jnp.concatenate([flat(mine(all_one)), shared_for(core)], axis=1)
        their_one = jnp.concatenate([flat(other(all_one)), shared_for(1 - core)], axis=1)
        weight_one = lax.all_gather(
            in_order(own_one, swapped(their_one), 0), "plane", axis=0, tiled=True
        )
        all_two = lax.all_gather(pack_two, "tensor", axis=0)
        weight_two = lax.all_gather(
            in_order(flat(mine(all_two)), swapped(flat(other(all_two))), 0),
            "plane",
            axis=0,
            tiled=True,
        )
        rows_up, rows_down = (
            in_order(
                lax.dynamic_index_in_dim(pack, core, 0, False),
                swapped(lax.dynamic_index_in_dim(pack, 1 - core, 0, False)),
                0,
            )
            for pack in (pack_ups, pack_downs)
        )
        rows_up, rows_down = (
            lax.all_gather(rows, "tensor", axis=1, tiled=True) for rows in (rows_up, rows_down)
        )
        down_weight = lax.all_gather(rows_down, "plane", axis=0, tiled=True)
        small_mine = mine(lax.all_gather(small_in, "tensor", axis=0))
    small_mine = small_mine.reshape(held, -1)

    gate_up_weight = lax.all_gather(rows_up, "plane", axis=0, tiled=True)

    cuts = []
    at = 0
    for size in (KCONV * chans_dev, heads_dev, heads_dev, heads_dev, chans_dev):
        cuts.append(small_mine[:, at : at + size])
        at += size
    taps = cuts[0].reshape(held, KCONV, chans_dev).transpose(1, 0, 2).reshape(KCONV, -1)
    taps = jnp.concatenate([taps, conv_states.reshape(KCONV, 2 * N)], axis=1)
    bias = jnp.pad(cuts[1], ((0, 0), (0, step_pad - heads_dev)))
    decay = jnp.pad(cuts[2], ((0, 0), (0, step_pad - heads_dev)))
    skip = jnp.repeat(cuts[3].reshape(1, -1), HEAD_SIZE, axis=1)
    gain = cuts[4].reshape(1, -1)

    lengths = in_order(seq_lengths, swapped(seq_lengths), 0)
    seq_len = lengths[place]
    len_one = seq_len.reshape(1)
    valid_rows = (jnp.arange(seq_total, dtype=jnp.int32) < seq_len).astype(jnp.float32)[:, None]

    x_rows = wide(x_low)
    normed = low(rms_norm(x_rows, norm_gain))
    proj = dot(normed, weight_one)
    group_cols = 2 * chans_dev + query_dev + step_pad
    cosine, sine = turn_tables(seq_total, 2)
    attn, log_sums = attention_forward(len_one, proj, cosine, sine, group_cols)
    both_low, state_out, states = mamba_forward(proj, attn, taps, bias, decay, skip, gain)

    grad_own = positions_in(lax.optimization_barrier((out_grad, proj))[0])
    grad_own, both_low = lax.optimization_barrier((grad_own, both_low))
    mixed_part = low(dot_nt(both_low, weight_two))
    mixed = wide(mixed_part) + wide(swapped(mixed_part))
    hidden = x_rows + mixed
    normed_two = low(rms_norm(hidden, ffn_gain))
    gate_up = dot(normed_two, gate_up_weight)
    act, act_pull = jax.vjp(swiglu, gate_up)
    act_low = low(act)
    ffn_part = low(dot_nt(act_low, down_weight))
    ffn_own = wide(own_half(ffn_part)) + wide(swapped(other_half(ffn_part)))
    out_own = own_half(valid_rows) * (own_half(hidden) + ffn_own)
    layer_out = positions_out(low(out_own))

    grad_rows = valid_rows * wide(both_halves(grad_own))
    grad_low = low(grad_rows)
    grad_down = low(dot_tn(grad_low, act_low))
    (grad_gate_up,) = act_pull(dot(grad_low, down_weight))
    gate_up_low = low(grad_gate_up)
    grad_gate_up_weight = low(dot_tn(normed_two, gate_up_low))
    grad_two_part = low(dot_nt(gate_up_low, gate_up_weight))
    grad_n2 = wide(grad_two_part) + wide(swapped(grad_two_part))
    r_two = lax.rsqrt(jnp.mean(hidden * hidden, axis=-1, keepdims=True) + EPS)
    scaled = grad_n2 * ffn_gain
    grad_hidden = (
        grad_rows
        + r_two * scaled
        - hidden * (r_two**3 * jnp.mean(hidden * scaled, axis=-1, keepdims=True))
    )
    grad_ffn_gain = jnp.sum(own_half(hidden * r_two * grad_n2), axis=(0, 1))
    grad_mixed = low(grad_hidden)

    def scatter(values):
        return lax.psum_scatter(values, "plane", scatter_dimension=0, tiled=True)

    def to_groups(values):
        by_part = values.reshape(2, share, held, -1).transpose(0, 2, 1, 3)
        own = lax.dynamic_index_in_dim(by_part, core, 0, False)
        theirs = swapped(lax.dynamic_index_in_dim(by_part, 1 - core, 0, False))
        whole = in_order(own, theirs, 0)
        return wide(lax.psum_scatter(whole, "tensor", scatter_dimension=0, tiled=True)[0])

    def to_units(values):
        return lax.psum_scatter(values, "tensor", scatter_dimension=1, tiled=True)

    units = jnp.concatenate(
        [to_units(scatter(grad_gate_up_weight)), to_units(scatter(grad_down))], axis=1
    )
    units = units.reshape(2, share, -1)
    own_part = lax.dynamic_index_in_dim(units, core, 0, True)
    their_part = swapped(lax.dynamic_index_in_dim(units, 1 - core, 0, True))
    units = wide(in_order(own_part, their_part, 0))
    sum_up = units[:, :, :hidden_dev].reshape(2, share, 2, own_units).transpose(1, 2, 0, 3)
    sum_down = units[:, :, hidden_dev:].transpose(0, 2, 1).reshape(hidden_dev, share)

    back = dot(grad_mixed, weight_two)
    attn_back = jnp.concatenate(
        [low(back[:, chans_dev:out_dev]), low(back[:, out_dev + chans_dev :])], axis=1
    )
    grad_q, grad_kv = attention_backward(
        len_one, proj, cosine, sine, log_sums, attn_back, group_cols, 0
    )
    proj_grad, grad_taps, grad_gain, grad_skip_cols, grad_bias, grad_decay = mamba_backward(
        proj, state_out, states, back, grad_q, grad_kv, taps, bias, decay, skip, gain
    )
    edge = held * group_cols
    grad_skip = jnp.sum(grad_skip_cols.reshape(held, heads_dev, HEAD_SIZE), axis=-1)
    chan_taps = grad_taps[:, : held * chans_dev].reshape(KCONV, held, chans_dev)
    group_small = jnp.concatenate(
        [
            chan_taps.transpose(1, 0, 2).reshape(held, -1),
            grad_bias[:, :heads_dev],
            grad_decay[:, :heads_dev],
            grad_skip,
            grad_gain.reshape(held, -1),
        ],
        axis=1,
    )
    small_groups = in_order(group_small, jnp.zeros_like(group_small), 0)
    small_out = jnp.concatenate(
        [
            jnp.zeros_like(norm_gain),
            grad_ffn_gain,
            grad_taps[:, held * chans_dev :].reshape(-1),
            small_groups.reshape(-1),
        ]
    )
    if quad:
        small_size = small_out.shape[0]
        small_room = -(-small_size // 1024) * 1024
        (
            sum_mixer,
            sum_query,
            sum_step,
            shared_sum,
            small_sum,
            input_grad,
            sum_mamba,
            sum_attn,
        ) = collect(
            normed,
            proj_grad,
            weight_one,
            grad_mixed,
            both_low,
            x_low,
            grad_hidden,
            norm_gain,
            jnp.pad(small_out, (0, small_room - small_size)).reshape(-1, 128),
            (chans_dev, query_dev, group_cols),
        )
        small_sum = small_sum.reshape(-1)[:small_size]
    else:
        grad_one = low(dot_tn(normed, proj_grad))
        grad_norm_part = low(dot_nt(proj_grad, weight_one))
        grad_norm_own = wide(own_half(grad_norm_part)) + wide(swapped(other_half(grad_norm_part)))
        x_own = wide(own_half(x_low))
        r_one = lax.rsqrt(jnp.mean(x_own * x_own, axis=-1, keepdims=True) + EPS)
        scaled = grad_norm_own * norm_gain
        grad_x = low(
            own_half(grad_hidden)
            + r_one * scaled
            - x_own * (r_one**3 * jnp.mean(x_own * scaled, axis=-1, keepdims=True))
        )
        grad_norm_gain = jnp.sum(x_own * r_one * grad_norm_own, axis=(0, 1))
        small_out = small_out.at[:model_dim].set(grad_norm_gain)
        part_one = scatter(grad_one)
        both_parts = part_one[:, edge:].reshape(2, share, -1)
        own_rest = lax.dynamic_index_in_dim(both_parts, core, 0, False)
        their_rest = swapped(lax.dynamic_index_in_dim(both_parts, 1 - core, 0, False))
        shared_own = wide(own_rest[:, : 2 * N]) + wide(their_rest[:, : 2 * N])
        kv_both = in_order(own_rest[:, 2 * N :], their_rest[:, 2 * N :], 1)
        shared_low = jnp.concatenate([low(shared_own), kv_both], axis=1)
        shared_sum = jnp.sum(wide(lax.all_gather(shared_low, "tensor", axis=0)), axis=0)
        sum_one = to_groups(part_one[:, :edge])
        sum_mixer = sum_one[:, : 2 * chans_dev]
        sum_query = sum_one[:, 2 * chans_dev : 2 * chans_dev + query_dev]
        sum_step = sum_one[:, 2 * chans_dev + query_dev :]
        sum_two = to_groups(scatter(low(dot_tn(grad_mixed, both_low)))).T
        sum_mamba, sum_attn = sum_two[:chans_dev], sum_two[chans_dev:]
        input_grad = positions_out(grad_x)
        small_sum = lax.psum(small_out, ("plane", "core", "tensor"))
    kv_sum = shared_sum[:, 2 * N :].reshape(share, 2, 2, HEAD_SIZE).transpose(0, 2, 1, 3)
    group_sum = lax.dynamic_index_in_dim(
        small_sum[2 * model_dim + KCONV * 2 * N :].reshape(groups, -1), place, 0, False
    )
    pieces = []
    at = 0
    for size in (KCONV * chans_dev, heads_dev, heads_dev, heads_dev, chans_dev):
        pieces.append(group_sum[at : at + size])
        at += size

    return (
        layer_out,
        input_grad,
        small_sum[:model_dim],
        sum_mixer.reshape(share, 2, chans_dev),
        sum_step[:, :heads_dev],
        shared_sum[:, : 2 * N].reshape(share, 2, N),
        sum_query,
        kv_sum.reshape(share, 2, 2 * HEAD_SIZE),
        pieces[0].reshape(KCONV, chans_dev),
        small_sum[2 * model_dim : 2 * model_dim + KCONV * 2 * N].reshape(KCONV, 2, N),
        pieces[1],
        pieces[2],
        pieces[3],
        pieces[4],
        sum_mamba,
        sum_attn,
        small_sum[model_dim : 2 * model_dim],
        sum_up.reshape(share, 2, hidden_dev),
        sum_down,
    )


def solution(mesh):
    rows, columns = mesh.devices.shape
    fine = Mesh(mesh.devices.reshape(rows // 2, 2, columns), ("plane", "core", "tensor"))
    dp = ("plane", "core")
    return jax.shard_map(
        body,
        mesh=fine,
        in_specs=(
            P(dp, "tensor", None),
            P(dp),
            P(dp, "tensor", None),
            P(),
            P(dp, None, "tensor"),
            P(dp, "tensor"),
            P(dp, None, None),
            P(dp, "tensor"),
            P(dp, None, None),
            P(None, "tensor"),
            P(),
            P("tensor"),
            P("tensor"),
            P("tensor"),
            P("tensor"),
            P("tensor", dp),
            P("tensor", dp),
            P(),
            P(dp, None, "tensor"),
            P("tensor", dp),
        ),
        out_specs=(
            P(dp, "tensor", None),
            P(dp, "tensor", None),
            P(),
            P(dp, None, "tensor"),
            P(dp, "tensor"),
            P(dp, None, None),
            P(dp, "tensor"),
            P(dp, None, None),
            P(None, "tensor"),
            P(),
            P("tensor"),
            P("tensor"),
            P("tensor"),
            P("tensor"),
            P("tensor", dp),
            P("tensor", dp),
            P(),
            P(dp, None, "tensor"),
            P("tensor", dp),
        ),
        check_vma=False,
    )
```

```python
import jax
import jax.numpy as jnp
import numpy as np
from jax import lax
from jax.experimental import pallas as pl
from jax.experimental.pallas import tpu as pltpu
from jax.sharding import Mesh
from jax.sharding import PartitionSpec as P

HEAD_SIZE = 64
N = 128
KCONV = 4
GH = 6
EPS = 1e-05
THETA = 10000.0
MASKED = -1e30
SWAP = [(0, 1), (1, 0)]


def low(values):
    return values.astype(jnp.bfloat16)


def wide(values):
    return values.astype(jnp.float32)


def dot(left, right):
    return jnp.dot(left, right, preferred_element_type=jnp.float32)


def dot_nt(left, right):
    return lax.dot_general(
        left, right, (((1,), (1,)), ((), ())), preferred_element_type=jnp.float32
    )


def dot_tn(left, right):
    return lax.dot_general(
        left, right, (((0,), (0,)), ((), ())), preferred_element_type=jnp.float32
    )


def dot_fine(left, right):
    high = low(right)
    rest = right - wide(high)
    mid = low(rest)
    last = low(rest - wide(mid))
    return dot(left, high) + dot(left, mid) + dot(left, last)


def dot_by(left, right):
    high = low(left)
    rest = low(left - wide(high))
    return dot(high, right) + dot(rest, right)


def sigmoid(values):
    return 1.0 / (1.0 + jnp.exp(-values))


def turn(values, cosine, sine):
    lane = lax.broadcasted_iota(jnp.int32, values.shape, 1)
    half = HEAD_SIZE // 2
    up = pltpu.roll(values, 128 - half, 1)
    down = pltpu.roll(values, half, 1)
    return values * cosine + jnp.where(lane % HEAD_SIZE < half, up, down) * sine


def turn_back(values, cosine, sine):
    lane = lax.broadcasted_iota(jnp.int32, values.shape, 1)
    half = HEAD_SIZE // 2
    turned = values * sine
    up = pltpu.roll(turned, 128 - half, 1)
    down = pltpu.roll(turned, half, 1)
    return values * cosine + jnp.where(lane % HEAD_SIZE < half, up, down)


def cost(micros):
    return pl.CostEstimate(flops=int(micros * 1e9), bytes_accessed=0, transcendentals=0)


SCALE = HEAD_SIZE ** (-0.5)
ROWS = 256


def key_value_parts(kv, cosine, sine):
    lane = lax.broadcasted_iota(jnp.int32, kv.shape, 1)
    key = jnp.where(lane < HEAD_SIZE, turn(kv, cosine, sine), 0.0)
    value = jnp.where(lane < HEAD_SIZE, 0.0, kv)
    keys = (low(key), low(pltpu.roll(key, HEAD_SIZE, 1)))
    values = (low(pltpu.roll(value, HEAD_SIZE, 1)), low(value))
    return keys, values


def block_scores(query, keys, begin, seq_len):
    scores = dot_nt(query, keys)
    row = lax.broadcasted_iota(jnp.int32, (scores.shape[0], 1), 0) + begin
    col = lax.broadcasted_iota(jnp.int32, scores.shape, 1)
    return jnp.where(col < jnp.minimum(row + 1, seq_len), scores, MASKED)


def attention_forward_kernel(len_ref, q_ref, kv_ref, cos_ref, sin_ref, out_ref, sum_ref):
    seq_len = len_ref[0]
    cosine, sine = cos_ref[...], sin_ref[...]
    keys, values = key_value_parts(kv_ref[...], cosine, sine)
    query = low(turn(q_ref[...], cosine, sine) * SCALE)
    rows = query.shape[0]
    lane = lax.broadcasted_iota(jnp.int32, (ROWS, 128), 1)
    for begin in range(0, rows, ROWS):
        end = begin + ROWS
        outs, sums = [], []
        for head in range(2):
            scores = block_scores(query[begin:end], keys[head][:end], begin, seq_len)
            peak = jnp.max(scores, axis=1, keepdims=True)
            exps = jnp.exp(scores - peak)
            total = jnp.sum(exps, axis=1, keepdims=True)
            probs = low(exps * (1.0 / total))
            outs.append(dot(probs, values[head][:end]))
            sums.append(peak + jnp.log(total))
        out_ref[begin:end, :] = low(outs[0] + outs[1])
        sum_ref[begin:end, :] = jnp.where(lane < HEAD_SIZE, sums[0], sums[1])


def attention_backward_kernel(
    len_ref, q_ref, kv_ref, cos_ref, sin_ref, sum_ref, grad_ref, dq_ref, dkv_ref, dk_acc, dv_acc
):
    seq_len = len_ref[0]
    cosine, sine = cos_ref[...], sin_ref[...]
    keys, values = key_value_parts(kv_ref[...], cosine, sine)
    query = low(turn(q_ref[...], cosine, sine) * SCALE)
    query_t = query.T
    rows = query.shape[0]
    group = pl.program_id(0)
    grad = low(grad_ref[...])
    grad_t = grad.T

    @pl.when(group == 0)
    def _():
        dk_acc[...] = jnp.zeros_like(dk_acc)
        dv_acc[...] = jnp.zeros_like(dv_acc)

    for begin in range(0, rows, ROWS):
        end = begin + ROWS
        dq = jnp.zeros((ROWS, 128), jnp.float32)
        for head in range(2):
            lanes = slice(head * HEAD_SIZE, (head + 1) * HEAD_SIZE)
            scores = block_scores(query[begin:end], keys[head][:end], begin, seq_len)
            at = head * HEAD_SIZE
            probs = jnp.exp(scores - sum_ref[begin:end, at : at + 1])
            dv_acc[:, :end] += dot(grad_t[lanes, begin:end], low(probs))
            dp = dot_nt(grad[begin:end], values[head][:end])
            inner = jnp.sum(probs * dp, axis=1, keepdims=True)
            ds = low(probs * (dp - inner))
            dq = dq + dot(ds, keys[head][:end])
            dk_acc[:, :end] += dot(query_t[lanes, begin:end], ds)
        dq = turn_back(dq * SCALE, cosine[begin:end], sine[begin:end])
        dq_ref[begin:end, :] = low(dq)

    @pl.when(group == pl.num_programs(0) - 1)
    def _():
        both = jnp.concatenate([dk_acc[...], dv_acc[...]], axis=0).T
        lane = lax.broadcasted_iota(jnp.int32, both.shape, 1)
        dkv_ref[...] = low(jnp.where(lane < HEAD_SIZE, turn_back(both, cosine, sine), both))


def attention_specs(rows, group_cols):
    whole = pl.BlockSpec((rows, 128), lambda g: (0, 0))
    return [
        pl.BlockSpec(memory_space=pltpu.SMEM),
        pl.BlockSpec((rows, 128), lambda g: (0, g * (group_cols // 128) + 6)),
        pl.BlockSpec((rows, 128), lambda g: (0, 2 * (group_cols // 128) + 2)),
        whole,
        whole,
    ]


BIG = 60 * 1024 * 1024


def attention_forward(seq_len, proj, cosine, sine, group_cols):
    rows = proj.shape[0]
    pairs = pl.BlockSpec((rows, 128), lambda g: (0, g))
    return pl.pallas_call(
        attention_forward_kernel,
        grid=(2,),
        in_specs=attention_specs(rows, group_cols),
        out_specs=[pairs, pairs],
        out_shape=[
            jax.ShapeDtypeStruct((rows, 256), jnp.bfloat16),
            jax.ShapeDtypeStruct((rows, 256), jnp.float32),
        ],
        compiler_params=pltpu.CompilerParams(vmem_limit_bytes=BIG),
        cost_estimate=cost(11),
        name="attention_forward",
    )(seq_len, proj, proj, cosine, sine)


def attention_backward(seq_len, proj, cosine, sine, sums, grad, group_cols, grad_at):
    rows = proj.shape[0]
    pairs = pl.BlockSpec((rows, 128), lambda g: (0, g))
    return pl.pallas_call(
        attention_backward_kernel,
        grid=(2,),
        in_specs=attention_specs(rows, group_cols)
        + [pairs, pl.BlockSpec((rows, 128), lambda g: (0, 4 * g + grad_at))],
        out_specs=[pairs, pl.BlockSpec((rows, 128), lambda g: (0, 0))],
        out_shape=[
            jax.ShapeDtypeStruct((rows, 256), jnp.bfloat16),
            jax.ShapeDtypeStruct((rows, 128), jnp.bfloat16),
        ],
        scratch_shapes=[
            pltpu.VMEM((HEAD_SIZE, rows), jnp.float32),
            pltpu.VMEM((HEAD_SIZE, rows), jnp.float32),
        ],
        compiler_params=pltpu.CompilerParams(vmem_limit_bytes=BIG),
        cost_estimate=cost(18),
        name="attention_backward",
    )(seq_len, proj, proj, cosine, sine, sums, grad)


CHUNK = 128
GROUP = GH * HEAD_SIZE
PAIRS = GH // 2
CONV = 2 * GROUP + 2 * N
SHARED = 2048


def triangle():
    row = lax.broadcasted_iota(jnp.int32, (CHUNK, CHUNK), 0)
    col = lax.broadcasted_iota(jnp.int32, (CHUNK, CHUNK), 1)
    return col <= row


def pair_lanes(values, pair):
    lane = lax.broadcasted_iota(jnp.int32, (values.shape[0], 128), 1)
    at = 2 * pair
    return jnp.where(lane < HEAD_SIZE, values[:, at : at + 1], values[:, at + 1 : at + 2])


def split_pair(values):
    lane = lax.broadcasted_iota(jnp.int32, values.shape, 1)
    empty = jnp.zeros_like(values)
    return jnp.concatenate(
        [jnp.where(lane < HEAD_SIZE, values, empty), jnp.where(lane < HEAD_SIZE, empty, values)],
        axis=0,
    )


def conv_pre(buf_ref, taps_ref, begin, size):
    total = buf_ref[5 : 5 + CHUNK, begin : begin + size] * taps_ref[0:1, begin : begin + size]
    for tap in range(1, KCONV):
        total = total + (
            buf_ref[5 + tap : 5 + tap + CHUNK, begin : begin + size]
            * taps_ref[tap : tap + 1, begin : begin + size]
        )
    return total


def load_conv(buf_ref, proj_ref):
    for group in range(2):
        at = group * 1024 + GROUP
        buf_ref[8:, group * GROUP : (group + 1) * GROUP] = proj_ref[:, at : at + GROUP]
    buf_ref[8:, 2 * GROUP :] = proj_ref[:, SHARED : SHARED + 2 * N]


def group_steps(proj_ref, bias_ref, decay_ref, group, lower):
    at = group * 1024 + 896
    raw = proj_ref[:, at : at + 128] + bias_ref[group : group + 1, :]
    step = jnp.log1p(jnp.exp(-jnp.abs(raw))) + jnp.maximum(raw, 0.0)
    rate = -jnp.exp(decay_ref[group : group + 1, :])
    cumul = dot_fine(lower, rate * step)
    return raw, step, rate, cumul


def head_decay(cumul, cumul_t, head, mask):
    spread = cumul[:, head : head + 1] - cumul_t[head : head + 1, :]
    return jnp.exp(jnp.where(mask, spread, MASKED))


def mamba_chunk(
    proj_ref,
    attn_ref,
    taps_ref,
    bias_ref,
    decay_ref,
    skip_ref,
    gain_ref,
    both_ref,
    out_ref,
    state_out,
    buf_ref,
    state_ref,
):
    load_conv(buf_ref, proj_ref)
    mask = triangle()
    lower = mask.astype(jnp.bfloat16)
    pre = conv_pre(buf_ref, taps_ref, 2 * GROUP, 2 * N)
    state_act = low(pre * sigmoid(pre))
    b_rows, c_rows = state_act[:, :N], state_act[:, N:]
    gram = dot_nt(c_rows, b_rows)
    b_cols = b_rows.T
    for group in range(2):
        cols = slice(group * GROUP, (group + 1) * GROUP)
        _, step, _, cumul = group_steps(proj_ref, bias_ref, decay_ref, group, lower)
        cumul_t = cumul.T
        last = cumul[CHUNK - 1 : CHUNK, :]
        state = state_ref[:, cols]
        state_out[:, cols] = state
        from_state = dot(c_rows, low(state))
        gated = []
        for pair in range(PAIRS):
            at = group * GROUP + pair * 128
            pre = conv_pre(buf_ref, taps_ref, at, 128)
            chan = pre * sigmoid(pre)
            inputs = low(chan * pair_lanes(step, pair))
            mixing = jnp.concatenate(
                [
                    low(gram * head_decay(cumul, cumul_t, 2 * pair + side, mask))
                    for side in range(2)
                ],
                axis=1,
            )
            lanes = slice(pair * 128, (pair + 1) * 128)
            inner = pair_lanes(cumul, pair)
            out = dot(mixing, split_pair(inputs)) + jnp.exp(inner) * from_state[:, lanes]
            out_ref[:, at : at + 128] = out
            last_lanes = pair_lanes(last, pair)
            x_end = low(jnp.exp(last_lanes - inner) * wide(inputs))
            state_ref[:, at : at + 128] = jnp.exp(last_lanes) * state[:, lanes] + dot(
                b_cols, x_end
            )
            gate = proj_ref[:, group * 1024 + pair * 128 : group * 1024 + pair * 128 + 128]
            skipped = out + chan * skip_ref[:, at : at + 128]
            gated.append(skipped * (gate * sigmoid(gate)))
        square = jnp.sum(sum(part * part for part in gated), axis=1, keepdims=True)
        scale = lax.rsqrt(square * (1.0 / GROUP) + EPS)
        for pair in range(PAIRS):
            at = group * GROUP + pair * 128
            to = group * 512 + pair * 128
            both_ref[:, to : to + 128] = low(gated[pair] * scale * gain_ref[:, at : at + 128])
        to = group * 512 + GROUP
        both_ref[:, to : to + 128] = attn_ref[:, group * 128 : (group + 1) * 128]
    buf_ref[0:8, :] = buf_ref[CHUNK : CHUNK + 8, :]


def mamba_start(buf_ref, state_ref):
    buf_ref[0:8, :] = jnp.zeros((8, CONV), jnp.float32)
    state_ref[...] = jnp.zeros_like(state_ref)


def mamba_forward_kernel(*refs):
    @pl.when(pl.program_id(0) == 0)
    def _():
        mamba_start(*refs[-2:])

    mamba_chunk(*refs[:9], refs[9].at[0], *refs[10:])


def mamba_forward(proj, attn, taps, bias, decay, skip, gain):
    rows, columns = proj.shape
    chunks = rows // CHUNK

    def whole(value):
        return pl.BlockSpec(value.shape, lambda k: (0, 0))

    return pl.pallas_call(
        mamba_forward_kernel,
        grid=(chunks,),
        in_specs=[
            pl.BlockSpec((CHUNK, columns), lambda k: (k, 0)),
            pl.BlockSpec((CHUNK, 256), lambda k: (k, 0)),
        ]
        + [whole(value) for value in (taps, bias, decay, skip, gain)],
        out_specs=[
            pl.BlockSpec((CHUNK, 1024), lambda k: (k, 0)),
            pl.BlockSpec((CHUNK, 2 * GROUP), lambda k: (k, 0)),
            pl.BlockSpec((1, N, 2 * GROUP), lambda k: (k, 0, 0)),
        ],
        out_shape=[
            jax.ShapeDtypeStruct((rows, 1024), jnp.bfloat16),
            jax.ShapeDtypeStruct((rows, 2 * GROUP), jnp.float32),
            jax.ShapeDtypeStruct((chunks, N, 2 * GROUP), jnp.float32),
        ],
        scratch_shapes=[
            pltpu.VMEM((CHUNK + 8, CONV), jnp.float32),
            pltpu.VMEM((N, 2 * GROUP), jnp.float32),
        ],
        compiler_params=pltpu.CompilerParams(vmem_limit_bytes=BIG),
        cost_estimate=cost(14),
        name="mamba_forward",
    )(proj, attn, taps, bias, decay, skip, gain)


def silu_slope(values, sig):
    return sig * (1.0 + values * (1.0 - sig))


def mamba_backward_kernel(
    proj_ref,
    before_ref,
    out_ref,
    states_ref,
    back_ref,
    dq_ref,
    dkv_ref,
    taps_ref,
    bias_ref,
    decay_ref,
    skip_ref,
    gain_ref,
    dproj_ref,
    dtaps_ref,
    dgain_ref,
    dskip_ref,
    dbias_ref,
    ddecay_ref,
    buf_ref,
    grad_buf,
    after_ref,
    flow_ref,
):
    step_at = pl.program_id(0)

    @pl.when(step_at == 0)
    def _():
        for ref in (dtaps_ref, dgain_ref, dskip_ref, dbias_ref, ddecay_ref, after_ref, flow_ref):
            ref[...] = jnp.zeros_like(ref)
        grad_buf[CHUNK:, :] = jnp.zeros((8, CONV), jnp.float32)

    inside = jnp.where(step_at == pl.num_programs(0) - 1, 0.0, 1.0)
    for group in range(2):
        at = group * 1024 + GROUP
        buf_ref[0:8, group * GROUP : (group + 1) * GROUP] = before_ref[:, at : at + GROUP] * inside
    buf_ref[0:8, 2 * GROUP :] = before_ref[:, SHARED : SHARED + 2 * N] * inside
    load_conv(buf_ref, proj_ref)
    mask = triangle()
    lower = mask.astype(jnp.bfloat16)
    row = lax.broadcasted_iota(jnp.int32, (CHUNK, CHUNK), 0)
    col = lax.broadcasted_iota(jnp.int32, (CHUNK, CHUNK), 1)
    upper = (row <= col).astype(jnp.bfloat16)
    pre_state = conv_pre(buf_ref, taps_ref, 2 * GROUP, 2 * N)
    sig_state = sigmoid(pre_state)
    state_act = low(pre_state * sig_state)
    b_rows, c_rows = state_act[:, :N], state_act[:, N:]
    gram = dot_nt(c_rows, b_rows)
    c_cols = c_rows.T
    dgram = jnp.zeros((CHUNK, CHUNK), jnp.float32)
    d_c = jnp.zeros((CHUNK, N), jnp.float32)
    d_b = jnp.zeros((CHUNK, N), jnp.float32)
    for group in range(2):
        raw, step, rate, cumul = group_steps(proj_ref, bias_ref, decay_ref, group, lower)
        cumul_t = cumul.T
        last = cumul[CHUNK - 1 : CHUNK, :]
        pres, sigs, chans, gates, gate_sigs, skips, gated = [], [], [], [], [], [], []
        for pair in range(PAIRS):
            at = group * GROUP + pair * 128
            pre = conv_pre(buf_ref, taps_ref, at, 128)
            sig = sigmoid(pre)
            chan = pre * sig
            gate = proj_ref[:, group * 1024 + pair * 128 : group * 1024 + pair * 128 + 128]
            gate_sig = sigmoid(gate)
            skipped = out_ref[:, at : at + 128] + chan * skip_ref[:, at : at + 128]
            pres.append(pre)
            sigs.append(sig)
            chans.append(chan)
            gates.append(gate)
            gate_sigs.append(gate_sig)
            skips.append(skipped)
            gated.append(skipped * (gate * gate_sig))
        square = jnp.sum(sum(part * part for part in gated), axis=1, keepdims=True)
        scale = lax.rsqrt(square * (1.0 / GROUP) + EPS)
        grads = []
        cross = jnp.zeros((CHUNK, 128), jnp.float32)
        for pair in range(PAIRS):
            at = group * GROUP + pair * 128
            grad = back_ref[:, group * 512 + pair * 128 : group * 512 + pair * 128 + 128]
            dgain_ref[:, at : at + 128] += jnp.sum(grad * gated[pair] * scale, axis=0, keepdims=True)
            grad = grad * gain_ref[:, at : at + 128]
            cross = cross + gated[pair] * grad
            grads.append(grad)
        cross = jnp.sum(cross, axis=1, keepdims=True) * (1.0 / GROUP) * scale * scale * scale
        dstep = jnp.zeros((CHUNK, 128), jnp.float32)
        flow = jnp.zeros((CHUNK, 128), jnp.float32)
        flow_end = flow_ref[group : group + 1, :]
        flow_next = jnp.zeros((1, 128), jnp.float32)
        for pair in range(PAIRS):
            at = group * GROUP + pair * 128
            head_of_lane = lax.broadcasted_iota(jnp.int32, (128, 128), 0) // HEAD_SIZE + 2 * pair
            lane = lax.broadcasted_iota(jnp.int32, (128, 128), 1)
            pick = (head_of_lane == lane).astype(jnp.bfloat16)
            chan = chans[pair]
            grad = scale * grads[pair] - gated[pair] * cross
            gate, gate_sig = gates[pair], gate_sigs[pair]
            dgate = grad * skips[pair] * silu_slope(gate, gate_sig)
            to = group * 1024 + pair * 128
            dproj_ref[:, to : to + 128] = low(dgate)
            grad = grad * (gate * gate_sig)
            dskip_ref[:, at : at + 128] += jnp.sum(grad * chan, axis=0, keepdims=True)
            dchan = grad * skip_ref[:, at : at + 128]
            dout = low(grad)
            step_lanes = pair_lanes(step, pair)
            inputs = low(chan * step_lanes)
            halves = split_pair(inputs)
            decays = [head_decay(cumul, cumul_t, 2 * pair + side, mask) for side in range(2)]
            mixing = jnp.concatenate([low(gram * decay) for decay in decays], axis=1)
            dmix = dot_nt(dout, halves)
            dgram = dgram + dmix[:, :CHUNK] * decays[0] + dmix[:, CHUNK:] * decays[1]
            dinputs = dot_tn(mixing, dout)
            lane = lax.broadcasted_iota(jnp.int32, (CHUNK, 128), 1)
            dinputs = jnp.where(lane < HEAD_SIZE, dinputs[:CHUNK], dinputs[CHUNK:])
            inner = pair_lanes(cumul, pair)
            last_lanes = pair_lanes(last, pair)
            to_end = jnp.exp(last_lanes - inner)
            after = after_ref[:, at : at + 128]
            after_low = low(after)
            dinputs = dinputs + to_end * dot(b_rows, after_low)
            x_end = low(to_end * wide(inputs))
            g_start = low(jnp.exp(inner) * wide(dout))
            state = states_ref[0, :, at : at + 128]
            d_c = d_c + dot_nt(g_start, low(state))
            d_b = d_b + dot_nt(x_end, after_low)
            after = jnp.exp(last_lanes) * after + dot(c_cols, g_start)
            after_ref[:, at : at + 128] = after
            through = jnp.sum(after * state, axis=0, keepdims=True)
            flow_next = flow_next + dot_by(jnp.broadcast_to(through, (8, 128)), pick)[0:1]
            flow = flow + dot_by(
                wide(dout) * out_ref[:, at : at + 128] - wide(inputs) * dinputs, pick
            )
            dstep = dstep + dot_by(dinputs * chan, pick)
            dchan = dchan + dinputs * step_lanes
            grad_buf[0:CHUNK, at : at + 128] = dchan * silu_slope(pres[pair], sigs[pair])
        dcumul = dot_fine(upper, flow) + flow_end
        flow_ref[group : group + 1, :] = flow_next
        dstep = dstep + rate * dcumul
        ddecay_ref[group : group + 1, :] += jnp.sum(rate * step * dcumul, axis=0, keepdims=True)
        draw = dstep * sigmoid(raw)
        dbias_ref[group : group + 1, :] += jnp.sum(draw, axis=0, keepdims=True)
        to = group * 1024 + 896
        lane = lax.broadcasted_iota(jnp.int32, (CHUNK, 128), 1)
        dproj_ref[:, to : to + 128] = low(jnp.where(lane < GH, draw, 0.0))
        to = group * 1024 + 2 * GROUP
        dproj_ref[:, to : to + 128] = dq_ref[:, group * 128 : (group + 1) * 128]
    dgram_low = low(dgram)
    d_c = d_c + dot(dgram_low, b_rows)
    d_b = d_b + dot_tn(dgram_low, c_rows)
    slope = silu_slope(pre_state, sig_state)
    grad_buf[0:CHUNK, 2 * GROUP : 2 * GROUP + N] = d_b * slope[:, :N]
    grad_buf[0:CHUNK, 2 * GROUP + N :] = d_c * slope[:, N:]
    for at in range(0, CONV, 128):
        grad = jnp.zeros((CHUNK, 128), jnp.float32)
        here = grad_buf[0:CHUNK, at : at + 128]
        for tap in range(KCONV):
            shift = KCONV - 1 - tap
            grad = grad + (
                grad_buf[shift : shift + CHUNK, at : at + 128] * taps_ref[tap : tap + 1, at : at + 128]
            )
            dtaps_ref[tap : tap + 1, at : at + 128] += jnp.sum(
                here * buf_ref[5 + tap : 5 + tap + CHUNK, at : at + 128], axis=0, keepdims=True
            )
        if at < 2 * GROUP:
            to = (at // GROUP) * 1024 + GROUP + at % GROUP
        else:
            to = SHARED + at - 2 * GROUP
        dproj_ref[:, to : to + 128] = low(grad)
    dproj_ref[:, SHARED + 2 * N :] = dkv_ref[...]
    grad_buf[CHUNK:, :] = grad_buf[0:8, :]


def mamba_backward(proj, out, states, back, dq, dkv, taps, bias, decay, skip, gain):
    rows, columns = proj.shape
    chunks = rows // CHUNK

    def whole(value):
        return pl.BlockSpec(value.shape, lambda k: (0, 0))

    def rows_of(width):
        return pl.BlockSpec((CHUNK, width), lambda k: (chunks - 1 - k, 0))

    params = (taps, bias, decay, skip, gain)
    return pl.pallas_call(
        mamba_backward_kernel,
        grid=(chunks,),
        in_specs=[
            rows_of(columns),
            pl.BlockSpec(
                (8, columns),
                lambda k: (jnp.maximum((chunks - 1 - k) * (CHUNK // 8) - 1, 0), 0),
            ),
            rows_of(2 * GROUP),
            pl.BlockSpec((1, N, 2 * GROUP), lambda k: (chunks - 1 - k, 0, 0)),
            rows_of(1024),
            rows_of(256),
            rows_of(128),
        ]
        + [whole(value) for value in params],
        out_specs=[rows_of(columns)]
        + [whole(value) for value in (taps, gain, skip, bias, decay)],
        out_shape=[jax.ShapeDtypeStruct((rows, columns), jnp.bfloat16)]
        + [
            jax.ShapeDtypeStruct(value.shape, jnp.float32)
            for value in (taps, gain, skip, bias, decay)
        ],
        scratch_shapes=[
            pltpu.VMEM((CHUNK + 8, CONV), jnp.float32),
            pltpu.VMEM((CHUNK + 8, CONV), jnp.float32),
            pltpu.VMEM((N, 2 * GROUP), jnp.float32),
            pltpu.VMEM((8, 128), jnp.float32),
        ],
        compiler_params=pltpu.CompilerParams(vmem_limit_bytes=BIG),
        cost_estimate=cost(36),
        name="mamba_backward",
    )(proj, proj, out, states, back, dq, dkv, *params)


def ffn_kernel(
    x_ref,
    own_ref,
    their_ref,
    gain_ref,
    grad_ref,
    up_ref,
    down_ref,
    hidden_ref,
    normed_ref,
    act_ref,
    dgate_ref,
):
    units = down_ref.shape[1]
    rows = x_ref.shape[0]

    @pl.when(pl.program_id(0) == 0)
    def _():
        @pl.loop(0, rows // 128)
        def _(at):
            here = pl.ds(pl.multiple_of(at * 128, 128), 128)
            hidden = wide(x_ref[here, :]) + (wide(own_ref[here, :]) + wide(their_ref[here, :]))
            hidden_ref[here, :] = hidden
            size = 1.0 / hidden.shape[1]
            root = lax.rsqrt(jnp.sum(hidden * hidden, axis=1, keepdims=True) * size + EPS)
            normed_ref[here, :] = low(hidden * root * gain_ref[...])

    @pl.loop(0, rows // 256)
    def _(at):
        here = pl.ds(pl.multiple_of(at * 256, 256), 256)
        gate_up = dot(normed_ref[here, :], up_ref[...])
        gate, up = gate_up[:, :units], gate_up[:, units:]
        sig = sigmoid(gate)
        act = gate * sig
        act_ref[here, :] = low(act * up)
        grad = dot(grad_ref[here, :], down_ref[...])
        dgate_ref[here, :units] = low(grad * up * silu_slope(gate, sig))
        dgate_ref[here, units:] = low(grad * act)


def ffn_middle(x_rows, own, theirs, gain, grad, up_weight, down_weight, blocks):
    rows, model = x_rows.shape
    units = down_weight.shape[1] // blocks

    def whole(value):
        return pl.BlockSpec(value.shape, lambda z: (0, 0))

    full = pl.BlockSpec((rows, model), lambda z: (0, 0))
    return pl.pallas_call(
        ffn_kernel,
        grid=(blocks,),
        in_specs=[whole(value) for value in (x_rows, own, theirs, gain, grad)]
        + [
            pl.BlockSpec((model, 2 * units), lambda z: (0, z)),
            pl.BlockSpec((model, units), lambda z: (0, z)),
        ],
        out_specs=[
            full,
            full,
            pl.BlockSpec((rows, units), lambda z: (0, z)),
            pl.BlockSpec((rows, 2 * units), lambda z: (0, z)),
        ],
        out_shape=[
            jax.ShapeDtypeStruct((rows, model), jnp.float32),
            jax.ShapeDtypeStruct((rows, model), jnp.bfloat16),
            jax.ShapeDtypeStruct((rows, blocks * units), jnp.bfloat16),
            jax.ShapeDtypeStruct((rows, 2 * blocks * units), jnp.bfloat16),
        ],
        compiler_params=pltpu.CompilerParams(vmem_limit_bytes=BIG),
        cost_estimate=cost(14),
        name="ffn_middle",
    )(x_rows, own, theirs, gain, grad, up_weight, down_weight)


def hidden_kernel(
    hidden_ref, own_ref, their_ref, grad_ref, gain_ref, weight_ref, dhidden_ref, mixed_ref, back_ref, dgain_ref
):
    @pl.when(pl.program_id(0) == 0)
    def _():
        dgain_ref[...] = jnp.zeros_like(dgain_ref)

    hidden = hidden_ref[...]
    grad = wide(own_ref[...]) + wide(their_ref[...])
    size = 1.0 / hidden.shape[1]
    root = lax.rsqrt(jnp.sum(hidden * hidden, axis=1, keepdims=True) * size + EPS)
    scaled = grad * gain_ref[...]
    inner = jnp.sum(hidden * scaled, axis=1, keepdims=True) * size
    dhidden = wide(grad_ref[...]) + root * scaled - hidden * (root * root * root * inner)
    dhidden_ref[...] = dhidden
    dgain_ref[...] += 0.5 * jnp.sum(hidden * root * grad, axis=0, keepdims=True)
    mixed = low(dhidden)
    mixed_ref[...] = mixed
    back_ref[...] = dot(mixed, weight_ref[...])


def hidden_backward(hidden, own, theirs, grad, gain, weight):
    rows, model = hidden.shape

    def whole(value):
        return pl.BlockSpec(value.shape, lambda k: (0, 0))

    part = pl.BlockSpec((256, model), lambda k: (k, 0))
    return pl.pallas_call(
        hidden_kernel,
        grid=(rows // 256,),
        in_specs=[part] * 4 + [whole(gain), whole(weight)],
        out_specs=[part, part, pl.BlockSpec((256, weight.shape[1]), lambda k: (k, 0)), whole(gain)],
        out_shape=[
            jax.ShapeDtypeStruct((rows, model), jnp.float32),
            jax.ShapeDtypeStruct((rows, model), jnp.bfloat16),
            jax.ShapeDtypeStruct((rows, weight.shape[1]), jnp.float32),
            jax.ShapeDtypeStruct(gain.shape, jnp.float32),
        ],
        compiler_params=pltpu.CompilerParams(vmem_limit_bytes=BIG),
        cost_estimate=cost(7),
        name="hidden_backward",
    )(hidden, own, theirs, grad, gain, weight)


def ffn_grad_kernel(grad_ref, act_ref, normed_ref, dgate_ref, out_ref):
    kind = pl.program_id(0) % 3

    @pl.when(kind == 2)
    def _():
        out_ref[...] = low(dot_tn(grad_ref[...], act_ref[...]))

    @pl.when(kind < 2)
    def _():
        out_ref[...] = low(dot_tn(normed_ref[...], dgate_ref[...]))


def ffn_gradients(grad, act, normed, dgate, blocks):
    rows, model = grad.shape
    units = act.shape[1] // blocks
    whole = pl.BlockSpec((rows, model), lambda j: (0, 0))
    return pl.pallas_call(
        ffn_grad_kernel,
        grid=(3 * blocks,),
        in_specs=[
            whole,
            pl.BlockSpec((rows, units), lambda j: (0, j // 3)),
            whole,
            pl.BlockSpec((rows, units), lambda j: (0, (j // 3) * 2 + jnp.minimum(j % 3, 1))),
        ],
        out_specs=pl.BlockSpec((model, units), lambda j: (0, j)),
        out_shape=jax.ShapeDtypeStruct((model, 3 * blocks * units), jnp.bfloat16),
        compiler_params=pltpu.CompilerParams(vmem_limit_bytes=BIG),
        cost_estimate=cost(12),
        name="ffn_gradients",
    )(grad, act, normed, dgate)


MESH = pl.DeviceIdType.MESH


def landed(ref, sem):
    pltpu.make_async_copy(ref, ref, sem).wait()


def front_kernel(*refs):
    (pack_ref, next_ref, ups_ref, downs_ref, shared_ref, x_ref, small_ref, og_ref) = refs[:8]
    (state_taps, gain_in, len_ref, cos_ref, sin_ref) = refs[8:13]
    (w_hbm, v_hbm, u_ref, d_ref, x_hbm, normed_hbm, proj_hbm, og_full) = refs[13:21]
    (taps_ref, bias_ref, decay_ref, skip_ref, gain_ref) = refs[21:26]
    (sums_ref, both_ref, out_ref, states_ref, mixed_ref, other_ref) = refs[26:32]
    (w_ref, v_ref, full_ref, normed_ref, proj_ref, attn_ref, params_ref) = refs[32:39]
    (buf_ref, state_ref) = refs[39:41]
    (near_sem, out_sem, part_sem, fromx_sem, fromy_sem, overx_sem, overy_sem) = refs[41:48]
    (tox_sem, toy_sem, relx_sem, rely_sem, row_sem, row_out, pair_sem, pair_out) = refs[48:56]
    (param_sem, param_out, ffn_out, store_sem, mixed_sem) = refs[56:]
    plane = lax.axis_index("plane")
    core = lax.axis_index("core")
    place = lax.axis_index("tensor")
    xside = plane + 1 - 2 * (plane % 2)
    yside = plane + 2 - 4 * (plane // 2)
    across = xside + 2 - 4 * (xside // 2)
    target = place // 2
    column = place % 2
    share, width = pack_ref.shape
    narrow = next_ref.shape[1]
    rest = shared_ref.shape[2]
    half = share
    rows_dev = x_ref.shape[1]

    barrier = pltpu.get_barrier_semaphore()
    for step in range(4):
        for side in range(2):
            if step or side:
                pl.semaphore_signal(
                    barrier,
                    inc=1,
                    device_id={"core": (core + side) % 2, "tensor": (place + step) % 4},
                    device_id_type=MESH,
                )
    for neighbour in (xside, yside):
        pl.semaphore_signal(
            barrier, inc=1, device_id={"plane": neighbour}, device_id_type=MESH
        )
    pl.semaphore_wait(barrier, 9)

    def block(at, part):
        return pl.ds(pl.multiple_of(at * 2 * share + part * share, share), share)

    def piece(at, part, col):
        return w_ref.at[block(at, part), pl.ds(pl.multiple_of(col * width, width), width)]

    def next_piece(at, part, col):
        return v_ref.at[block(at, part), pl.ds(pl.multiple_of(col * narrow, narrow), narrow)]

    def rest_piece(at, part):
        return w_ref.at[block(at, part), pl.ds(2 * width, rest)]

    started = []

    def send(src, dst, send_sem, recv_sem, device):
        copy = pltpu.make_async_remote_copy(
            src_ref=src,
            dst_ref=dst,
            send_sem=send_sem,
            recv_sem=recv_sem,
            device_id=device,
            device_id_type=MESH,
        )
        copy.start()
        started.append((src, send_sem))

    mine = piece(plane, core, column)
    slot = core * 2 + column
    mine_next = next_piece(plane, core, column)

    def send_parts(src, dst, at, recv_sem):
        for step in (2, 1, 3):
            send(
                src,
                dst,
                out_sem.at[at + step],
                recv_sem,
                {"core": target, "tensor": (place + step) % 4},
            )

    send_parts(pack_ref, mine, 0, part_sem.at[slot])

    params = params_ref.at[column]

    @pl.when(target == core)
    def _():
        pltpu.make_async_copy(pack_ref, mine, part_sem.at[slot]).start()
        pltpu.make_async_copy(next_ref, mine_next, part_sem.at[6 + slot]).start()
        pltpu.make_async_copy(small_ref, params, param_sem.at[column]).start()
        for step in range(1, 4):
            pltpu.make_async_remote_copy(
                src_ref=small_ref,
                dst_ref=params,
                send_sem=param_out.at[step],
                recv_sem=param_sem.at[column],
                device_id={"tensor": (place + step) % 4},
                device_id_type=MESH,
            ).start()

    @pl.when(target != core)
    def _():
        pltpu.make_async_remote_copy(
            src_ref=pack_ref,
            dst_ref=mine,
            send_sem=out_sem.at[0],
            recv_sem=part_sem.at[slot],
            device_id={"core": 1 - core},
            device_id_type=MESH,
        ).start()
        pltpu.make_async_remote_copy(
            src_ref=next_ref,
            dst_ref=mine_next,
            send_sem=out_sem.at[4],
            recv_sem=part_sem.at[6 + slot],
            device_id={"core": 1 - core},
            device_id_type=MESH,
        ).start()

    own_rest = rest_piece(plane, core)
    near = pltpu.make_async_copy(shared_ref.at[core], own_rest, part_sem.at[4 + core])
    near.start()
    send(
        shared_ref.at[1 - core],
        own_rest,
        near_sem.at[0],
        part_sem.at[4 + core],
        {"core": 1 - core},
    )

    def rows_at(ref, at, side):
        return ref.at[pl.ds(pl.multiple_of(at * rows_dev + side * half, half), half)]

    wide_up, wide_down = ups_ref.shape[2], downs_ref.shape[2]

    def down_piece(at, part, place_at):
        cols = pl.ds(pl.multiple_of(place_at * wide_down, wide_down), wide_down)
        return d_ref.at[block(at, part), cols]

    def up_piece(at, part, place_at):
        cols = pl.ds(pl.multiple_of(place_at * wide_up, wide_up), wide_up)
        return u_ref.at[block(at, part), cols]

    def row_parts(src_ref, dst_ref):
        for seq in range(2):
            for side in range(2):
                goal = 2 * core + seq
                here = jnp.logical_and(core == side, goal == place)
                src = src_ref.at[seq, pl.ds(side * half, half)]
                yield seq * 2 + side, here, src, rows_at(dst_ref, place, side), side, goal

    def send_rows(src_ref, dst_ref, kind):
        for number, here, src, dst, side, goal in row_parts(src_ref, dst_ref):

            @pl.when(here)
            def _():
                pltpu.make_async_copy(src, dst, row_sem.at[kind, place]).start()

            @pl.when(jnp.logical_not(here))
            def _():
                pltpu.make_async_remote_copy(
                    src_ref=src,
                    dst_ref=dst,
                    send_sem=row_out.at[kind, number],
                    recv_sem=row_sem.at[kind, place],
                    device_id={"core": side, "tensor": goal},
                    device_id_type=MESH,
                ).start()

    def share_rows(ref, kind, steps=(0, 1, 2, 3)):
        for step in steps:
            at = (place + step) % 4
            part = rows_at(ref, at, core)
            landed(part, row_sem.at[kind, at])
            send(part, part, pair_out.at[kind, at], pair_sem.at[kind, at], {"core": 1 - core})

    def shared_rows(ref, kind):
        for step in range(4):
            at = (place + step) % 4
            landed(rows_at(ref, at, 1 - core), pair_sem.at[kind, at])


    def send_halves(number, src, goal_ref, recv_sem):
        for step in (2, 1, 3):
            for side in range(2):
                send(
                    src.at[side],
                    goal_ref,
                    ffn_out.at[number, 2 * step + side],
                    recv_sem,
                    {"core": side, "tensor": (place + step) % 4},
                )
        send(
            src.at[1 - core], goal_ref, ffn_out.at[number, 0], recv_sem, {"core": 1 - core}
        )
        pltpu.make_async_copy(src.at[core], goal_ref, recv_sem).start()

    def issue_next():
        send_parts(next_ref, mine_next, 4, part_sem.at[6 + slot])

    def issue_downs():
        send_halves(
            0, downs_ref, down_piece(plane, core, place), part_sem.at[10 + 2 * place + core]
        )

    def issue_ups():
        send_halves(
            1, ups_ref, up_piece(plane, core, place), part_sem.at[18 + 2 * place + core]
        )

    first_col = jnp.where(place // 2 == core, place % 2, 1 - core)
    order = [(0, None, 0), (0, None, 1)]
    for kind in (1, 2):
        for turn in range(2):
            for part in range(2):
                order.append((kind, (first_col + turn) % 2, part))

    for kind in (3, 4):
        for step in (0, 1, 3, 2):
            for part in range(2):
                order.append((kind, (place + step) % 4, part))

    def at_piece(at, item):
        kind, col, part = item
        if kind >= 3:
            return (down_piece, up_piece)[kind - 3](at, part, col)
        if kind == 0:
            return rest_piece(at, part)
        return piece(at, part, col) if kind == 1 else next_piece(at, part, col)

    def index(item):
        kind, col, part = item
        if kind >= 3:
            return 8 * kind - 14 + 2 * col + part
        return 4 + part if kind == 0 else (kind - 1) * 6 + part * 2 + col

    def relay(item):
        at = index(item)
        if item[2] == 0:
            landed(at_piece(xside, item), fromx_sem.at[at])
            ref = at_piece(xside, item)
            send(ref, ref, rely_sem.at[at], overy_sem.at[at], {"plane": yside})
        else:
            landed(at_piece(yside, item), fromy_sem.at[at])
            ref = at_piece(yside, item)
            send(ref, ref, relx_sem.at[at], overx_sem.at[at], {"plane": xside})

    def serve(items):
        for item in items:
            at = index(item)
            ref = at_piece(plane, item)
            landed(ref, part_sem.at[at])
            send(ref, ref, tox_sem.at[at], fromx_sem.at[at], {"plane": xside})
            send(ref, ref, toy_sem.at[at], fromy_sem.at[at], {"plane": yside})

    def relays(items):
        for item in items:
            relay(item)

    def complete(items):
        for item in items:
            at = index(item)
            if item[2] == 0:
                landed(at_piece(yside, item), fromy_sem.at[at])
                landed(at_piece(across, item), overy_sem.at[at])
            else:
                landed(at_piece(xside, item), fromx_sem.at[at])
                landed(at_piece(across, item), overx_sem.at[at])

    stores = []

    def store(src, dst):
        sem = store_sem.at[len(stores)]
        pltpu.make_async_copy(src, dst, sem).start()
        stores.append((src, dst, sem))

    issue_next()
    send_rows(x_ref, full_ref, 0)
    serve(order[:4])
    relays(order[:2])
    serve(order[4:6])
    issue_downs()
    relays(order[2:4])
    serve(order[6:8])
    relays(order[4:6])
    serve(order[8:10])
    issue_ups()
    relays(order[6:8])
    complete(order[:6])
    for at in range(2):
        landed(params_ref.at[at], param_sem.at[at])
    taps_ref[:, 2 * GROUP :] = state_taps[...]
    for col in range(2):
        for tap in range(KCONV):
            for at in range(3):
                lanes = pl.ds(col * GROUP + at * 128, 128)
                taps_ref[tap : tap + 1, lanes] = params_ref[col, 3 * tap + at : 3 * tap + at + 1, :]
        for at in range(3):
            lanes = pl.ds(col * GROUP + at * 128, 128)
            skip_ref[:, lanes] = params_ref[col, 12 + at : 13 + at, :]
            gain_ref[:, lanes] = params_ref[col, 15 + at : 16 + at, :]
        bias_ref[col : col + 1, :] = params_ref[col, 18:19, :]
        decay_ref[col : col + 1, :] = params_ref[col, 19:20, :]
    share_rows(full_ref, 0)
    relays(order[8:10])
    shared_rows(full_ref, 0)
    store(w_ref, w_hbm)
    store(full_ref, x_hbm)

    rows = full_ref.shape[0]

    @pl.loop(0, rows // 128)
    def _(at):
        here = pl.ds(pl.multiple_of(at * 128, 128), 128)
        values = wide(full_ref[here, :])
        size = 1.0 / values.shape[1]
        root = lax.rsqrt(jnp.sum(values * values, axis=1, keepdims=True) * size + EPS)
        normed_ref[here, :] = low(values * root * gain_in[...])

    store(normed_ref, normed_hbm)

    def project(begin, end):
        @pl.loop(0, (end - begin) // 256)
        def _(at):
            cols = pl.ds(pl.multiple_of(begin + at * 256, 128), 256)
            proj_ref[:, cols] = dot(normed_ref[...], w_ref[:, cols])

    def attend(col):
        lanes = pl.ds(col * 128, 128)
        attention_forward_kernel(
            len_ref,
            proj_ref.at[:, pl.ds(col * width + 768, 128)],
            proj_ref.at[:, pl.ds(2 * width + 2 * N, 128)],
            cos_ref,
            sin_ref,
            attn_ref.at[:, lanes],
            sums_ref.at[:, lanes],
        )

    def chunks(begin, end):
        @pl.loop(begin, end)
        def _(at):
            here = pl.ds(pl.multiple_of(at * CHUNK, CHUNK), CHUNK)
            mamba_chunk(
                proj_ref.at[here, :],
                attn_ref.at[here, :],
                taps_ref,
                bias_ref,
                decay_ref,
                skip_ref,
                gain_ref,
                both_ref.at[here, :],
                out_ref.at[here, :],
                states_ref.at[at],
                buf_ref,
                state_ref,
            )

    serve(order[10:12])
    project(0, 1024)
    serve(order[12:14])
    relays(order[10:12])
    project(1024, 2304)
    last = pl.ds(2304, proj_ref.shape[1] - 2304)
    proj_ref[:, last] = dot(normed_ref[...], w_ref[:, last])
    store(proj_ref, proj_hbm)
    serve(order[14:18])
    send_rows(og_ref, og_full, 1)
    relays(order[12:14])
    attend(0)
    serve(order[18:20])
    relays(order[14:18])
    attend(1)
    serve(order[20:22])
    relays(order[18:20])
    mamba_start(buf_ref, state_ref)
    count = rows // CHUNK
    chunks(0, count // 4)
    serve(order[22:24])
    relays(order[20:22])
    chunks(count // 4, count // 2)
    complete(order[6:10])
    store(v_ref, v_hbm)
    serve(order[24:26])
    relays(order[22:24])
    chunks(count // 2, count)
    relays(order[24:26])

    @pl.loop(0, 4)
    def _(at):
        here = pl.ds(pl.multiple_of(at * 256, 256), 256)
        mixed_ref[here, :] = low(dot_nt(both_ref[here, :], v_ref[...]))

    send(mixed_ref, other_ref, mixed_sem.at[0], mixed_sem.at[1], {"core": 1 - core})
    share_rows(og_full, 1)
    complete(order[10:26])
    shared_rows(og_full, 1)
    landed(other_ref, mixed_sem.at[1])
    for src, dst, sem in stores:
        pltpu.make_async_copy(src, dst, sem).wait()
    for src, sem in started:
        landed(src, sem)

    @pl.when(target == core)
    def _():
        for step in range(1, 4):
            landed(small_ref, param_out.at[step])

    @pl.when(target != core)
    def _():
        landed(pack_ref, out_sem.at[0])
        landed(next_ref, out_sem.at[4])

    for kind, (src_ref, dst_ref) in enumerate(((x_ref, full_ref), (og_ref, og_full))):
        for number, here, src, _, _, _ in row_parts(src_ref, dst_ref):

            @pl.when(jnp.logical_not(here))
            def _():
                landed(src, row_out.at[kind, number])


def front(
    pack,
    following,
    ups,
    downs,
    shared,
    x_rows,
    small,
    out_grad,
    state_taps,
    gain,
    seq_len,
    cosine,
    sine,
):
    share, width = pack.shape
    narrow = following.shape[1]
    rest = shared.shape[2]
    rows = x_rows.shape[1] * 4
    model = x_rows.shape[2]
    columns = 2 * width + rest
    dma = pltpu.SemaphoreType.DMA
    any_space = pl.BlockSpec(memory_space=pl.ANY)
    near = pl.BlockSpec(memory_space=pltpu.VMEM)
    f32, bf16 = jnp.float32, pack.dtype
    return pl.pallas_call(
        front_kernel,
        in_specs=[any_space] * 8
        + [near, near, pl.BlockSpec(memory_space=pltpu.SMEM), near, near],
        out_specs=[any_space] * 8 + [near] * 11,
        out_shape=[
            jax.ShapeDtypeStruct((8 * share, columns), bf16),
            jax.ShapeDtypeStruct((8 * share, 2 * narrow), bf16),
            jax.ShapeDtypeStruct((8 * share, 4 * ups.shape[2]), bf16),
            jax.ShapeDtypeStruct((8 * share, 4 * downs.shape[2]), bf16),
            jax.ShapeDtypeStruct((rows, model), bf16),
            jax.ShapeDtypeStruct((rows, model), bf16),
            jax.ShapeDtypeStruct((rows, columns), f32),
            jax.ShapeDtypeStruct((rows, model), bf16),
            jax.ShapeDtypeStruct((KCONV, CONV), f32),
            jax.ShapeDtypeStruct((2, 128), f32),
            jax.ShapeDtypeStruct((2, 128), f32),
            jax.ShapeDtypeStruct((1, 2 * GROUP), f32),
            jax.ShapeDtypeStruct((1, 2 * GROUP), f32),
            jax.ShapeDtypeStruct((rows, 256), f32),
            jax.ShapeDtypeStruct((rows, 1024), bf16),
            jax.ShapeDtypeStruct((rows, 2 * GROUP), f32),
            jax.ShapeDtypeStruct((rows // CHUNK, N, 2 * GROUP), f32),
            jax.ShapeDtypeStruct((rows, 8 * share), bf16),
            jax.ShapeDtypeStruct((rows, 8 * share), bf16),
        ],
        scratch_shapes=[
            pltpu.VMEM((8 * share, columns), bf16),
            pltpu.VMEM((8 * share, 2 * narrow), bf16),
            pltpu.VMEM((rows, model), bf16),
            pltpu.VMEM((rows, model), bf16),
            pltpu.VMEM((rows, columns), f32),
            pltpu.VMEM((rows, 256), bf16),
            pltpu.VMEM((2,) + small.shape, f32),
            pltpu.VMEM((CHUNK + 8, CONV), f32),
            pltpu.VMEM((N, 2 * GROUP), f32),
            dma((1,)),
            dma((8,)),
        ]
        + [dma((26,))] * 9
        + [dma((2, 4))] * 4
        + [dma((4,))] * 2
        + [dma((2, 8)), dma((5,)), dma((2,))],
        compiler_params=pltpu.CompilerParams(
            collective_id=1, has_side_effects=True, vmem_limit_bytes=BIG
        ),
        cost_estimate=cost(120),
        name="front",
    )(
        pack,
        following,
        ups,
        downs,
        shared,
        x_rows,
        small,
        out_grad,
        state_taps,
        gain,
        seq_len,
        cosine,
        sine,
    )


def collect_kernel(*refs):
    (mixed_ref, both_ref, normed_hbm, dproj_hbm, weight_hbm, x_hbm, hidden_hbm) = refs[:7]
    (gain_ref, small_ref) = refs[7:9]
    (mixer_out, query_out, step_out, shared_ref, total_ref, back_ref) = refs[9:15]
    (mamba_out, attn_out) = refs[15:17]
    (normed_ref, dproj_ref, weight_ref, x_ref, hidden_ref, grad_ref, next_ref) = refs[17:24]
    (norm_ref, norm_in, rows_ref, in_ref, next_in, sum_ref, next_sum) = refs[24:31]
    (piece_ref, next_buf, pair_ref, mix_ref, near_ref, far_ref) = refs[31:37]
    (in_sem, out_sem, piece_sem, piece_out, pair_sem, mix_sem, mix_out) = refs[37:44]
    (near_sem, near_out, far_sem, far_out, row_sem, row_out, load_sem, norm_sem) = refs[44:]
    plane = lax.axis_index("plane")
    core = lax.axis_index("core")
    place = lax.axis_index("tensor")
    xside = plane + 1 - 2 * (plane % 2)
    yside = plane + 2 - 4 * (plane // 2)
    across = xside + 2 - 4 * (xside // 2)
    share = pair_ref.shape[0]
    width = piece_ref.shape[2]
    rest = grad_ref.shape[1] - 2 * width

    loads = [
        (dproj_hbm, dproj_ref),
        (weight_hbm, weight_ref),
        (normed_hbm, normed_ref),
        (x_hbm.at[:, core], x_ref),
        (hidden_hbm.at[:, core], hidden_ref),
    ]
    for number, (src, dst) in enumerate(loads):
        pltpu.make_async_copy(src, dst, load_sem.at[number]).start()

    def loaded(number):
        src, dst = loads[number]
        pltpu.make_async_copy(src, dst, load_sem.at[number]).wait()

    barrier = pltpu.get_barrier_semaphore()
    for step in range(4):
        for side in range(2):
            if step or side:
                pl.semaphore_signal(
                    barrier,
                    inc=1,
                    device_id={"core": (core + side) % 2, "tensor": (place + step) % 4},
                    device_id_type=MESH,
                )
    for neighbour in (xside, yside):
        pl.semaphore_signal(
            barrier, inc=1, device_id={"plane": neighbour}, device_id_type=MESH
        )
    pl.semaphore_wait(barrier, 9)

    started = []

    def send(src, dst, send_sem, recv_sem, device):
        pltpu.make_async_remote_copy(
            src_ref=src,
            dst_ref=dst,
            send_sem=send_sem,
            recv_sem=recv_sem,
            device_id=device,
            device_id_type=MESH,
        ).start()
        started.append((src, send_sem))

    narrow = next_ref.shape[1] // 2
    spans = [(0, 2 * width, rest), (0, 0, width), (0, width, width)]
    spans += [(1, 0, narrow), (1, narrow, narrow)]

    def block(at, part, span):
        rows = pl.ds(pl.multiple_of(at * 2 * share + part * share, share), share)
        return (grad_ref, next_ref)[span[0]].at[rows, pl.ds(*span[1:])]

    def held(slot, span):
        return (in_ref, next_in)[span[0]].at[slot, :, pl.ds(*span[1:])]

    def summed(part, span):
        return (sum_ref, next_sum)[span[0]].at[part, :, pl.ds(*span[1:])]

    def begin(number):
        span = spans[number]
        send(
            block(across, 0, span),
            held(0, span),
            out_sem.at[0, number],
            in_sem.at[0, number],
            {"plane": xside},
        )
        send(
            block(across, 1, span),
            held(1, span),
            out_sem.at[1, number],
            in_sem.at[1, number],
            {"plane": yside},
        )
        send(
            block(xside, 0, span),
            held(2, span),
            out_sem.at[2, number],
            in_sem.at[2, number],
            {"plane": xside},
        )
        send(
            block(yside, 1, span),
            held(3, span),
            out_sem.at[3, number],
            in_sem.at[3, number],
            {"plane": yside},
        )

    def work(number):
        kind, begin_at, size = spans[number]
        left = (normed_ref, mixed_ref)[kind]
        right = (dproj_ref, both_ref)[kind]
        result = (grad_ref, next_ref)[kind]
        tile = 256 if size % 256 == 0 else size

        @pl.loop(0, size // tile)
        def _(at):
            cols = pl.ds(pl.multiple_of(begin_at + at * tile, 128), tile)
            result[:, cols] = low(dot_tn(left[...], right[:, cols]))

    seq = place % 2
    owner = place // 2
    dst_rows = back_ref.at[seq, pl.ds(pl.multiple_of(core * share, share), share)]

    def send_back():
        for step in (2, 1, 3):
            at = (place + step) % 4
            send(
                rows_ref.at[at],
                dst_rows,
                row_out.at[step],
                row_sem.at[seq * 2 + core],
                {"core": owner, "tensor": at},
            )

        @pl.when(owner == core)
        def _():
            pltpu.make_async_copy(
                rows_ref.at[place], dst_rows, row_sem.at[seq * 2 + core]
            ).start()

        @pl.when(owner != core)
        def _():
            pltpu.make_async_remote_copy(
                src_ref=rows_ref.at[place],
                dst_ref=dst_rows,
                send_sem=row_out.at[0],
                recv_sem=row_sem.at[seq * 2 + core],
                device_id={"core": 1 - core},
                device_id_type=MESH,
            ).start()

    def norm_product():
        loaded(0)
        loaded(1)
        for at in range(4):
            rows = pl.ds(at * 2 * share, 2 * share)
            part = low(dot_nt(dproj_ref[rows, :], weight_ref[...]))
            norm_ref[at, 0] = part[:share]
            norm_ref[at, 1] = part[share:]
        send(
            norm_ref.at[:, 1 - core],
            norm_in,
            norm_sem.at[0],
            norm_sem.at[1],
            {"core": 1 - core},
        )

    def norm_back():
        loaded(3)
        loaded(4)
        landed(norm_in, norm_sem.at[1])
        gain_total = jnp.zeros((1, x_ref.shape[2]), jnp.float32)
        for at in range(4):
            grad = wide(norm_ref[at, core]) + wide(norm_in[at])
            values = wide(x_ref[at])
            size = 1.0 / values.shape[1]
            root = lax.rsqrt(jnp.sum(values * values, axis=1, keepdims=True) * size + EPS)
            scaled = grad * gain_ref[...]
            inner = jnp.sum(values * scaled, axis=1, keepdims=True) * size
            rows_ref[at] = low(
                hidden_ref[at] + root * scaled - values * (root * root * root * inner)
            )
            gain_total = gain_total + jnp.sum(values * root * grad, axis=0, keepdims=True)
        near_ref[5] = small_ref[...]
        for at in range(gain_total.shape[1] // 128):
            near_ref[5, at : at + 1, :] = gain_total[:, at * 128 : (at + 1) * 128]

    def pass_on(number):
        span = spans[number]
        landed(held(0, span), in_sem.at[0, number])
        held(0, span)[...] = low(wide(held(0, span)[...]) + wide(block(yside, 0, span)[...]))
        send(
            held(0, span),
            held(5, span),
            out_sem.at[4, number],
            in_sem.at[5, number],
            {"plane": yside},
        )
        landed(held(1, span), in_sem.at[1, number])
        held(1, span)[...] = low(wide(held(1, span)[...]) + wide(block(xside, 1, span)[...]))
        send(
            held(1, span),
            held(4, span),
            out_sem.at[5, number],
            in_sem.at[4, number],
            {"plane": xside},
        )

    def finish(number):
        span = spans[number]
        landed(held(2, span), in_sem.at[2, number])
        landed(held(5, span), in_sem.at[5, number])
        summed(0, span)[...] = low(
            wide(block(plane, 0, span)[...]) + wide(held(2, span)[...]) + wide(held(5, span)[...])
        )
        landed(held(3, span), in_sem.at[3, number])
        landed(held(4, span), in_sem.at[4, number])
        summed(1, span)[...] = low(
            wide(block(plane, 1, span)[...]) + wide(held(3, span)[...]) + wide(held(4, span)[...])
        )

    def send_pieces(number):
        span = spans[number]
        kind, col = span[0], span[1] // span[2]
        buf = (piece_ref, next_buf)[kind]
        goal = 2 * core + col
        for part in range(2):
            src = summed(part, span)
            here = jnp.logical_and(core == part, goal == place)

            @pl.when(here)
            def _():
                pltpu.make_async_copy(src, buf.at[place], piece_sem.at[kind, place]).start()

            @pl.when(jnp.logical_not(here))
            def _():
                pltpu.make_async_remote_copy(
                    src_ref=src,
                    dst_ref=buf.at[place],
                    send_sem=piece_out.at[kind, 2 * col + part],
                    recv_sem=piece_sem.at[kind, place],
                    device_id={"core": part, "tensor": goal},
                    device_id_type=MESH,
                ).start()

    rest_cols = pl.ds(2 * width, rest)
    state = rest * 2 // 3

    def pair_up():
        send(
            sum_ref.at[1 - core, :, rest_cols],
            pair_ref,
            pair_sem.at[0],
            pair_sem.at[1],
            {"core": 1 - core},
        )

    def mix():
        landed(pair_ref, pair_sem.at[1])
        mine = sum_ref[core, :, rest_cols]
        mix_ref[place, :, 0:state] = low(wide(mine[:, :state]) + wide(pair_ref[:, :state]))
        first = core == 0
        mix_ref[place, :, state:rest] = jnp.where(first, mine[:, state:], pair_ref[:, state:])
        mix_ref[place, :, rest:] = jnp.where(first, pair_ref[:, state:], mine[:, state:])
        own_mix = mix_ref.at[place]
        for step in (2, 1, 3):
            send(
                own_mix,
                own_mix,
                mix_out.at[step],
                mix_sem.at[place],
                {"tensor": (place + step) % 4},
            )

    work(3)
    begin(3)
    work(4)
    begin(4)
    norm_product()
    pass_on(3)
    loaded(2)
    work(0)
    begin(0)
    finish(3)
    send_pieces(3)
    pass_on(4)
    norm_back()
    send_back()
    send(near_ref.at[5], near_ref.at[0], near_out.at[0], near_sem.at[0], {"plane": xside})
    work(1)
    begin(1)
    finish(4)
    send_pieces(4)
    pass_on(0)
    work(2)
    landed(near_ref.at[0], near_sem.at[0])
    near_ref[3] = near_ref[5] + near_ref[0]
    send(near_ref.at[3], near_ref.at[1], near_out.at[1], near_sem.at[1], {"plane": yside})
    finish(0)
    pair_up()
    pass_on(1)
    begin(2)
    landed(near_ref.at[1], near_sem.at[1])
    near_ref[4] = near_ref[3] + near_ref[1]
    send(near_ref.at[4], near_ref.at[2], near_out.at[2], near_sem.at[2], {"core": 1 - core})
    mix()
    finish(1)
    send_pieces(1)
    landed(near_ref.at[2], near_sem.at[2])
    far_ref[place] = near_ref[4] + near_ref[2]
    own_far = far_ref.at[place]
    for step in (2, 1, 3):
        send(
            own_far,
            own_far,
            far_out.at[step],
            far_sem.at[place],
            {"tensor": (place + step) % 4},
        )
    pass_on(2)
    finish(2)
    send_pieces(2)

    for step in (1, 2, 3):
        at = (place + step) % 4
        landed(mix_ref.at[at], mix_sem.at[at])
        landed(far_ref.at[at], far_sem.at[at])
    shared_ref[...] = (
        wide(mix_ref[0]) + wide(mix_ref[1]) + wide(mix_ref[2]) + wide(mix_ref[3])
    )
    total_ref[...] = (far_ref[0] + far_ref[1]) + (far_ref[2] + far_ref[3])
    def gathered(buf, kind):
        for at in range(4):
            landed(buf.at[at], piece_sem.at[kind, at])
        return wide(buf[0]) + wide(buf[1]) + wide(buf[2]) + wide(buf[3])

    one = gathered(piece_ref, 0)
    cut = mixer_out.shape[1]
    mixer_out[...] = one[:, :cut]
    query_out[...] = one[:, cut : cut + query_out.shape[1]]
    step_out[...] = one[:, cut + query_out.shape[1] :]
    both = gathered(next_buf, 1).T
    mamba_out[...] = both[: mamba_out.shape[0]]
    attn_out[...] = both[mamba_out.shape[0] :]
    for at in range(4):
        landed(dst_rows, row_sem.at[at])
    for src, sem in started:
        landed(src, sem)

    @pl.when(owner != core)
    def _():
        landed(rows_ref.at[place], row_out.at[0])

    for span in spans[1:]:
        col = span[1] // span[2]
        for part in range(2):
            here = jnp.logical_and(core == part, 2 * core + col == place)

            @pl.when(jnp.logical_not(here))
            def _():
                landed(summed(part, span), piece_out.at[span[0], 2 * col + part])


def collect(normed, dproj, weight, mixed, both, x_rows, hidden, gain, small, sizes):
    chans, queries, width = sizes
    share = weight.shape[0] // 8
    model = weight.shape[0]
    columns = weight.shape[1]
    rest = columns - 2 * width
    narrow = both.shape[1] // 2
    dma = pltpu.SemaphoreType.DMA
    any_space = pl.BlockSpec(memory_space=pl.ANY)
    near = pl.BlockSpec(memory_space=pltpu.VMEM)
    shared_cols = rest + rest // 3
    bf16, f32 = jnp.bfloat16, jnp.float32
    split = (4, 2, x_rows.shape[0] // 8, model)
    half = (4, x_rows.shape[0] // 8, model)
    return pl.pallas_call(
        collect_kernel,
        in_specs=[near, near] + [any_space] * 5 + [near, near],
        out_specs=[near] * 5 + [any_space] + [near] * 2,
        out_shape=[
            jax.ShapeDtypeStruct((share, 2 * chans), f32),
            jax.ShapeDtypeStruct((share, queries), f32),
            jax.ShapeDtypeStruct((share, width - 2 * chans - queries), f32),
            jax.ShapeDtypeStruct((share, shared_cols), f32),
            jax.ShapeDtypeStruct(small.shape, f32),
            jax.ShapeDtypeStruct((2, 2 * half[1], model), bf16),
            jax.ShapeDtypeStruct((chans, share), f32),
            jax.ShapeDtypeStruct((narrow - chans, share), f32),
        ],
        scratch_shapes=[
            pltpu.VMEM(normed.shape, bf16),
            pltpu.VMEM(dproj.shape, bf16),
            pltpu.VMEM(weight.shape, bf16),
            pltpu.VMEM(half, bf16),
            pltpu.VMEM(half, f32),
            pltpu.VMEM((model, columns), bf16),
            pltpu.VMEM((model, 2 * narrow), bf16),
            pltpu.VMEM(split, bf16),
            pltpu.VMEM(half, bf16),
            pltpu.VMEM(half, bf16),
            pltpu.VMEM((6, share, columns), bf16),
            pltpu.VMEM((6, share, 2 * narrow), bf16),
            pltpu.VMEM((2, share, columns), bf16),
            pltpu.VMEM((2, share, 2 * narrow), bf16),
            pltpu.VMEM((4, share, width), bf16),
            pltpu.VMEM((4, share, narrow), bf16),
            pltpu.VMEM((share, rest), bf16),
            pltpu.VMEM((4, share, shared_cols), bf16),
            pltpu.VMEM((6,) + small.shape, f32),
            pltpu.VMEM((4,) + small.shape, f32),
            dma((6, 5)),
            dma((6, 5)),
            dma((2, 4)),
            dma((2, 4)),
            dma((2,)),
            dma((4,)),
            dma((4,)),
            dma((3,)),
            dma((3,)),
            dma((4,)),
            dma((4,)),
            dma((4,)),
            dma((4,)),
            dma((5,)),
            dma((2,)),
        ],
        compiler_params=pltpu.CompilerParams(
            collective_id=2, has_side_effects=True, vmem_limit_bytes=BIG
        ),
        cost_estimate=cost(80),
        name="collect",
    )(
        mixed,
        both,
        normed,
        dproj,
        weight,
        x_rows.reshape(split),
        hidden.reshape(split),
        gain.reshape(1, -1),
        small,
    )


def rms_norm(values, gain_vec):
    return values * lax.rsqrt(jnp.mean(values * values, axis=-1, keepdims=True) + EPS) * gain_vec


def turn_tables(seq_count, head_count):
    half_dim = HEAD_SIZE // 2
    freqs = np.float32(THETA) ** (-np.arange(half_dim, dtype=np.float32) * 2.0 / HEAD_SIZE)
    angles = np.arange(seq_count, dtype=np.float32)[:, None] * freqs.astype(np.float32)[None, :]
    cosine, sine = np.cos(angles), np.sin(angles)
    return (
        jnp.asarray(np.tile(np.concatenate([cosine, cosine], axis=1), (1, head_count))),
        jnp.asarray(np.tile(np.concatenate([-sine, sine], axis=1), (1, head_count))),
    )


def swapped(values):
    return lax.ppermute(values, "core", SWAP)


def body(
    layer_in,
    seq_lengths,
    out_grad,
    norm_gain,
    mixer_weight,
    step_weight,
    state_weight,
    query_weight,
    key_value_weight,
    conv_channels,
    conv_states,
    step_bias,
    decay_log,
    skip_scale,
    group_gain,
    mamba_proj,
    attn_proj,
    ffn_gain,
    ffn_weight,
    ffn_down,
):
    core = lax.axis_index("core")
    place = lax.axis_index("tensor")
    first = core == 0
    seq_dev, rows_dev, model_dim = layer_in.shape
    groups = lax.axis_size("tensor")
    seq_total = rows_dev * groups
    half_rows = rows_dev // 2
    share = mixer_weight.shape[0]
    chans_dev = mixer_weight.shape[2]
    heads_dev = step_weight.shape[1]
    query_dev = query_weight.shape[1]
    hidden_dev = ffn_weight.shape[2]
    held = groups // 2
    step_pad = 128

    def mine(values):
        return lax.dynamic_slice_in_dim(values, core * held, held, 0)

    def other(values):
        return lax.dynamic_slice_in_dim(values, (1 - core) * held, held, 0)

    def in_order(own, others, axis):
        return jnp.where(
            first,
            jnp.concatenate([own, others], axis=axis),
            jnp.concatenate([others, own], axis=axis),
        )

    def flat(values):
        return values.transpose(1, 0, 2).reshape(values.shape[1], -1)

    spot = 2 * core + place % 2

    def positions_in(values):
        shaped = values.reshape(seq_dev, 2, half_rows, model_dim)
        keep = lax.dynamic_index_in_dim(shaped, core, 1, False)
        send = lax.dynamic_index_in_dim(shaped, 1 - core, 1, False)
        return lax.all_to_all(in_order(keep, swapped(send), 0), "tensor", 0, 0, tiled=True)

    def both_halves(own):
        both = in_order(own[:, None], swapped(own)[:, None], 1)
        return both.reshape(seq_total, model_dim)

    def positions_out(own):
        four = lax.all_to_all(own, "tensor", 0, 0, tiled=True)
        keep = lax.dynamic_slice_in_dim(four, core * seq_dev, seq_dev, 0)
        send = lax.dynamic_slice_in_dim(four, (1 - core) * seq_dev, seq_dev, 0)
        both = in_order(keep[:, None], swapped(send)[:, None], 1)
        return both.reshape(seq_dev, rows_dev, model_dim)

    def own_half(values):
        shaped = values.reshape(groups, 2, half_rows, -1)
        return lax.dynamic_index_in_dim(shaped, core, 1, False)

    def other_half(values):
        shaped = values.reshape(groups, 2, half_rows, -1)
        return lax.dynamic_index_in_dim(shaped, 1 - core, 1, False)

    out_dev = chans_dev + query_dev
    pack_two = jnp.concatenate([mamba_proj.T, attn_proj.T], axis=1)
    own_units = hidden_dev // 2
    pack_ups = ffn_weight.reshape(share, 2, 2, own_units).transpose(2, 0, 1, 3)
    pack_ups = pack_ups.reshape(2, share, hidden_dev)
    pack_downs = ffn_down.reshape(2, own_units, share).transpose(0, 2, 1)
    out_dev = chans_dev + query_dev
    pack_two = jnp.concatenate([mamba_proj.T, attn_proj.T], axis=1)
    pack_one = jnp.concatenate(
        [
            mixer_weight.reshape(share, 2 * chans_dev),
            query_weight,
            jnp.pad(step_weight, ((0, 0), (0, step_pad - heads_dev))),
        ],
        axis=1,
    )
    kv_heads = key_value_weight.reshape(share, 2, 2, HEAD_SIZE)

    def shared_for(at):
        return jnp.concatenate(
            [
                state_weight.reshape(share, 2 * N),
                lax.dynamic_index_in_dim(kv_heads, at, 2, False).reshape(share, 2 * HEAD_SIZE),
            ],
            axis=1,
        )

    def lanes(values):
        return jnp.pad(values, (0, -values.shape[0] % 128)).reshape(-1, 128)

    small_in = jnp.concatenate(
        [
            lanes(conv_channels.reshape(-1)),
            lanes(jnp.repeat(skip_scale, HEAD_SIZE)),
            lanes(group_gain),
            lanes(step_bias),
            lanes(decay_log),
        ]
    )
    small_in = jnp.pad(small_in, ((0, -small_in.shape[0] % 8), (0, 0)))
    lengths = in_order(seq_lengths, swapped(seq_lengths), 0)
    seq_len = lengths[place]
    len_one = seq_len.reshape(1)
    valid_rows = (jnp.arange(seq_total, dtype=jnp.int32) < seq_len).astype(jnp.float32)[:, None]
    group_cols = 2 * chans_dev + query_dev + step_pad
    cosine, sine = turn_tables(seq_total, 2)
    state_taps = conv_states.reshape(KCONV, 2 * N)
    quad = lax.axis_size("plane") == 4 and groups == 4 and share == 128
    quad = quad and share == half_rows
    if quad:
        shared = jnp.stack([shared_for(0), shared_for(1)])
        (
            weight_one,
            weight_two,
            gate_up_weight,
            down_weight,
            x_low,
            normed,
            proj,
            grad_whole,
            taps,
            bias,
            decay,
            skip,
            gain,
            log_sums,
            both_low,
            state_out,
            states,
            mixed_part,
            mixed_other,
        ) = front(
            pack_one,
            pack_two,
            pack_ups,
            pack_downs,
            shared,
            layer_in,
            small_in,
            out_grad,
            state_taps,
            norm_gain.reshape(1, -1),
            len_one,
            cosine,
            sine,
        )
    else:
        x_low = both_halves(positions_in(layer_in))
        all_one = lax.all_gather(pack_one, "tensor", axis=0)
        own_one = jnp.concatenate([flat(mine(all_one)), shared_for(core)], axis=1)
        their_one = jnp.concatenate([flat(other(all_one)), shared_for(1 - core)], axis=1)
        weight_one = lax.all_gather(
            in_order(own_one, swapped(their_one), 0), "plane", axis=0, tiled=True
        )
        all_two = lax.all_gather(pack_two, "tensor", axis=0)
        weight_two = lax.all_gather(
            in_order(flat(mine(all_two)), swapped(flat(other(all_two))), 0),
            "plane",
            axis=0,
            tiled=True,
        )
        rows_up, rows_down = (
            in_order(
                lax.dynamic_index_in_dim(pack, core, 0, False),
                swapped(lax.dynamic_index_in_dim(pack, 1 - core, 0, False)),
                0,
            )
            for pack in (pack_ups, pack_downs)
        )
        rows_up, rows_down = (
            lax.all_gather(rows, "tensor", axis=1, tiled=True) for rows in (rows_up, rows_down)
        )
        down_weight = lax.all_gather(rows_down, "plane", axis=0, tiled=True)
        params = mine(lax.all_gather(small_in, "tensor", axis=0))
        span = chans_dev // 128

        def spread_lanes(at):
            return params[:, at : at + span].reshape(1, -1)

        taps = jnp.concatenate([spread_lanes(span * tap) for tap in range(KCONV)], axis=0)
        taps = jnp.concatenate([taps, state_taps], axis=1)
        skip, gain = spread_lanes(KCONV * span), spread_lanes((KCONV + 1) * span)
        bias, decay = params[:, (KCONV + 2) * span], params[:, (KCONV + 2) * span + 1]
        normed = low(rms_norm(wide(x_low), norm_gain))
        proj = dot(normed, weight_one)
        attn, log_sums = attention_forward(len_one, proj, cosine, sine, group_cols)
        both_low, state_out, states = mamba_forward(proj, attn, taps, bias, decay, skip, gain)
        gate_up_weight = lax.all_gather(rows_up, "plane", axis=0, tiled=True)
        grad_whole = both_halves(positions_in(out_grad))
        mixed_part = low(dot_nt(both_low, weight_two))
        mixed_other = swapped(mixed_part)

    grad_low = low(valid_rows * wide(grad_whole))
    hidden, normed_two, act_low, gate_up_low = ffn_middle(
        x_low,
        mixed_part,
        mixed_other,
        ffn_gain.reshape(1, -1),
        grad_low,
        gate_up_weight,
        down_weight,
        groups,
    )
    grad_three = ffn_gradients(grad_low, act_low, normed_two, gate_up_low, groups)
    grad_two_part = low(dot_nt(gate_up_low, gate_up_weight))
    ffn_part = low(dot_nt(act_low, down_weight))
    ffn_own = wide(own_half(ffn_part)) + wide(swapped(other_half(ffn_part)))
    out_own = own_half(valid_rows) * (own_half(hidden) + ffn_own)
    layer_out = positions_out(low(out_own))

    grad_hidden, grad_mixed, back, grad_ffn_gain = hidden_backward(
        hidden,
        grad_two_part,
        swapped(grad_two_part),
        grad_low,
        ffn_gain.reshape(1, -1),
        weight_two,
    )
    grad_ffn_gain = grad_ffn_gain.reshape(-1)

    def scatter(values):
        return lax.psum_scatter(values, "plane", scatter_dimension=0, tiled=True)

    def to_groups(values):
        by_part = values.reshape(2, share, held, -1).transpose(0, 2, 1, 3)
        own = lax.dynamic_index_in_dim(by_part, core, 0, False)
        theirs = swapped(lax.dynamic_index_in_dim(by_part, 1 - core, 0, False))
        whole = in_order(own, theirs, 0)
        return wide(lax.psum_scatter(whole, "tensor", scatter_dimension=0, tiled=True)[0])

    units = lax.psum_scatter(scatter(grad_three), "tensor", scatter_dimension=1, tiled=True)
    units = units.reshape(2, share, -1)
    own_part = lax.dynamic_index_in_dim(units, core, 0, True)
    their_part = swapped(lax.dynamic_index_in_dim(units, 1 - core, 0, True))
    units = wide(in_order(own_part, their_part, 0))
    sum_up = units[:, :, :hidden_dev].reshape(2, share, 2, own_units).transpose(1, 2, 0, 3)
    sum_down = units[:, :, hidden_dev:].transpose(0, 2, 1).reshape(hidden_dev, share)

    grad_q, grad_kv = attention_backward(
        len_one, proj, cosine, sine, log_sums, back, group_cols, 3
    )
    proj_grad, grad_taps, grad_gain, grad_skip_cols, grad_bias, grad_decay = mamba_backward(
        proj, state_out, states, back, grad_q, grad_kv, taps, bias, decay, skip, gain
    )
    edge = held * group_cols
    grad_skip = jnp.sum(grad_skip_cols.reshape(held, heads_dev, HEAD_SIZE), axis=-1)
    chan_taps = grad_taps[:, : held * chans_dev].reshape(KCONV, held, chans_dev)
    group_small = jnp.concatenate(
        [
            chan_taps.transpose(1, 0, 2).reshape(held, -1),
            grad_bias[:, :heads_dev],
            grad_decay[:, :heads_dev],
            grad_skip,
            grad_gain.reshape(held, -1),
        ],
        axis=1,
    )
    small_groups = in_order(group_small, jnp.zeros_like(group_small), 0)
    small_out = jnp.concatenate(
        [
            jnp.zeros_like(norm_gain),
            grad_ffn_gain,
            grad_taps[:, held * chans_dev :].reshape(-1),
            small_groups.reshape(-1),
        ]
    )
    if quad:
        small_size = small_out.shape[0]
        small_room = -(-small_size // 1024) * 1024
        (
            sum_mixer,
            sum_query,
            sum_step,
            shared_sum,
            small_sum,
            input_grad,
            sum_mamba,
            sum_attn,
        ) = collect(
            normed,
            proj_grad,
            weight_one,
            grad_mixed,
            both_low,
            x_low,
            grad_hidden,
            norm_gain,
            jnp.pad(small_out, (0, small_room - small_size)).reshape(-1, 128),
            (chans_dev, query_dev, group_cols),
        )
        small_sum = small_sum.reshape(-1)[:small_size]
    else:
        grad_one = low(dot_tn(normed, proj_grad))
        grad_norm_part = low(dot_nt(proj_grad, weight_one))
        grad_norm_own = wide(own_half(grad_norm_part)) + wide(swapped(other_half(grad_norm_part)))
        x_own = wide(own_half(x_low))
        r_one = lax.rsqrt(jnp.mean(x_own * x_own, axis=-1, keepdims=True) + EPS)
        scaled = grad_norm_own * norm_gain
        grad_x = low(
            own_half(grad_hidden)
            + r_one * scaled
            - x_own * (r_one**3 * jnp.mean(x_own * scaled, axis=-1, keepdims=True))
        )
        grad_norm_gain = jnp.sum(x_own * r_one * grad_norm_own, axis=(0, 1))
        small_out = small_out.at[:model_dim].set(grad_norm_gain)
        part_one = scatter(grad_one)
        both_parts = part_one[:, edge:].reshape(2, share, -1)
        own_rest = lax.dynamic_index_in_dim(both_parts, core, 0, False)
        their_rest = swapped(lax.dynamic_index_in_dim(both_parts, 1 - core, 0, False))
        shared_own = wide(own_rest[:, : 2 * N]) + wide(their_rest[:, : 2 * N])
        kv_both = in_order(own_rest[:, 2 * N :], their_rest[:, 2 * N :], 1)
        shared_low = jnp.concatenate([low(shared_own), kv_both], axis=1)
        shared_sum = jnp.sum(wide(lax.all_gather(shared_low, "tensor", axis=0)), axis=0)
        sum_one = to_groups(part_one[:, :edge])
        sum_mixer = sum_one[:, : 2 * chans_dev]
        sum_query = sum_one[:, 2 * chans_dev : 2 * chans_dev + query_dev]
        sum_step = sum_one[:, 2 * chans_dev + query_dev :]
        sum_two = to_groups(scatter(low(dot_tn(grad_mixed, both_low)))).T
        sum_mamba, sum_attn = sum_two[:chans_dev], sum_two[chans_dev:]
        input_grad = positions_out(grad_x)
        small_sum = lax.psum(small_out, ("plane", "core", "tensor"))
    kv_sum = shared_sum[:, 2 * N :].reshape(share, 2, 2, HEAD_SIZE).transpose(0, 2, 1, 3)
    group_sum = lax.dynamic_index_in_dim(
        small_sum[2 * model_dim + KCONV * 2 * N :].reshape(groups, -1), place, 0, False
    )
    pieces = []
    at = 0
    for size in (KCONV * chans_dev, heads_dev, heads_dev, heads_dev, chans_dev):
        pieces.append(group_sum[at : at + size])
        at += size

    return (
        layer_out,
        input_grad,
        small_sum[:model_dim],
        sum_mixer.reshape(share, 2, chans_dev),
        sum_step[:, :heads_dev],
        shared_sum[:, : 2 * N].reshape(share, 2, N),
        sum_query,
        kv_sum.reshape(share, 2, 2 * HEAD_SIZE),
        pieces[0].reshape(KCONV, chans_dev),
        small_sum[2 * model_dim : 2 * model_dim + KCONV * 2 * N].reshape(KCONV, 2, N),
        pieces[1],
        pieces[2],
        pieces[3],
        pieces[4],
        sum_mamba,
        sum_attn,
        small_sum[model_dim : 2 * model_dim],
        sum_up.reshape(share, 2, hidden_dev),
        sum_down,
    )


def solution(mesh):
    rows, columns = mesh.devices.shape
    fine = Mesh(mesh.devices.reshape(rows // 2, 2, columns), ("plane", "core", "tensor"))
    dp = ("plane", "core")
    return jax.shard_map(
        body,
        mesh=fine,
        in_specs=(
            P(dp, "tensor", None),
            P(dp),
            P(dp, "tensor", None),
            P(),
            P(dp, None, "tensor"),
            P(dp, "tensor"),
            P(dp, None, None),
            P(dp, "tensor"),
            P(dp, None, None),
            P(None, "tensor"),
            P(),
            P("tensor"),
            P("tensor"),
            P("tensor"),
            P("tensor"),
            P("tensor", dp),
            P("tensor", dp),
            P(),
            P(dp, None, "tensor"),
            P("tensor", dp),
        ),
        out_specs=(
            P(dp, "tensor", None),
            P(dp, "tensor", None),
            P(),
            P(dp, None, "tensor"),
            P(dp, "tensor"),
            P(dp, None, None),
            P(dp, "tensor"),
            P(dp, None, None),
            P(None, "tensor"),
            P(),
            P("tensor"),
            P("tensor"),
            P("tensor"),
            P("tensor"),
            P("tensor", dp),
            P("tensor", dp),
            P(),
            P(dp, None, "tensor"),
            P("tensor", dp),
        ),
        check_vma=False,
    )
```

```python
import jax
import jax.numpy as jnp
import numpy as np
from jax import lax
from jax.experimental import pallas as pl
from jax.experimental.pallas import tpu as pltpu
from jax.sharding import Mesh
from jax.sharding import PartitionSpec as P

HEAD_SIZE = 64
N = 128
KCONV = 4
GH = 6
EPS = 1e-05
THETA = 10000.0
MASKED = -1e30
SWAP = [(0, 1), (1, 0)]


def low(values):
    return values.astype(jnp.bfloat16)


def wide(values):
    return values.astype(jnp.float32)


def dot(left, right):
    return jnp.dot(left, right, preferred_element_type=jnp.float32)


def dot_nt(left, right):
    return lax.dot_general(
        left, right, (((1,), (1,)), ((), ())), preferred_element_type=jnp.float32
    )


def dot_tn(left, right):
    return lax.dot_general(
        left, right, (((0,), (0,)), ((), ())), preferred_element_type=jnp.float32
    )


def dot_fine(left, right):
    high = low(right)
    rest = right - wide(high)
    mid = low(rest)
    last = low(rest - wide(mid))
    return dot(left, high) + dot(left, mid) + dot(left, last)


def dot_by(left, right):
    high = low(left)
    rest = low(left - wide(high))
    return dot(high, right) + dot(rest, right)


def sigmoid(values):
    return 1.0 / (1.0 + jnp.exp(-values))


def turn(values, cosine, sine):
    lane = lax.broadcasted_iota(jnp.int32, values.shape, 1)
    half = HEAD_SIZE // 2
    up = pltpu.roll(values, 128 - half, 1)
    down = pltpu.roll(values, half, 1)
    return values * cosine + jnp.where(lane % HEAD_SIZE < half, up, down) * sine


def turn_back(values, cosine, sine):
    lane = lax.broadcasted_iota(jnp.int32, values.shape, 1)
    half = HEAD_SIZE // 2
    turned = values * sine
    up = pltpu.roll(turned, 128 - half, 1)
    down = pltpu.roll(turned, half, 1)
    return values * cosine + jnp.where(lane % HEAD_SIZE < half, up, down)


def cost(micros):
    return pl.CostEstimate(flops=int(micros * 1e9), bytes_accessed=0, transcendentals=0)


SCALE = HEAD_SIZE ** (-0.5)
ROWS = 256


def key_value_parts(kv, cosine, sine):
    lane = lax.broadcasted_iota(jnp.int32, kv.shape, 1)
    key = jnp.where(lane < HEAD_SIZE, turn(kv, cosine, sine), 0.0)
    value = jnp.where(lane < HEAD_SIZE, 0.0, kv)
    keys = (low(key), low(pltpu.roll(key, HEAD_SIZE, 1)))
    values = (low(pltpu.roll(value, HEAD_SIZE, 1)), low(value))
    return keys, values


def block_scores(query, keys, begin, seq_len):
    scores = dot_nt(query, keys)
    row = lax.broadcasted_iota(jnp.int32, (scores.shape[0], 1), 0) + begin
    col = lax.broadcasted_iota(jnp.int32, scores.shape, 1)
    return jnp.where(col < jnp.minimum(row + 1, seq_len), scores, MASKED)


def attention_forward_kernel(len_ref, q_ref, kv_ref, cos_ref, sin_ref, out_ref, sum_ref):
    seq_len = len_ref[0]
    cosine, sine = cos_ref[...], sin_ref[...]
    keys, values = key_value_parts(kv_ref[...], cosine, sine)
    query = low(turn(q_ref[...], cosine, sine) * SCALE)
    rows = query.shape[0]
    lane = lax.broadcasted_iota(jnp.int32, (ROWS, 128), 1)
    for begin in range(0, rows, ROWS):
        end = begin + ROWS
        outs, sums = [], []
        for head in range(2):
            scores = block_scores(query[begin:end], keys[head][:end], begin, seq_len)
            peak = jnp.max(scores, axis=1, keepdims=True)
            exps = jnp.exp(scores - peak)
            total = jnp.sum(exps, axis=1, keepdims=True)
            probs = low(exps * (1.0 / total))
            outs.append(dot(probs, values[head][:end]))
            sums.append(peak + jnp.log(total))
        out_ref[begin:end, :] = low(outs[0] + outs[1])
        sum_ref[begin:end, :] = jnp.where(lane < HEAD_SIZE, sums[0], sums[1])


def attention_backward_kernel(
    len_ref, q_ref, kv_ref, cos_ref, sin_ref, sum_ref, grad_ref, dq_ref, dkv_ref, dk_acc, dv_acc
):
    seq_len = len_ref[0]
    cosine, sine = cos_ref[...], sin_ref[...]
    keys, values = key_value_parts(kv_ref[...], cosine, sine)
    query = low(turn(q_ref[...], cosine, sine) * SCALE)
    query_t = query.T
    rows = query.shape[0]
    group = pl.program_id(0)
    grad = low(grad_ref[...])
    grad_t = grad.T

    @pl.when(group == 0)
    def _():
        dk_acc[...] = jnp.zeros_like(dk_acc)
        dv_acc[...] = jnp.zeros_like(dv_acc)

    for begin in range(0, rows, ROWS):
        end = begin + ROWS
        dq = jnp.zeros((ROWS, 128), jnp.float32)
        for head in range(2):
            lanes = slice(head * HEAD_SIZE, (head + 1) * HEAD_SIZE)
            scores = block_scores(query[begin:end], keys[head][:end], begin, seq_len)
            at = head * HEAD_SIZE
            probs = jnp.exp(scores - sum_ref[begin:end, at : at + 1])
            dv_acc[:, :end] += dot(grad_t[lanes, begin:end], low(probs))
            dp = dot_nt(grad[begin:end], values[head][:end])
            inner = jnp.sum(probs * dp, axis=1, keepdims=True)
            ds = low(probs * (dp - inner))
            dq = dq + dot(ds, keys[head][:end])
            dk_acc[:, :end] += dot(query_t[lanes, begin:end], ds)
        dq = turn_back(dq * SCALE, cosine[begin:end], sine[begin:end])
        dq_ref[begin:end, :] = low(dq)

    @pl.when(group == pl.num_programs(0) - 1)
    def _():
        both = jnp.concatenate([dk_acc[...], dv_acc[...]], axis=0).T
        lane = lax.broadcasted_iota(jnp.int32, both.shape, 1)
        dkv_ref[...] = low(jnp.where(lane < HEAD_SIZE, turn_back(both, cosine, sine), both))


def attention_specs(rows, group_cols):
    whole = pl.BlockSpec((rows, 128), lambda g: (0, 0))
    return [
        pl.BlockSpec(memory_space=pltpu.SMEM),
        pl.BlockSpec((rows, 128), lambda g: (0, g * (group_cols // 128) + 6)),
        pl.BlockSpec((rows, 128), lambda g: (0, 2 * (group_cols // 128) + 2)),
        whole,
        whole,
    ]


BIG = 60 * 1024 * 1024


def attention_forward(seq_len, proj, cosine, sine, group_cols):
    rows = proj.shape[0]
    pairs = pl.BlockSpec((rows, 128), lambda g: (0, g))
    return pl.pallas_call(
        attention_forward_kernel,
        grid=(2,),
        in_specs=attention_specs(rows, group_cols),
        out_specs=[pairs, pairs],
        out_shape=[
            jax.ShapeDtypeStruct((rows, 256), jnp.bfloat16),
            jax.ShapeDtypeStruct((rows, 256), jnp.float32),
        ],
        compiler_params=pltpu.CompilerParams(vmem_limit_bytes=BIG),
        cost_estimate=cost(11),
        name="attention_forward",
    )(seq_len, proj, proj, cosine, sine)


def attention_backward(seq_len, proj, cosine, sine, sums, grad, group_cols, grad_at):
    rows = proj.shape[0]
    pairs = pl.BlockSpec((rows, 128), lambda g: (0, g))
    return pl.pallas_call(
        attention_backward_kernel,
        grid=(2,),
        in_specs=attention_specs(rows, group_cols)
        + [pairs, pl.BlockSpec((rows, 128), lambda g: (0, 4 * g + grad_at))],
        out_specs=[pairs, pl.BlockSpec((rows, 128), lambda g: (0, 0))],
        out_shape=[
            jax.ShapeDtypeStruct((rows, 256), jnp.bfloat16),
            jax.ShapeDtypeStruct((rows, 128), jnp.bfloat16),
        ],
        scratch_shapes=[
            pltpu.VMEM((HEAD_SIZE, rows), jnp.float32),
            pltpu.VMEM((HEAD_SIZE, rows), jnp.float32),
        ],
        compiler_params=pltpu.CompilerParams(vmem_limit_bytes=BIG),
        cost_estimate=cost(18),
        name="attention_backward",
    )(seq_len, proj, proj, cosine, sine, sums, grad)


CHUNK = 128
GROUP = GH * HEAD_SIZE
PAIRS = GH // 2
CONV = 2 * GROUP + 2 * N
SHARED = 2048


def triangle():
    row = lax.broadcasted_iota(jnp.int32, (CHUNK, CHUNK), 0)
    col = lax.broadcasted_iota(jnp.int32, (CHUNK, CHUNK), 1)
    return col <= row


def pair_lanes(values, pair):
    lane = lax.broadcasted_iota(jnp.int32, (values.shape[0], 128), 1)
    at = 2 * pair
    return jnp.where(lane < HEAD_SIZE, values[:, at : at + 1], values[:, at + 1 : at + 2])


def split_pair(values):
    lane = lax.broadcasted_iota(jnp.int32, values.shape, 1)
    empty = jnp.zeros_like(values)
    return jnp.concatenate(
        [jnp.where(lane < HEAD_SIZE, values, empty), jnp.where(lane < HEAD_SIZE, empty, values)],
        axis=0,
    )


def conv_pre(buf_ref, taps_ref, begin, size):
    total = buf_ref[5 : 5 + CHUNK, begin : begin + size] * taps_ref[0:1, begin : begin + size]
    for tap in range(1, KCONV):
        total = total + (
            buf_ref[5 + tap : 5 + tap + CHUNK, begin : begin + size]
            * taps_ref[tap : tap + 1, begin : begin + size]
        )
    return total


def load_conv(buf_ref, proj_ref):
    for group in range(2):
        at = group * 1024 + GROUP
        buf_ref[8:, group * GROUP : (group + 1) * GROUP] = proj_ref[:, at : at + GROUP]
    buf_ref[8:, 2 * GROUP :] = proj_ref[:, SHARED : SHARED + 2 * N]


def group_steps(proj_ref, bias_ref, decay_ref, group, lower):
    at = group * 1024 + 896
    raw = proj_ref[:, at : at + 128] + bias_ref[group : group + 1, :]
    step = jnp.log1p(jnp.exp(-jnp.abs(raw))) + jnp.maximum(raw, 0.0)
    rate = -jnp.exp(decay_ref[group : group + 1, :])
    cumul = dot_fine(lower, rate * step)
    return raw, step, rate, cumul


def head_decay(cumul, cumul_t, head, mask):
    spread = cumul[:, head : head + 1] - cumul_t[head : head + 1, :]
    return jnp.exp(jnp.where(mask, spread, MASKED))


def mamba_chunk(
    proj_ref,
    attn_ref,
    taps_ref,
    bias_ref,
    decay_ref,
    skip_ref,
    gain_ref,
    both_ref,
    out_ref,
    state_out,
    buf_ref,
    state_ref,
):
    load_conv(buf_ref, proj_ref)
    mask = triangle()
    lower = mask.astype(jnp.bfloat16)
    pre = conv_pre(buf_ref, taps_ref, 2 * GROUP, 2 * N)
    state_act = low(pre * sigmoid(pre))
    b_rows, c_rows = state_act[:, :N], state_act[:, N:]
    gram = dot_nt(c_rows, b_rows)
    b_cols = b_rows.T
    for group in range(2):
        cols = slice(group * GROUP, (group + 1) * GROUP)
        _, step, _, cumul = group_steps(proj_ref, bias_ref, decay_ref, group, lower)
        cumul_t = cumul.T
        last = cumul[CHUNK - 1 : CHUNK, :]
        state = state_ref[:, cols]
        state_out[:, cols] = state
        from_state = dot(c_rows, low(state))
        gated, lasts, x_ends = [], [], []
        for pair in range(PAIRS):
            at = group * GROUP + pair * 128
            pre = conv_pre(buf_ref, taps_ref, at, 128)
            chan = pre * sigmoid(pre)
            inputs = low(chan * pair_lanes(step, pair))
            mixing = jnp.concatenate(
                [
                    low(gram * head_decay(cumul, cumul_t, 2 * pair + side, mask))
                    for side in range(2)
                ],
                axis=1,
            )
            lanes = slice(pair * 128, (pair + 1) * 128)
            inner = pair_lanes(cumul, pair)
            out = dot(mixing, split_pair(inputs)) + jnp.exp(inner) * from_state[:, lanes]
            out_ref[:, at : at + 128] = out
            last_lanes = pair_lanes(last, pair)
            lasts.append(last_lanes)
            x_ends.append(low(jnp.exp(last_lanes - inner) * wide(inputs)))
            gate = proj_ref[:, group * 1024 + pair * 128 : group * 1024 + pair * 128 + 128]
            skipped = out + chan * skip_ref[:, at : at + 128]
            gated.append(skipped * (gate * sigmoid(gate)))
        state_ref[:, cols] = jnp.exp(jnp.concatenate(lasts, axis=1)) * state + dot(
            b_cols, jnp.concatenate(x_ends, axis=1)
        )
        square = jnp.sum(sum(part * part for part in gated), axis=1, keepdims=True)
        scale = lax.rsqrt(square * (1.0 / GROUP) + EPS)
        for pair in range(PAIRS):
            at = group * GROUP + pair * 128
            to = group * 512 + pair * 128
            both_ref[:, to : to + 128] = low(gated[pair] * scale * gain_ref[:, at : at + 128])
        to = group * 512 + GROUP
        both_ref[:, to : to + 128] = attn_ref[:, group * 128 : (group + 1) * 128]
    buf_ref[0:8, :] = buf_ref[CHUNK : CHUNK + 8, :]


def mamba_start(buf_ref, state_ref):
    buf_ref[0:8, :] = jnp.zeros((8, CONV), jnp.float32)
    state_ref[...] = jnp.zeros_like(state_ref)


def mamba_forward_kernel(*refs):
    @pl.when(pl.program_id(0) == 0)
    def _():
        mamba_start(*refs[-2:])

    mamba_chunk(*refs[:9], refs[9].at[0], *refs[10:])


def mamba_forward(proj, attn, taps, bias, decay, skip, gain):
    rows, columns = proj.shape
    chunks = rows // CHUNK

    def whole(value):
        return pl.BlockSpec(value.shape, lambda k: (0, 0))

    return pl.pallas_call(
        mamba_forward_kernel,
        grid=(chunks,),
        in_specs=[
            pl.BlockSpec((CHUNK, columns), lambda k: (k, 0)),
            pl.BlockSpec((CHUNK, 256), lambda k: (k, 0)),
        ]
        + [whole(value) for value in (taps, bias, decay, skip, gain)],
        out_specs=[
            pl.BlockSpec((CHUNK, 1024), lambda k: (k, 0)),
            pl.BlockSpec((CHUNK, 2 * GROUP), lambda k: (k, 0)),
            pl.BlockSpec((1, N, 2 * GROUP), lambda k: (k, 0, 0)),
        ],
        out_shape=[
            jax.ShapeDtypeStruct((rows, 1024), jnp.bfloat16),
            jax.ShapeDtypeStruct((rows, 2 * GROUP), jnp.float32),
            jax.ShapeDtypeStruct((chunks, N, 2 * GROUP), jnp.float32),
        ],
        scratch_shapes=[
            pltpu.VMEM((CHUNK + 8, CONV), jnp.float32),
            pltpu.VMEM((N, 2 * GROUP), jnp.float32),
        ],
        compiler_params=pltpu.CompilerParams(vmem_limit_bytes=BIG),
        cost_estimate=cost(14),
        name="mamba_forward",
    )(proj, attn, taps, bias, decay, skip, gain)


def silu_slope(values, sig):
    return sig * (1.0 + values * (1.0 - sig))


def mamba_backward_kernel(
    proj_ref,
    before_ref,
    out_ref,
    states_ref,
    back_ref,
    dq_ref,
    dkv_ref,
    taps_ref,
    bias_ref,
    decay_ref,
    skip_ref,
    gain_ref,
    dproj_ref,
    dtaps_ref,
    dgain_ref,
    dskip_ref,
    dbias_ref,
    ddecay_ref,
    buf_ref,
    grad_buf,
    after_ref,
    flow_ref,
):
    step_at = pl.program_id(0)

    @pl.when(step_at == 0)
    def _():
        for ref in (dtaps_ref, dgain_ref, dskip_ref, dbias_ref, ddecay_ref, after_ref, flow_ref):
            ref[...] = jnp.zeros_like(ref)
        grad_buf[CHUNK:, :] = jnp.zeros((8, CONV), jnp.float32)

    inside = jnp.where(step_at == pl.num_programs(0) - 1, 0.0, 1.0)
    for group in range(2):
        at = group * 1024 + GROUP
        buf_ref[0:8, group * GROUP : (group + 1) * GROUP] = before_ref[:, at : at + GROUP] * inside
    buf_ref[0:8, 2 * GROUP :] = before_ref[:, SHARED : SHARED + 2 * N] * inside
    load_conv(buf_ref, proj_ref)
    mask = triangle()
    lower = mask.astype(jnp.bfloat16)
    row = lax.broadcasted_iota(jnp.int32, (CHUNK, CHUNK), 0)
    col = lax.broadcasted_iota(jnp.int32, (CHUNK, CHUNK), 1)
    upper = (row <= col).astype(jnp.bfloat16)
    pre_state = conv_pre(buf_ref, taps_ref, 2 * GROUP, 2 * N)
    sig_state = sigmoid(pre_state)
    state_act = low(pre_state * sig_state)
    b_rows, c_rows = state_act[:, :N], state_act[:, N:]
    gram = dot_nt(c_rows, b_rows)
    c_cols = c_rows.T
    head_of_row = lax.broadcasted_iota(jnp.int32, (GROUP, 128), 0) // HEAD_SIZE
    head_lane = lax.broadcasted_iota(jnp.int32, (GROUP, 128), 1)
    pick = (head_of_row == head_lane).astype(jnp.bfloat16)
    dgram = jnp.zeros((CHUNK, CHUNK), jnp.float32)
    d_c = jnp.zeros((CHUNK, N), jnp.float32)
    d_b = jnp.zeros((CHUNK, N), jnp.float32)
    for group in range(2):
        raw, step, rate, cumul = group_steps(proj_ref, bias_ref, decay_ref, group, lower)
        cumul_t = cumul.T
        last = cumul[CHUNK - 1 : CHUNK, :]
        pres, sigs, chans, gates, gate_sigs, skips, gated = [], [], [], [], [], [], []
        for pair in range(PAIRS):
            at = group * GROUP + pair * 128
            pre = conv_pre(buf_ref, taps_ref, at, 128)
            sig = sigmoid(pre)
            chan = pre * sig
            gate = proj_ref[:, group * 1024 + pair * 128 : group * 1024 + pair * 128 + 128]
            gate_sig = sigmoid(gate)
            skipped = out_ref[:, at : at + 128] + chan * skip_ref[:, at : at + 128]
            pres.append(pre)
            sigs.append(sig)
            chans.append(chan)
            gates.append(gate)
            gate_sigs.append(gate_sig)
            skips.append(skipped)
            gated.append(skipped * (gate * gate_sig))
        square = jnp.sum(sum(part * part for part in gated), axis=1, keepdims=True)
        scale = lax.rsqrt(square * (1.0 / GROUP) + EPS)
        grads = []
        cross = jnp.zeros((CHUNK, 128), jnp.float32)
        for pair in range(PAIRS):
            at = group * GROUP + pair * 128
            grad = back_ref[:, group * 512 + pair * 128 : group * 512 + pair * 128 + 128]
            dgain_ref[:, at : at + 128] += jnp.sum(grad * gated[pair] * scale, axis=0, keepdims=True)
            grad = grad * gain_ref[:, at : at + 128]
            cross = cross + gated[pair] * grad
            grads.append(grad)
        cross = jnp.sum(cross, axis=1, keepdims=True) * (1.0 / GROUP) * scale * scale * scale
        cols = slice(group * GROUP, (group + 1) * GROUP)
        lane = lax.broadcasted_iota(jnp.int32, (CHUNK, 128), 1)
        after = after_ref[:, cols]
        after_low = low(after)
        state = states_ref[0, :, cols]
        from_after = dot(b_rows, after_low)
        x_ends, g_starts, lasts, flows, dsteps = [], [], [], [], []
        for pair in range(PAIRS):
            at = group * GROUP + pair * 128
            lanes = slice(pair * 128, (pair + 1) * 128)
            chan = chans[pair]
            grad = scale * grads[pair] - gated[pair] * cross
            gate, gate_sig = gates[pair], gate_sigs[pair]
            dgate = grad * skips[pair] * silu_slope(gate, gate_sig)
            to = group * 1024 + pair * 128
            dproj_ref[:, to : to + 128] = low(dgate)
            grad = grad * (gate * gate_sig)
            dskip_ref[:, at : at + 128] += jnp.sum(grad * chan, axis=0, keepdims=True)
            dchan = grad * skip_ref[:, at : at + 128]
            dout = low(grad)
            step_lanes = pair_lanes(step, pair)
            inputs = low(chan * step_lanes)
            halves = split_pair(inputs)
            decays = [head_decay(cumul, cumul_t, 2 * pair + side, mask) for side in range(2)]
            mixing = jnp.concatenate([low(gram * decay) for decay in decays], axis=1)
            dmix = dot_nt(dout, halves)
            dgram = dgram + dmix[:, :CHUNK] * decays[0] + dmix[:, CHUNK:] * decays[1]
            dinputs = dot_tn(mixing, dout)
            dinputs = jnp.where(lane < HEAD_SIZE, dinputs[:CHUNK], dinputs[CHUNK:])
            inner = pair_lanes(cumul, pair)
            last_lanes = pair_lanes(last, pair)
            to_end = jnp.exp(last_lanes - inner)
            dinputs = dinputs + to_end * from_after[:, lanes]
            x_ends.append(low(to_end * wide(inputs)))
            g_starts.append(low(jnp.exp(inner) * wide(dout)))
            lasts.append(last_lanes)
            flows.append(wide(dout) * out_ref[:, at : at + 128] - wide(inputs) * dinputs)
            dsteps.append(dinputs * chan)
            dchan = dchan + dinputs * step_lanes
            grad_buf[0:CHUNK, at : at + 128] = dchan * silu_slope(pres[pair], sigs[pair])
        g_start = jnp.concatenate(g_starts, axis=1)
        d_c = d_c + dot_nt(g_start, low(state))
        d_b = d_b + dot_nt(jnp.concatenate(x_ends, axis=1), after_low)
        after = jnp.exp(jnp.concatenate(lasts, axis=1)) * after + dot(c_cols, g_start)
        after_ref[:, cols] = after
        through = jnp.sum(after * state, axis=0, keepdims=True)
        stacked = jnp.concatenate(
            [
                jnp.concatenate(flows, axis=1),
                jnp.concatenate(dsteps, axis=1),
                jnp.broadcast_to(through, (8, GROUP)),
            ],
            axis=0,
        )
        picked = dot_by(stacked, pick)
        flow, dstep = picked[:CHUNK], picked[CHUNK : 2 * CHUNK]
        flow_end = flow_ref[group : group + 1, :]
        flow_next = picked[2 * CHUNK : 2 * CHUNK + 1]
        dcumul = dot_fine(upper, flow) + flow_end
        flow_ref[group : group + 1, :] = flow_next
        dstep = dstep + rate * dcumul
        ddecay_ref[group : group + 1, :] += jnp.sum(rate * step * dcumul, axis=0, keepdims=True)
        draw = dstep * sigmoid(raw)
        dbias_ref[group : group + 1, :] += jnp.sum(draw, axis=0, keepdims=True)
        to = group * 1024 + 896
        lane = lax.broadcasted_iota(jnp.int32, (CHUNK, 128), 1)
        dproj_ref[:, to : to + 128] = low(jnp.where(lane < GH, draw, 0.0))
        to = group * 1024 + 2 * GROUP
        dproj_ref[:, to : to + 128] = dq_ref[:, group * 128 : (group + 1) * 128]
    dgram_low = low(dgram)
    d_c = d_c + dot(dgram_low, b_rows)
    d_b = d_b + dot_tn(dgram_low, c_rows)
    slope = silu_slope(pre_state, sig_state)
    grad_buf[0:CHUNK, 2 * GROUP : 2 * GROUP + N] = d_b * slope[:, :N]
    grad_buf[0:CHUNK, 2 * GROUP + N :] = d_c * slope[:, N:]
    for at in range(0, CONV, 128):
        grad = jnp.zeros((CHUNK, 128), jnp.float32)
        here = grad_buf[0:CHUNK, at : at + 128]
        for tap in range(KCONV):
            shift = KCONV - 1 - tap
            grad = grad + (
                grad_buf[shift : shift + CHUNK, at : at + 128] * taps_ref[tap : tap + 1, at : at + 128]
            )
            dtaps_ref[tap : tap + 1, at : at + 128] += jnp.sum(
                here * buf_ref[5 + tap : 5 + tap + CHUNK, at : at + 128], axis=0, keepdims=True
            )
        if at < 2 * GROUP:
            to = (at // GROUP) * 1024 + GROUP + at % GROUP
        else:
            to = SHARED + at - 2 * GROUP
        dproj_ref[:, to : to + 128] = low(grad)
    dproj_ref[:, SHARED + 2 * N :] = dkv_ref[...]
    grad_buf[CHUNK:, :] = grad_buf[0:8, :]


def mamba_backward(proj, out, states, back, dq, dkv, taps, bias, decay, skip, gain):
    rows, columns = proj.shape
    chunks = rows // CHUNK

    def whole(value):
        return pl.BlockSpec(value.shape, lambda k: (0, 0))

    def rows_of(width):
        return pl.BlockSpec((CHUNK, width), lambda k: (chunks - 1 - k, 0))

    params = (taps, bias, decay, skip, gain)
    return pl.pallas_call(
        mamba_backward_kernel,
        grid=(chunks,),
        in_specs=[
            rows_of(columns),
            pl.BlockSpec(
                (8, columns),
                lambda k: (jnp.maximum((chunks - 1 - k) * (CHUNK // 8) - 1, 0), 0),
            ),
            rows_of(2 * GROUP),
            pl.BlockSpec((1, N, 2 * GROUP), lambda k: (chunks - 1 - k, 0, 0)),
            rows_of(1024),
            rows_of(256),
            rows_of(128),
        ]
        + [whole(value) for value in params],
        out_specs=[rows_of(columns)]
        + [whole(value) for value in (taps, gain, skip, bias, decay)],
        out_shape=[jax.ShapeDtypeStruct((rows, columns), jnp.bfloat16)]
        + [
            jax.ShapeDtypeStruct(value.shape, jnp.float32)
            for value in (taps, gain, skip, bias, decay)
        ],
        scratch_shapes=[
            pltpu.VMEM((CHUNK + 8, CONV), jnp.float32),
            pltpu.VMEM((CHUNK + 8, CONV), jnp.float32),
            pltpu.VMEM((N, 2 * GROUP), jnp.float32),
            pltpu.VMEM((8, 128), jnp.float32),
        ],
        compiler_params=pltpu.CompilerParams(vmem_limit_bytes=BIG),
        cost_estimate=cost(36),
        name="mamba_backward",
    )(proj, proj, out, states, back, dq, dkv, *params)


def ffn_kernel(
    len_ref,
    x_ref,
    own_ref,
    their_ref,
    gain_ref,
    raw_ref,
    up_ref,
    down_ref,
    grad_ref,
    hidden_ref,
    normed_ref,
    act_ref,
    dgate_ref,
):
    units = down_ref.shape[1]
    rows = x_ref.shape[0]

    @pl.when(pl.program_id(0) == 0)
    def _():
        @pl.loop(0, rows // 128)
        def _(at):
            here = pl.ds(pl.multiple_of(at * 128, 128), 128)
            hidden = wide(x_ref[here, :]) + (wide(own_ref[here, :]) + wide(their_ref[here, :]))
            hidden_ref[here, :] = hidden
            size = 1.0 / hidden.shape[1]
            root = lax.rsqrt(jnp.sum(hidden * hidden, axis=1, keepdims=True) * size + EPS)
            normed_ref[here, :] = low(hidden * root * gain_ref[...])
            row = lax.broadcasted_iota(jnp.int32, (128, 1), 0) + at * 128
            grad = wide(raw_ref[here, :])
            grad_ref[here, :] = low(jnp.where(row < len_ref[0], grad, 0.0))

    @pl.loop(0, rows // 512)
    def _(at):
        here = pl.ds(pl.multiple_of(at * 512, 512), 512)
        gate_up = dot(normed_ref[here, :], up_ref[...])
        gate, up = gate_up[:, :units], gate_up[:, units:]
        sig = sigmoid(gate)
        act = gate * sig
        act_ref[here, :] = low(act * up)
        grad = dot(grad_ref[here, :], down_ref[...])
        dgate_ref[here, :units] = low(grad * up * silu_slope(gate, sig))
        dgate_ref[here, units:] = low(grad * act)


def ffn_middle(seq_len, x_rows, own, theirs, gain, grad, up_weight, down_weight, blocks):
    rows, model = x_rows.shape
    units = down_weight.shape[1] // blocks

    def whole(value):
        return pl.BlockSpec(value.shape, lambda z: (0, 0))

    full = pl.BlockSpec((rows, model), lambda z: (0, 0))
    return pl.pallas_call(
        ffn_kernel,
        grid=(blocks,),
        in_specs=[pl.BlockSpec(memory_space=pltpu.SMEM)]
        + [whole(value) for value in (x_rows, own, theirs, gain, grad)]
        + [
            pl.BlockSpec((model, 2 * units), lambda z: (0, z)),
            pl.BlockSpec((model, units), lambda z: (0, z)),
        ],
        out_specs=[
            full,
            full,
            full,
            pl.BlockSpec((rows, units), lambda z: (0, z)),
            pl.BlockSpec((rows, 2 * units), lambda z: (0, z)),
        ],
        out_shape=[
            jax.ShapeDtypeStruct((rows, model), jnp.bfloat16),
            jax.ShapeDtypeStruct((rows, model), jnp.float32),
            jax.ShapeDtypeStruct((rows, model), jnp.bfloat16),
            jax.ShapeDtypeStruct((rows, blocks * units), jnp.bfloat16),
            jax.ShapeDtypeStruct((rows, 2 * blocks * units), jnp.bfloat16),
        ],
        compiler_params=pltpu.CompilerParams(vmem_limit_bytes=BIG),
        cost_estimate=cost(14),
        name="ffn_middle",
    )(seq_len, x_rows, own, theirs, gain, grad, up_weight, down_weight)


def hidden_kernel(
    hidden_ref, own_ref, their_ref, grad_ref, gain_ref, weight_ref, dhidden_ref, mixed_ref, back_ref, dgain_ref
):
    @pl.when(pl.program_id(0) == 0)
    def _():
        dgain_ref[...] = jnp.zeros_like(dgain_ref)

    hidden = hidden_ref[...]
    grad = wide(own_ref[...]) + wide(their_ref[...])
    size = 1.0 / hidden.shape[1]
    root = lax.rsqrt(jnp.sum(hidden * hidden, axis=1, keepdims=True) * size + EPS)
    scaled = grad * gain_ref[...]
    inner = jnp.sum(hidden * scaled, axis=1, keepdims=True) * size
    dhidden = wide(grad_ref[...]) + root * scaled - hidden * (root * root * root * inner)
    dhidden_ref[...] = dhidden
    dgain_ref[...] += 0.5 * jnp.sum(hidden * root * grad, axis=0, keepdims=True)
    mixed = low(dhidden)
    mixed_ref[...] = mixed
    back_ref[...] = dot(mixed, weight_ref[...])


def hidden_backward(hidden, own, theirs, grad, gain, weight):
    rows, model = hidden.shape

    def whole(value):
        return pl.BlockSpec(value.shape, lambda k: (0, 0))

    part = pl.BlockSpec((256, model), lambda k: (k, 0))
    return pl.pallas_call(
        hidden_kernel,
        grid=(rows // 256,),
        in_specs=[part] * 4 + [whole(gain), whole(weight)],
        out_specs=[part, part, pl.BlockSpec((256, weight.shape[1]), lambda k: (k, 0)), whole(gain)],
        out_shape=[
            jax.ShapeDtypeStruct((rows, model), jnp.float32),
            jax.ShapeDtypeStruct((rows, model), jnp.bfloat16),
            jax.ShapeDtypeStruct((rows, weight.shape[1]), jnp.float32),
            jax.ShapeDtypeStruct(gain.shape, jnp.float32),
        ],
        compiler_params=pltpu.CompilerParams(vmem_limit_bytes=BIG),
        cost_estimate=cost(7),
        name="hidden_backward",
    )(hidden, own, theirs, grad, gain, weight)


def ffn_grad_kernel(grad_ref, act_ref, normed_ref, dgate_ref, out_ref):
    cut = dgate_ref.shape[1]
    out_ref[:, :cut] = low(dot_tn(normed_ref[...], dgate_ref[...]))
    out_ref[:, cut:] = low(dot_tn(grad_ref[...], act_ref[...]))


def ffn_gradients(grad, act, normed, dgate, blocks):
    rows, model = grad.shape
    units = act.shape[1] // blocks
    whole = pl.BlockSpec((rows, model), lambda z: (0, 0))
    return pl.pallas_call(
        ffn_grad_kernel,
        grid=(blocks,),
        in_specs=[
            whole,
            pl.BlockSpec((rows, units), lambda z: (0, z)),
            whole,
            pl.BlockSpec((rows, 2 * units), lambda z: (0, z)),
        ],
        out_specs=pl.BlockSpec((model, 3 * units), lambda z: (0, z)),
        out_shape=jax.ShapeDtypeStruct((model, 3 * blocks * units), jnp.bfloat16),
        compiler_params=pltpu.CompilerParams(vmem_limit_bytes=BIG),
        cost_estimate=cost(12),
        name="ffn_gradients",
    )(grad, act, normed, dgate)


MESH = pl.DeviceIdType.MESH


def landed(ref, sem):
    pltpu.make_async_copy(ref, ref, sem).wait()


def front_kernel(*refs):
    (pack_ref, next_ref, ups_ref, downs_ref, shared_ref, x_ref, small_ref, og_ref) = refs[:8]
    (state_taps, gain_in, len_ref, cos_ref, sin_ref) = refs[8:13]
    (w_hbm, v_hbm, u_ref, d_ref, x_hbm, normed_hbm, proj_hbm, og_full) = refs[13:21]
    (taps_ref, bias_ref, decay_ref, skip_ref, gain_ref) = refs[21:26]
    (sums_ref, both_ref, out_ref, states_ref, mixed_ref, other_ref) = refs[26:32]
    (w_ref, v_ref, full_ref, normed_ref, proj_ref, attn_ref, params_ref) = refs[32:39]
    (buf_ref, state_ref) = refs[39:41]
    (near_sem, out_sem, part_sem, fromx_sem, fromy_sem, overx_sem, overy_sem) = refs[41:48]
    (tox_sem, toy_sem, relx_sem, rely_sem, row_sem, row_out, pair_sem, pair_out) = refs[48:56]
    (param_sem, param_out, ffn_out, store_sem, mixed_sem) = refs[56:]
    plane = lax.axis_index("plane")
    core = lax.axis_index("core")
    place = lax.axis_index("tensor")
    xside = plane + 1 - 2 * (plane % 2)
    yside = plane + 2 - 4 * (plane // 2)
    across = xside + 2 - 4 * (xside // 2)
    target = place // 2
    column = place % 2
    share, width = pack_ref.shape
    narrow = next_ref.shape[1]
    rest = shared_ref.shape[2]
    half = share
    rows_dev = x_ref.shape[1]

    barrier = pltpu.get_barrier_semaphore()
    for step in range(4):
        for side in range(2):
            if step or side:
                pl.semaphore_signal(
                    barrier,
                    inc=1,
                    device_id={"core": (core + side) % 2, "tensor": (place + step) % 4},
                    device_id_type=MESH,
                )
    for neighbour in (xside, yside):
        pl.semaphore_signal(
            barrier, inc=1, device_id={"plane": neighbour}, device_id_type=MESH
        )
    pl.semaphore_wait(barrier, 9)

    def block(at, part):
        return pl.ds(pl.multiple_of(at * 2 * share + part * share, share), share)

    def piece(at, part, col):
        return w_ref.at[block(at, part), pl.ds(pl.multiple_of(col * width, width), width)]

    def next_piece(at, part, col):
        return v_ref.at[block(at, part), pl.ds(pl.multiple_of(col * narrow, narrow), narrow)]

    def rest_piece(at, part):
        return w_ref.at[block(at, part), pl.ds(2 * width, rest)]

    started = []

    def send(src, dst, send_sem, recv_sem, device):
        copy = pltpu.make_async_remote_copy(
            src_ref=src,
            dst_ref=dst,
            send_sem=send_sem,
            recv_sem=recv_sem,
            device_id=device,
            device_id_type=MESH,
        )
        copy.start()
        started.append((src, send_sem))

    mine = piece(plane, core, column)
    slot = core * 2 + column
    mine_next = next_piece(plane, core, column)

    def send_parts(src, dst, at, recv_sem):
        for step in (2, 1, 3):
            send(
                src,
                dst,
                out_sem.at[at + step],
                recv_sem,
                {"core": target, "tensor": (place + step) % 4},
            )

    send_parts(pack_ref, mine, 0, part_sem.at[slot])

    params = params_ref.at[column]

    @pl.when(target == core)
    def _():
        pltpu.make_async_copy(pack_ref, mine, part_sem.at[slot]).start()
        pltpu.make_async_copy(next_ref, mine_next, part_sem.at[6 + slot]).start()
        pltpu.make_async_copy(small_ref, params, param_sem.at[column]).start()
        for step in range(1, 4):
            pltpu.make_async_remote_copy(
                src_ref=small_ref,
                dst_ref=params,
                send_sem=param_out.at[step],
                recv_sem=param_sem.at[column],
                device_id={"tensor": (place + step) % 4},
                device_id_type=MESH,
            ).start()

    @pl.when(target != core)
    def _():
        pltpu.make_async_remote_copy(
            src_ref=pack_ref,
            dst_ref=mine,
            send_sem=out_sem.at[0],
            recv_sem=part_sem.at[slot],
            device_id={"core": 1 - core},
            device_id_type=MESH,
        ).start()
        pltpu.make_async_remote_copy(
            src_ref=next_ref,
            dst_ref=mine_next,
            send_sem=out_sem.at[4],
            recv_sem=part_sem.at[6 + slot],
            device_id={"core": 1 - core},
            device_id_type=MESH,
        ).start()

    own_rest = rest_piece(plane, core)
    near = pltpu.make_async_copy(shared_ref.at[core], own_rest, part_sem.at[4 + core])
    near.start()
    send(
        shared_ref.at[1 - core],
        own_rest,
        near_sem.at[0],
        part_sem.at[4 + core],
        {"core": 1 - core},
    )

    def rows_at(ref, at, side):
        return ref.at[pl.ds(pl.multiple_of(at * rows_dev + side * half, half), half)]

    wide_up, wide_down = ups_ref.shape[1] // 2, downs_ref.shape[2]

    def down_piece(at, part, place_at):
        cols = pl.ds(pl.multiple_of(place_at * wide_down, wide_down), wide_down)
        return d_ref.at[block(at, part), cols]

    def up_piece(at, part, place_at):
        cols = pl.ds(pl.multiple_of(place_at * wide_up, wide_up), wide_up)
        return u_ref.at[block(at, part), cols]

    def row_parts(src_ref, dst_ref):
        for seq in range(2):
            for side in range(2):
                goal = 2 * core + seq
                here = jnp.logical_and(core == side, goal == place)
                src = src_ref.at[seq, pl.ds(side * half, half)]
                yield seq * 2 + side, here, src, rows_at(dst_ref, place, side), side, goal

    def send_rows(src_ref, dst_ref, kind):
        for number, here, src, dst, side, goal in row_parts(src_ref, dst_ref):

            @pl.when(here)
            def _():
                pltpu.make_async_copy(src, dst, row_sem.at[kind, place]).start()

            @pl.when(jnp.logical_not(here))
            def _():
                pltpu.make_async_remote_copy(
                    src_ref=src,
                    dst_ref=dst,
                    send_sem=row_out.at[kind, number],
                    recv_sem=row_sem.at[kind, place],
                    device_id={"core": side, "tensor": goal},
                    device_id_type=MESH,
                ).start()

    def share_rows(ref, kind, steps=(0, 1, 2, 3)):
        for step in steps:
            at = (place + step) % 4
            part = rows_at(ref, at, core)
            landed(part, row_sem.at[kind, at])
            send(part, part, pair_out.at[kind, at], pair_sem.at[kind, at], {"core": 1 - core})

    def shared_rows(ref, kind):
        for step in range(4):
            at = (place + step) % 4
            landed(rows_at(ref, at, 1 - core), pair_sem.at[kind, at])


    def send_halves(own, number, parts_of, goal_ref, recv_sem):
        def send_parts_to(side, send_sem, device):
            for src, cols in parts_of(side):
                pltpu.make_async_remote_copy(
                    src_ref=src,
                    dst_ref=goal_ref.at[:, cols],
                    send_sem=send_sem,
                    recv_sem=recv_sem,
                    device_id=device,
                    device_id_type=MESH,
                ).start()
            started.append((goal_ref, send_sem))

        if own:
            send_parts_to(1 - core, ffn_out.at[number, 0], {"core": 1 - core})
            for src, cols in parts_of(core):
                pltpu.make_async_copy(src, goal_ref.at[:, cols], recv_sem).start()
            return
        for step in (2, 1, 3):
            for side in range(2):
                send_parts_to(
                    side,
                    ffn_out.at[number, 2 * step + side],
                    {"core": side, "tensor": (place + step) % 4},
                )

    def down_parts(side):
        return [(downs_ref.at[side], pl.ds(0, wide_down))]

    def up_parts(side):
        unit = wide_up // 2
        return [
            (
                ups_ref.at[:, pl.ds(pl.multiple_of((2 * at + side) * unit, unit), unit)],
                pl.ds(at * unit, unit),
            )
            for at in range(2)
        ]

    def issue_next():
        send_parts(next_ref, mine_next, 4, part_sem.at[6 + slot])

    def issue_downs(own=False):
        send_halves(
            own, 0, down_parts, down_piece(plane, core, place), part_sem.at[10 + 2 * place + core]
        )

    def issue_ups(own=False):
        send_halves(
            own, 1, up_parts, up_piece(plane, core, place), part_sem.at[18 + 2 * place + core]
        )

    first_col = jnp.where(place // 2 == core, place % 2, 1 - core)
    order = [(0, None, 0), (0, None, 1)]
    for kind in (1, 2):
        for turn in range(2):
            for part in range(2):
                order.append((kind, (first_col + turn) % 2, part))

    for kind in (3, 4):
        for step in (0, 1, 3, 2):
            for part in range(2):
                order.append((kind, (place + step) % 4, part))

    def at_piece(at, item):
        kind, col, part = item
        if kind >= 3:
            return (down_piece, up_piece)[kind - 3](at, part, col)
        if kind == 0:
            return rest_piece(at, part)
        return piece(at, part, col) if kind == 1 else next_piece(at, part, col)

    def index(item):
        kind, col, part = item
        if kind >= 3:
            return 8 * kind - 14 + 2 * col + part
        return 4 + part if kind == 0 else (kind - 1) * 6 + part * 2 + col

    def relay(item):
        at = index(item)
        if item[2] == 0:
            landed(at_piece(xside, item), fromx_sem.at[at])
            ref = at_piece(xside, item)
            send(ref, ref, rely_sem.at[at], overy_sem.at[at], {"plane": yside})
        else:
            landed(at_piece(yside, item), fromy_sem.at[at])
            ref = at_piece(yside, item)
            send(ref, ref, relx_sem.at[at], overx_sem.at[at], {"plane": xside})

    def serve(items):
        for item in items:
            at = index(item)
            ref = at_piece(plane, item)
            landed(ref, part_sem.at[at])
            send(ref, ref, tox_sem.at[at], fromx_sem.at[at], {"plane": xside})
            send(ref, ref, toy_sem.at[at], fromy_sem.at[at], {"plane": yside})

    def relays(items):
        for item in items:
            relay(item)

    def complete(items):
        for item in items:
            at = index(item)
            if item[2] == 0:
                landed(at_piece(yside, item), fromy_sem.at[at])
                landed(at_piece(across, item), overy_sem.at[at])
            else:
                landed(at_piece(xside, item), fromx_sem.at[at])
                landed(at_piece(across, item), overx_sem.at[at])

    stores = []

    def store(src, dst):
        sem = store_sem.at[len(stores)]
        pltpu.make_async_copy(src, dst, sem).start()
        stores.append((src, dst, sem))

    issue_ups(True)
    issue_downs(True)
    serve(order[:2])
    serve(order[18:20])
    serve(order[10:12])
    serve(order[2:4])
    relays(order[:2])
    relays(order[18:20])
    serve(order[4:6])
    issue_ups()
    relays(order[10:12])
    relays(order[2:6])
    serve(order[20:26])
    send_rows(x_ref, full_ref, 0)
    issue_next()
    complete(order[:6])
    relays(order[20:22])
    for at in range(2):
        landed(params_ref.at[at], param_sem.at[at])
    taps_ref[:, 2 * GROUP :] = state_taps[...]
    for col in range(2):
        for tap in range(KCONV):
            for at in range(3):
                lanes = pl.ds(col * GROUP + at * 128, 128)
                taps_ref[tap : tap + 1, lanes] = params_ref[col, 3 * tap + at : 3 * tap + at + 1, :]
        for at in range(3):
            lanes = pl.ds(col * GROUP + at * 128, 128)
            skip_ref[:, lanes] = params_ref[col, 12 + at : 13 + at, :]
            gain_ref[:, lanes] = params_ref[col, 15 + at : 16 + at, :]
        bias_ref[col : col + 1, :] = params_ref[col, 18:19, :]
        decay_ref[col : col + 1, :] = params_ref[col, 19:20, :]
    share_rows(full_ref, 0)
    relays(order[22:26])
    shared_rows(full_ref, 0)
    store(w_ref, w_hbm)
    store(full_ref, x_hbm)

    rows = full_ref.shape[0]

    @pl.loop(0, rows // 128)
    def _(at):
        here = pl.ds(pl.multiple_of(at * 128, 128), 128)
        values = wide(full_ref[here, :])
        size = 1.0 / values.shape[1]
        root = lax.rsqrt(jnp.sum(values * values, axis=1, keepdims=True) * size + EPS)
        normed_ref[here, :] = low(values * root * gain_in[...])

    store(normed_ref, normed_hbm)

    def project(begin, end):
        @pl.loop(0, (end - begin) // 256)
        def _(at):
            cols = pl.ds(pl.multiple_of(begin + at * 256, 128), 256)
            proj_ref[:, cols] = dot(normed_ref[...], w_ref[:, cols])

    def attend(col):
        lanes = pl.ds(col * 128, 128)
        attention_forward_kernel(
            len_ref,
            proj_ref.at[:, pl.ds(col * width + 768, 128)],
            proj_ref.at[:, pl.ds(2 * width + 2 * N, 128)],
            cos_ref,
            sin_ref,
            attn_ref.at[:, lanes],
            sums_ref.at[:, lanes],
        )

    def chunks(begin, end):
        @pl.loop(begin, end)
        def _(at):
            here = pl.ds(pl.multiple_of(at * CHUNK, CHUNK), CHUNK)
            mamba_chunk(
                proj_ref.at[here, :],
                attn_ref.at[here, :],
                taps_ref,
                bias_ref,
                decay_ref,
                skip_ref,
                gain_ref,
                both_ref.at[here, :],
                out_ref.at[here, :],
                states_ref.at[at],
                buf_ref,
                state_ref,
            )

    project(0, 1024)
    serve(order[6:10])
    issue_downs()
    project(1024, 2304)
    last = pl.ds(2304, proj_ref.shape[1] - 2304)
    proj_ref[:, last] = dot(normed_ref[...], w_ref[:, last])
    store(proj_ref, proj_hbm)
    relays(order[6:8])
    attend(0)
    relays(order[8:10])
    serve(order[12:14])
    attend(1)
    serve(order[14:18])
    send_rows(og_ref, og_full, 1)
    mamba_start(buf_ref, state_ref)
    count = rows // CHUNK
    chunks(0, count // 4)
    relays(order[12:14])
    chunks(count // 4, count // 2)
    complete(order[6:10])
    store(v_ref, v_hbm)
    relays(order[14:18])
    chunks(count // 2, count)

    @pl.loop(0, 4)
    def _(at):
        here = pl.ds(pl.multiple_of(at * 256, 256), 256)
        mixed_ref[here, :] = low(dot_nt(both_ref[here, :], v_ref[...]))

    send(mixed_ref, other_ref, mixed_sem.at[0], mixed_sem.at[1], {"core": 1 - core})
    share_rows(og_full, 1)
    complete(order[10:26])
    shared_rows(og_full, 1)
    landed(other_ref, mixed_sem.at[1])
    for src, dst, sem in stores:
        pltpu.make_async_copy(src, dst, sem).wait()
    for src, sem in started:
        landed(src, sem)

    @pl.when(target == core)
    def _():
        for step in range(1, 4):
            landed(small_ref, param_out.at[step])

    @pl.when(target != core)
    def _():
        landed(pack_ref, out_sem.at[0])
        landed(next_ref, out_sem.at[4])

    for kind, (src_ref, dst_ref) in enumerate(((x_ref, full_ref), (og_ref, og_full))):
        for number, here, src, _, _, _ in row_parts(src_ref, dst_ref):

            @pl.when(jnp.logical_not(here))
            def _():
                landed(src, row_out.at[kind, number])


def front(
    pack,
    following,
    ups,
    downs,
    shared,
    x_rows,
    small,
    out_grad,
    state_taps,
    gain,
    seq_len,
    cosine,
    sine,
):
    share, width = pack.shape
    narrow = following.shape[1]
    rest = shared.shape[2]
    rows = x_rows.shape[1] * 4
    model = x_rows.shape[2]
    columns = 2 * width + rest
    dma = pltpu.SemaphoreType.DMA
    any_space = pl.BlockSpec(memory_space=pl.ANY)
    near = pl.BlockSpec(memory_space=pltpu.VMEM)
    f32, bf16 = jnp.float32, pack.dtype
    return pl.pallas_call(
        front_kernel,
        in_specs=[any_space] * 8
        + [near, near, pl.BlockSpec(memory_space=pltpu.SMEM), near, near],
        out_specs=[any_space] * 8 + [near] * 11,
        out_shape=[
            jax.ShapeDtypeStruct((8 * share, columns), bf16),
            jax.ShapeDtypeStruct((8 * share, 2 * narrow), bf16),
            jax.ShapeDtypeStruct((8 * share, 2 * ups.shape[1]), bf16),
            jax.ShapeDtypeStruct((8 * share, 4 * downs.shape[2]), bf16),
            jax.ShapeDtypeStruct((rows, model), bf16),
            jax.ShapeDtypeStruct((rows, model), bf16),
            jax.ShapeDtypeStruct((rows, columns), f32),
            jax.ShapeDtypeStruct((rows, model), bf16),
            jax.ShapeDtypeStruct((KCONV, CONV), f32),
            jax.ShapeDtypeStruct((2, 128), f32),
            jax.ShapeDtypeStruct((2, 128), f32),
            jax.ShapeDtypeStruct((1, 2 * GROUP), f32),
            jax.ShapeDtypeStruct((1, 2 * GROUP), f32),
            jax.ShapeDtypeStruct((rows, 256), f32),
            jax.ShapeDtypeStruct((rows, 1024), bf16),
            jax.ShapeDtypeStruct((rows, 2 * GROUP), f32),
            jax.ShapeDtypeStruct((rows // CHUNK, N, 2 * GROUP), f32),
            jax.ShapeDtypeStruct((rows, 8 * share), bf16),
            jax.ShapeDtypeStruct((rows, 8 * share), bf16),
        ],
        scratch_shapes=[
            pltpu.VMEM((8 * share, columns), bf16),
            pltpu.VMEM((8 * share, 2 * narrow), bf16),
            pltpu.VMEM((rows, model), bf16),
            pltpu.VMEM((rows, model), bf16),
            pltpu.VMEM((rows, columns), f32),
            pltpu.VMEM((rows, 256), bf16),
            pltpu.VMEM((2,) + small.shape, f32),
            pltpu.VMEM((CHUNK + 8, CONV), f32),
            pltpu.VMEM((N, 2 * GROUP), f32),
            dma((1,)),
            dma((8,)),
        ]
        + [dma((26,))] * 9
        + [dma((2, 4))] * 4
        + [dma((4,))] * 2
        + [dma((2, 8)), dma((5,)), dma((2,))],
        compiler_params=pltpu.CompilerParams(
            collective_id=1, has_side_effects=True, vmem_limit_bytes=BIG
        ),
        cost_estimate=cost(120),
        name="front",
    )(
        pack,
        following,
        ups,
        downs,
        shared,
        x_rows,
        small,
        out_grad,
        state_taps,
        gain,
        seq_len,
        cosine,
        sine,
    )


def collect_kernel(*refs):
    (mixed_ref, both_ref, normed_hbm, dproj_hbm, weight_hbm, x_hbm, hidden_hbm) = refs[:7]
    (gain_ref, small_ref) = refs[7:9]
    (mixer_out, query_out, step_out, shared_ref, total_ref, back_ref) = refs[9:15]
    (mamba_out, attn_out) = refs[15:17]
    (normed_ref, dproj_ref, weight_ref, x_ref, hidden_ref, grad_ref, next_ref) = refs[17:24]
    (norm_ref, norm_in, rows_ref, in_ref, next_in, sum_ref, next_sum) = refs[24:31]
    (piece_ref, next_buf, pair_ref, mix_ref, near_ref, far_ref) = refs[31:37]
    (in_sem, out_sem, piece_sem, piece_out, pair_sem, mix_sem, mix_out) = refs[37:44]
    (near_sem, near_out, far_sem, far_out, row_sem, row_out, load_sem, norm_sem) = refs[44:]
    plane = lax.axis_index("plane")
    core = lax.axis_index("core")
    place = lax.axis_index("tensor")
    xside = plane + 1 - 2 * (plane % 2)
    yside = plane + 2 - 4 * (plane // 2)
    across = xside + 2 - 4 * (xside // 2)
    share = pair_ref.shape[0]
    width = piece_ref.shape[2]
    rest = grad_ref.shape[1] - 2 * width

    loads = [
        (dproj_hbm, dproj_ref),
        (weight_hbm, weight_ref),
        (normed_hbm, normed_ref),
        (x_hbm.at[:, core], x_ref),
        (hidden_hbm.at[:, core], hidden_ref),
    ]
    for number, (src, dst) in enumerate(loads):
        pltpu.make_async_copy(src, dst, load_sem.at[number]).start()

    def loaded(number):
        src, dst = loads[number]
        pltpu.make_async_copy(src, dst, load_sem.at[number]).wait()

    barrier = pltpu.get_barrier_semaphore()
    for step in range(4):
        for side in range(2):
            if step or side:
                pl.semaphore_signal(
                    barrier,
                    inc=1,
                    device_id={"core": (core + side) % 2, "tensor": (place + step) % 4},
                    device_id_type=MESH,
                )
    for neighbour in (xside, yside):
        pl.semaphore_signal(
            barrier, inc=1, device_id={"plane": neighbour}, device_id_type=MESH
        )
    pl.semaphore_wait(barrier, 9)

    started = []

    def send(src, dst, send_sem, recv_sem, device):
        pltpu.make_async_remote_copy(
            src_ref=src,
            dst_ref=dst,
            send_sem=send_sem,
            recv_sem=recv_sem,
            device_id=device,
            device_id_type=MESH,
        ).start()
        started.append((src, send_sem))

    narrow = next_ref.shape[1] // 2
    spans = [(0, 2 * width, rest), (0, 0, width), (0, width, width)]
    spans += [(1, 0, narrow), (1, narrow, narrow)]

    def block(at, part, span):
        rows = pl.ds(pl.multiple_of(at * 2 * share + part * share, share), share)
        return (grad_ref, next_ref)[span[0]].at[rows, pl.ds(*span[1:])]

    def held(slot, span):
        return (in_ref, next_in)[span[0]].at[slot, :, pl.ds(*span[1:])]

    def summed(part, span):
        return (sum_ref, next_sum)[span[0]].at[part, :, pl.ds(*span[1:])]

    def begin(number):
        span = spans[number]
        send(
            block(across, 0, span),
            held(0, span),
            out_sem.at[0, number],
            in_sem.at[0, number],
            {"plane": xside},
        )
        send(
            block(across, 1, span),
            held(1, span),
            out_sem.at[1, number],
            in_sem.at[1, number],
            {"plane": yside},
        )
        send(
            block(xside, 0, span),
            held(2, span),
            out_sem.at[2, number],
            in_sem.at[2, number],
            {"plane": xside},
        )
        send(
            block(yside, 1, span),
            held(3, span),
            out_sem.at[3, number],
            in_sem.at[3, number],
            {"plane": yside},
        )

    def work(number):
        kind, begin_at, size = spans[number]
        left = (normed_ref, mixed_ref)[kind]
        right = (dproj_ref, both_ref)[kind]
        result = (grad_ref, next_ref)[kind]
        tile = 256 if size % 256 == 0 else size

        @pl.loop(0, size // tile)
        def _(at):
            cols = pl.ds(pl.multiple_of(begin_at + at * tile, 128), tile)
            result[:, cols] = low(dot_tn(left[...], right[:, cols]))

    seq = place % 2
    owner = place // 2
    dst_rows = back_ref.at[seq, pl.ds(pl.multiple_of(core * share, share), share)]

    def send_back():
        for step in (2, 1, 3):
            at = (place + step) % 4
            send(
                rows_ref.at[at],
                dst_rows,
                row_out.at[step],
                row_sem.at[seq * 2 + core],
                {"core": owner, "tensor": at},
            )

        @pl.when(owner == core)
        def _():
            pltpu.make_async_copy(
                rows_ref.at[place], dst_rows, row_sem.at[seq * 2 + core]
            ).start()

        @pl.when(owner != core)
        def _():
            pltpu.make_async_remote_copy(
                src_ref=rows_ref.at[place],
                dst_ref=dst_rows,
                send_sem=row_out.at[0],
                recv_sem=row_sem.at[seq * 2 + core],
                device_id={"core": 1 - core},
                device_id_type=MESH,
            ).start()

    def norm_product():
        loaded(0)
        loaded(1)
        for at in range(4):
            rows = pl.ds(at * 2 * share, 2 * share)
            part = low(dot_nt(dproj_ref[rows, :], weight_ref[...]))
            norm_ref[at, 0] = part[:share]
            norm_ref[at, 1] = part[share:]
        send(
            norm_ref.at[:, 1 - core],
            norm_in,
            norm_sem.at[0],
            norm_sem.at[1],
            {"core": 1 - core},
        )

    def norm_back():
        loaded(3)
        loaded(4)
        landed(norm_in, norm_sem.at[1])
        gain_total = jnp.zeros((1, x_ref.shape[2]), jnp.float32)
        for at in range(4):
            grad = wide(norm_ref[at, core]) + wide(norm_in[at])
            values = wide(x_ref[at])
            size = 1.0 / values.shape[1]
            root = lax.rsqrt(jnp.sum(values * values, axis=1, keepdims=True) * size + EPS)
            scaled = grad * gain_ref[...]
            inner = jnp.sum(values * scaled, axis=1, keepdims=True) * size
            rows_ref[at] = low(
                hidden_ref[at] + root * scaled - values * (root * root * root * inner)
            )
            gain_total = gain_total + jnp.sum(values * root * grad, axis=0, keepdims=True)
        near_ref[5] = small_ref[...]
        for at in range(gain_total.shape[1] // 128):
            near_ref[5, at : at + 1, :] = gain_total[:, at * 128 : (at + 1) * 128]

    def pass_on(number):
        span = spans[number]
        landed(held(0, span), in_sem.at[0, number])
        held(0, span)[...] = low(wide(held(0, span)[...]) + wide(block(yside, 0, span)[...]))
        send(
            held(0, span),
            held(5, span),
            out_sem.at[4, number],
            in_sem.at[5, number],
            {"plane": yside},
        )
        landed(held(1, span), in_sem.at[1, number])
        held(1, span)[...] = low(wide(held(1, span)[...]) + wide(block(xside, 1, span)[...]))
        send(
            held(1, span),
            held(4, span),
            out_sem.at[5, number],
            in_sem.at[4, number],
            {"plane": xside},
        )

    def finish(number):
        span = spans[number]
        landed(held(2, span), in_sem.at[2, number])
        landed(held(5, span), in_sem.at[5, number])
        summed(0, span)[...] = low(
            wide(block(plane, 0, span)[...]) + wide(held(2, span)[...]) + wide(held(5, span)[...])
        )
        landed(held(3, span), in_sem.at[3, number])
        landed(held(4, span), in_sem.at[4, number])
        summed(1, span)[...] = low(
            wide(block(plane, 1, span)[...]) + wide(held(3, span)[...]) + wide(held(4, span)[...])
        )

    def send_pieces(number):
        span = spans[number]
        kind, col = span[0], span[1] // span[2]
        buf = (piece_ref, next_buf)[kind]
        goal = 2 * core + col
        for part in range(2):
            src = summed(part, span)
            here = jnp.logical_and(core == part, goal == place)

            @pl.when(here)
            def _():
                pltpu.make_async_copy(src, buf.at[place], piece_sem.at[kind, place]).start()

            @pl.when(jnp.logical_not(here))
            def _():
                pltpu.make_async_remote_copy(
                    src_ref=src,
                    dst_ref=buf.at[place],
                    send_sem=piece_out.at[kind, 2 * col + part],
                    recv_sem=piece_sem.at[kind, place],
                    device_id={"core": part, "tensor": goal},
                    device_id_type=MESH,
                ).start()

    rest_cols = pl.ds(2 * width, rest)
    state = rest * 2 // 3

    def pair_up():
        send(
            sum_ref.at[1 - core, :, rest_cols],
            pair_ref,
            pair_sem.at[0],
            pair_sem.at[1],
            {"core": 1 - core},
        )

    def mix():
        landed(pair_ref, pair_sem.at[1])
        mine = sum_ref[core, :, rest_cols]
        mix_ref[place, :, 0:state] = low(wide(mine[:, :state]) + wide(pair_ref[:, :state]))
        first = core == 0
        mix_ref[place, :, state:rest] = jnp.where(first, mine[:, state:], pair_ref[:, state:])
        mix_ref[place, :, rest:] = jnp.where(first, pair_ref[:, state:], mine[:, state:])
        own_mix = mix_ref.at[place]
        for step in (2, 1, 3):
            send(
                own_mix,
                own_mix,
                mix_out.at[step],
                mix_sem.at[place],
                {"tensor": (place + step) % 4},
            )

    work(3)
    begin(3)
    work(4)
    begin(4)
    norm_product()
    pass_on(3)
    loaded(2)
    work(0)
    begin(0)
    finish(3)
    send_pieces(3)
    pass_on(4)
    norm_back()
    send_back()
    send(near_ref.at[5], near_ref.at[0], near_out.at[0], near_sem.at[0], {"plane": xside})
    work(1)
    begin(1)
    finish(4)
    send_pieces(4)
    pass_on(0)
    work(2)
    landed(near_ref.at[0], near_sem.at[0])
    near_ref[3] = near_ref[5] + near_ref[0]
    send(near_ref.at[3], near_ref.at[1], near_out.at[1], near_sem.at[1], {"plane": yside})
    finish(0)
    pair_up()
    pass_on(1)
    begin(2)
    landed(near_ref.at[1], near_sem.at[1])
    near_ref[4] = near_ref[3] + near_ref[1]
    send(near_ref.at[4], near_ref.at[2], near_out.at[2], near_sem.at[2], {"core": 1 - core})
    mix()
    finish(1)
    send_pieces(1)
    landed(near_ref.at[2], near_sem.at[2])
    far_ref[place] = near_ref[4] + near_ref[2]
    own_far = far_ref.at[place]
    for step in (2, 1, 3):
        send(
            own_far,
            own_far,
            far_out.at[step],
            far_sem.at[place],
            {"tensor": (place + step) % 4},
        )
    pass_on(2)
    finish(2)
    send_pieces(2)

    for step in (1, 2, 3):
        at = (place + step) % 4
        landed(mix_ref.at[at], mix_sem.at[at])
        landed(far_ref.at[at], far_sem.at[at])
    shared_ref[...] = (
        wide(mix_ref[0]) + wide(mix_ref[1]) + wide(mix_ref[2]) + wide(mix_ref[3])
    )
    total_ref[...] = (far_ref[0] + far_ref[1]) + (far_ref[2] + far_ref[3])
    def gathered(buf, kind):
        for at in range(4):
            landed(buf.at[at], piece_sem.at[kind, at])
        return wide(buf[0]) + wide(buf[1]) + wide(buf[2]) + wide(buf[3])

    one = gathered(piece_ref, 0)
    cut = mixer_out.shape[1]
    mixer_out[...] = one[:, :cut]
    query_out[...] = one[:, cut : cut + query_out.shape[1]]
    step_out[...] = one[:, cut + query_out.shape[1] :]
    both = gathered(next_buf, 1).T
    mamba_out[...] = both[: mamba_out.shape[0]]
    attn_out[...] = both[mamba_out.shape[0] :]
    for at in range(4):
        landed(dst_rows, row_sem.at[at])
    for src, sem in started:
        landed(src, sem)

    @pl.when(owner != core)
    def _():
        landed(rows_ref.at[place], row_out.at[0])

    for span in spans[1:]:
        col = span[1] // span[2]
        for part in range(2):
            here = jnp.logical_and(core == part, 2 * core + col == place)

            @pl.when(jnp.logical_not(here))
            def _():
                landed(summed(part, span), piece_out.at[span[0], 2 * col + part])


def collect(normed, dproj, weight, mixed, both, x_rows, hidden, gain, small, sizes):
    chans, queries, width = sizes
    share = weight.shape[0] // 8
    model = weight.shape[0]
    columns = weight.shape[1]
    rest = columns - 2 * width
    narrow = both.shape[1] // 2
    dma = pltpu.SemaphoreType.DMA
    any_space = pl.BlockSpec(memory_space=pl.ANY)
    near = pl.BlockSpec(memory_space=pltpu.VMEM)
    shared_cols = rest + rest // 3
    bf16, f32 = jnp.bfloat16, jnp.float32
    split = (4, 2, x_rows.shape[0] // 8, model)
    half = (4, x_rows.shape[0] // 8, model)
    return pl.pallas_call(
        collect_kernel,
        in_specs=[near, near] + [any_space] * 5 + [near, near],
        out_specs=[near] * 5 + [any_space] + [near] * 2,
        out_shape=[
            jax.ShapeDtypeStruct((share, 2 * chans), f32),
            jax.ShapeDtypeStruct((share, queries), f32),
            jax.ShapeDtypeStruct((share, width - 2 * chans - queries), f32),
            jax.ShapeDtypeStruct((share, shared_cols), f32),
            jax.ShapeDtypeStruct(small.shape, f32),
            jax.ShapeDtypeStruct((2, 2 * half[1], model), bf16),
            jax.ShapeDtypeStruct((chans, share), f32),
            jax.ShapeDtypeStruct((narrow - chans, share), f32),
        ],
        scratch_shapes=[
            pltpu.VMEM(normed.shape, bf16),
            pltpu.VMEM(dproj.shape, bf16),
            pltpu.VMEM(weight.shape, bf16),
            pltpu.VMEM(half, bf16),
            pltpu.VMEM(half, f32),
            pltpu.VMEM((model, columns), bf16),
            pltpu.VMEM((model, 2 * narrow), bf16),
            pltpu.VMEM(split, bf16),
            pltpu.VMEM(half, bf16),
            pltpu.VMEM(half, bf16),
            pltpu.VMEM((6, share, columns), bf16),
            pltpu.VMEM((6, share, 2 * narrow), bf16),
            pltpu.VMEM((2, share, columns), bf16),
            pltpu.VMEM((2, share, 2 * narrow), bf16),
            pltpu.VMEM((4, share, width), bf16),
            pltpu.VMEM((4, share, narrow), bf16),
            pltpu.VMEM((share, rest), bf16),
            pltpu.VMEM((4, share, shared_cols), bf16),
            pltpu.VMEM((6,) + small.shape, f32),
            pltpu.VMEM((4,) + small.shape, f32),
            dma((6, 5)),
            dma((6, 5)),
            dma((2, 4)),
            dma((2, 4)),
            dma((2,)),
            dma((4,)),
            dma((4,)),
            dma((3,)),
            dma((3,)),
            dma((4,)),
            dma((4,)),
            dma((4,)),
            dma((4,)),
            dma((5,)),
            dma((2,)),
        ],
        compiler_params=pltpu.CompilerParams(
            collective_id=2, has_side_effects=True, vmem_limit_bytes=BIG
        ),
        cost_estimate=cost(80),
        name="collect",
    )(
        mixed,
        both,
        normed,
        dproj,
        weight,
        x_rows.reshape(split),
        hidden.reshape(split),
        gain.reshape(1, -1),
        small,
    )


def rms_norm(values, gain_vec):
    return values * lax.rsqrt(jnp.mean(values * values, axis=-1, keepdims=True) + EPS) * gain_vec


def turn_tables(seq_count, head_count):
    half_dim = HEAD_SIZE // 2
    freqs = np.float32(THETA) ** (-np.arange(half_dim, dtype=np.float32) * 2.0 / HEAD_SIZE)
    angles = np.arange(seq_count, dtype=np.float32)[:, None] * freqs.astype(np.float32)[None, :]
    cosine, sine = np.cos(angles), np.sin(angles)
    return (
        jnp.asarray(np.tile(np.concatenate([cosine, cosine], axis=1), (1, head_count))),
        jnp.asarray(np.tile(np.concatenate([-sine, sine], axis=1), (1, head_count))),
    )


def swapped(values):
    return lax.ppermute(values, "core", SWAP)


def body(
    layer_in,
    seq_lengths,
    out_grad,
    norm_gain,
    mixer_weight,
    step_weight,
    state_weight,
    query_weight,
    key_value_weight,
    conv_channels,
    conv_states,
    step_bias,
    decay_log,
    skip_scale,
    group_gain,
    mamba_proj,
    attn_proj,
    ffn_gain,
    ffn_weight,
    ffn_down,
):
    core = lax.axis_index("core")
    place = lax.axis_index("tensor")
    first = core == 0
    seq_dev, rows_dev, model_dim = layer_in.shape
    groups = lax.axis_size("tensor")
    seq_total = rows_dev * groups
    half_rows = rows_dev // 2
    share = mixer_weight.shape[0]
    chans_dev = mixer_weight.shape[2]
    heads_dev = step_weight.shape[1]
    query_dev = query_weight.shape[1]
    hidden_dev = ffn_weight.shape[2]
    held = groups // 2
    step_pad = 128

    def mine(values):
        return lax.dynamic_slice_in_dim(values, core * held, held, 0)

    def other(values):
        return lax.dynamic_slice_in_dim(values, (1 - core) * held, held, 0)

    def in_order(own, others, axis):
        return jnp.where(
            first,
            jnp.concatenate([own, others], axis=axis),
            jnp.concatenate([others, own], axis=axis),
        )

    def flat(values):
        return values.transpose(1, 0, 2).reshape(values.shape[1], -1)

    spot = 2 * core + place % 2

    def positions_in(values):
        shaped = values.reshape(seq_dev, 2, half_rows, model_dim)
        keep = lax.dynamic_index_in_dim(shaped, core, 1, False)
        send = lax.dynamic_index_in_dim(shaped, 1 - core, 1, False)
        return lax.all_to_all(in_order(keep, swapped(send), 0), "tensor", 0, 0, tiled=True)

    def both_halves(own):
        both = in_order(own[:, None], swapped(own)[:, None], 1)
        return both.reshape(seq_total, model_dim)

    def positions_out(own):
        four = lax.all_to_all(own, "tensor", 0, 0, tiled=True)
        keep = lax.dynamic_slice_in_dim(four, core * seq_dev, seq_dev, 0)
        send = lax.dynamic_slice_in_dim(four, (1 - core) * seq_dev, seq_dev, 0)
        both = in_order(keep[:, None], swapped(send)[:, None], 1)
        return both.reshape(seq_dev, rows_dev, model_dim)

    def own_half(values):
        shaped = values.reshape(groups, 2, half_rows, -1)
        return lax.dynamic_index_in_dim(shaped, core, 1, False)

    def other_half(values):
        shaped = values.reshape(groups, 2, half_rows, -1)
        return lax.dynamic_index_in_dim(shaped, 1 - core, 1, False)

    out_dev = chans_dev + query_dev
    pack_two = jnp.concatenate([mamba_proj.T, attn_proj.T], axis=1)
    own_units = hidden_dev // 2
    pack_ups = ffn_weight.reshape(share, 2 * hidden_dev)
    pack_downs = ffn_down.reshape(2, own_units, share).transpose(0, 2, 1)
    out_dev = chans_dev + query_dev
    pack_two = jnp.concatenate([mamba_proj.T, attn_proj.T], axis=1)
    pack_one = jnp.concatenate(
        [
            mixer_weight.reshape(share, 2 * chans_dev),
            query_weight,
            jnp.pad(step_weight, ((0, 0), (0, step_pad - heads_dev))),
        ],
        axis=1,
    )
    kv_heads = key_value_weight.reshape(share, 2, 2, HEAD_SIZE)

    def shared_for(at):
        return jnp.concatenate(
            [
                state_weight.reshape(share, 2 * N),
                lax.dynamic_index_in_dim(kv_heads, at, 2, False).reshape(share, 2 * HEAD_SIZE),
            ],
            axis=1,
        )

    def lanes(values):
        return jnp.pad(values, (0, -values.shape[0] % 128)).reshape(-1, 128)

    small_in = jnp.concatenate(
        [
            lanes(conv_channels.reshape(-1)),
            lanes(jnp.repeat(skip_scale, HEAD_SIZE)),
            lanes(group_gain),
            lanes(step_bias),
            lanes(decay_log),
        ]
    )
    small_in = jnp.pad(small_in, ((0, -small_in.shape[0] % 8), (0, 0)))
    lengths = in_order(seq_lengths, swapped(seq_lengths), 0)
    seq_len = lengths[place]
    len_one = seq_len.reshape(1)
    valid_rows = (jnp.arange(seq_total, dtype=jnp.int32) < seq_len).astype(jnp.float32)[:, None]
    group_cols = 2 * chans_dev + query_dev + step_pad
    cosine, sine = turn_tables(seq_total, 2)
    state_taps = conv_states.reshape(KCONV, 2 * N)
    quad = lax.axis_size("plane") == 4 and groups == 4 and share == 128
    quad = quad and share == half_rows
    if quad:
        shared = jnp.stack([shared_for(0), shared_for(1)])
        (
            weight_one,
            weight_two,
            gate_up_weight,
            down_weight,
            x_low,
            normed,
            proj,
            grad_whole,
            taps,
            bias,
            decay,
            skip,
            gain,
            log_sums,
            both_low,
            state_out,
            states,
            mixed_part,
            mixed_other,
        ) = front(
            pack_one,
            pack_two,
            pack_ups,
            pack_downs,
            shared,
            layer_in,
            small_in,
            out_grad,
            state_taps,
            norm_gain.reshape(1, -1),
            len_one,
            cosine,
            sine,
        )
    else:
        x_low = both_halves(positions_in(layer_in))
        all_one = lax.all_gather(pack_one, "tensor", axis=0)
        own_one = jnp.concatenate([flat(mine(all_one)), shared_for(core)], axis=1)
        their_one = jnp.concatenate([flat(other(all_one)), shared_for(1 - core)], axis=1)
        weight_one = lax.all_gather(
            in_order(own_one, swapped(their_one), 0), "plane", axis=0, tiled=True
        )
        all_two = lax.all_gather(pack_two, "tensor", axis=0)
        weight_two = lax.all_gather(
            in_order(flat(mine(all_two)), swapped(flat(other(all_two))), 0),
            "plane",
            axis=0,
            tiled=True,
        )
        split_ups = pack_ups.reshape(share, 2, 2, own_units).transpose(2, 0, 1, 3)
        split_ups = split_ups.reshape(2, share, hidden_dev)
        rows_up, rows_down = (
            in_order(
                lax.dynamic_index_in_dim(pack, core, 0, False),
                swapped(lax.dynamic_index_in_dim(pack, 1 - core, 0, False)),
                0,
            )
            for pack in (split_ups, pack_downs)
        )
        rows_up, rows_down = (
            lax.all_gather(rows, "tensor", axis=1, tiled=True) for rows in (rows_up, rows_down)
        )
        down_weight = lax.all_gather(rows_down, "plane", axis=0, tiled=True)
        params = mine(lax.all_gather(small_in, "tensor", axis=0))
        span = chans_dev // 128

        def spread_lanes(at):
            return params[:, at : at + span].reshape(1, -1)

        taps = jnp.concatenate([spread_lanes(span * tap) for tap in range(KCONV)], axis=0)
        taps = jnp.concatenate([taps, state_taps], axis=1)
        skip, gain = spread_lanes(KCONV * span), spread_lanes((KCONV + 1) * span)
        bias, decay = params[:, (KCONV + 2) * span], params[:, (KCONV + 2) * span + 1]
        normed = low(rms_norm(wide(x_low), norm_gain))
        proj = dot(normed, weight_one)
        attn, log_sums = attention_forward(len_one, proj, cosine, sine, group_cols)
        both_low, state_out, states = mamba_forward(proj, attn, taps, bias, decay, skip, gain)
        gate_up_weight = lax.all_gather(rows_up, "plane", axis=0, tiled=True)
        grad_whole = both_halves(positions_in(out_grad))
        mixed_part = low(dot_nt(both_low, weight_two))
        mixed_other = swapped(mixed_part)

    grad_low, hidden, normed_two, act_low, gate_up_low = ffn_middle(
        len_one,
        x_low,
        mixed_part,
        mixed_other,
        ffn_gain.reshape(1, -1),
        grad_whole,
        gate_up_weight,
        down_weight,
        groups,
    )
    grad_three = ffn_gradients(grad_low, act_low, normed_two, gate_up_low, groups)
    grad_two_part = low(dot_nt(gate_up_low, gate_up_weight))
    ffn_part = low(dot_nt(act_low, down_weight))
    ffn_own = wide(own_half(ffn_part)) + wide(swapped(other_half(ffn_part)))
    out_own = own_half(valid_rows) * (own_half(hidden) + ffn_own)

    grad_hidden, grad_mixed, back, grad_ffn_gain = hidden_backward(
        hidden,
        grad_two_part,
        swapped(grad_two_part),
        grad_low,
        ffn_gain.reshape(1, -1),
        weight_two,
    )
    grad_ffn_gain = grad_ffn_gain.reshape(-1)

    def scatter(values):
        return lax.psum_scatter(values, "plane", scatter_dimension=0, tiled=True)

    def to_groups(values):
        by_part = values.reshape(2, share, held, -1).transpose(0, 2, 1, 3)
        own = lax.dynamic_index_in_dim(by_part, core, 0, False)
        theirs = swapped(lax.dynamic_index_in_dim(by_part, 1 - core, 0, False))
        whole = in_order(own, theirs, 0)
        return wide(lax.psum_scatter(whole, "tensor", scatter_dimension=0, tiled=True)[0])

    units = lax.psum_scatter(scatter(grad_three), "tensor", scatter_dimension=1, tiled=True)
    units = units.reshape(2, share, -1)
    own_part = lax.dynamic_index_in_dim(units, core, 0, True)
    their_part = swapped(lax.dynamic_index_in_dim(units, 1 - core, 0, True))
    units = wide(in_order(own_part, their_part, 0))
    sum_up = units[:, :, :hidden_dev].reshape(2, share, 2, own_units).transpose(1, 2, 0, 3)
    sum_down = units[:, :, hidden_dev:].transpose(0, 2, 1).reshape(hidden_dev, share)

    grad_q, grad_kv = attention_backward(
        len_one, proj, cosine, sine, log_sums, back, group_cols, 3
    )
    layer_out = positions_out(low(out_own))
    proj_grad, grad_taps, grad_gain, grad_skip_cols, grad_bias, grad_decay = mamba_backward(
        proj, state_out, states, back, grad_q, grad_kv, taps, bias, decay, skip, gain
    )
    edge = held * group_cols
    grad_skip = jnp.sum(grad_skip_cols.reshape(held, heads_dev, HEAD_SIZE), axis=-1)
    chan_taps = grad_taps[:, : held * chans_dev].reshape(KCONV, held, chans_dev)
    group_small = jnp.concatenate(
        [
            chan_taps.transpose(1, 0, 2).reshape(held, -1),
            grad_bias[:, :heads_dev],
            grad_decay[:, :heads_dev],
            grad_skip,
            grad_gain.reshape(held, -1),
        ],
        axis=1,
    )
    small_groups = in_order(group_small, jnp.zeros_like(group_small), 0)
    small_out = jnp.concatenate(
        [
            jnp.zeros_like(norm_gain),
            grad_ffn_gain,
            grad_taps[:, held * chans_dev :].reshape(-1),
            small_groups.reshape(-1),
        ]
    )
    if quad:
        small_size = small_out.shape[0]
        small_room = -(-small_size // 1024) * 1024
        (
            sum_mixer,
            sum_query,
            sum_step,
            shared_sum,
            small_sum,
            input_grad,
            sum_mamba,
            sum_attn,
        ) = collect(
            normed,
            proj_grad,
            weight_one,
            grad_mixed,
            both_low,
            x_low,
            grad_hidden,
            norm_gain,
            jnp.pad(small_out, (0, small_room - small_size)).reshape(-1, 128),
            (chans_dev, query_dev, group_cols),
        )
        small_sum = small_sum.reshape(-1)[:small_size]
    else:
        grad_one = low(dot_tn(normed, proj_grad))
        grad_norm_part = low(dot_nt(proj_grad, weight_one))
        grad_norm_own = wide(own_half(grad_norm_part)) + wide(swapped(other_half(grad_norm_part)))
        x_own = wide(own_half(x_low))
        r_one = lax.rsqrt(jnp.mean(x_own * x_own, axis=-1, keepdims=True) + EPS)
        scaled = grad_norm_own * norm_gain
        grad_x = low(
            own_half(grad_hidden)
            + r_one * scaled
            - x_own * (r_one**3 * jnp.mean(x_own * scaled, axis=-1, keepdims=True))
        )
        grad_norm_gain = jnp.sum(x_own * r_one * grad_norm_own, axis=(0, 1))
        small_out = small_out.at[:model_dim].set(grad_norm_gain)
        part_one = scatter(grad_one)
        both_parts = part_one[:, edge:].reshape(2, share, -1)
        own_rest = lax.dynamic_index_in_dim(both_parts, core, 0, False)
        their_rest = swapped(lax.dynamic_index_in_dim(both_parts, 1 - core, 0, False))
        shared_own = wide(own_rest[:, : 2 * N]) + wide(their_rest[:, : 2 * N])
        kv_both = in_order(own_rest[:, 2 * N :], their_rest[:, 2 * N :], 1)
        shared_low = jnp.concatenate([low(shared_own), kv_both], axis=1)
        shared_sum = jnp.sum(wide(lax.all_gather(shared_low, "tensor", axis=0)), axis=0)
        sum_one = to_groups(part_one[:, :edge])
        sum_mixer = sum_one[:, : 2 * chans_dev]
        sum_query = sum_one[:, 2 * chans_dev : 2 * chans_dev + query_dev]
        sum_step = sum_one[:, 2 * chans_dev + query_dev :]
        sum_two = to_groups(scatter(low(dot_tn(grad_mixed, both_low)))).T
        sum_mamba, sum_attn = sum_two[:chans_dev], sum_two[chans_dev:]
        input_grad = positions_out(grad_x)
        small_sum = lax.psum(small_out, ("plane", "core", "tensor"))
    kv_sum = shared_sum[:, 2 * N :].reshape(share, 2, 2, HEAD_SIZE).transpose(0, 2, 1, 3)
    group_sum = lax.dynamic_index_in_dim(
        small_sum[2 * model_dim + KCONV * 2 * N :].reshape(groups, -1), place, 0, False
    )
    pieces = []
    at = 0
    for size in (KCONV * chans_dev, heads_dev, heads_dev, heads_dev, chans_dev):
        pieces.append(group_sum[at : at + size])
        at += size

    return (
        layer_out,
        input_grad,
        small_sum[:model_dim],
        sum_mixer.reshape(share, 2, chans_dev),
        sum_step[:, :heads_dev],
        shared_sum[:, : 2 * N].reshape(share, 2, N),
        sum_query,
        kv_sum.reshape(share, 2, 2 * HEAD_SIZE),
        pieces[0].reshape(KCONV, chans_dev),
        small_sum[2 * model_dim : 2 * model_dim + KCONV * 2 * N].reshape(KCONV, 2, N),
        pieces[1],
        pieces[2],
        pieces[3],
        pieces[4],
        sum_mamba,
        sum_attn,
        small_sum[model_dim : 2 * model_dim],
        sum_up.reshape(share, 2, hidden_dev),
        sum_down,
    )


def solution(mesh):
    rows, columns = mesh.devices.shape
    fine = Mesh(mesh.devices.reshape(rows // 2, 2, columns), ("plane", "core", "tensor"))
    dp = ("plane", "core")
    return jax.shard_map(
        body,
        mesh=fine,
        in_specs=(
            P(dp, "tensor", None),
            P(dp),
            P(dp, "tensor", None),
            P(),
            P(dp, None, "tensor"),
            P(dp, "tensor"),
            P(dp, None, None),
            P(dp, "tensor"),
            P(dp, None, None),
            P(None, "tensor"),
            P(),
            P("tensor"),
            P("tensor"),
            P("tensor"),
            P("tensor"),
            P("tensor", dp),
            P("tensor", dp),
            P(),
            P(dp, None, "tensor"),
            P("tensor", dp),
        ),
        out_specs=(
            P(dp, "tensor", None),
            P(dp, "tensor", None),
            P(),
            P(dp, None, "tensor"),
            P(dp, "tensor"),
            P(dp, None, None),
            P(dp, "tensor"),
            P(dp, None, None),
            P(None, "tensor"),
            P(),
            P("tensor"),
            P("tensor"),
            P("tensor"),
            P("tensor"),
            P("tensor", dp),
            P("tensor", dp),
            P(),
            P(dp, None, "tensor"),
            P("tensor", dp),
        ),
        check_vma=False,
    )
```

```python
import jax
import jax.numpy as jnp
import numpy as np
from jax import lax
from jax.experimental import pallas as pl
from jax.experimental.pallas import tpu as pltpu
from jax.sharding import Mesh
from jax.sharding import PartitionSpec as P

HEAD_SIZE = 64
N = 128
KCONV = 4
GH = 6
EPS = 1e-05
THETA = 10000.0
MASKED = -1e30
SWAP = [(0, 1), (1, 0)]


def low(values):
    return values.astype(jnp.bfloat16)


def wide(values):
    return values.astype(jnp.float32)


def dot(left, right):
    return jnp.dot(left, right, preferred_element_type=jnp.float32)


def dot_nt(left, right):
    return lax.dot_general(
        left, right, (((1,), (1,)), ((), ())), preferred_element_type=jnp.float32
    )


def dot_tn(left, right):
    return lax.dot_general(
        left, right, (((0,), (0,)), ((), ())), preferred_element_type=jnp.float32
    )


def dot_fine(left, right):
    high = low(right)
    rest = right - wide(high)
    mid = low(rest)
    last = low(rest - wide(mid))
    return dot(left, high) + dot(left, mid) + dot(left, last)


def dot_by(left, right):
    high = low(left)
    rest = low(left - wide(high))
    return dot(high, right) + dot(rest, right)


def sigmoid(values):
    return 1.0 / (1.0 + jnp.exp(-values))


def turn(values, cosine, sine):
    lane = lax.broadcasted_iota(jnp.int32, values.shape, 1)
    half = HEAD_SIZE // 2
    up = pltpu.roll(values, 128 - half, 1)
    down = pltpu.roll(values, half, 1)
    return values * cosine + jnp.where(lane % HEAD_SIZE < half, up, down) * sine


def turn_back(values, cosine, sine):
    lane = lax.broadcasted_iota(jnp.int32, values.shape, 1)
    half = HEAD_SIZE // 2
    turned = values * sine
    up = pltpu.roll(turned, 128 - half, 1)
    down = pltpu.roll(turned, half, 1)
    return values * cosine + jnp.where(lane % HEAD_SIZE < half, up, down)


def cost(micros):
    return pl.CostEstimate(flops=int(micros * 1e9), bytes_accessed=0, transcendentals=0)


SCALE = HEAD_SIZE ** (-0.5)
ROWS = 256


def key_value_parts(kv, cosine, sine):
    lane = lax.broadcasted_iota(jnp.int32, kv.shape, 1)
    key = jnp.where(lane < HEAD_SIZE, turn(kv, cosine, sine), 0.0)
    value = jnp.where(lane < HEAD_SIZE, 0.0, kv)
    keys = (low(key), low(pltpu.roll(key, HEAD_SIZE, 1)))
    values = (low(pltpu.roll(value, HEAD_SIZE, 1)), low(value))
    return keys, values


def block_scores(query, keys, begin, seq_len):
    scores = dot_nt(query, keys)
    row = lax.broadcasted_iota(jnp.int32, (scores.shape[0], 1), 0) + begin
    col = lax.broadcasted_iota(jnp.int32, scores.shape, 1)
    return jnp.where(col < jnp.minimum(row + 1, seq_len), scores, MASKED)


def attention_forward_kernel(len_ref, q_ref, kv_ref, cos_ref, sin_ref, out_ref, sum_ref):
    seq_len = len_ref[0]
    cosine, sine = cos_ref[...], sin_ref[...]
    keys, values = key_value_parts(kv_ref[...], cosine, sine)
    query = low(turn(q_ref[...], cosine, sine) * SCALE)
    rows = query.shape[0]
    lane = lax.broadcasted_iota(jnp.int32, (ROWS, 128), 1)
    for begin in range(0, rows, ROWS):
        end = begin + ROWS
        outs, sums = [], []
        for head in range(2):
            scores = block_scores(query[begin:end], keys[head][:end], begin, seq_len)
            peak = jnp.max(scores, axis=1, keepdims=True)
            exps = jnp.exp(scores - peak)
            total = jnp.sum(exps, axis=1, keepdims=True)
            probs = low(exps * (1.0 / total))
            outs.append(dot(probs, values[head][:end]))
            sums.append(peak + jnp.log(total))
        out_ref[begin:end, :] = low(outs[0] + outs[1])
        sum_ref[begin:end, :] = jnp.where(lane < HEAD_SIZE, sums[0], sums[1])


def attention_backward_kernel(
    len_ref, q_ref, kv_ref, cos_ref, sin_ref, sum_ref, grad_ref, dq_ref, dkv_ref, dk_acc, dv_acc
):
    seq_len = len_ref[0]
    cosine, sine = cos_ref[...], sin_ref[...]
    keys, values = key_value_parts(kv_ref[...], cosine, sine)
    query = low(turn(q_ref[...], cosine, sine) * SCALE)
    query_t = query.T
    rows = query.shape[0]
    group = pl.program_id(0)
    grad = low(grad_ref[...])
    grad_t = grad.T

    @pl.when(group == 0)
    def _():
        dk_acc[...] = jnp.zeros_like(dk_acc)
        dv_acc[...] = jnp.zeros_like(dv_acc)

    for begin in range(0, rows, ROWS):
        end = begin + ROWS
        dq = jnp.zeros((ROWS, 128), jnp.float32)
        for head in range(2):
            lanes = slice(head * HEAD_SIZE, (head + 1) * HEAD_SIZE)
            scores = block_scores(query[begin:end], keys[head][:end], begin, seq_len)
            at = head * HEAD_SIZE
            probs = jnp.exp(scores - sum_ref[begin:end, at : at + 1])
            dv_acc[:, :end] += dot(grad_t[lanes, begin:end], low(probs))
            dp = dot_nt(grad[begin:end], values[head][:end])
            inner = jnp.sum(probs * dp, axis=1, keepdims=True)
            ds = low(probs * (dp - inner))
            dq = dq + dot(ds, keys[head][:end])
            dk_acc[:, :end] += dot(query_t[lanes, begin:end], ds)
        dq = turn_back(dq * SCALE, cosine[begin:end], sine[begin:end])
        dq_ref[begin:end, :] = low(dq)

    @pl.when(group == pl.num_programs(0) - 1)
    def _():
        both = jnp.concatenate([dk_acc[...], dv_acc[...]], axis=0).T
        lane = lax.broadcasted_iota(jnp.int32, both.shape, 1)
        dkv_ref[...] = low(jnp.where(lane < HEAD_SIZE, turn_back(both, cosine, sine), both))


def attention_specs(rows, group_cols):
    whole = pl.BlockSpec((rows, 128), lambda g: (0, 0))
    return [
        pl.BlockSpec(memory_space=pltpu.SMEM),
        pl.BlockSpec((rows, 128), lambda g: (0, g * (group_cols // 128) + 6)),
        pl.BlockSpec((rows, 128), lambda g: (0, 2 * (group_cols // 128) + 2)),
        whole,
        whole,
    ]


BIG = 60 * 1024 * 1024


def attention_forward(seq_len, proj, cosine, sine, group_cols):
    rows = proj.shape[0]
    pairs = pl.BlockSpec((rows, 128), lambda g: (0, g))
    return pl.pallas_call(
        attention_forward_kernel,
        grid=(2,),
        in_specs=attention_specs(rows, group_cols),
        out_specs=[pairs, pairs],
        out_shape=[
            jax.ShapeDtypeStruct((rows, 256), jnp.bfloat16),
            jax.ShapeDtypeStruct((rows, 256), jnp.float32),
        ],
        compiler_params=pltpu.CompilerParams(vmem_limit_bytes=BIG),
        cost_estimate=cost(11),
        name="attention_forward",
    )(seq_len, proj, proj, cosine, sine)


def attention_backward(seq_len, proj, cosine, sine, sums, grad, group_cols, grad_at):
    rows = proj.shape[0]
    pairs = pl.BlockSpec((rows, 128), lambda g: (0, g))
    return pl.pallas_call(
        attention_backward_kernel,
        grid=(2,),
        in_specs=attention_specs(rows, group_cols)
        + [pairs, pl.BlockSpec((rows, 128), lambda g: (0, 4 * g + grad_at))],
        out_specs=[pairs, pl.BlockSpec((rows, 128), lambda g: (0, 0))],
        out_shape=[
            jax.ShapeDtypeStruct((rows, 256), jnp.bfloat16),
            jax.ShapeDtypeStruct((rows, 128), jnp.bfloat16),
        ],
        scratch_shapes=[
            pltpu.VMEM((HEAD_SIZE, rows), jnp.float32),
            pltpu.VMEM((HEAD_SIZE, rows), jnp.float32),
        ],
        compiler_params=pltpu.CompilerParams(vmem_limit_bytes=BIG),
        cost_estimate=cost(18),
        name="attention_backward",
    )(seq_len, proj, proj, cosine, sine, sums, grad)


CHUNK = 128
GROUP = GH * HEAD_SIZE
PAIRS = GH // 2
CONV = 2 * GROUP + 2 * N
SHARED = 2048


def triangle():
    row = lax.broadcasted_iota(jnp.int32, (CHUNK, CHUNK), 0)
    col = lax.broadcasted_iota(jnp.int32, (CHUNK, CHUNK), 1)
    return col <= row


def pair_lanes(values, pair):
    lane = lax.broadcasted_iota(jnp.int32, (values.shape[0], 128), 1)
    at = 2 * pair
    return jnp.where(lane < HEAD_SIZE, values[:, at : at + 1], values[:, at + 1 : at + 2])


def split_pair(values):
    lane = lax.broadcasted_iota(jnp.int32, values.shape, 1)
    empty = jnp.zeros_like(values)
    return jnp.concatenate(
        [jnp.where(lane < HEAD_SIZE, values, empty), jnp.where(lane < HEAD_SIZE, empty, values)],
        axis=0,
    )


def conv_pre(buf_ref, taps_ref, begin, size):
    total = buf_ref[5 : 5 + CHUNK, begin : begin + size] * taps_ref[0:1, begin : begin + size]
    for tap in range(1, KCONV):
        total = total + (
            buf_ref[5 + tap : 5 + tap + CHUNK, begin : begin + size]
            * taps_ref[tap : tap + 1, begin : begin + size]
        )
    return total


def load_conv(buf_ref, proj_ref):
    for group in range(2):
        at = group * 1024 + GROUP
        buf_ref[8:, group * GROUP : (group + 1) * GROUP] = proj_ref[:, at : at + GROUP]
    buf_ref[8:, 2 * GROUP :] = proj_ref[:, SHARED : SHARED + 2 * N]


def group_steps(proj_ref, bias_ref, decay_ref, group, lower):
    at = group * 1024 + 896
    raw = proj_ref[:, at : at + 128] + bias_ref[group : group + 1, :]
    step = jnp.log1p(jnp.exp(-jnp.abs(raw))) + jnp.maximum(raw, 0.0)
    rate = -jnp.exp(decay_ref[group : group + 1, :])
    cumul = dot_fine(lower, rate * step)
    return raw, step, rate, cumul


def head_decay(cumul, cumul_t, head, mask):
    spread = cumul[:, head : head + 1] - cumul_t[head : head + 1, :]
    return jnp.exp(jnp.where(mask, spread, MASKED))


def mamba_chunk(
    proj_ref,
    attn_ref,
    taps_ref,
    bias_ref,
    decay_ref,
    skip_ref,
    gain_ref,
    both_ref,
    out_ref,
    state_out,
    buf_ref,
    state_ref,
):
    load_conv(buf_ref, proj_ref)
    mask = triangle()
    lower = mask.astype(jnp.bfloat16)
    pre = conv_pre(buf_ref, taps_ref, 2 * GROUP, 2 * N)
    state_act = low(pre * sigmoid(pre))
    b_rows, c_rows = state_act[:, :N], state_act[:, N:]
    gram = dot_nt(c_rows, b_rows)
    b_cols = b_rows.T
    for group in range(2):
        cols = slice(group * GROUP, (group + 1) * GROUP)
        _, step, _, cumul = group_steps(proj_ref, bias_ref, decay_ref, group, lower)
        cumul_t = cumul.T
        last = cumul[CHUNK - 1 : CHUNK, :]
        state = state_ref[:, cols]
        state_out[:, cols] = state
        from_state = dot(c_rows, low(state))
        gated, lasts, x_ends = [], [], []
        for pair in range(PAIRS):
            at = group * GROUP + pair * 128
            pre = conv_pre(buf_ref, taps_ref, at, 128)
            chan = pre * sigmoid(pre)
            inputs = low(chan * pair_lanes(step, pair))
            mixing = jnp.concatenate(
                [
                    low(gram * head_decay(cumul, cumul_t, 2 * pair + side, mask))
                    for side in range(2)
                ],
                axis=1,
            )
            lanes = slice(pair * 128, (pair + 1) * 128)
            inner = pair_lanes(cumul, pair)
            out = dot(mixing, split_pair(inputs)) + jnp.exp(inner) * from_state[:, lanes]
            out_ref[:, at : at + 128] = out
            last_lanes = pair_lanes(last, pair)
            lasts.append(last_lanes)
            x_ends.append(low(jnp.exp(last_lanes - inner) * wide(inputs)))
            gate = proj_ref[:, group * 1024 + pair * 128 : group * 1024 + pair * 128 + 128]
            skipped = out + chan * skip_ref[:, at : at + 128]
            gated.append(skipped * (gate * sigmoid(gate)))
        state_ref[:, cols] = jnp.exp(jnp.concatenate(lasts, axis=1)) * state + dot(
            b_cols, jnp.concatenate(x_ends, axis=1)
        )
        square = jnp.sum(sum(part * part for part in gated), axis=1, keepdims=True)
        scale = lax.rsqrt(square * (1.0 / GROUP) + EPS)
        for pair in range(PAIRS):
            at = group * GROUP + pair * 128
            to = group * 512 + pair * 128
            both_ref[:, to : to + 128] = low(gated[pair] * scale * gain_ref[:, at : at + 128])
        to = group * 512 + GROUP
        both_ref[:, to : to + 128] = attn_ref[:, group * 128 : (group + 1) * 128]
    buf_ref[0:8, :] = buf_ref[CHUNK : CHUNK + 8, :]


def mamba_start(buf_ref, state_ref):
    buf_ref[0:8, :] = jnp.zeros((8, CONV), jnp.float32)
    state_ref[...] = jnp.zeros_like(state_ref)


def mamba_forward_kernel(*refs):
    @pl.when(pl.program_id(0) == 0)
    def _():
        mamba_start(*refs[-2:])

    mamba_chunk(*refs[:9], refs[9].at[0], *refs[10:])


def mamba_forward(proj, attn, taps, bias, decay, skip, gain):
    rows, columns = proj.shape
    chunks = rows // CHUNK

    def whole(value):
        return pl.BlockSpec(value.shape, lambda k: (0, 0))

    return pl.pallas_call(
        mamba_forward_kernel,
        grid=(chunks,),
        in_specs=[
            pl.BlockSpec((CHUNK, columns), lambda k: (k, 0)),
            pl.BlockSpec((CHUNK, 256), lambda k: (k, 0)),
        ]
        + [whole(value) for value in (taps, bias, decay, skip, gain)],
        out_specs=[
            pl.BlockSpec((CHUNK, 1024), lambda k: (k, 0)),
            pl.BlockSpec((CHUNK, 2 * GROUP), lambda k: (k, 0)),
            pl.BlockSpec((1, N, 2 * GROUP), lambda k: (k, 0, 0)),
        ],
        out_shape=[
            jax.ShapeDtypeStruct((rows, 1024), jnp.bfloat16),
            jax.ShapeDtypeStruct((rows, 2 * GROUP), jnp.float32),
            jax.ShapeDtypeStruct((chunks, N, 2 * GROUP), jnp.float32),
        ],
        scratch_shapes=[
            pltpu.VMEM((CHUNK + 8, CONV), jnp.float32),
            pltpu.VMEM((N, 2 * GROUP), jnp.float32),
        ],
        compiler_params=pltpu.CompilerParams(vmem_limit_bytes=BIG),
        cost_estimate=cost(14),
        name="mamba_forward",
    )(proj, attn, taps, bias, decay, skip, gain)


def silu_slope(values, sig):
    return sig * (1.0 + values * (1.0 - sig))


def mamba_backward_kernel(
    proj_ref,
    before_ref,
    out_ref,
    states_ref,
    back_ref,
    dq_ref,
    dkv_ref,
    taps_ref,
    bias_ref,
    decay_ref,
    skip_ref,
    gain_ref,
    dproj_ref,
    dtaps_ref,
    dgain_ref,
    dskip_ref,
    dbias_ref,
    ddecay_ref,
    buf_ref,
    grad_buf,
    after_ref,
    flow_ref,
):
    step_at = pl.program_id(0)

    @pl.when(step_at == 0)
    def _():
        for ref in (dtaps_ref, dgain_ref, dskip_ref, dbias_ref, ddecay_ref, after_ref, flow_ref):
            ref[...] = jnp.zeros_like(ref)
        grad_buf[CHUNK:, :] = jnp.zeros((8, CONV), jnp.float32)

    inside = jnp.where(step_at == pl.num_programs(0) - 1, 0.0, 1.0)
    for group in range(2):
        at = group * 1024 + GROUP
        buf_ref[0:8, group * GROUP : (group + 1) * GROUP] = before_ref[:, at : at + GROUP] * inside
    buf_ref[0:8, 2 * GROUP :] = before_ref[:, SHARED : SHARED + 2 * N] * inside
    load_conv(buf_ref, proj_ref)
    mask = triangle()
    lower = mask.astype(jnp.bfloat16)
    row = lax.broadcasted_iota(jnp.int32, (CHUNK, CHUNK), 0)
    col = lax.broadcasted_iota(jnp.int32, (CHUNK, CHUNK), 1)
    upper = (row <= col).astype(jnp.bfloat16)
    pre_state = conv_pre(buf_ref, taps_ref, 2 * GROUP, 2 * N)
    sig_state = sigmoid(pre_state)
    state_act = low(pre_state * sig_state)
    b_rows, c_rows = state_act[:, :N], state_act[:, N:]
    gram = dot_nt(c_rows, b_rows)
    c_cols = c_rows.T
    head_of_row = lax.broadcasted_iota(jnp.int32, (GROUP, 128), 0) // HEAD_SIZE
    head_lane = lax.broadcasted_iota(jnp.int32, (GROUP, 128), 1)
    pick = (head_of_row == head_lane).astype(jnp.bfloat16)
    dgram = jnp.zeros((CHUNK, CHUNK), jnp.float32)
    d_c = jnp.zeros((CHUNK, N), jnp.float32)
    d_b = jnp.zeros((CHUNK, N), jnp.float32)
    for group in range(2):
        raw, step, rate, cumul = group_steps(proj_ref, bias_ref, decay_ref, group, lower)
        cumul_t = cumul.T
        last = cumul[CHUNK - 1 : CHUNK, :]
        pres, sigs, chans, gates, gate_sigs, skips, gated = [], [], [], [], [], [], []
        for pair in range(PAIRS):
            at = group * GROUP + pair * 128
            pre = conv_pre(buf_ref, taps_ref, at, 128)
            sig = sigmoid(pre)
            chan = pre * sig
            gate = proj_ref[:, group * 1024 + pair * 128 : group * 1024 + pair * 128 + 128]
            gate_sig = sigmoid(gate)
            skipped = out_ref[:, at : at + 128] + chan * skip_ref[:, at : at + 128]
            pres.append(pre)
            sigs.append(sig)
            chans.append(chan)
            gates.append(gate)
            gate_sigs.append(gate_sig)
            skips.append(skipped)
            gated.append(skipped * (gate * gate_sig))
        square = jnp.sum(sum(part * part for part in gated), axis=1, keepdims=True)
        scale = lax.rsqrt(square * (1.0 / GROUP) + EPS)
        grads = []
        cross = jnp.zeros((CHUNK, 128), jnp.float32)
        for pair in range(PAIRS):
            at = group * GROUP + pair * 128
            grad = back_ref[:, group * 512 + pair * 128 : group * 512 + pair * 128 + 128]
            dgain_ref[:, at : at + 128] += jnp.sum(grad * gated[pair] * scale, axis=0, keepdims=True)
            grad = grad * gain_ref[:, at : at + 128]
            cross = cross + gated[pair] * grad
            grads.append(grad)
        cross = jnp.sum(cross, axis=1, keepdims=True) * (1.0 / GROUP) * scale * scale * scale
        cols = slice(group * GROUP, (group + 1) * GROUP)
        lane = lax.broadcasted_iota(jnp.int32, (CHUNK, 128), 1)
        after = after_ref[:, cols]
        after_low = low(after)
        state = states_ref[0, :, cols]
        from_after = dot(b_rows, after_low)
        x_ends, g_starts, lasts, flows, dsteps = [], [], [], [], []
        for pair in range(PAIRS):
            at = group * GROUP + pair * 128
            lanes = slice(pair * 128, (pair + 1) * 128)
            chan = chans[pair]
            grad = scale * grads[pair] - gated[pair] * cross
            gate, gate_sig = gates[pair], gate_sigs[pair]
            dgate = grad * skips[pair] * silu_slope(gate, gate_sig)
            to = group * 1024 + pair * 128
            dproj_ref[:, to : to + 128] = low(dgate)
            grad = grad * (gate * gate_sig)
            dskip_ref[:, at : at + 128] += jnp.sum(grad * chan, axis=0, keepdims=True)
            dchan = grad * skip_ref[:, at : at + 128]
            dout = low(grad)
            step_lanes = pair_lanes(step, pair)
            inputs = low(chan * step_lanes)
            halves = split_pair(inputs)
            decays = [head_decay(cumul, cumul_t, 2 * pair + side, mask) for side in range(2)]
            mixing = jnp.concatenate([low(gram * decay) for decay in decays], axis=1)
            dmix = dot_nt(dout, halves)
            dgram = dgram + dmix[:, :CHUNK] * decays[0] + dmix[:, CHUNK:] * decays[1]
            dinputs = dot_tn(mixing, dout)
            dinputs = jnp.where(lane < HEAD_SIZE, dinputs[:CHUNK], dinputs[CHUNK:])
            inner = pair_lanes(cumul, pair)
            last_lanes = pair_lanes(last, pair)
            to_end = jnp.exp(last_lanes - inner)
            dinputs = dinputs + to_end * from_after[:, lanes]
            x_ends.append(low(to_end * wide(inputs)))
            g_starts.append(low(jnp.exp(inner) * wide(dout)))
            lasts.append(last_lanes)
            flows.append(wide(dout) * out_ref[:, at : at + 128] - wide(inputs) * dinputs)
            dsteps.append(dinputs * chan)
            dchan = dchan + dinputs * step_lanes
            grad_buf[0:CHUNK, at : at + 128] = dchan * silu_slope(pres[pair], sigs[pair])
        g_start = jnp.concatenate(g_starts, axis=1)
        d_c = d_c + dot_nt(g_start, low(state))
        d_b = d_b + dot_nt(jnp.concatenate(x_ends, axis=1), after_low)
        after = jnp.exp(jnp.concatenate(lasts, axis=1)) * after + dot(c_cols, g_start)
        after_ref[:, cols] = after
        through = jnp.sum(after * state, axis=0, keepdims=True)
        stacked = jnp.concatenate(
            [
                jnp.concatenate(flows, axis=1),
                jnp.concatenate(dsteps, axis=1),
                jnp.broadcast_to(through, (8, GROUP)),
            ],
            axis=0,
        )
        picked = dot_by(stacked, pick)
        flow, dstep = picked[:CHUNK], picked[CHUNK : 2 * CHUNK]
        flow_end = flow_ref[group : group + 1, :]
        flow_next = picked[2 * CHUNK : 2 * CHUNK + 1]
        dcumul = dot_fine(upper, flow) + flow_end
        flow_ref[group : group + 1, :] = flow_next
        dstep = dstep + rate * dcumul
        ddecay_ref[group : group + 1, :] += jnp.sum(rate * step * dcumul, axis=0, keepdims=True)
        draw = dstep * sigmoid(raw)
        dbias_ref[group : group + 1, :] += jnp.sum(draw, axis=0, keepdims=True)
        to = group * 1024 + 896
        lane = lax.broadcasted_iota(jnp.int32, (CHUNK, 128), 1)
        dproj_ref[:, to : to + 128] = low(jnp.where(lane < GH, draw, 0.0))
        to = group * 1024 + 2 * GROUP
        dproj_ref[:, to : to + 128] = dq_ref[:, group * 128 : (group + 1) * 128]
    dgram_low = low(dgram)
    d_c = d_c + dot(dgram_low, b_rows)
    d_b = d_b + dot_tn(dgram_low, c_rows)
    slope = silu_slope(pre_state, sig_state)
    grad_buf[0:CHUNK, 2 * GROUP : 2 * GROUP + N] = d_b * slope[:, :N]
    grad_buf[0:CHUNK, 2 * GROUP + N :] = d_c * slope[:, N:]
    for at in range(0, CONV, 128):
        grad = jnp.zeros((CHUNK, 128), jnp.float32)
        here = grad_buf[0:CHUNK, at : at + 128]
        for tap in range(KCONV):
            shift = KCONV - 1 - tap
            grad = grad + (
                grad_buf[shift : shift + CHUNK, at : at + 128] * taps_ref[tap : tap + 1, at : at + 128]
            )
            dtaps_ref[tap : tap + 1, at : at + 128] += jnp.sum(
                here * buf_ref[5 + tap : 5 + tap + CHUNK, at : at + 128], axis=0, keepdims=True
            )
        if at < 2 * GROUP:
            to = (at // GROUP) * 1024 + GROUP + at % GROUP
        else:
            to = SHARED + at - 2 * GROUP
        dproj_ref[:, to : to + 128] = low(grad)
    dproj_ref[:, SHARED + 2 * N :] = dkv_ref[...]
    grad_buf[CHUNK:, :] = grad_buf[0:8, :]


def mamba_backward(proj, out, states, back, dq, dkv, taps, bias, decay, skip, gain):
    rows, columns = proj.shape
    chunks = rows // CHUNK

    def whole(value):
        return pl.BlockSpec(value.shape, lambda k: (0, 0))

    def rows_of(width):
        return pl.BlockSpec((CHUNK, width), lambda k: (chunks - 1 - k, 0))

    params = (taps, bias, decay, skip, gain)
    return pl.pallas_call(
        mamba_backward_kernel,
        grid=(chunks,),
        in_specs=[
            rows_of(columns),
            pl.BlockSpec(
                (8, columns),
                lambda k: (jnp.maximum((chunks - 1 - k) * (CHUNK // 8) - 1, 0), 0),
            ),
            rows_of(2 * GROUP),
            pl.BlockSpec((1, N, 2 * GROUP), lambda k: (chunks - 1 - k, 0, 0)),
            rows_of(1024),
            rows_of(256),
            rows_of(128),
        ]
        + [whole(value) for value in params],
        out_specs=[rows_of(columns)]
        + [whole(value) for value in (taps, gain, skip, bias, decay)],
        out_shape=[jax.ShapeDtypeStruct((rows, columns), jnp.bfloat16)]
        + [
            jax.ShapeDtypeStruct(value.shape, jnp.float32)
            for value in (taps, gain, skip, bias, decay)
        ],
        scratch_shapes=[
            pltpu.VMEM((CHUNK + 8, CONV), jnp.float32),
            pltpu.VMEM((CHUNK + 8, CONV), jnp.float32),
            pltpu.VMEM((N, 2 * GROUP), jnp.float32),
            pltpu.VMEM((8, 128), jnp.float32),
        ],
        compiler_params=pltpu.CompilerParams(vmem_limit_bytes=BIG),
        cost_estimate=cost(36),
        name="mamba_backward",
    )(proj, proj, out, states, back, dq, dkv, *params)


def ffn_kernel(
    len_ref,
    x_ref,
    own_ref,
    their_ref,
    gain_ref,
    raw_ref,
    up_ref,
    down_ref,
    grad_ref,
    hidden_ref,
    normed_ref,
    act_ref,
    dgate_ref,
):
    units = down_ref.shape[1]
    rows = x_ref.shape[0]

    @pl.when(pl.program_id(0) == 0)
    def _():
        @pl.loop(0, rows // 128)
        def _(at):
            here = pl.ds(pl.multiple_of(at * 128, 128), 128)
            hidden = wide(x_ref[here, :]) + (wide(own_ref[here, :]) + wide(their_ref[here, :]))
            hidden_ref[here, :] = hidden
            size = 1.0 / hidden.shape[1]
            root = lax.rsqrt(jnp.sum(hidden * hidden, axis=1, keepdims=True) * size + EPS)
            normed_ref[here, :] = low(hidden * root * gain_ref[...])
            row = lax.broadcasted_iota(jnp.int32, (128, 1), 0) + at * 128
            grad = wide(raw_ref[here, :])
            grad_ref[here, :] = low(jnp.where(row < len_ref[0], grad, 0.0))

    @pl.loop(0, rows // 512)
    def _(at):
        here = pl.ds(pl.multiple_of(at * 512, 512), 512)
        gate_up = dot(normed_ref[here, :], up_ref[...])
        gate, up = gate_up[:, :units], gate_up[:, units:]
        sig = sigmoid(gate)
        act = gate * sig
        act_ref[here, :] = low(act * up)
        grad = dot(grad_ref[here, :], down_ref[...])
        dgate_ref[here, :units] = low(grad * up * silu_slope(gate, sig))
        dgate_ref[here, units:] = low(grad * act)


def ffn_middle(seq_len, x_rows, own, theirs, gain, grad, up_weight, down_weight, blocks):
    rows, model = x_rows.shape
    units = down_weight.shape[1] // blocks

    def whole(value):
        return pl.BlockSpec(value.shape, lambda z: (0, 0))

    full = pl.BlockSpec((rows, model), lambda z: (0, 0))
    return pl.pallas_call(
        ffn_kernel,
        grid=(blocks,),
        in_specs=[pl.BlockSpec(memory_space=pltpu.SMEM)]
        + [whole(value) for value in (x_rows, own, theirs, gain, grad)]
        + [
            pl.BlockSpec((model, 2 * units), lambda z: (0, z)),
            pl.BlockSpec((model, units), lambda z: (0, z)),
        ],
        out_specs=[
            full,
            full,
            full,
            pl.BlockSpec((rows, units), lambda z: (0, z)),
            pl.BlockSpec((rows, 2 * units), lambda z: (0, z)),
        ],
        out_shape=[
            jax.ShapeDtypeStruct((rows, model), jnp.bfloat16),
            jax.ShapeDtypeStruct((rows, model), jnp.float32),
            jax.ShapeDtypeStruct((rows, model), jnp.bfloat16),
            jax.ShapeDtypeStruct((rows, blocks * units), jnp.bfloat16),
            jax.ShapeDtypeStruct((rows, 2 * blocks * units), jnp.bfloat16),
        ],
        compiler_params=pltpu.CompilerParams(vmem_limit_bytes=BIG),
        cost_estimate=cost(14),
        name="ffn_middle",
    )(seq_len, x_rows, own, theirs, gain, grad, up_weight, down_weight)


def hidden_kernel(
    hidden_ref, own_ref, their_ref, grad_ref, gain_ref, weight_ref, dhidden_ref, mixed_ref, back_ref, dgain_ref
):
    @pl.when(pl.program_id(0) == 0)
    def _():
        dgain_ref[...] = jnp.zeros_like(dgain_ref)

    hidden = hidden_ref[...]
    grad = wide(own_ref[...]) + wide(their_ref[...])
    size = 1.0 / hidden.shape[1]
    root = lax.rsqrt(jnp.sum(hidden * hidden, axis=1, keepdims=True) * size + EPS)
    scaled = grad * gain_ref[...]
    inner = jnp.sum(hidden * scaled, axis=1, keepdims=True) * size
    dhidden = wide(grad_ref[...]) + root * scaled - hidden * (root * root * root * inner)
    dhidden_ref[...] = dhidden
    dgain_ref[...] += 0.5 * jnp.sum(hidden * root * grad, axis=0, keepdims=True)
    mixed = low(dhidden)
    mixed_ref[...] = mixed
    back_ref[...] = dot(mixed, weight_ref[...])


def hidden_backward(hidden, own, theirs, grad, gain, weight):
    rows, model = hidden.shape

    def whole(value):
        return pl.BlockSpec(value.shape, lambda k: (0, 0))

    part = pl.BlockSpec((256, model), lambda k: (k, 0))
    return pl.pallas_call(
        hidden_kernel,
        grid=(rows // 256,),
        in_specs=[part] * 4 + [whole(gain), whole(weight)],
        out_specs=[part, part, pl.BlockSpec((256, weight.shape[1]), lambda k: (k, 0)), whole(gain)],
        out_shape=[
            jax.ShapeDtypeStruct((rows, model), jnp.float32),
            jax.ShapeDtypeStruct((rows, model), jnp.bfloat16),
            jax.ShapeDtypeStruct((rows, weight.shape[1]), jnp.float32),
            jax.ShapeDtypeStruct(gain.shape, jnp.float32),
        ],
        compiler_params=pltpu.CompilerParams(vmem_limit_bytes=BIG),
        cost_estimate=cost(7),
        name="hidden_backward",
    )(hidden, own, theirs, grad, gain, weight)


def ffn_grad_kernel(grad_ref, act_ref, normed_ref, dgate_ref, out_ref):
    cut = dgate_ref.shape[1]
    out_ref[:, :cut] = low(dot_tn(normed_ref[...], dgate_ref[...]))
    out_ref[:, cut:] = low(dot_tn(grad_ref[...], act_ref[...]))


def ffn_gradients(grad, act, normed, dgate, blocks):
    rows, model = grad.shape
    units = act.shape[1] // blocks
    whole = pl.BlockSpec((rows, model), lambda z: (0, 0))
    return pl.pallas_call(
        ffn_grad_kernel,
        grid=(blocks,),
        in_specs=[
            whole,
            pl.BlockSpec((rows, units), lambda z: (0, z)),
            whole,
            pl.BlockSpec((rows, 2 * units), lambda z: (0, z)),
        ],
        out_specs=pl.BlockSpec((model, 3 * units), lambda z: (0, z)),
        out_shape=jax.ShapeDtypeStruct((model, 3 * blocks * units), jnp.bfloat16),
        compiler_params=pltpu.CompilerParams(vmem_limit_bytes=BIG),
        cost_estimate=cost(12),
        name="ffn_gradients",
    )(grad, act, normed, dgate)


MESH = pl.DeviceIdType.MESH


def landed(ref, sem):
    pltpu.make_async_copy(ref, ref, sem).wait()


def front_kernel(*refs):
    (pack_ref, next_ref, ups_ref, downs_ref, shared_ref, x_ref, small_ref, og_ref) = refs[:8]
    (state_taps, gain_in, len_ref, cos_ref, sin_ref) = refs[8:13]
    (w_hbm, v_hbm, u_ref, d_ref, x_hbm, normed_hbm, proj_hbm, og_full) = refs[13:21]
    (taps_ref, bias_ref, decay_ref, skip_ref, gain_ref) = refs[21:26]
    (sums_ref, both_ref, out_ref, states_ref, mixed_ref, other_ref) = refs[26:32]
    (w_ref, v_ref, full_ref, normed_ref, proj_ref, attn_ref, params_ref) = refs[32:39]
    (buf_ref, state_ref) = refs[39:41]
    (near_sem, out_sem, part_sem, fromx_sem, fromy_sem, overx_sem, overy_sem) = refs[41:48]
    (tox_sem, toy_sem, relx_sem, rely_sem, row_sem, row_out, pair_sem, pair_out) = refs[48:56]
    (param_sem, param_out, ffn_out, store_sem, mixed_sem) = refs[56:]
    plane = lax.axis_index("plane")
    core = lax.axis_index("core")
    place = lax.axis_index("tensor")
    xside = plane + 1 - 2 * (plane % 2)
    yside = plane + 2 - 4 * (plane // 2)
    across = xside + 2 - 4 * (xside // 2)
    target = place // 2
    column = place % 2
    share, width = pack_ref.shape
    narrow = next_ref.shape[1]
    rest = shared_ref.shape[2]
    half = share
    rows_dev = x_ref.shape[1]

    barrier = pltpu.get_barrier_semaphore()
    for step in range(4):
        for side in range(2):
            if step or side:
                pl.semaphore_signal(
                    barrier,
                    inc=1,
                    device_id={"core": (core + side) % 2, "tensor": (place + step) % 4},
                    device_id_type=MESH,
                )
    for neighbour in (xside, yside):
        pl.semaphore_signal(
            barrier, inc=1, device_id={"plane": neighbour}, device_id_type=MESH
        )
    pl.semaphore_wait(barrier, 9)

    def block(at, part):
        return pl.ds(pl.multiple_of(at * 2 * share + part * share, share), share)

    def piece(at, part, col):
        return w_ref.at[block(at, part), pl.ds(pl.multiple_of(col * width, width), width)]

    def next_piece(at, part, col):
        return v_ref.at[block(at, part), pl.ds(pl.multiple_of(col * narrow, narrow), narrow)]

    def rest_piece(at, part):
        return w_ref.at[block(at, part), pl.ds(2 * width, rest)]

    started = []

    def send(src, dst, send_sem, recv_sem, device):
        copy = pltpu.make_async_remote_copy(
            src_ref=src,
            dst_ref=dst,
            send_sem=send_sem,
            recv_sem=recv_sem,
            device_id=device,
            device_id_type=MESH,
        )
        copy.start()
        started.append((src, send_sem))

    mine = piece(plane, core, column)
    slot = core * 2 + column
    mine_next = next_piece(plane, core, column)

    def send_parts(src, dst, at, recv_sem):
        for step in (2, 1, 3):
            send(
                src,
                dst,
                out_sem.at[at + step],
                recv_sem,
                {"core": target, "tensor": (place + step) % 4},
            )

    send_parts(pack_ref, mine, 0, part_sem.at[slot])

    params = params_ref.at[column]

    @pl.when(target == core)
    def _():
        pltpu.make_async_copy(pack_ref, mine, part_sem.at[slot]).start()
        pltpu.make_async_copy(next_ref, mine_next, part_sem.at[6 + slot]).start()
        pltpu.make_async_copy(small_ref, params, param_sem.at[column]).start()
        for step in range(1, 4):
            pltpu.make_async_remote_copy(
                src_ref=small_ref,
                dst_ref=params,
                send_sem=param_out.at[step],
                recv_sem=param_sem.at[column],
                device_id={"tensor": (place + step) % 4},
                device_id_type=MESH,
            ).start()

    @pl.when(target != core)
    def _():
        pltpu.make_async_remote_copy(
            src_ref=pack_ref,
            dst_ref=mine,
            send_sem=out_sem.at[0],
            recv_sem=part_sem.at[slot],
            device_id={"core": 1 - core},
            device_id_type=MESH,
        ).start()
        pltpu.make_async_remote_copy(
            src_ref=next_ref,
            dst_ref=mine_next,
            send_sem=out_sem.at[4],
            recv_sem=part_sem.at[6 + slot],
            device_id={"core": 1 - core},
            device_id_type=MESH,
        ).start()

    own_rest = rest_piece(plane, core)
    near = pltpu.make_async_copy(shared_ref.at[core], own_rest, part_sem.at[4 + core])
    near.start()
    send(
        shared_ref.at[1 - core],
        own_rest,
        near_sem.at[0],
        part_sem.at[4 + core],
        {"core": 1 - core},
    )

    def rows_at(ref, at, side):
        return ref.at[pl.ds(pl.multiple_of(at * rows_dev + side * half, half), half)]

    wide_up, wide_down = ups_ref.shape[1] // 2, downs_ref.shape[2]

    def down_piece(at, part, place_at):
        cols = pl.ds(pl.multiple_of(place_at * wide_down, wide_down), wide_down)
        return d_ref.at[block(at, part), cols]

    def up_piece(at, part, place_at):
        cols = pl.ds(pl.multiple_of(place_at * wide_up, wide_up), wide_up)
        return u_ref.at[block(at, part), cols]

    def row_parts(src_ref, dst_ref):
        for seq in range(2):
            for side in range(2):
                goal = 2 * core + seq
                here = jnp.logical_and(core == side, goal == place)
                src = src_ref.at[seq, pl.ds(side * half, half)]
                yield seq * 2 + side, here, src, rows_at(dst_ref, place, side), side, goal

    def send_rows(src_ref, dst_ref, kind):
        for number, here, src, dst, side, goal in row_parts(src_ref, dst_ref):

            @pl.when(here)
            def _():
                pltpu.make_async_copy(src, dst, row_sem.at[kind, place]).start()

            @pl.when(jnp.logical_not(here))
            def _():
                pltpu.make_async_remote_copy(
                    src_ref=src,
                    dst_ref=dst,
                    send_sem=row_out.at[kind, number],
                    recv_sem=row_sem.at[kind, place],
                    device_id={"core": side, "tensor": goal},
                    device_id_type=MESH,
                ).start()

    def share_rows(ref, kind, steps=(0, 1, 2, 3)):
        for step in steps:
            at = (place + step) % 4
            part = rows_at(ref, at, core)
            landed(part, row_sem.at[kind, at])
            send(part, part, pair_out.at[kind, at], pair_sem.at[kind, at], {"core": 1 - core})

    def shared_rows(ref, kind):
        for step in range(4):
            at = (place + step) % 4
            landed(rows_at(ref, at, 1 - core), pair_sem.at[kind, at])


    def send_halves(own, number, parts_of, goal_ref, recv_sem):
        def send_parts_to(side, send_sem, device):
            for src, cols in parts_of(side):
                pltpu.make_async_remote_copy(
                    src_ref=src,
                    dst_ref=goal_ref.at[:, cols],
                    send_sem=send_sem,
                    recv_sem=recv_sem,
                    device_id=device,
                    device_id_type=MESH,
                ).start()
            started.append((goal_ref, send_sem))

        if own:
            send_parts_to(1 - core, ffn_out.at[number, 0], {"core": 1 - core})
            for src, cols in parts_of(core):
                pltpu.make_async_copy(src, goal_ref.at[:, cols], recv_sem).start()
            return
        for step in (2, 1, 3):
            for side in range(2):
                send_parts_to(
                    side,
                    ffn_out.at[number, 2 * step + side],
                    {"core": side, "tensor": (place + step) % 4},
                )

    def down_parts(side):
        return [(downs_ref.at[side], pl.ds(0, wide_down))]

    def up_parts(side):
        unit = wide_up // 2
        return [
            (
                ups_ref.at[:, pl.ds(pl.multiple_of((2 * at + side) * unit, unit), unit)],
                pl.ds(at * unit, unit),
            )
            for at in range(2)
        ]

    def issue_next():
        send_parts(next_ref, mine_next, 4, part_sem.at[6 + slot])

    def issue_downs(own=False):
        send_halves(
            own, 0, down_parts, down_piece(plane, core, place), part_sem.at[10 + 2 * place + core]
        )

    def issue_ups(own=False):
        send_halves(
            own, 1, up_parts, up_piece(plane, core, place), part_sem.at[18 + 2 * place + core]
        )

    first_col = jnp.where(place // 2 == core, place % 2, 1 - core)
    order = [(0, None, 0), (0, None, 1)]
    for kind in (1, 2):
        for turn in range(2):
            for part in range(2):
                order.append((kind, (first_col + turn) % 2, part))

    for kind in (3, 4):
        for step in (0, 1, 3, 2):
            for part in range(2):
                order.append((kind, (place + step) % 4, part))

    def at_piece(at, item):
        kind, col, part = item
        if kind >= 3:
            return (down_piece, up_piece)[kind - 3](at, part, col)
        if kind == 0:
            return rest_piece(at, part)
        return piece(at, part, col) if kind == 1 else next_piece(at, part, col)

    def index(item):
        kind, col, part = item
        if kind >= 3:
            return 8 * kind - 14 + 2 * col + part
        return 4 + part if kind == 0 else (kind - 1) * 6 + part * 2 + col

    def relay(item):
        at = index(item)
        if item[2] == 0:
            landed(at_piece(xside, item), fromx_sem.at[at])
            ref = at_piece(xside, item)
            send(ref, ref, rely_sem.at[at], overy_sem.at[at], {"plane": yside})
        else:
            landed(at_piece(yside, item), fromy_sem.at[at])
            ref = at_piece(yside, item)
            send(ref, ref, relx_sem.at[at], overx_sem.at[at], {"plane": xside})

    def serve(items):
        for item in items:
            at = index(item)
            ref = at_piece(plane, item)
            landed(ref, part_sem.at[at])
            send(ref, ref, tox_sem.at[at], fromx_sem.at[at], {"plane": xside})
            send(ref, ref, toy_sem.at[at], fromy_sem.at[at], {"plane": yside})

    def relays(items):
        for item in items:
            relay(item)

    def complete(items):
        for item in items:
            at = index(item)
            if item[2] == 0:
                landed(at_piece(yside, item), fromy_sem.at[at])
                landed(at_piece(across, item), overy_sem.at[at])
            else:
                landed(at_piece(xside, item), fromx_sem.at[at])
                landed(at_piece(across, item), overx_sem.at[at])

    stores = []

    def store(src, dst):
        sem = store_sem.at[len(stores)]
        pltpu.make_async_copy(src, dst, sem).start()
        stores.append((src, dst, sem))

    issue_ups(True)
    issue_downs(True)
    serve(order[:2])
    serve(order[18:20])
    serve(order[10:12])
    serve(order[2:4])
    relays(order[:2])
    relays(order[18:20])
    serve(order[4:6])
    issue_ups()
    relays(order[10:12])
    relays(order[2:6])
    serve(order[20:26])
    send_rows(x_ref, full_ref, 0)
    issue_next()
    complete(order[:6])
    relays(order[20:22])
    for at in range(2):
        landed(params_ref.at[at], param_sem.at[at])
    taps_ref[:, 2 * GROUP :] = state_taps[...]
    for col in range(2):
        for tap in range(KCONV):
            for at in range(3):
                lanes = pl.ds(col * GROUP + at * 128, 128)
                taps_ref[tap : tap + 1, lanes] = params_ref[col, 3 * tap + at : 3 * tap + at + 1, :]
        for at in range(3):
            lanes = pl.ds(col * GROUP + at * 128, 128)
            skip_ref[:, lanes] = params_ref[col, 12 + at : 13 + at, :]
            gain_ref[:, lanes] = params_ref[col, 15 + at : 16 + at, :]
        bias_ref[col : col + 1, :] = params_ref[col, 18:19, :]
        decay_ref[col : col + 1, :] = params_ref[col, 19:20, :]
    share_rows(full_ref, 0)
    relays(order[22:26])
    shared_rows(full_ref, 0)
    store(w_ref, w_hbm)
    store(full_ref, x_hbm)

    rows = full_ref.shape[0]

    @pl.loop(0, rows // 128)
    def _(at):
        here = pl.ds(pl.multiple_of(at * 128, 128), 128)
        values = wide(full_ref[here, :])
        size = 1.0 / values.shape[1]
        root = lax.rsqrt(jnp.sum(values * values, axis=1, keepdims=True) * size + EPS)
        normed_ref[here, :] = low(values * root * gain_in[...])

    store(normed_ref, normed_hbm)

    def project(begin, end):
        @pl.loop(0, (end - begin) // 256)
        def _(at):
            cols = pl.ds(pl.multiple_of(begin + at * 256, 128), 256)
            proj_ref[:, cols] = dot(normed_ref[...], w_ref[:, cols])

    def attend(col):
        lanes = pl.ds(col * 128, 128)
        attention_forward_kernel(
            len_ref,
            proj_ref.at[:, pl.ds(col * width + 768, 128)],
            proj_ref.at[:, pl.ds(2 * width + 2 * N, 128)],
            cos_ref,
            sin_ref,
            attn_ref.at[:, lanes],
            sums_ref.at[:, lanes],
        )

    def chunks(begin, end):
        @pl.loop(begin, end)
        def _(at):
            here = pl.ds(pl.multiple_of(at * CHUNK, CHUNK), CHUNK)
            mamba_chunk(
                proj_ref.at[here, :],
                attn_ref.at[here, :],
                taps_ref,
                bias_ref,
                decay_ref,
                skip_ref,
                gain_ref,
                both_ref.at[here, :],
                out_ref.at[here, :],
                states_ref.at[at],
                buf_ref,
                state_ref,
            )

    project(0, 1024)
    serve(order[6:10])
    issue_downs()
    project(1024, 2304)
    last = pl.ds(2304, proj_ref.shape[1] - 2304)
    proj_ref[:, last] = dot(normed_ref[...], w_ref[:, last])
    store(proj_ref, proj_hbm)
    relays(order[6:8])
    attend(0)
    relays(order[8:10])
    serve(order[12:14])
    attend(1)
    serve(order[14:18])
    send_rows(og_ref, og_full, 1)
    mamba_start(buf_ref, state_ref)
    count = rows // CHUNK
    chunks(0, count // 4)
    relays(order[12:14])
    chunks(count // 4, count // 2)
    complete(order[6:10])
    store(v_ref, v_hbm)
    relays(order[14:18])
    chunks(count // 2, count)

    @pl.loop(0, 4)
    def _(at):
        here = pl.ds(pl.multiple_of(at * 256, 256), 256)
        mixed_ref[here, :] = low(dot_nt(both_ref[here, :], v_ref[...]))

    send(mixed_ref, other_ref, mixed_sem.at[0], mixed_sem.at[1], {"core": 1 - core})
    share_rows(og_full, 1)
    complete(order[10:26])
    shared_rows(og_full, 1)
    landed(other_ref, mixed_sem.at[1])
    for src, dst, sem in stores:
        pltpu.make_async_copy(src, dst, sem).wait()
    for src, sem in started:
        landed(src, sem)

    @pl.when(target == core)
    def _():
        for step in range(1, 4):
            landed(small_ref, param_out.at[step])

    @pl.when(target != core)
    def _():
        landed(pack_ref, out_sem.at[0])
        landed(next_ref, out_sem.at[4])

    for kind, (src_ref, dst_ref) in enumerate(((x_ref, full_ref), (og_ref, og_full))):
        for number, here, src, _, _, _ in row_parts(src_ref, dst_ref):

            @pl.when(jnp.logical_not(here))
            def _():
                landed(src, row_out.at[kind, number])


def front(
    pack,
    following,
    ups,
    downs,
    shared,
    x_rows,
    small,
    out_grad,
    state_taps,
    gain,
    seq_len,
    cosine,
    sine,
):
    share, width = pack.shape
    narrow = following.shape[1]
    rest = shared.shape[2]
    rows = x_rows.shape[1] * 4
    model = x_rows.shape[2]
    columns = 2 * width + rest
    dma = pltpu.SemaphoreType.DMA
    any_space = pl.BlockSpec(memory_space=pl.ANY)
    near = pl.BlockSpec(memory_space=pltpu.VMEM)
    f32, bf16 = jnp.float32, pack.dtype
    return pl.pallas_call(
        front_kernel,
        in_specs=[any_space] * 8
        + [near, near, pl.BlockSpec(memory_space=pltpu.SMEM), near, near],
        out_specs=[any_space] * 8 + [near] * 11,
        out_shape=[
            jax.ShapeDtypeStruct((8 * share, columns), bf16),
            jax.ShapeDtypeStruct((8 * share, 2 * narrow), bf16),
            jax.ShapeDtypeStruct((8 * share, 2 * ups.shape[1]), bf16),
            jax.ShapeDtypeStruct((8 * share, 4 * downs.shape[2]), bf16),
            jax.ShapeDtypeStruct((rows, model), bf16),
            jax.ShapeDtypeStruct((rows, model), bf16),
            jax.ShapeDtypeStruct((rows, columns), f32),
            jax.ShapeDtypeStruct((rows, model), bf16),
            jax.ShapeDtypeStruct((KCONV, CONV), f32),
            jax.ShapeDtypeStruct((2, 128), f32),
            jax.ShapeDtypeStruct((2, 128), f32),
            jax.ShapeDtypeStruct((1, 2 * GROUP), f32),
            jax.ShapeDtypeStruct((1, 2 * GROUP), f32),
            jax.ShapeDtypeStruct((rows, 256), f32),
            jax.ShapeDtypeStruct((rows, 1024), bf16),
            jax.ShapeDtypeStruct((rows, 2 * GROUP), f32),
            jax.ShapeDtypeStruct((rows // CHUNK, N, 2 * GROUP), f32),
            jax.ShapeDtypeStruct((rows, 8 * share), bf16),
            jax.ShapeDtypeStruct((rows, 8 * share), bf16),
        ],
        scratch_shapes=[
            pltpu.VMEM((8 * share, columns), bf16),
            pltpu.VMEM((8 * share, 2 * narrow), bf16),
            pltpu.VMEM((rows, model), bf16),
            pltpu.VMEM((rows, model), bf16),
            pltpu.VMEM((rows, columns), f32),
            pltpu.VMEM((rows, 256), bf16),
            pltpu.VMEM((2,) + small.shape, f32),
            pltpu.VMEM((CHUNK + 8, CONV), f32),
            pltpu.VMEM((N, 2 * GROUP), f32),
            dma((1,)),
            dma((8,)),
        ]
        + [dma((26,))] * 9
        + [dma((2, 4))] * 4
        + [dma((4,))] * 2
        + [dma((2, 8)), dma((5,)), dma((2,))],
        compiler_params=pltpu.CompilerParams(
            collective_id=1, has_side_effects=True, vmem_limit_bytes=BIG
        ),
        cost_estimate=cost(120),
        name="front",
    )(
        pack,
        following,
        ups,
        downs,
        shared,
        x_rows,
        small,
        out_grad,
        state_taps,
        gain,
        seq_len,
        cosine,
        sine,
    )


def collect_kernel(*refs):
    (normed_ref, dproj_ref, weight_hbm, mixed_hbm, both_hbm, x_hbm, hidden_hbm) = refs[:7]
    (gain_ref, small_ref) = refs[7:9]
    (mixer_out, query_out, step_out, shared_ref, total_ref, back_ref) = refs[9:15]
    (mamba_out, attn_out) = refs[15:17]
    (weight_ref, mixed_ref, both_ref, x_ref, hidden_ref, grad_ref, next_ref) = refs[17:24]
    (norm_ref, norm_in, rows_ref, in_ref, next_in, sum_ref, next_sum) = refs[24:31]
    (piece_ref, next_buf, pair_ref, mix_ref, near_ref, far_ref) = refs[31:37]
    (in_sem, out_sem, piece_sem, piece_out, pair_sem, mix_sem, mix_out) = refs[37:44]
    (near_sem, near_out, far_sem, far_out, row_sem, row_out, load_sem, norm_sem) = refs[44:]
    plane = lax.axis_index("plane")
    core = lax.axis_index("core")
    place = lax.axis_index("tensor")
    xside = plane + 1 - 2 * (plane % 2)
    yside = plane + 2 - 4 * (plane // 2)
    across = xside + 2 - 4 * (xside // 2)
    share = pair_ref.shape[0]
    width = piece_ref.shape[2]
    rest = grad_ref.shape[1] - 2 * width

    loads = [
        (weight_hbm, weight_ref),
        (mixed_hbm, mixed_ref),
        (both_hbm, both_ref),
        (x_hbm.at[:, core], x_ref),
        (hidden_hbm.at[:, core], hidden_ref),
    ]
    for number, (src, dst) in enumerate(loads):
        pltpu.make_async_copy(src, dst, load_sem.at[number]).start()

    def loaded(number):
        src, dst = loads[number]
        pltpu.make_async_copy(src, dst, load_sem.at[number]).wait()

    barrier = pltpu.get_barrier_semaphore()
    for step in range(4):
        for side in range(2):
            if step or side:
                pl.semaphore_signal(
                    barrier,
                    inc=1,
                    device_id={"core": (core + side) % 2, "tensor": (place + step) % 4},
                    device_id_type=MESH,
                )
    for neighbour in (xside, yside):
        pl.semaphore_signal(
            barrier, inc=1, device_id={"plane": neighbour}, device_id_type=MESH
        )
    pl.semaphore_wait(barrier, 9)

    started = []

    def send(src, dst, send_sem, recv_sem, device):
        pltpu.make_async_remote_copy(
            src_ref=src,
            dst_ref=dst,
            send_sem=send_sem,
            recv_sem=recv_sem,
            device_id=device,
            device_id_type=MESH,
        ).start()
        started.append((src, send_sem))

    narrow = next_ref.shape[1] // 2
    spans = [(0, 2 * width, rest), (0, 0, width), (0, width, width)]
    spans += [(1, 0, narrow), (1, narrow, narrow)]

    def block(at, part, span):
        rows = pl.ds(pl.multiple_of(at * 2 * share + part * share, share), share)
        return (grad_ref, next_ref)[span[0]].at[rows, pl.ds(*span[1:])]

    def held(slot, span):
        return (in_ref, next_in)[span[0]].at[slot, :, pl.ds(*span[1:])]

    def summed(part, span):
        return (sum_ref, next_sum)[span[0]].at[part, :, pl.ds(*span[1:])]

    def begin(number):
        span = spans[number]
        send(
            block(across, 0, span),
            held(0, span),
            out_sem.at[0, number],
            in_sem.at[0, number],
            {"plane": xside},
        )
        send(
            block(across, 1, span),
            held(1, span),
            out_sem.at[1, number],
            in_sem.at[1, number],
            {"plane": yside},
        )
        send(
            block(xside, 0, span),
            held(2, span),
            out_sem.at[2, number],
            in_sem.at[2, number],
            {"plane": xside},
        )
        send(
            block(yside, 1, span),
            held(3, span),
            out_sem.at[3, number],
            in_sem.at[3, number],
            {"plane": yside},
        )

    def work(number):
        kind, begin_at, size = spans[number]
        left = (normed_ref, mixed_ref)[kind]
        right = (dproj_ref, both_ref)[kind]
        result = (grad_ref, next_ref)[kind]
        tile = 256 if size % 256 == 0 else size

        @pl.loop(0, size // tile)
        def _(at):
            cols = pl.ds(pl.multiple_of(begin_at + at * tile, 128), tile)
            result[:, cols] = low(dot_tn(left[...], right[:, cols]))

    seq = place % 2
    owner = place // 2
    dst_rows = back_ref.at[seq, pl.ds(pl.multiple_of(core * share, share), share)]

    def send_back():
        for step in (2, 1, 3):
            at = (place + step) % 4
            send(
                rows_ref.at[at],
                dst_rows,
                row_out.at[step],
                row_sem.at[seq * 2 + core],
                {"core": owner, "tensor": at},
            )

        @pl.when(owner == core)
        def _():
            pltpu.make_async_copy(
                rows_ref.at[place], dst_rows, row_sem.at[seq * 2 + core]
            ).start()

        @pl.when(owner != core)
        def _():
            pltpu.make_async_remote_copy(
                src_ref=rows_ref.at[place],
                dst_ref=dst_rows,
                send_sem=row_out.at[0],
                recv_sem=row_sem.at[seq * 2 + core],
                device_id={"core": 1 - core},
                device_id_type=MESH,
            ).start()

    def norm_product():
        loaded(0)
        for at in range(4):
            rows = pl.ds(at * 2 * share, 2 * share)
            part = low(dot_nt(dproj_ref[rows, :], weight_ref[...]))
            norm_ref[at, 0] = part[:share]
            norm_ref[at, 1] = part[share:]
        send(
            norm_ref.at[:, 1 - core],
            norm_in,
            norm_sem.at[0],
            norm_sem.at[1],
            {"core": 1 - core},
        )

    def norm_back():
        loaded(3)
        loaded(4)
        landed(norm_in, norm_sem.at[1])
        gain_total = jnp.zeros((1, x_ref.shape[2]), jnp.float32)
        for at in range(4):
            grad = wide(norm_ref[at, core]) + wide(norm_in[at])
            values = wide(x_ref[at])
            size = 1.0 / values.shape[1]
            root = lax.rsqrt(jnp.sum(values * values, axis=1, keepdims=True) * size + EPS)
            scaled = grad * gain_ref[...]
            inner = jnp.sum(values * scaled, axis=1, keepdims=True) * size
            rows_ref[at] = low(
                hidden_ref[at] + root * scaled - values * (root * root * root * inner)
            )
            gain_total = gain_total + jnp.sum(values * root * grad, axis=0, keepdims=True)
        near_ref[5] = small_ref[...]
        for at in range(gain_total.shape[1] // 128):
            near_ref[5, at : at + 1, :] = gain_total[:, at * 128 : (at + 1) * 128]

    def pass_on(number):
        span = spans[number]
        landed(held(0, span), in_sem.at[0, number])
        held(0, span)[...] = low(wide(held(0, span)[...]) + wide(block(yside, 0, span)[...]))
        send(
            held(0, span),
            held(5, span),
            out_sem.at[4, number],
            in_sem.at[5, number],
            {"plane": yside},
        )
        landed(held(1, span), in_sem.at[1, number])
        held(1, span)[...] = low(wide(held(1, span)[...]) + wide(block(xside, 1, span)[...]))
        send(
            held(1, span),
            held(4, span),
            out_sem.at[5, number],
            in_sem.at[4, number],
            {"plane": xside},
        )

    def finish(number):
        span = spans[number]
        landed(held(2, span), in_sem.at[2, number])
        landed(held(5, span), in_sem.at[5, number])
        summed(0, span)[...] = low(
            wide(block(plane, 0, span)[...]) + wide(held(2, span)[...]) + wide(held(5, span)[...])
        )
        landed(held(3, span), in_sem.at[3, number])
        landed(held(4, span), in_sem.at[4, number])
        summed(1, span)[...] = low(
            wide(block(plane, 1, span)[...]) + wide(held(3, span)[...]) + wide(held(4, span)[...])
        )

    def send_pieces(number):
        span = spans[number]
        kind, col = span[0], span[1] // span[2]
        buf = (piece_ref, next_buf)[kind]
        goal = 2 * core + col
        for part in range(2):
            src = summed(part, span)
            here = jnp.logical_and(core == part, goal == place)

            @pl.when(here)
            def _():
                pltpu.make_async_copy(src, buf.at[place], piece_sem.at[kind, place]).start()

            @pl.when(jnp.logical_not(here))
            def _():
                pltpu.make_async_remote_copy(
                    src_ref=src,
                    dst_ref=buf.at[place],
                    send_sem=piece_out.at[kind, 2 * col + part],
                    recv_sem=piece_sem.at[kind, place],
                    device_id={"core": part, "tensor": goal},
                    device_id_type=MESH,
                ).start()

    rest_cols = pl.ds(2 * width, rest)
    state = rest * 2 // 3

    def pair_up():
        send(
            sum_ref.at[1 - core, :, rest_cols],
            pair_ref,
            pair_sem.at[0],
            pair_sem.at[1],
            {"core": 1 - core},
        )

    def mix():
        landed(pair_ref, pair_sem.at[1])
        mine = sum_ref[core, :, rest_cols]
        mix_ref[place, :, 0:state] = low(wide(mine[:, :state]) + wide(pair_ref[:, :state]))
        first = core == 0
        mix_ref[place, :, state:rest] = jnp.where(first, mine[:, state:], pair_ref[:, state:])
        mix_ref[place, :, rest:] = jnp.where(first, pair_ref[:, state:], mine[:, state:])
        own_mix = mix_ref.at[place]
        for step in (2, 1, 3):
            send(
                own_mix,
                own_mix,
                mix_out.at[step],
                mix_sem.at[place],
                {"tensor": (place + step) % 4},
            )

    work(1)
    begin(1)
    norm_product()
    work(2)
    begin(2)
    pass_on(1)
    norm_back()
    send_back()
    send(near_ref.at[5], near_ref.at[0], near_out.at[0], near_sem.at[0], {"plane": xside})
    work(0)
    begin(0)
    finish(1)
    send_pieces(1)
    loaded(1)
    loaded(2)
    work(3)
    pass_on(2)
    begin(3)
    landed(near_ref.at[0], near_sem.at[0])
    near_ref[3] = near_ref[5] + near_ref[0]
    send(near_ref.at[3], near_ref.at[1], near_out.at[1], near_sem.at[1], {"plane": yside})
    finish(2)
    send_pieces(2)
    work(4)
    pass_on(0)
    begin(4)
    landed(near_ref.at[1], near_sem.at[1])
    near_ref[4] = near_ref[3] + near_ref[1]
    send(near_ref.at[4], near_ref.at[2], near_out.at[2], near_sem.at[2], {"core": 1 - core})
    finish(0)
    pair_up()
    pass_on(3)
    mix()
    landed(near_ref.at[2], near_sem.at[2])
    far_ref[place] = near_ref[4] + near_ref[2]
    own_far = far_ref.at[place]
    for step in (2, 1, 3):
        send(
            own_far,
            own_far,
            far_out.at[step],
            far_sem.at[place],
            {"tensor": (place + step) % 4},
        )
    finish(3)
    send_pieces(3)
    pass_on(4)
    finish(4)
    send_pieces(4)

    for step in (1, 2, 3):
        at = (place + step) % 4
        landed(mix_ref.at[at], mix_sem.at[at])
        landed(far_ref.at[at], far_sem.at[at])
    shared_ref[...] = (
        wide(mix_ref[0]) + wide(mix_ref[1]) + wide(mix_ref[2]) + wide(mix_ref[3])
    )
    total_ref[...] = (far_ref[0] + far_ref[1]) + (far_ref[2] + far_ref[3])
    def gathered(buf, kind):
        for at in range(4):
            landed(buf.at[at], piece_sem.at[kind, at])
        return wide(buf[0]) + wide(buf[1]) + wide(buf[2]) + wide(buf[3])

    one = gathered(piece_ref, 0)
    cut = mixer_out.shape[1]
    mixer_out[...] = one[:, :cut]
    query_out[...] = one[:, cut : cut + query_out.shape[1]]
    step_out[...] = one[:, cut + query_out.shape[1] :]
    both = gathered(next_buf, 1).T
    mamba_out[...] = both[: mamba_out.shape[0]]
    attn_out[...] = both[mamba_out.shape[0] :]
    for at in range(4):
        landed(dst_rows, row_sem.at[at])
    for src, sem in started:
        landed(src, sem)

    @pl.when(owner != core)
    def _():
        landed(rows_ref.at[place], row_out.at[0])

    for span in spans[1:]:
        col = span[1] // span[2]
        for part in range(2):
            here = jnp.logical_and(core == part, 2 * core + col == place)

            @pl.when(jnp.logical_not(here))
            def _():
                landed(summed(part, span), piece_out.at[span[0], 2 * col + part])


def collect(normed, dproj, weight, mixed, both, x_rows, hidden, gain, small, sizes):
    chans, queries, width = sizes
    share = weight.shape[0] // 8
    model = weight.shape[0]
    columns = weight.shape[1]
    rest = columns - 2 * width
    narrow = both.shape[1] // 2
    dma = pltpu.SemaphoreType.DMA
    any_space = pl.BlockSpec(memory_space=pl.ANY)
    near = pl.BlockSpec(memory_space=pltpu.VMEM)
    shared_cols = rest + rest // 3
    bf16, f32 = jnp.bfloat16, jnp.float32
    split = (4, 2, x_rows.shape[0] // 8, model)
    half = (4, x_rows.shape[0] // 8, model)
    return pl.pallas_call(
        collect_kernel,
        in_specs=[near, near] + [any_space] * 5 + [near, near],
        out_specs=[near] * 5 + [any_space] + [near] * 2,
        out_shape=[
            jax.ShapeDtypeStruct((share, 2 * chans), f32),
            jax.ShapeDtypeStruct((share, queries), f32),
            jax.ShapeDtypeStruct((share, width - 2 * chans - queries), f32),
            jax.ShapeDtypeStruct((share, shared_cols), f32),
            jax.ShapeDtypeStruct(small.shape, f32),
            jax.ShapeDtypeStruct((2, 2 * half[1], model), bf16),
            jax.ShapeDtypeStruct((chans, share), f32),
            jax.ShapeDtypeStruct((narrow - chans, share), f32),
        ],
        scratch_shapes=[
            pltpu.VMEM(weight.shape, bf16),
            pltpu.VMEM(mixed.shape, bf16),
            pltpu.VMEM(both.shape, bf16),
            pltpu.VMEM(half, bf16),
            pltpu.VMEM(half, f32),
            pltpu.VMEM((model, columns), bf16),
            pltpu.VMEM((model, 2 * narrow), bf16),
            pltpu.VMEM(split, bf16),
            pltpu.VMEM(half, bf16),
            pltpu.VMEM(half, bf16),
            pltpu.VMEM((6, share, columns), bf16),
            pltpu.VMEM((6, share, 2 * narrow), bf16),
            pltpu.VMEM((2, share, columns), bf16),
            pltpu.VMEM((2, share, 2 * narrow), bf16),
            pltpu.VMEM((4, share, width), bf16),
            pltpu.VMEM((4, share, narrow), bf16),
            pltpu.VMEM((share, rest), bf16),
            pltpu.VMEM((4, share, shared_cols), bf16),
            pltpu.VMEM((6,) + small.shape, f32),
            pltpu.VMEM((4,) + small.shape, f32),
            dma((6, 5)),
            dma((6, 5)),
            dma((2, 4)),
            dma((2, 4)),
            dma((2,)),
            dma((4,)),
            dma((4,)),
            dma((3,)),
            dma((3,)),
            dma((4,)),
            dma((4,)),
            dma((4,)),
            dma((4,)),
            dma((5,)),
            dma((2,)),
        ],
        compiler_params=pltpu.CompilerParams(
            collective_id=2, has_side_effects=True, vmem_limit_bytes=BIG
        ),
        cost_estimate=cost(80),
        name="collect",
    )(
        normed,
        dproj,
        weight,
        mixed,
        both,
        x_rows.reshape(split),
        hidden.reshape(split),
        gain.reshape(1, -1),
        small,
    )


def rms_norm(values, gain_vec):
    return values * lax.rsqrt(jnp.mean(values * values, axis=-1, keepdims=True) + EPS) * gain_vec


def turn_tables(seq_count, head_count):
    half_dim = HEAD_SIZE // 2
    freqs = np.float32(THETA) ** (-np.arange(half_dim, dtype=np.float32) * 2.0 / HEAD_SIZE)
    angles = np.arange(seq_count, dtype=np.float32)[:, None] * freqs.astype(np.float32)[None, :]
    cosine, sine = np.cos(angles), np.sin(angles)
    return (
        jnp.asarray(np.tile(np.concatenate([cosine, cosine], axis=1), (1, head_count))),
        jnp.asarray(np.tile(np.concatenate([-sine, sine], axis=1), (1, head_count))),
    )


def swapped(values):
    return lax.ppermute(values, "core", SWAP)


def body(
    layer_in,
    seq_lengths,
    out_grad,
    norm_gain,
    mixer_weight,
    step_weight,
    state_weight,
    query_weight,
    key_value_weight,
    conv_channels,
    conv_states,
    step_bias,
    decay_log,
    skip_scale,
    group_gain,
    mamba_proj,
    attn_proj,
    ffn_gain,
    ffn_weight,
    ffn_down,
):
    core = lax.axis_index("core")
    place = lax.axis_index("tensor")
    first = core == 0
    seq_dev, rows_dev, model_dim = layer_in.shape
    groups = lax.axis_size("tensor")
    seq_total = rows_dev * groups
    half_rows = rows_dev // 2
    share = mixer_weight.shape[0]
    chans_dev = mixer_weight.shape[2]
    heads_dev = step_weight.shape[1]
    query_dev = query_weight.shape[1]
    hidden_dev = ffn_weight.shape[2]
    held = groups // 2
    step_pad = 128

    def mine(values):
        return lax.dynamic_slice_in_dim(values, core * held, held, 0)

    def other(values):
        return lax.dynamic_slice_in_dim(values, (1 - core) * held, held, 0)

    def in_order(own, others, axis):
        return jnp.where(
            first,
            jnp.concatenate([own, others], axis=axis),
            jnp.concatenate([others, own], axis=axis),
        )

    def flat(values):
        return values.transpose(1, 0, 2).reshape(values.shape[1], -1)

    spot = 2 * core + place % 2

    def positions_in(values):
        shaped = values.reshape(seq_dev, 2, half_rows, model_dim)
        keep = lax.dynamic_index_in_dim(shaped, core, 1, False)
        send = lax.dynamic_index_in_dim(shaped, 1 - core, 1, False)
        return lax.all_to_all(in_order(keep, swapped(send), 0), "tensor", 0, 0, tiled=True)

    def both_halves(own):
        both = in_order(own[:, None], swapped(own)[:, None], 1)
        return both.reshape(seq_total, model_dim)

    def positions_out(own):
        four = lax.all_to_all(own, "tensor", 0, 0, tiled=True)
        keep = lax.dynamic_slice_in_dim(four, core * seq_dev, seq_dev, 0)
        send = lax.dynamic_slice_in_dim(four, (1 - core) * seq_dev, seq_dev, 0)
        both = in_order(keep[:, None], swapped(send)[:, None], 1)
        return both.reshape(seq_dev, rows_dev, model_dim)

    def own_half(values):
        shaped = values.reshape(groups, 2, half_rows, -1)
        return lax.dynamic_index_in_dim(shaped, core, 1, False)

    def other_half(values):
        shaped = values.reshape(groups, 2, half_rows, -1)
        return lax.dynamic_index_in_dim(shaped, 1 - core, 1, False)

    out_dev = chans_dev + query_dev
    pack_two = jnp.concatenate([mamba_proj.T, attn_proj.T], axis=1)
    own_units = hidden_dev // 2
    pack_ups = jnp.concatenate([ffn_weight[:, 0], ffn_weight[:, 1]], axis=1)
    pack_downs = ffn_down.reshape(2, own_units, share).transpose(0, 2, 1)
    out_dev = chans_dev + query_dev
    pack_two = jnp.concatenate([mamba_proj.T, attn_proj.T], axis=1)
    pack_one = jnp.concatenate(
        [
            mixer_weight[:, 0],
            mixer_weight[:, 1],
            query_weight,
            jnp.pad(step_weight, ((0, 0), (0, step_pad - heads_dev))),
        ],
        axis=1,
    )
    def shared_for(at):
        pair = key_value_weight.reshape(share, 2, 2 * HEAD_SIZE)
        if not isinstance(at, int):
            pair = jnp.where(at == 0, pair, jnp.roll(pair, -HEAD_SIZE, axis=2))
            at = 0
        cols = slice(at * HEAD_SIZE, (at + 1) * HEAD_SIZE)
        return jnp.concatenate(
            [state_weight[:, 0], state_weight[:, 1], pair[:, 0, cols], pair[:, 1, cols]], axis=1
        )

    def lanes(values):
        return jnp.pad(values, (0, -values.shape[0] % 128)).reshape(-1, 128)

    small_in = jnp.concatenate(
        [
            lanes(conv_channels.reshape(-1)),
            lanes(jnp.repeat(skip_scale, HEAD_SIZE)),
            lanes(group_gain),
            lanes(step_bias),
            lanes(decay_log),
        ]
    )
    small_in = jnp.pad(small_in, ((0, -small_in.shape[0] % 8), (0, 0)))
    lengths = in_order(seq_lengths, swapped(seq_lengths), 0)
    seq_len = lengths[place]
    len_one = seq_len.reshape(1)
    valid_rows = (jnp.arange(seq_total, dtype=jnp.int32) < seq_len).astype(jnp.float32)[:, None]
    group_cols = 2 * chans_dev + query_dev + step_pad
    cosine, sine = turn_tables(seq_total, 2)
    state_taps = conv_states.reshape(KCONV, 2 * N)
    quad = lax.axis_size("plane") == 4 and groups == 4 and share == 128
    quad = quad and share == half_rows
    if quad:
        shared = jnp.stack([shared_for(0), shared_for(1)])
        (
            weight_one,
            weight_two,
            gate_up_weight,
            down_weight,
            x_low,
            normed,
            proj,
            grad_whole,
            taps,
            bias,
            decay,
            skip,
            gain,
            log_sums,
            both_low,
            state_out,
            states,
            mixed_part,
            mixed_other,
        ) = front(
            pack_one,
            pack_two,
            pack_ups,
            pack_downs,
            shared,
            layer_in,
            small_in,
            out_grad,
            state_taps,
            norm_gain.reshape(1, -1),
            len_one,
            cosine,
            sine,
        )
    else:
        x_low = both_halves(positions_in(layer_in))
        all_one = lax.all_gather(pack_one, "tensor", axis=0)
        own_one = jnp.concatenate([flat(mine(all_one)), shared_for(core)], axis=1)
        their_one = jnp.concatenate([flat(other(all_one)), shared_for(1 - core)], axis=1)
        weight_one = lax.all_gather(
            in_order(own_one, swapped(their_one), 0), "plane", axis=0, tiled=True
        )
        all_two = lax.all_gather(pack_two, "tensor", axis=0)
        weight_two = lax.all_gather(
            in_order(flat(mine(all_two)), swapped(flat(other(all_two))), 0),
            "plane",
            axis=0,
            tiled=True,
        )
        split_ups = pack_ups.reshape(share, 2, 2, own_units).transpose(2, 0, 1, 3)
        split_ups = split_ups.reshape(2, share, hidden_dev)
        rows_up, rows_down = (
            in_order(
                lax.dynamic_index_in_dim(pack, core, 0, False),
                swapped(lax.dynamic_index_in_dim(pack, 1 - core, 0, False)),
                0,
            )
            for pack in (split_ups, pack_downs)
        )
        rows_up, rows_down = (
            lax.all_gather(rows, "tensor", axis=1, tiled=True) for rows in (rows_up, rows_down)
        )
        down_weight = lax.all_gather(rows_down, "plane", axis=0, tiled=True)
        params = mine(lax.all_gather(small_in, "tensor", axis=0))
        span = chans_dev // 128

        def spread_lanes(at):
            return params[:, at : at + span].reshape(1, -1)

        taps = jnp.concatenate([spread_lanes(span * tap) for tap in range(KCONV)], axis=0)
        taps = jnp.concatenate([taps, state_taps], axis=1)
        skip, gain = spread_lanes(KCONV * span), spread_lanes((KCONV + 1) * span)
        bias, decay = params[:, (KCONV + 2) * span], params[:, (KCONV + 2) * span + 1]
        normed = low(rms_norm(wide(x_low), norm_gain))
        proj = dot(normed, weight_one)
        attn, log_sums = attention_forward(len_one, proj, cosine, sine, group_cols)
        both_low, state_out, states = mamba_forward(proj, attn, taps, bias, decay, skip, gain)
        gate_up_weight = lax.all_gather(rows_up, "plane", axis=0, tiled=True)
        grad_whole = both_halves(positions_in(out_grad))
        mixed_part = low(dot_nt(both_low, weight_two))
        mixed_other = swapped(mixed_part)

    grad_low, hidden, normed_two, act_low, gate_up_low = ffn_middle(
        len_one,
        x_low,
        mixed_part,
        mixed_other,
        ffn_gain.reshape(1, -1),
        grad_whole,
        gate_up_weight,
        down_weight,
        groups,
    )
    grad_three = ffn_gradients(grad_low, act_low, normed_two, gate_up_low, groups)
    grad_two_part = low(dot_nt(gate_up_low, gate_up_weight))
    ffn_part = low(dot_nt(act_low, down_weight))
    ffn_own = wide(own_half(ffn_part)) + wide(swapped(other_half(ffn_part)))
    out_own = own_half(valid_rows) * (own_half(hidden) + ffn_own)

    grad_hidden, grad_mixed, back, grad_ffn_gain = hidden_backward(
        hidden,
        grad_two_part,
        swapped(grad_two_part),
        grad_low,
        ffn_gain.reshape(1, -1),
        weight_two,
    )
    grad_ffn_gain = grad_ffn_gain.reshape(-1)

    def scatter(values):
        return lax.psum_scatter(values, "plane", scatter_dimension=0, tiled=True)

    def to_groups(values):
        by_part = values.reshape(2, share, held, -1).transpose(0, 2, 1, 3)
        own = lax.dynamic_index_in_dim(by_part, core, 0, False)
        theirs = swapped(lax.dynamic_index_in_dim(by_part, 1 - core, 0, False))
        whole = in_order(own, theirs, 0)
        return wide(lax.psum_scatter(whole, "tensor", scatter_dimension=0, tiled=True)[0])

    units = lax.psum_scatter(scatter(grad_three), "tensor", scatter_dimension=1, tiled=True)
    units = units.reshape(2, share, -1)
    own_part = lax.dynamic_index_in_dim(units, core, 0, True)
    their_part = swapped(lax.dynamic_index_in_dim(units, 1 - core, 0, True))
    units = wide(in_order(own_part, their_part, 0))
    sum_up = units[:, :, :hidden_dev].reshape(2, share, 2, own_units).transpose(1, 2, 0, 3)
    sum_down = units[:, :, hidden_dev:].transpose(0, 2, 1).reshape(hidden_dev, share)

    grad_q, grad_kv = attention_backward(
        len_one, proj, cosine, sine, log_sums, back, group_cols, 3
    )
    layer_out = positions_out(low(out_own))
    proj_grad, grad_taps, grad_gain, grad_skip_cols, grad_bias, grad_decay = mamba_backward(
        proj, state_out, states, back, grad_q, grad_kv, taps, bias, decay, skip, gain
    )
    edge = held * group_cols
    grad_skip = jnp.sum(grad_skip_cols.reshape(held, heads_dev, HEAD_SIZE), axis=-1)
    chan_taps = grad_taps[:, : held * chans_dev].reshape(KCONV, held, chans_dev)
    group_small = jnp.concatenate(
        [
            chan_taps.transpose(1, 0, 2).reshape(held, -1),
            grad_bias[:, :heads_dev],
            grad_decay[:, :heads_dev],
            grad_skip,
            grad_gain.reshape(held, -1),
        ],
        axis=1,
    )
    small_groups = in_order(group_small, jnp.zeros_like(group_small), 0)
    small_out = jnp.concatenate(
        [
            jnp.zeros_like(norm_gain),
            grad_ffn_gain,
            grad_taps[:, held * chans_dev :].reshape(-1),
            small_groups.reshape(-1),
        ]
    )
    if quad:
        small_size = small_out.shape[0]
        small_room = -(-small_size // 1024) * 1024
        (
            sum_mixer,
            sum_query,
            sum_step,
            shared_sum,
            small_sum,
            input_grad,
            sum_mamba,
            sum_attn,
        ) = collect(
            normed,
            proj_grad,
            weight_one,
            grad_mixed,
            both_low,
            x_low,
            grad_hidden,
            norm_gain,
            jnp.pad(small_out, (0, small_room - small_size)).reshape(-1, 128),
            (chans_dev, query_dev, group_cols),
        )
        small_sum = small_sum.reshape(-1)[:small_size]
    else:
        grad_one = low(dot_tn(normed, proj_grad))
        grad_norm_part = low(dot_nt(proj_grad, weight_one))
        grad_norm_own = wide(own_half(grad_norm_part)) + wide(swapped(other_half(grad_norm_part)))
        x_own = wide(own_half(x_low))
        r_one = lax.rsqrt(jnp.mean(x_own * x_own, axis=-1, keepdims=True) + EPS)
        scaled = grad_norm_own * norm_gain
        grad_x = low(
            own_half(grad_hidden)
            + r_one * scaled
            - x_own * (r_one**3 * jnp.mean(x_own * scaled, axis=-1, keepdims=True))
        )
        grad_norm_gain = jnp.sum(x_own * r_one * grad_norm_own, axis=(0, 1))
        small_out = small_out.at[:model_dim].set(grad_norm_gain)
        part_one = scatter(grad_one)
        both_parts = part_one[:, edge:].reshape(2, share, -1)
        own_rest = lax.dynamic_index_in_dim(both_parts, core, 0, False)
        their_rest = swapped(lax.dynamic_index_in_dim(both_parts, 1 - core, 0, False))
        shared_own = wide(own_rest[:, : 2 * N]) + wide(their_rest[:, : 2 * N])
        kv_both = in_order(own_rest[:, 2 * N :], their_rest[:, 2 * N :], 1)
        shared_low = jnp.concatenate([low(shared_own), kv_both], axis=1)
        shared_sum = jnp.sum(wide(lax.all_gather(shared_low, "tensor", axis=0)), axis=0)
        sum_one = to_groups(part_one[:, :edge])
        sum_mixer = sum_one[:, : 2 * chans_dev]
        sum_query = sum_one[:, 2 * chans_dev : 2 * chans_dev + query_dev]
        sum_step = sum_one[:, 2 * chans_dev + query_dev :]
        sum_two = to_groups(scatter(low(dot_tn(grad_mixed, both_low)))).T
        sum_mamba, sum_attn = sum_two[:chans_dev], sum_two[chans_dev:]
        input_grad = positions_out(grad_x)
        small_sum = lax.psum(small_out, ("plane", "core", "tensor"))
    kv_sum = shared_sum[:, 2 * N :].reshape(share, 2, 2, HEAD_SIZE).transpose(0, 2, 1, 3)
    group_sum = lax.dynamic_index_in_dim(
        small_sum[2 * model_dim + KCONV * 2 * N :].reshape(groups, -1), place, 0, False
    )
    pieces = []
    at = 0
    for size in (KCONV * chans_dev, heads_dev, heads_dev, heads_dev, chans_dev):
        pieces.append(group_sum[at : at + size])
        at += size

    return (
        layer_out,
        input_grad,
        small_sum[:model_dim],
        sum_mixer.reshape(share, 2, chans_dev),
        sum_step[:, :heads_dev],
        shared_sum[:, : 2 * N].reshape(share, 2, N),
        sum_query,
        kv_sum.reshape(share, 2, 2 * HEAD_SIZE),
        pieces[0].reshape(KCONV, chans_dev),
        small_sum[2 * model_dim : 2 * model_dim + KCONV * 2 * N].reshape(KCONV, 2, N),
        pieces[1],
        pieces[2],
        pieces[3],
        pieces[4],
        sum_mamba,
        sum_attn,
        small_sum[model_dim : 2 * model_dim],
        sum_up.reshape(share, 2, hidden_dev),
        sum_down,
    )


def solution(mesh):
    rows, columns = mesh.devices.shape
    fine = Mesh(mesh.devices.reshape(rows // 2, 2, columns), ("plane", "core", "tensor"))
    dp = ("plane", "core")
    return jax.shard_map(
        body,
        mesh=fine,
        in_specs=(
            P(dp, "tensor", None),
            P(dp),
            P(dp, "tensor", None),
            P(),
            P(dp, None, "tensor"),
            P(dp, "tensor"),
            P(dp, None, None),
            P(dp, "tensor"),
            P(dp, None, None),
            P(None, "tensor"),
            P(),
            P("tensor"),
            P("tensor"),
            P("tensor"),
            P("tensor"),
            P("tensor", dp),
            P("tensor", dp),
            P(),
            P(dp, None, "tensor"),
            P("tensor", dp),
        ),
        out_specs=(
            P(dp, "tensor", None),
            P(dp, "tensor", None),
            P(),
            P(dp, None, "tensor"),
            P(dp, "tensor"),
            P(dp, None, None),
            P(dp, "tensor"),
            P(dp, None, None),
            P(None, "tensor"),
            P(),
            P("tensor"),
            P("tensor"),
            P("tensor"),
            P("tensor"),
            P("tensor", dp),
            P("tensor", dp),
            P(),
            P(dp, None, "tensor"),
            P("tensor", dp),
        ),
        check_vma=False,
    )
```

```python
import jax
import jax.numpy as jnp
import numpy as np
from jax import lax
from jax.experimental import pallas as pl
from jax.experimental.pallas import tpu as pltpu
from jax.sharding import Mesh
from jax.sharding import PartitionSpec as P

HEAD_SIZE = 64
N = 128
KCONV = 4
GH = 6
EPS = 1e-05
THETA = 10000.0
MASKED = -1e30
SWAP = [(0, 1), (1, 0)]


def low(values):
    return values.astype(jnp.bfloat16)


def wide(values):
    return values.astype(jnp.float32)


def dot(left, right):
    return jnp.dot(left, right, preferred_element_type=jnp.float32)


def dot_nt(left, right):
    return lax.dot_general(
        left, right, (((1,), (1,)), ((), ())), preferred_element_type=jnp.float32
    )


def dot_tn(left, right):
    return lax.dot_general(
        left, right, (((0,), (0,)), ((), ())), preferred_element_type=jnp.float32
    )


def dot_fine(left, right):
    high = low(right)
    rest = right - wide(high)
    mid = low(rest)
    last = low(rest - wide(mid))
    return dot(left, high) + dot(left, mid) + dot(left, last)


def dot_by(left, right):
    high = low(left)
    rest = low(left - wide(high))
    return dot(high, right) + dot(rest, right)


def sigmoid(values):
    return 1.0 / (1.0 + jnp.exp(-values))


def turn(values, cosine, sine):
    lane = lax.broadcasted_iota(jnp.int32, values.shape, 1)
    half = HEAD_SIZE // 2
    up = pltpu.roll(values, 128 - half, 1)
    down = pltpu.roll(values, half, 1)
    return values * cosine + jnp.where(lane % HEAD_SIZE < half, up, down) * sine


def turn_back(values, cosine, sine):
    lane = lax.broadcasted_iota(jnp.int32, values.shape, 1)
    half = HEAD_SIZE // 2
    turned = values * sine
    up = pltpu.roll(turned, 128 - half, 1)
    down = pltpu.roll(turned, half, 1)
    return values * cosine + jnp.where(lane % HEAD_SIZE < half, up, down)


def cost(micros):
    return pl.CostEstimate(flops=int(micros * 1e9), bytes_accessed=0, transcendentals=0)


SCALE = HEAD_SIZE ** (-0.5)
ROWS = 256


def key_value_parts(kv, cosine, sine):
    lane = lax.broadcasted_iota(jnp.int32, kv.shape, 1)
    key = jnp.where(lane < HEAD_SIZE, turn(kv, cosine, sine), 0.0)
    value = jnp.where(lane < HEAD_SIZE, 0.0, kv)
    keys = (low(key), low(pltpu.roll(key, HEAD_SIZE, 1)))
    values = (low(pltpu.roll(value, HEAD_SIZE, 1)), low(value))
    return keys, values


def block_scores(query, keys, begin, seq_len):
    scores = dot_nt(query, keys)
    row = lax.broadcasted_iota(jnp.int32, (scores.shape[0], 1), 0) + begin
    col = lax.broadcasted_iota(jnp.int32, scores.shape, 1)
    return jnp.where(col < jnp.minimum(row + 1, seq_len), scores, MASKED)


def attention_forward_kernel(len_ref, q_ref, kv_ref, cos_ref, sin_ref, out_ref, sum_ref):
    seq_len = len_ref[0]
    cosine, sine = cos_ref[...], sin_ref[...]
    keys, values = key_value_parts(kv_ref[...], cosine, sine)
    query = low(turn(q_ref[...], cosine, sine) * SCALE)
    rows = query.shape[0]
    lane = lax.broadcasted_iota(jnp.int32, (ROWS, 128), 1)
    for begin in range(0, rows, ROWS):
        end = begin + ROWS
        outs, sums = [], []
        for head in range(2):
            scores = block_scores(query[begin:end], keys[head][:end], begin, seq_len)
            peak = jnp.max(scores, axis=1, keepdims=True)
            exps = jnp.exp(scores - peak)
            total = jnp.sum(exps, axis=1, keepdims=True)
            probs = low(exps * (1.0 / total))
            outs.append(dot(probs, values[head][:end]))
            sums.append(peak + jnp.log(total))
        out_ref[begin:end, :] = low(outs[0] + outs[1])
        sum_ref[begin:end, :] = jnp.where(lane < HEAD_SIZE, sums[0], sums[1])


def attention_backward_kernel(
    len_ref, q_ref, kv_ref, cos_ref, sin_ref, sum_ref, grad_ref, dq_ref, dkv_ref, dk_acc, dv_acc
):
    seq_len = len_ref[0]
    cosine, sine = cos_ref[...], sin_ref[...]
    keys, values = key_value_parts(kv_ref[...], cosine, sine)
    query = low(turn(q_ref[...], cosine, sine) * SCALE)
    query_t = query.T
    rows = query.shape[0]
    group = pl.program_id(0)
    grad = low(grad_ref[...])
    grad_t = grad.T

    @pl.when(group == 0)
    def _():
        dk_acc[...] = jnp.zeros_like(dk_acc)
        dv_acc[...] = jnp.zeros_like(dv_acc)

    for begin in range(0, rows, ROWS):
        end = begin + ROWS
        dq = jnp.zeros((ROWS, 128), jnp.float32)
        for head in range(2):
            lanes = slice(head * HEAD_SIZE, (head + 1) * HEAD_SIZE)
            scores = block_scores(query[begin:end], keys[head][:end], begin, seq_len)
            at = head * HEAD_SIZE
            probs = jnp.exp(scores - sum_ref[begin:end, at : at + 1])
            dv_acc[:, :end] += dot(grad_t[lanes, begin:end], low(probs))
            dp = dot_nt(grad[begin:end], values[head][:end])
            inner = jnp.sum(probs * dp, axis=1, keepdims=True)
            ds = low(probs * (dp - inner))
            dq = dq + dot(ds, keys[head][:end])
            dk_acc[:, :end] += dot(query_t[lanes, begin:end], ds)
        dq = turn_back(dq * SCALE, cosine[begin:end], sine[begin:end])
        dq_ref[begin:end, :] = low(dq)

    @pl.when(group == pl.num_programs(0) - 1)
    def _():
        both = jnp.concatenate([dk_acc[...], dv_acc[...]], axis=0).T
        lane = lax.broadcasted_iota(jnp.int32, both.shape, 1)
        dkv_ref[...] = low(jnp.where(lane < HEAD_SIZE, turn_back(both, cosine, sine), both))


def attention_specs(rows, group_cols):
    whole = pl.BlockSpec((rows, 128), lambda g: (0, 0))
    return [
        pl.BlockSpec(memory_space=pltpu.SMEM),
        pl.BlockSpec((rows, 128), lambda g: (0, g * (group_cols // 128) + 6)),
        pl.BlockSpec((rows, 128), lambda g: (0, 2 * (group_cols // 128) + 2)),
        whole,
        whole,
    ]


BIG = 60 * 1024 * 1024


def attention_forward(seq_len, proj, cosine, sine, group_cols):
    rows = proj.shape[0]
    pairs = pl.BlockSpec((rows, 128), lambda g: (0, g))
    return pl.pallas_call(
        attention_forward_kernel,
        grid=(2,),
        in_specs=attention_specs(rows, group_cols),
        out_specs=[pairs, pairs],
        out_shape=[
            jax.ShapeDtypeStruct((rows, 256), jnp.bfloat16),
            jax.ShapeDtypeStruct((rows, 256), jnp.float32),
        ],
        compiler_params=pltpu.CompilerParams(vmem_limit_bytes=BIG),
        cost_estimate=cost(11),
        name="attention_forward",
    )(seq_len, proj, proj, cosine, sine)


def attention_backward(seq_len, proj, cosine, sine, sums, grad, group_cols, grad_at):
    rows = proj.shape[0]
    pairs = pl.BlockSpec((rows, 128), lambda g: (0, g))
    return pl.pallas_call(
        attention_backward_kernel,
        grid=(2,),
        in_specs=attention_specs(rows, group_cols)
        + [pairs, pl.BlockSpec((rows, 128), lambda g: (0, 4 * g + grad_at))],
        out_specs=[pairs, pl.BlockSpec((rows, 128), lambda g: (0, 0))],
        out_shape=[
            jax.ShapeDtypeStruct((rows, 256), jnp.bfloat16),
            jax.ShapeDtypeStruct((rows, 128), jnp.bfloat16),
        ],
        scratch_shapes=[
            pltpu.VMEM((HEAD_SIZE, rows), jnp.float32),
            pltpu.VMEM((HEAD_SIZE, rows), jnp.float32),
        ],
        compiler_params=pltpu.CompilerParams(vmem_limit_bytes=BIG),
        cost_estimate=cost(18),
        name="attention_backward",
    )(seq_len, proj, proj, cosine, sine, sums, grad)


CHUNK = 128
GROUP = GH * HEAD_SIZE
PAIRS = GH // 2
CONV = 2 * GROUP + 2 * N
SHARED = 2048


def triangle():
    row = lax.broadcasted_iota(jnp.int32, (CHUNK, CHUNK), 0)
    col = lax.broadcasted_iota(jnp.int32, (CHUNK, CHUNK), 1)
    return col <= row


def pair_lanes(values, pair):
    lane = lax.broadcasted_iota(jnp.int32, (values.shape[0], 128), 1)
    at = 2 * pair
    return jnp.where(lane < HEAD_SIZE, values[:, at : at + 1], values[:, at + 1 : at + 2])


def split_pair(values):
    lane = lax.broadcasted_iota(jnp.int32, values.shape, 1)
    empty = jnp.zeros_like(values)
    return jnp.concatenate(
        [jnp.where(lane < HEAD_SIZE, values, empty), jnp.where(lane < HEAD_SIZE, empty, values)],
        axis=0,
    )


def conv_pre(buf_ref, taps_ref, begin, size):
    total = buf_ref[5 : 5 + CHUNK, begin : begin + size] * taps_ref[0:1, begin : begin + size]
    for tap in range(1, KCONV):
        total = total + (
            buf_ref[5 + tap : 5 + tap + CHUNK, begin : begin + size]
            * taps_ref[tap : tap + 1, begin : begin + size]
        )
    return total


def load_conv(buf_ref, proj_ref):
    for group in range(2):
        at = group * 1024 + GROUP
        buf_ref[8:, group * GROUP : (group + 1) * GROUP] = proj_ref[:, at : at + GROUP]
    buf_ref[8:, 2 * GROUP :] = proj_ref[:, SHARED : SHARED + 2 * N]


def group_steps(proj_ref, bias_ref, decay_ref, group, lower):
    at = group * 1024 + 896
    raw = proj_ref[:, at : at + 128] + bias_ref[group : group + 1, :]
    step = jnp.log1p(jnp.exp(-jnp.abs(raw))) + jnp.maximum(raw, 0.0)
    rate = -jnp.exp(decay_ref[group : group + 1, :])
    cumul = dot_fine(lower, rate * step)
    return raw, step, rate, cumul


def head_decay(cumul, cumul_t, head, mask):
    spread = cumul[:, head : head + 1] - cumul_t[head : head + 1, :]
    return jnp.exp(jnp.where(mask, spread, MASKED))


def mamba_chunk(
    proj_ref,
    attn_ref,
    taps_ref,
    bias_ref,
    decay_ref,
    skip_ref,
    gain_ref,
    both_ref,
    out_ref,
    state_out,
    buf_ref,
    state_ref,
):
    load_conv(buf_ref, proj_ref)
    mask = triangle()
    lower = mask.astype(jnp.bfloat16)
    pre = conv_pre(buf_ref, taps_ref, 2 * GROUP, 2 * N)
    state_act = low(pre * sigmoid(pre))
    b_rows, c_rows = state_act[:, :N], state_act[:, N:]
    gram = dot_nt(c_rows, b_rows)
    b_cols = b_rows.T
    for group in range(2):
        cols = slice(group * GROUP, (group + 1) * GROUP)
        _, step, _, cumul = group_steps(proj_ref, bias_ref, decay_ref, group, lower)
        cumul_t = cumul.T
        last = cumul[CHUNK - 1 : CHUNK, :]
        state = state_ref[:, cols]
        state_out[:, cols] = state
        from_state = dot(c_rows, low(state))
        gated, lasts, x_ends = [], [], []
        for pair in range(PAIRS):
            at = group * GROUP + pair * 128
            pre = conv_pre(buf_ref, taps_ref, at, 128)
            chan = pre * sigmoid(pre)
            inputs = low(chan * pair_lanes(step, pair))
            mixing = jnp.concatenate(
                [
                    low(gram * head_decay(cumul, cumul_t, 2 * pair + side, mask))
                    for side in range(2)
                ],
                axis=1,
            )
            lanes = slice(pair * 128, (pair + 1) * 128)
            inner = pair_lanes(cumul, pair)
            out = dot(mixing, split_pair(inputs)) + jnp.exp(inner) * from_state[:, lanes]
            out_ref[:, at : at + 128] = out
            last_lanes = pair_lanes(last, pair)
            lasts.append(last_lanes)
            x_ends.append(low(jnp.exp(last_lanes - inner) * wide(inputs)))
            gate = proj_ref[:, group * 1024 + pair * 128 : group * 1024 + pair * 128 + 128]
            skipped = out + chan * skip_ref[:, at : at + 128]
            gated.append(skipped * (gate * sigmoid(gate)))
        state_ref[:, cols] = jnp.exp(jnp.concatenate(lasts, axis=1)) * state + dot(
            b_cols, jnp.concatenate(x_ends, axis=1)
        )
        square = jnp.sum(sum(part * part for part in gated), axis=1, keepdims=True)
        scale = lax.rsqrt(square * (1.0 / GROUP) + EPS)
        for pair in range(PAIRS):
            at = group * GROUP + pair * 128
            to = group * 512 + pair * 128
            both_ref[:, to : to + 128] = low(gated[pair] * scale * gain_ref[:, at : at + 128])
        to = group * 512 + GROUP
        both_ref[:, to : to + 128] = attn_ref[:, group * 128 : (group + 1) * 128]
    buf_ref[0:8, :] = buf_ref[CHUNK : CHUNK + 8, :]


def mamba_start(buf_ref, state_ref):
    buf_ref[0:8, :] = jnp.zeros((8, CONV), jnp.float32)
    state_ref[...] = jnp.zeros_like(state_ref)


def mamba_forward_kernel(*refs):
    @pl.when(pl.program_id(0) == 0)
    def _():
        mamba_start(*refs[-2:])

    mamba_chunk(*refs[:9], refs[9].at[0], *refs[10:])


def mamba_forward(proj, attn, taps, bias, decay, skip, gain):
    rows, columns = proj.shape
    chunks = rows // CHUNK

    def whole(value):
        return pl.BlockSpec(value.shape, lambda k: (0, 0))

    return pl.pallas_call(
        mamba_forward_kernel,
        grid=(chunks,),
        in_specs=[
            pl.BlockSpec((CHUNK, columns), lambda k: (k, 0)),
            pl.BlockSpec((CHUNK, 256), lambda k: (k, 0)),
        ]
        + [whole(value) for value in (taps, bias, decay, skip, gain)],
        out_specs=[
            pl.BlockSpec((CHUNK, 1024), lambda k: (k, 0)),
            pl.BlockSpec((CHUNK, 2 * GROUP), lambda k: (k, 0)),
            pl.BlockSpec((1, N, 2 * GROUP), lambda k: (k, 0, 0)),
        ],
        out_shape=[
            jax.ShapeDtypeStruct((rows, 1024), jnp.bfloat16),
            jax.ShapeDtypeStruct((rows, 2 * GROUP), jnp.float32),
            jax.ShapeDtypeStruct((chunks, N, 2 * GROUP), jnp.float32),
        ],
        scratch_shapes=[
            pltpu.VMEM((CHUNK + 8, CONV), jnp.float32),
            pltpu.VMEM((N, 2 * GROUP), jnp.float32),
        ],
        compiler_params=pltpu.CompilerParams(vmem_limit_bytes=BIG),
        cost_estimate=cost(14),
        name="mamba_forward",
    )(proj, attn, taps, bias, decay, skip, gain)


def silu_slope(values, sig):
    return sig * (1.0 + values * (1.0 - sig))


def mamba_backward_kernel(
    proj_ref,
    before_ref,
    out_ref,
    states_ref,
    back_ref,
    dq_ref,
    dkv_ref,
    taps_ref,
    bias_ref,
    decay_ref,
    skip_ref,
    gain_ref,
    dproj_ref,
    dtaps_ref,
    dgain_ref,
    dskip_ref,
    dbias_ref,
    ddecay_ref,
    buf_ref,
    grad_buf,
    after_ref,
    flow_ref,
):
    step_at = pl.program_id(0)

    @pl.when(step_at == 0)
    def _():
        for ref in (dtaps_ref, dgain_ref, dskip_ref, dbias_ref, ddecay_ref, after_ref, flow_ref):
            ref[...] = jnp.zeros_like(ref)
        grad_buf[CHUNK:, :] = jnp.zeros((8, CONV), jnp.float32)

    inside = jnp.where(step_at == pl.num_programs(0) - 1, 0.0, 1.0)
    for group in range(2):
        at = group * 1024 + GROUP
        buf_ref[0:8, group * GROUP : (group + 1) * GROUP] = before_ref[:, at : at + GROUP] * inside
    buf_ref[0:8, 2 * GROUP :] = before_ref[:, SHARED : SHARED + 2 * N] * inside
    load_conv(buf_ref, proj_ref)
    mask = triangle()
    lower = mask.astype(jnp.bfloat16)
    row = lax.broadcasted_iota(jnp.int32, (CHUNK, CHUNK), 0)
    col = lax.broadcasted_iota(jnp.int32, (CHUNK, CHUNK), 1)
    upper = (row <= col).astype(jnp.bfloat16)
    pre_state = conv_pre(buf_ref, taps_ref, 2 * GROUP, 2 * N)
    sig_state = sigmoid(pre_state)
    state_act = low(pre_state * sig_state)
    b_rows, c_rows = state_act[:, :N], state_act[:, N:]
    gram = dot_nt(c_rows, b_rows)
    c_cols = c_rows.T
    head_of_row = lax.broadcasted_iota(jnp.int32, (GROUP, 128), 0) // HEAD_SIZE
    head_lane = lax.broadcasted_iota(jnp.int32, (GROUP, 128), 1)
    pick = (head_of_row == head_lane).astype(jnp.bfloat16)
    dgram = jnp.zeros((CHUNK, CHUNK), jnp.float32)
    d_c = jnp.zeros((CHUNK, N), jnp.float32)
    d_b = jnp.zeros((CHUNK, N), jnp.float32)
    for group in range(2):
        raw, step, rate, cumul = group_steps(proj_ref, bias_ref, decay_ref, group, lower)
        cumul_t = cumul.T
        last = cumul[CHUNK - 1 : CHUNK, :]
        pres, sigs, chans, gates, gate_sigs, skips, gated = [], [], [], [], [], [], []
        for pair in range(PAIRS):
            at = group * GROUP + pair * 128
            pre = conv_pre(buf_ref, taps_ref, at, 128)
            sig = sigmoid(pre)
            chan = pre * sig
            gate = proj_ref[:, group * 1024 + pair * 128 : group * 1024 + pair * 128 + 128]
            gate_sig = sigmoid(gate)
            skipped = out_ref[:, at : at + 128] + chan * skip_ref[:, at : at + 128]
            pres.append(pre)
            sigs.append(sig)
            chans.append(chan)
            gates.append(gate)
            gate_sigs.append(gate_sig)
            skips.append(skipped)
            gated.append(skipped * (gate * gate_sig))
        square = jnp.sum(sum(part * part for part in gated), axis=1, keepdims=True)
        scale = lax.rsqrt(square * (1.0 / GROUP) + EPS)
        grads = []
        cross = jnp.zeros((CHUNK, 128), jnp.float32)
        for pair in range(PAIRS):
            at = group * GROUP + pair * 128
            grad = back_ref[:, group * 512 + pair * 128 : group * 512 + pair * 128 + 128]
            dgain_ref[:, at : at + 128] += jnp.sum(grad * gated[pair] * scale, axis=0, keepdims=True)
            grad = grad * gain_ref[:, at : at + 128]
            cross = cross + gated[pair] * grad
            grads.append(grad)
        cross = jnp.sum(cross, axis=1, keepdims=True) * (1.0 / GROUP) * scale * scale * scale
        cols = slice(group * GROUP, (group + 1) * GROUP)
        lane = lax.broadcasted_iota(jnp.int32, (CHUNK, 128), 1)
        after = after_ref[:, cols]
        after_low = low(after)
        state = states_ref[0, :, cols]
        from_after = dot(b_rows, after_low)
        x_ends, g_starts, lasts, flows, dsteps = [], [], [], [], []
        for pair in range(PAIRS):
            at = group * GROUP + pair * 128
            lanes = slice(pair * 128, (pair + 1) * 128)
            chan = chans[pair]
            grad = scale * grads[pair] - gated[pair] * cross
            gate, gate_sig = gates[pair], gate_sigs[pair]
            dgate = grad * skips[pair] * silu_slope(gate, gate_sig)
            to = group * 1024 + pair * 128
            dproj_ref[:, to : to + 128] = low(dgate)
            grad = grad * (gate * gate_sig)
            dskip_ref[:, at : at + 128] += jnp.sum(grad * chan, axis=0, keepdims=True)
            dchan = grad * skip_ref[:, at : at + 128]
            dout = low(grad)
            step_lanes = pair_lanes(step, pair)
            inputs = low(chan * step_lanes)
            halves = split_pair(inputs)
            decays = [head_decay(cumul, cumul_t, 2 * pair + side, mask) for side in range(2)]
            mixing = jnp.concatenate([low(gram * decay) for decay in decays], axis=1)
            dmix = dot_nt(dout, halves)
            dgram = dgram + dmix[:, :CHUNK] * decays[0] + dmix[:, CHUNK:] * decays[1]
            dinputs = dot_tn(mixing, dout)
            dinputs = jnp.where(lane < HEAD_SIZE, dinputs[:CHUNK], dinputs[CHUNK:])
            inner = pair_lanes(cumul, pair)
            last_lanes = pair_lanes(last, pair)
            to_end = jnp.exp(last_lanes - inner)
            dinputs = dinputs + to_end * from_after[:, lanes]
            x_ends.append(low(to_end * wide(inputs)))
            g_starts.append(low(jnp.exp(inner) * wide(dout)))
            lasts.append(last_lanes)
            flows.append(wide(dout) * out_ref[:, at : at + 128] - wide(inputs) * dinputs)
            dsteps.append(dinputs * chan)
            dchan = dchan + dinputs * step_lanes
            grad_buf[0:CHUNK, at : at + 128] = dchan * silu_slope(pres[pair], sigs[pair])
        g_start = jnp.concatenate(g_starts, axis=1)
        d_c = d_c + dot_nt(g_start, low(state))
        d_b = d_b + dot_nt(jnp.concatenate(x_ends, axis=1), after_low)
        after = jnp.exp(jnp.concatenate(lasts, axis=1)) * after + dot(c_cols, g_start)
        after_ref[:, cols] = after
        through = jnp.sum(after * state, axis=0, keepdims=True)
        stacked = jnp.concatenate(
            [
                jnp.concatenate(flows, axis=1),
                jnp.concatenate(dsteps, axis=1),
                jnp.broadcast_to(through, (8, GROUP)),
            ],
            axis=0,
        )
        picked = dot_by(stacked, pick)
        flow, dstep = picked[:CHUNK], picked[CHUNK : 2 * CHUNK]
        flow_end = flow_ref[group : group + 1, :]
        flow_next = picked[2 * CHUNK : 2 * CHUNK + 1]
        dcumul = dot_fine(upper, flow) + flow_end
        flow_ref[group : group + 1, :] = flow_next
        dstep = dstep + rate * dcumul
        ddecay_ref[group : group + 1, :] += jnp.sum(rate * step * dcumul, axis=0, keepdims=True)
        draw = dstep * sigmoid(raw)
        dbias_ref[group : group + 1, :] += jnp.sum(draw, axis=0, keepdims=True)
        to = group * 1024 + 896
        lane = lax.broadcasted_iota(jnp.int32, (CHUNK, 128), 1)
        dproj_ref[:, to : to + 128] = low(jnp.where(lane < GH, draw, 0.0))
        to = group * 1024 + 2 * GROUP
        dproj_ref[:, to : to + 128] = dq_ref[:, group * 128 : (group + 1) * 128]
    dgram_low = low(dgram)
    d_c = d_c + dot(dgram_low, b_rows)
    d_b = d_b + dot_tn(dgram_low, c_rows)
    slope = silu_slope(pre_state, sig_state)
    grad_buf[0:CHUNK, 2 * GROUP : 2 * GROUP + N] = d_b * slope[:, :N]
    grad_buf[0:CHUNK, 2 * GROUP + N :] = d_c * slope[:, N:]
    for at in range(0, CONV, 128):
        grad = jnp.zeros((CHUNK, 128), jnp.float32)
        here = grad_buf[0:CHUNK, at : at + 128]
        for tap in range(KCONV):
            shift = KCONV - 1 - tap
            grad = grad + (
                grad_buf[shift : shift + CHUNK, at : at + 128] * taps_ref[tap : tap + 1, at : at + 128]
            )
            dtaps_ref[tap : tap + 1, at : at + 128] += jnp.sum(
                here * buf_ref[5 + tap : 5 + tap + CHUNK, at : at + 128], axis=0, keepdims=True
            )
        if at < 2 * GROUP:
            to = (at // GROUP) * 1024 + GROUP + at % GROUP
        else:
            to = SHARED + at - 2 * GROUP
        dproj_ref[:, to : to + 128] = low(grad)
    dproj_ref[:, SHARED + 2 * N :] = dkv_ref[...]
    grad_buf[CHUNK:, :] = grad_buf[0:8, :]


def mamba_backward(proj, out, states, back, dq, dkv, taps, bias, decay, skip, gain):
    rows, columns = proj.shape
    chunks = rows // CHUNK

    def whole(value):
        return pl.BlockSpec(value.shape, lambda k: (0, 0))

    def rows_of(width):
        return pl.BlockSpec((CHUNK, width), lambda k: (chunks - 1 - k, 0))

    params = (taps, bias, decay, skip, gain)
    return pl.pallas_call(
        mamba_backward_kernel,
        grid=(chunks,),
        in_specs=[
            rows_of(columns),
            pl.BlockSpec(
                (8, columns),
                lambda k: (jnp.maximum((chunks - 1 - k) * (CHUNK // 8) - 1, 0), 0),
            ),
            rows_of(2 * GROUP),
            pl.BlockSpec((1, N, 2 * GROUP), lambda k: (chunks - 1 - k, 0, 0)),
            rows_of(1024),
            rows_of(256),
            rows_of(128),
        ]
        + [whole(value) for value in params],
        out_specs=[rows_of(columns)]
        + [whole(value) for value in (taps, gain, skip, bias, decay)],
        out_shape=[jax.ShapeDtypeStruct((rows, columns), jnp.bfloat16)]
        + [
            jax.ShapeDtypeStruct(value.shape, jnp.float32)
            for value in (taps, gain, skip, bias, decay)
        ],
        scratch_shapes=[
            pltpu.VMEM((CHUNK + 8, CONV), jnp.float32),
            pltpu.VMEM((CHUNK + 8, CONV), jnp.float32),
            pltpu.VMEM((N, 2 * GROUP), jnp.float32),
            pltpu.VMEM((8, 128), jnp.float32),
        ],
        compiler_params=pltpu.CompilerParams(vmem_limit_bytes=BIG),
        cost_estimate=cost(36),
        name="mamba_backward",
    )(proj, proj, out, states, back, dq, dkv, *params)


def ffn_kernel(
    len_ref,
    x_ref,
    own_ref,
    their_ref,
    gain_ref,
    raw_ref,
    up_ref,
    down_ref,
    grad_ref,
    hidden_ref,
    normed_ref,
    act_ref,
    dgate_ref,
):
    units = down_ref.shape[1]
    rows = x_ref.shape[0]

    @pl.when(pl.program_id(0) == 0)
    def _():
        @pl.loop(0, rows // 128)
        def _(at):
            here = pl.ds(pl.multiple_of(at * 128, 128), 128)
            hidden = wide(x_ref[here, :]) + (wide(own_ref[here, :]) + wide(their_ref[here, :]))
            hidden_ref[here, :] = hidden
            size = 1.0 / hidden.shape[1]
            root = lax.rsqrt(jnp.sum(hidden * hidden, axis=1, keepdims=True) * size + EPS)
            normed_ref[here, :] = low(hidden * root * gain_ref[...])
            row = lax.broadcasted_iota(jnp.int32, (128, 1), 0) + at * 128
            grad = wide(raw_ref[here, :])
            grad_ref[here, :] = low(jnp.where(row < len_ref[0], grad, 0.0))

    @pl.loop(0, rows // 512)
    def _(at):
        here = pl.ds(pl.multiple_of(at * 512, 512), 512)
        gate_up = dot(normed_ref[here, :], up_ref[...])
        gate, up = gate_up[:, :units], gate_up[:, units:]
        sig = sigmoid(gate)
        act = gate * sig
        act_ref[here, :] = low(act * up)
        grad = dot(grad_ref[here, :], down_ref[...])
        dgate_ref[here, :units] = low(grad * up * silu_slope(gate, sig))
        dgate_ref[here, units:] = low(grad * act)


def ffn_middle(seq_len, x_rows, own, theirs, gain, grad, up_weight, down_weight, blocks):
    rows, model = x_rows.shape
    units = down_weight.shape[1] // blocks

    def whole(value):
        return pl.BlockSpec(value.shape, lambda z: (0, 0))

    full = pl.BlockSpec((rows, model), lambda z: (0, 0))
    return pl.pallas_call(
        ffn_kernel,
        grid=(blocks,),
        in_specs=[pl.BlockSpec(memory_space=pltpu.SMEM)]
        + [whole(value) for value in (x_rows, own, theirs, gain, grad)]
        + [
            pl.BlockSpec((model, 2 * units), lambda z: (0, z)),
            pl.BlockSpec((model, units), lambda z: (0, z)),
        ],
        out_specs=[
            full,
            full,
            full,
            pl.BlockSpec((rows, units), lambda z: (0, z)),
            pl.BlockSpec((rows, 2 * units), lambda z: (0, z)),
        ],
        out_shape=[
            jax.ShapeDtypeStruct((rows, model), jnp.bfloat16),
            jax.ShapeDtypeStruct((rows, model), jnp.float32),
            jax.ShapeDtypeStruct((rows, model), jnp.bfloat16),
            jax.ShapeDtypeStruct((rows, blocks * units), jnp.bfloat16),
            jax.ShapeDtypeStruct((rows, 2 * blocks * units), jnp.bfloat16),
        ],
        compiler_params=pltpu.CompilerParams(vmem_limit_bytes=BIG),
        cost_estimate=cost(14),
        name="ffn_middle",
    )(seq_len, x_rows, own, theirs, gain, grad, up_weight, down_weight)


def hidden_kernel(
    hidden_ref, own_ref, their_ref, grad_ref, gain_ref, weight_ref, dhidden_ref, mixed_ref, back_ref, dgain_ref
):
    @pl.when(pl.program_id(0) == 0)
    def _():
        dgain_ref[...] = jnp.zeros_like(dgain_ref)

    hidden = hidden_ref[...]
    grad = wide(own_ref[...]) + wide(their_ref[...])
    size = 1.0 / hidden.shape[1]
    root = lax.rsqrt(jnp.sum(hidden * hidden, axis=1, keepdims=True) * size + EPS)
    scaled = grad * gain_ref[...]
    inner = jnp.sum(hidden * scaled, axis=1, keepdims=True) * size
    dhidden = wide(grad_ref[...]) + root * scaled - hidden * (root * root * root * inner)
    dhidden_ref[...] = dhidden
    dgain_ref[...] += 0.5 * jnp.sum(hidden * root * grad, axis=0, keepdims=True)
    mixed = low(dhidden)
    mixed_ref[...] = mixed
    back_ref[...] = dot(mixed, weight_ref[...])


def hidden_backward(hidden, own, theirs, grad, gain, weight):
    rows, model = hidden.shape

    def whole(value):
        return pl.BlockSpec(value.shape, lambda k: (0, 0))

    part = pl.BlockSpec((256, model), lambda k: (k, 0))
    return pl.pallas_call(
        hidden_kernel,
        grid=(rows // 256,),
        in_specs=[part] * 4 + [whole(gain), whole(weight)],
        out_specs=[part, part, pl.BlockSpec((256, weight.shape[1]), lambda k: (k, 0)), whole(gain)],
        out_shape=[
            jax.ShapeDtypeStruct((rows, model), jnp.float32),
            jax.ShapeDtypeStruct((rows, model), jnp.bfloat16),
            jax.ShapeDtypeStruct((rows, weight.shape[1]), jnp.float32),
            jax.ShapeDtypeStruct(gain.shape, jnp.float32),
        ],
        compiler_params=pltpu.CompilerParams(vmem_limit_bytes=BIG),
        cost_estimate=cost(7),
        name="hidden_backward",
    )(hidden, own, theirs, grad, gain, weight)


def ffn_grad_kernel(grad_ref, act_ref, normed_ref, dgate_ref, out_ref):
    cut = dgate_ref.shape[1]
    out_ref[:, :cut] = low(dot_tn(normed_ref[...], dgate_ref[...]))
    out_ref[:, cut:] = low(dot_tn(grad_ref[...], act_ref[...]))


def ffn_gradients(grad, act, normed, dgate, blocks):
    rows, model = grad.shape
    units = act.shape[1] // blocks
    whole = pl.BlockSpec((rows, model), lambda z: (0, 0))
    return pl.pallas_call(
        ffn_grad_kernel,
        grid=(blocks,),
        in_specs=[
            whole,
            pl.BlockSpec((rows, units), lambda z: (0, z)),
            whole,
            pl.BlockSpec((rows, 2 * units), lambda z: (0, z)),
        ],
        out_specs=pl.BlockSpec((model, 3 * units), lambda z: (0, z)),
        out_shape=jax.ShapeDtypeStruct((model, 3 * blocks * units), jnp.bfloat16),
        compiler_params=pltpu.CompilerParams(vmem_limit_bytes=BIG),
        cost_estimate=cost(12),
        name="ffn_gradients",
    )(grad, act, normed, dgate)


MESH = pl.DeviceIdType.MESH


def landed(ref, sem):
    pltpu.make_async_copy(ref, ref, sem).wait()


def front_kernel(*refs):
    (pack_ref, next_ref, ups_ref, downs_ref, shared_ref, x_ref, small_ref, og_ref) = refs[:8]
    (state_taps, gain_in, len_ref, cos_ref, sin_ref) = refs[8:13]
    (w_hbm, v_hbm, u_ref, d_ref, x_hbm, normed_hbm, proj_hbm, og_full) = refs[13:21]
    (taps_ref, bias_ref, decay_ref, skip_ref, gain_ref) = refs[21:26]
    (sums_ref, both_ref, out_ref, states_ref, mixed_ref, other_ref) = refs[26:32]
    (w_ref, v_ref, full_ref, normed_ref, proj_ref, attn_ref, params_ref) = refs[32:39]
    (buf_ref, state_ref) = refs[39:41]
    (near_sem, out_sem, part_sem, fromx_sem, fromy_sem, overx_sem, overy_sem) = refs[41:48]
    (tox_sem, toy_sem, relx_sem, rely_sem, row_sem, row_out, pair_sem, pair_out) = refs[48:56]
    (param_sem, param_out, ffn_out, store_sem, mixed_sem) = refs[56:]
    plane = lax.axis_index("plane")
    core = lax.axis_index("core")
    place = lax.axis_index("tensor")
    xside = plane + 1 - 2 * (plane % 2)
    yside = plane + 2 - 4 * (plane // 2)
    across = xside + 2 - 4 * (xside // 2)
    target = place // 2
    column = place % 2
    share, width = pack_ref.shape
    narrow = next_ref.shape[1]
    rest = shared_ref.shape[2]
    half = share
    rows_dev = x_ref.shape[1]

    barrier = pltpu.get_barrier_semaphore()
    for step in range(4):
        for side in range(2):
            if step or side:
                pl.semaphore_signal(
                    barrier,
                    inc=1,
                    device_id={"core": (core + side) % 2, "tensor": (place + step) % 4},
                    device_id_type=MESH,
                )
    for neighbour in (xside, yside):
        pl.semaphore_signal(
            barrier, inc=1, device_id={"plane": neighbour}, device_id_type=MESH
        )
    pl.semaphore_wait(barrier, 9)

    def block(at, part):
        return pl.ds(pl.multiple_of(at * 2 * share + part * share, share), share)

    def piece(at, part, col):
        return w_ref.at[block(at, part), pl.ds(pl.multiple_of(col * width, width), width)]

    def next_piece(at, part, col):
        return v_ref.at[block(at, part), pl.ds(pl.multiple_of(col * narrow, narrow), narrow)]

    def rest_piece(at, part):
        return w_ref.at[block(at, part), pl.ds(2 * width, rest)]

    started = []

    def send(src, dst, send_sem, recv_sem, device):
        copy = pltpu.make_async_remote_copy(
            src_ref=src,
            dst_ref=dst,
            send_sem=send_sem,
            recv_sem=recv_sem,
            device_id=device,
            device_id_type=MESH,
        )
        copy.start()
        started.append((src, send_sem))

    mine = piece(plane, core, column)
    slot = core * 2 + column
    mine_next = next_piece(plane, core, column)

    def send_parts(src, dst, at, recv_sem):
        for step in (2, 1, 3):
            send(
                src,
                dst,
                out_sem.at[at + step],
                recv_sem,
                {"core": target, "tensor": (place + step) % 4},
            )

    send_parts(pack_ref, mine, 0, part_sem.at[slot])

    params = params_ref.at[column]

    @pl.when(target == core)
    def _():
        pltpu.make_async_copy(pack_ref, mine, part_sem.at[slot]).start()
        pltpu.make_async_copy(next_ref, mine_next, part_sem.at[6 + slot]).start()
        pltpu.make_async_copy(small_ref, params, param_sem.at[column]).start()
        for step in range(1, 4):
            pltpu.make_async_remote_copy(
                src_ref=small_ref,
                dst_ref=params,
                send_sem=param_out.at[step],
                recv_sem=param_sem.at[column],
                device_id={"tensor": (place + step) % 4},
                device_id_type=MESH,
            ).start()

    @pl.when(target != core)
    def _():
        pltpu.make_async_remote_copy(
            src_ref=pack_ref,
            dst_ref=mine,
            send_sem=out_sem.at[0],
            recv_sem=part_sem.at[slot],
            device_id={"core": 1 - core},
            device_id_type=MESH,
        ).start()
        pltpu.make_async_remote_copy(
            src_ref=next_ref,
            dst_ref=mine_next,
            send_sem=out_sem.at[4],
            recv_sem=part_sem.at[6 + slot],
            device_id={"core": 1 - core},
            device_id_type=MESH,
        ).start()

    own_rest = rest_piece(plane, core)
    near = pltpu.make_async_copy(shared_ref.at[core], own_rest, part_sem.at[4 + core])
    near.start()
    send(
        shared_ref.at[1 - core],
        own_rest,
        near_sem.at[0],
        part_sem.at[4 + core],
        {"core": 1 - core},
    )

    def rows_at(ref, at, side):
        return ref.at[pl.ds(pl.multiple_of(at * rows_dev + side * half, half), half)]

    wide_up, wide_down = ups_ref.shape[1] // 2, downs_ref.shape[2]

    def down_piece(at, part, place_at):
        cols = pl.ds(pl.multiple_of(place_at * wide_down, wide_down), wide_down)
        return d_ref.at[block(at, part), cols]

    def up_piece(at, part, place_at):
        cols = pl.ds(pl.multiple_of(place_at * wide_up, wide_up), wide_up)
        return u_ref.at[block(at, part), cols]

    def row_parts(src_ref, dst_ref):
        for seq in range(2):
            for side in range(2):
                goal = 2 * core + seq
                here = jnp.logical_and(core == side, goal == place)
                src = src_ref.at[seq, pl.ds(side * half, half)]
                yield seq * 2 + side, here, src, rows_at(dst_ref, place, side), side, goal

    def send_rows(src_ref, dst_ref, kind):
        for number, here, src, dst, side, goal in row_parts(src_ref, dst_ref):

            @pl.when(here)
            def _():
                pltpu.make_async_copy(src, dst, row_sem.at[kind, place]).start()

            @pl.when(jnp.logical_not(here))
            def _():
                pltpu.make_async_remote_copy(
                    src_ref=src,
                    dst_ref=dst,
                    send_sem=row_out.at[kind, number],
                    recv_sem=row_sem.at[kind, place],
                    device_id={"core": side, "tensor": goal},
                    device_id_type=MESH,
                ).start()

    def share_rows(ref, kind, steps=(0, 1, 2, 3)):
        for step in steps:
            at = (place + step) % 4
            part = rows_at(ref, at, core)
            landed(part, row_sem.at[kind, at])
            send(part, part, pair_out.at[kind, at], pair_sem.at[kind, at], {"core": 1 - core})

    def shared_rows(ref, kind):
        for step in range(4):
            at = (place + step) % 4
            landed(rows_at(ref, at, 1 - core), pair_sem.at[kind, at])


    def send_halves(own, number, parts_of, goal_ref, recv_sem):
        def send_parts_to(side, send_sem, device):
            for src, cols in parts_of(side):
                pltpu.make_async_remote_copy(
                    src_ref=src,
                    dst_ref=goal_ref.at[:, cols],
                    send_sem=send_sem,
                    recv_sem=recv_sem,
                    device_id=device,
                    device_id_type=MESH,
                ).start()
            started.append((goal_ref, send_sem))

        if own:
            send_parts_to(1 - core, ffn_out.at[number, 0], {"core": 1 - core})
            for src, cols in parts_of(core):
                pltpu.make_async_copy(src, goal_ref.at[:, cols], recv_sem).start()
            return
        for step in (2, 1, 3):
            for side in range(2):
                send_parts_to(
                    side,
                    ffn_out.at[number, 2 * step + side],
                    {"core": side, "tensor": (place + step) % 4},
                )

    def down_parts(side):
        return [(downs_ref.at[side], pl.ds(0, wide_down))]

    def up_parts(side):
        unit = wide_up // 2
        return [
            (
                ups_ref.at[:, pl.ds(pl.multiple_of((2 * at + side) * unit, unit), unit)],
                pl.ds(at * unit, unit),
            )
            for at in range(2)
        ]

    def issue_next():
        send_parts(next_ref, mine_next, 4, part_sem.at[6 + slot])

    def issue_downs(own=False):
        send_halves(
            own, 0, down_parts, down_piece(plane, core, place), part_sem.at[10 + 2 * place + core]
        )

    def issue_ups(own=False):
        send_halves(
            own, 1, up_parts, up_piece(plane, core, place), part_sem.at[18 + 2 * place + core]
        )

    first_col = jnp.where(place // 2 == core, place % 2, 1 - core)
    order = [(0, None, 0), (0, None, 1)]
    for kind in (1, 2):
        for turn in range(2):
            for part in range(2):
                order.append((kind, (first_col + turn) % 2, part))

    for kind in (3, 4):
        for step in (0, 1, 3, 2):
            for part in range(2):
                order.append((kind, (place + step) % 4, part))

    def at_piece(at, item):
        kind, col, part = item
        if kind >= 3:
            return (down_piece, up_piece)[kind - 3](at, part, col)
        if kind == 0:
            return rest_piece(at, part)
        return piece(at, part, col) if kind == 1 else next_piece(at, part, col)

    def index(item):
        kind, col, part = item
        if kind >= 3:
            return 8 * kind - 14 + 2 * col + part
        return 4 + part if kind == 0 else (kind - 1) * 6 + part * 2 + col

    def relay(item):
        at = index(item)
        if item[2] == 0:
            landed(at_piece(xside, item), fromx_sem.at[at])
            ref = at_piece(xside, item)
            send(ref, ref, rely_sem.at[at], overy_sem.at[at], {"plane": yside})
        else:
            landed(at_piece(yside, item), fromy_sem.at[at])
            ref = at_piece(yside, item)
            send(ref, ref, relx_sem.at[at], overx_sem.at[at], {"plane": xside})

    def serve(items):
        for item in items:
            at = index(item)
            ref = at_piece(plane, item)
            landed(ref, part_sem.at[at])
            send(ref, ref, tox_sem.at[at], fromx_sem.at[at], {"plane": xside})
            send(ref, ref, toy_sem.at[at], fromy_sem.at[at], {"plane": yside})

    def relays(items):
        for item in items:
            relay(item)

    def complete(items):
        for item in items:
            at = index(item)
            if item[2] == 0:
                landed(at_piece(yside, item), fromy_sem.at[at])
                landed(at_piece(across, item), overy_sem.at[at])
            else:
                landed(at_piece(xside, item), fromx_sem.at[at])
                landed(at_piece(across, item), overx_sem.at[at])

    stores = []

    def store(src, dst):
        sem = store_sem.at[len(stores)]
        pltpu.make_async_copy(src, dst, sem).start()
        stores.append((src, dst, sem))

    issue_ups(True)
    issue_downs(True)
    serve(order[:2])
    serve(order[18:20])
    serve(order[10:12])
    serve(order[2:4])
    relays(order[:2])
    relays(order[18:20])
    serve(order[4:6])
    issue_ups()
    relays(order[10:12])
    relays(order[2:6])
    serve(order[20:26])
    send_rows(x_ref, full_ref, 0)
    issue_next()
    complete(order[:6])
    relays(order[20:22])
    for at in range(2):
        landed(params_ref.at[at], param_sem.at[at])
    taps_ref[:, 2 * GROUP :] = state_taps[...]
    for col in range(2):
        for tap in range(KCONV):
            for at in range(3):
                lanes = pl.ds(col * GROUP + at * 128, 128)
                taps_ref[tap : tap + 1, lanes] = params_ref[col, 3 * tap + at : 3 * tap + at + 1, :]
        for at in range(3):
            lanes = pl.ds(col * GROUP + at * 128, 128)
            skip_ref[:, lanes] = params_ref[col, 12 + at : 13 + at, :]
            gain_ref[:, lanes] = params_ref[col, 15 + at : 16 + at, :]
        bias_ref[col : col + 1, :] = params_ref[col, 18:19, :]
        decay_ref[col : col + 1, :] = params_ref[col, 19:20, :]
    share_rows(full_ref, 0)
    relays(order[22:26])
    shared_rows(full_ref, 0)
    store(w_ref, w_hbm)
    store(full_ref, x_hbm)

    rows = full_ref.shape[0]

    @pl.loop(0, rows // 128)
    def _(at):
        here = pl.ds(pl.multiple_of(at * 128, 128), 128)
        values = wide(full_ref[here, :])
        size = 1.0 / values.shape[1]
        root = lax.rsqrt(jnp.sum(values * values, axis=1, keepdims=True) * size + EPS)
        normed_ref[here, :] = low(values * root * gain_in[...])

    store(normed_ref, normed_hbm)

    def project(begin, end):
        @pl.loop(0, (end - begin) // 256)
        def _(at):
            cols = pl.ds(pl.multiple_of(begin + at * 256, 128), 256)
            proj_ref[:, cols] = dot(normed_ref[...], w_ref[:, cols])

    def attend(col):
        lanes = pl.ds(col * 128, 128)
        attention_forward_kernel(
            len_ref,
            proj_ref.at[:, pl.ds(col * width + 768, 128)],
            proj_ref.at[:, pl.ds(2 * width + 2 * N, 128)],
            cos_ref,
            sin_ref,
            attn_ref.at[:, lanes],
            sums_ref.at[:, lanes],
        )

    def chunks(begin, end):
        @pl.loop(begin, end)
        def _(at):
            here = pl.ds(pl.multiple_of(at * CHUNK, CHUNK), CHUNK)
            mamba_chunk(
                proj_ref.at[here, :],
                attn_ref.at[here, :],
                taps_ref,
                bias_ref,
                decay_ref,
                skip_ref,
                gain_ref,
                both_ref.at[here, :],
                out_ref.at[here, :],
                states_ref.at[at],
                buf_ref,
                state_ref,
            )

    project(0, 1024)
    serve(order[6:10])
    issue_downs()
    project(1024, 2304)
    last = pl.ds(2304, proj_ref.shape[1] - 2304)
    proj_ref[:, last] = dot(normed_ref[...], w_ref[:, last])
    store(proj_ref, proj_hbm)
    relays(order[6:8])
    attend(0)
    relays(order[8:10])
    serve(order[12:14])
    attend(1)
    serve(order[14:18])
    send_rows(og_ref, og_full, 1)
    mamba_start(buf_ref, state_ref)
    count = rows // CHUNK
    chunks(0, count // 4)
    relays(order[12:14])
    chunks(count // 4, count // 2)
    complete(order[6:10])
    store(v_ref, v_hbm)
    relays(order[14:18])
    chunks(count // 2, count)

    @pl.loop(0, 4)
    def _(at):
        here = pl.ds(pl.multiple_of(at * 256, 256), 256)
        mixed_ref[here, :] = low(dot_nt(both_ref[here, :], v_ref[...]))

    send(mixed_ref, other_ref, mixed_sem.at[0], mixed_sem.at[1], {"core": 1 - core})
    share_rows(og_full, 1)
    complete(order[10:26])
    shared_rows(og_full, 1)
    landed(other_ref, mixed_sem.at[1])
    for src, dst, sem in stores:
        pltpu.make_async_copy(src, dst, sem).wait()
    for src, sem in started:
        landed(src, sem)

    @pl.when(target == core)
    def _():
        for step in range(1, 4):
            landed(small_ref, param_out.at[step])

    @pl.when(target != core)
    def _():
        landed(pack_ref, out_sem.at[0])
        landed(next_ref, out_sem.at[4])

    for kind, (src_ref, dst_ref) in enumerate(((x_ref, full_ref), (og_ref, og_full))):
        for number, here, src, _, _, _ in row_parts(src_ref, dst_ref):

            @pl.when(jnp.logical_not(here))
            def _():
                landed(src, row_out.at[kind, number])


def front(
    pack,
    following,
    ups,
    downs,
    shared,
    x_rows,
    small,
    out_grad,
    state_taps,
    gain,
    seq_len,
    cosine,
    sine,
):
    share, width = pack.shape
    narrow = following.shape[1]
    rest = shared.shape[2]
    rows = x_rows.shape[1] * 4
    model = x_rows.shape[2]
    columns = 2 * width + rest
    dma = pltpu.SemaphoreType.DMA
    any_space = pl.BlockSpec(memory_space=pl.ANY)
    near = pl.BlockSpec(memory_space=pltpu.VMEM)
    f32, bf16 = jnp.float32, pack.dtype
    return pl.pallas_call(
        front_kernel,
        in_specs=[any_space] * 8
        + [near, near, pl.BlockSpec(memory_space=pltpu.SMEM), near, near],
        out_specs=[any_space] * 8 + [near] * 11,
        out_shape=[
            jax.ShapeDtypeStruct((8 * share, columns), bf16),
            jax.ShapeDtypeStruct((8 * share, 2 * narrow), bf16),
            jax.ShapeDtypeStruct((8 * share, 2 * ups.shape[1]), bf16),
            jax.ShapeDtypeStruct((8 * share, 4 * downs.shape[2]), bf16),
            jax.ShapeDtypeStruct((rows, model), bf16),
            jax.ShapeDtypeStruct((rows, model), bf16),
            jax.ShapeDtypeStruct((rows, columns), f32),
            jax.ShapeDtypeStruct((rows, model), bf16),
            jax.ShapeDtypeStruct((KCONV, CONV), f32),
            jax.ShapeDtypeStruct((2, 128), f32),
            jax.ShapeDtypeStruct((2, 128), f32),
            jax.ShapeDtypeStruct((1, 2 * GROUP), f32),
            jax.ShapeDtypeStruct((1, 2 * GROUP), f32),
            jax.ShapeDtypeStruct((rows, 256), f32),
            jax.ShapeDtypeStruct((rows, 1024), bf16),
            jax.ShapeDtypeStruct((rows, 2 * GROUP), f32),
            jax.ShapeDtypeStruct((rows // CHUNK, N, 2 * GROUP), f32),
            jax.ShapeDtypeStruct((rows, 8 * share), bf16),
            jax.ShapeDtypeStruct((rows, 8 * share), bf16),
        ],
        scratch_shapes=[
            pltpu.VMEM((8 * share, columns), bf16),
            pltpu.VMEM((8 * share, 2 * narrow), bf16),
            pltpu.VMEM((rows, model), bf16),
            pltpu.VMEM((rows, model), bf16),
            pltpu.VMEM((rows, columns), f32),
            pltpu.VMEM((rows, 256), bf16),
            pltpu.VMEM((2,) + small.shape, f32),
            pltpu.VMEM((CHUNK + 8, CONV), f32),
            pltpu.VMEM((N, 2 * GROUP), f32),
            dma((1,)),
            dma((8,)),
        ]
        + [dma((26,))] * 9
        + [dma((2, 4))] * 4
        + [dma((4,))] * 2
        + [dma((2, 8)), dma((5,)), dma((2,))],
        compiler_params=pltpu.CompilerParams(
            collective_id=1, has_side_effects=True, vmem_limit_bytes=BIG
        ),
        cost_estimate=cost(120),
        name="front",
    )(
        pack,
        following,
        ups,
        downs,
        shared,
        x_rows,
        small,
        out_grad,
        state_taps,
        gain,
        seq_len,
        cosine,
        sine,
    )


def collect_kernel(*refs):
    (normed_ref, dproj_ref, weight_hbm, mixed_hbm, both_hbm, x_hbm, hidden_hbm) = refs[:7]
    (gain_ref, small_ref) = refs[7:9]
    (mixer_out, query_out, step_out, shared_ref, total_ref, back_ref) = refs[9:15]
    (mamba_out, attn_out) = refs[15:17]
    (weight_ref, mixed_ref, both_ref, x_ref, hidden_ref, grad_ref, next_ref) = refs[17:24]
    (norm_ref, norm_in, rows_ref, in_ref, next_in, sum_ref, next_sum) = refs[24:31]
    (piece_ref, next_buf, pair_ref, mix_ref, near_ref, far_ref) = refs[31:37]
    (in_sem, out_sem, piece_sem, piece_out, pair_sem, mix_sem, mix_out) = refs[37:44]
    (near_sem, near_out, far_sem, far_out, row_sem, row_out, load_sem, norm_sem) = refs[44:]
    plane = lax.axis_index("plane")
    core = lax.axis_index("core")
    place = lax.axis_index("tensor")
    xside = plane + 1 - 2 * (plane % 2)
    yside = plane + 2 - 4 * (plane // 2)
    across = xside + 2 - 4 * (xside // 2)
    share = pair_ref.shape[0]
    width = piece_ref.shape[2]
    rest = grad_ref.shape[1] - 2 * width

    loads = [
        (weight_hbm, weight_ref),
        (mixed_hbm, mixed_ref),
        (both_hbm, both_ref),
        (x_hbm.at[:, core], x_ref),
        (hidden_hbm.at[:, core], hidden_ref),
    ]
    for number, (src, dst) in enumerate(loads):
        pltpu.make_async_copy(src, dst, load_sem.at[number]).start()

    def loaded(number):
        src, dst = loads[number]
        pltpu.make_async_copy(src, dst, load_sem.at[number]).wait()

    barrier = pltpu.get_barrier_semaphore()
    for step in range(4):
        for side in range(2):
            if step or side:
                pl.semaphore_signal(
                    barrier,
                    inc=1,
                    device_id={"core": (core + side) % 2, "tensor": (place + step) % 4},
                    device_id_type=MESH,
                )
    for neighbour in (xside, yside):
        pl.semaphore_signal(
            barrier, inc=1, device_id={"plane": neighbour}, device_id_type=MESH
        )
    pl.semaphore_wait(barrier, 9)

    started = []

    def send(src, dst, send_sem, recv_sem, device):
        pltpu.make_async_remote_copy(
            src_ref=src,
            dst_ref=dst,
            send_sem=send_sem,
            recv_sem=recv_sem,
            device_id=device,
            device_id_type=MESH,
        ).start()
        started.append((src, send_sem))

    narrow = next_ref.shape[1] // 2
    spans = [(0, 2 * width, rest), (0, 0, width), (0, width, width)]
    spans += [(1, 0, narrow), (1, narrow, narrow)]

    def block(at, part, span):
        rows = pl.ds(pl.multiple_of(at * 2 * share + part * share, share), share)
        return (grad_ref, next_ref)[span[0]].at[rows, pl.ds(*span[1:])]

    def held(slot, span):
        return (in_ref, next_in)[span[0]].at[slot, :, pl.ds(*span[1:])]

    def summed(part, span):
        return (sum_ref, next_sum)[span[0]].at[part, :, pl.ds(*span[1:])]

    def begin(number):
        span = spans[number]
        send(
            block(across, 0, span),
            held(0, span),
            out_sem.at[0, number],
            in_sem.at[0, number],
            {"plane": xside},
        )
        send(
            block(across, 1, span),
            held(1, span),
            out_sem.at[1, number],
            in_sem.at[1, number],
            {"plane": yside},
        )
        send(
            block(xside, 0, span),
            held(2, span),
            out_sem.at[2, number],
            in_sem.at[2, number],
            {"plane": xside},
        )
        send(
            block(yside, 1, span),
            held(3, span),
            out_sem.at[3, number],
            in_sem.at[3, number],
            {"plane": yside},
        )

    def work(number):
        kind, begin_at, size = spans[number]
        left = (normed_ref, mixed_ref)[kind]
        right = (dproj_ref, both_ref)[kind]
        result = (grad_ref, next_ref)[kind]
        tile = 256 if size % 256 == 0 else size

        @pl.loop(0, size // tile)
        def _(at):
            cols = pl.ds(pl.multiple_of(begin_at + at * tile, 128), tile)
            result[:, cols] = low(dot_tn(left[...], right[:, cols]))

    seq = place % 2
    owner = place // 2
    dst_rows = back_ref.at[seq, pl.ds(pl.multiple_of(core * share, share), share)]

    def send_back():
        for step in (2, 1, 3):
            at = (place + step) % 4
            send(
                rows_ref.at[at],
                dst_rows,
                row_out.at[step],
                row_sem.at[seq * 2 + core],
                {"core": owner, "tensor": at},
            )

        @pl.when(owner == core)
        def _():
            pltpu.make_async_copy(
                rows_ref.at[place], dst_rows, row_sem.at[seq * 2 + core]
            ).start()

        @pl.when(owner != core)
        def _():
            pltpu.make_async_remote_copy(
                src_ref=rows_ref.at[place],
                dst_ref=dst_rows,
                send_sem=row_out.at[0],
                recv_sem=row_sem.at[seq * 2 + core],
                device_id={"core": 1 - core},
                device_id_type=MESH,
            ).start()

    def norm_product():
        loaded(0)
        for at in range(4):
            rows = pl.ds(at * 2 * share, 2 * share)
            part = low(dot_nt(dproj_ref[rows, :], weight_ref[...]))
            norm_ref[at, 0] = part[:share]
            norm_ref[at, 1] = part[share:]
        send(
            norm_ref.at[:, 1 - core],
            norm_in,
            norm_sem.at[0],
            norm_sem.at[1],
            {"core": 1 - core},
        )

    def norm_back():
        loaded(3)
        loaded(4)
        landed(norm_in, norm_sem.at[1])
        gain_total = jnp.zeros((1, x_ref.shape[2]), jnp.float32)
        for at in range(4):
            grad = wide(norm_ref[at, core]) + wide(norm_in[at])
            values = wide(x_ref[at])
            size = 1.0 / values.shape[1]
            root = lax.rsqrt(jnp.sum(values * values, axis=1, keepdims=True) * size + EPS)
            scaled = grad * gain_ref[...]
            inner = jnp.sum(values * scaled, axis=1, keepdims=True) * size
            rows_ref[at] = low(
                hidden_ref[at] + root * scaled - values * (root * root * root * inner)
            )
            gain_total = gain_total + jnp.sum(values * root * grad, axis=0, keepdims=True)
        near_ref[5] = small_ref[...]
        for at in range(gain_total.shape[1] // 128):
            near_ref[5, at : at + 1, :] = gain_total[:, at * 128 : (at + 1) * 128]

    def pass_on(number):
        span = spans[number]
        landed(held(0, span), in_sem.at[0, number])
        held(0, span)[...] = low(wide(held(0, span)[...]) + wide(block(yside, 0, span)[...]))
        send(
            held(0, span),
            held(5, span),
            out_sem.at[4, number],
            in_sem.at[5, number],
            {"plane": yside},
        )
        landed(held(1, span), in_sem.at[1, number])
        held(1, span)[...] = low(wide(held(1, span)[...]) + wide(block(xside, 1, span)[...]))
        send(
            held(1, span),
            held(4, span),
            out_sem.at[5, number],
            in_sem.at[4, number],
            {"plane": xside},
        )

    def finish(number):
        span = spans[number]
        landed(held(2, span), in_sem.at[2, number])
        landed(held(5, span), in_sem.at[5, number])
        summed(0, span)[...] = low(
            wide(block(plane, 0, span)[...]) + wide(held(2, span)[...]) + wide(held(5, span)[...])
        )
        landed(held(3, span), in_sem.at[3, number])
        landed(held(4, span), in_sem.at[4, number])
        summed(1, span)[...] = low(
            wide(block(plane, 1, span)[...]) + wide(held(3, span)[...]) + wide(held(4, span)[...])
        )

    def send_pieces(number):
        span = spans[number]
        kind, col = span[0], span[1] // span[2]
        buf = (piece_ref, next_buf)[kind]
        goal = 2 * core + col
        for part in range(2):
            src = summed(part, span)
            here = jnp.logical_and(core == part, goal == place)

            @pl.when(here)
            def _():
                pltpu.make_async_copy(src, buf.at[place], piece_sem.at[kind, place]).start()

            @pl.when(jnp.logical_not(here))
            def _():
                pltpu.make_async_remote_copy(
                    src_ref=src,
                    dst_ref=buf.at[place],
                    send_sem=piece_out.at[kind, 2 * col + part],
                    recv_sem=piece_sem.at[kind, place],
                    device_id={"core": part, "tensor": goal},
                    device_id_type=MESH,
                ).start()

    rest_cols = pl.ds(2 * width, rest)
    state = rest * 2 // 3

    def pair_up():
        send(
            sum_ref.at[1 - core, :, rest_cols],
            pair_ref,
            pair_sem.at[0],
            pair_sem.at[1],
            {"core": 1 - core},
        )

    def mix():
        landed(pair_ref, pair_sem.at[1])
        mine = sum_ref[core, :, rest_cols]
        mix_ref[place, :, 0:state] = low(wide(mine[:, :state]) + wide(pair_ref[:, :state]))
        first = core == 0
        mix_ref[place, :, state:rest] = jnp.where(first, mine[:, state:], pair_ref[:, state:])
        mix_ref[place, :, rest:] = jnp.where(first, pair_ref[:, state:], mine[:, state:])
        own_mix = mix_ref.at[place]
        for step in (2, 1, 3):
            send(
                own_mix,
                own_mix,
                mix_out.at[step],
                mix_sem.at[place],
                {"tensor": (place + step) % 4},
            )

    work(1)
    begin(1)
    norm_product()
    work(2)
    begin(2)
    pass_on(1)
    norm_back()
    send_back()
    send(near_ref.at[5], near_ref.at[0], near_out.at[0], near_sem.at[0], {"plane": xside})
    work(0)
    begin(0)
    finish(1)
    send_pieces(1)
    loaded(1)
    loaded(2)
    work(3)
    pass_on(2)
    begin(3)
    landed(near_ref.at[0], near_sem.at[0])
    near_ref[3] = near_ref[5] + near_ref[0]
    send(near_ref.at[3], near_ref.at[1], near_out.at[1], near_sem.at[1], {"plane": yside})
    finish(2)
    send_pieces(2)
    work(4)
    pass_on(0)
    begin(4)
    landed(near_ref.at[1], near_sem.at[1])
    near_ref[4] = near_ref[3] + near_ref[1]
    send(near_ref.at[4], near_ref.at[2], near_out.at[2], near_sem.at[2], {"core": 1 - core})
    finish(0)
    pair_up()
    pass_on(3)
    mix()
    landed(near_ref.at[2], near_sem.at[2])
    far_ref[place] = near_ref[4] + near_ref[2]
    own_far = far_ref.at[place]
    for step in (2, 1, 3):
        send(
            own_far,
            own_far,
            far_out.at[step],
            far_sem.at[place],
            {"tensor": (place + step) % 4},
        )
    finish(3)
    send_pieces(3)
    pass_on(4)
    finish(4)
    send_pieces(4)

    for step in (1, 2, 3):
        at = (place + step) % 4
        landed(mix_ref.at[at], mix_sem.at[at])
        landed(far_ref.at[at], far_sem.at[at])
    shared_ref[...] = (
        wide(mix_ref[0]) + wide(mix_ref[1]) + wide(mix_ref[2]) + wide(mix_ref[3])
    )
    total_ref[...] = (far_ref[0] + far_ref[1]) + (far_ref[2] + far_ref[3])
    def gathered(buf, kind):
        for at in range(4):
            landed(buf.at[at], piece_sem.at[kind, at])
        return wide(buf[0]) + wide(buf[1]) + wide(buf[2]) + wide(buf[3])

    one = gathered(piece_ref, 0)
    cut = mixer_out.shape[1]
    mixer_out[...] = one[:, :cut]
    query_out[...] = one[:, cut : cut + query_out.shape[1]]
    step_out[...] = one[:, cut + query_out.shape[1] :]
    both = gathered(next_buf, 1).T
    mamba_out[...] = both[: mamba_out.shape[0]]
    attn_out[...] = both[mamba_out.shape[0] :]
    for at in range(4):
        landed(dst_rows, row_sem.at[at])
    for src, sem in started:
        landed(src, sem)

    @pl.when(owner != core)
    def _():
        landed(rows_ref.at[place], row_out.at[0])

    for span in spans[1:]:
        col = span[1] // span[2]
        for part in range(2):
            here = jnp.logical_and(core == part, 2 * core + col == place)

            @pl.when(jnp.logical_not(here))
            def _():
                landed(summed(part, span), piece_out.at[span[0], 2 * col + part])


def collect(normed, dproj, weight, mixed, both, x_rows, hidden, gain, small, sizes):
    chans, queries, width = sizes
    share = weight.shape[0] // 8
    model = weight.shape[0]
    columns = weight.shape[1]
    rest = columns - 2 * width
    narrow = both.shape[1] // 2
    dma = pltpu.SemaphoreType.DMA
    any_space = pl.BlockSpec(memory_space=pl.ANY)
    near = pl.BlockSpec(memory_space=pltpu.VMEM)
    shared_cols = rest + rest // 3
    bf16, f32 = jnp.bfloat16, jnp.float32
    split = (4, 2, x_rows.shape[0] // 8, model)
    half = (4, x_rows.shape[0] // 8, model)
    return pl.pallas_call(
        collect_kernel,
        in_specs=[near, near] + [any_space] * 5 + [near, near],
        out_specs=[near] * 5 + [any_space] + [near] * 2,
        out_shape=[
            jax.ShapeDtypeStruct((share, 2 * chans), f32),
            jax.ShapeDtypeStruct((share, queries), f32),
            jax.ShapeDtypeStruct((share, width - 2 * chans - queries), f32),
            jax.ShapeDtypeStruct((share, shared_cols), f32),
            jax.ShapeDtypeStruct(small.shape, f32),
            jax.ShapeDtypeStruct((2, 2 * half[1], model), bf16),
            jax.ShapeDtypeStruct((chans, share), f32),
            jax.ShapeDtypeStruct((narrow - chans, share), f32),
        ],
        scratch_shapes=[
            pltpu.VMEM(weight.shape, bf16),
            pltpu.VMEM(mixed.shape, bf16),
            pltpu.VMEM(both.shape, bf16),
            pltpu.VMEM(half, bf16),
            pltpu.VMEM(half, f32),
            pltpu.VMEM((model, columns), bf16),
            pltpu.VMEM((model, 2 * narrow), bf16),
            pltpu.VMEM(split, bf16),
            pltpu.VMEM(half, bf16),
            pltpu.VMEM(half, bf16),
            pltpu.VMEM((6, share, columns), bf16),
            pltpu.VMEM((6, share, 2 * narrow), bf16),
            pltpu.VMEM((2, share, columns), bf16),
            pltpu.VMEM((2, share, 2 * narrow), bf16),
            pltpu.VMEM((4, share, width), bf16),
            pltpu.VMEM((4, share, narrow), bf16),
            pltpu.VMEM((share, rest), bf16),
            pltpu.VMEM((4, share, shared_cols), bf16),
            pltpu.VMEM((6,) + small.shape, f32),
            pltpu.VMEM((4,) + small.shape, f32),
            dma((6, 5)),
            dma((6, 5)),
            dma((2, 4)),
            dma((2, 4)),
            dma((2,)),
            dma((4,)),
            dma((4,)),
            dma((3,)),
            dma((3,)),
            dma((4,)),
            dma((4,)),
            dma((4,)),
            dma((4,)),
            dma((5,)),
            dma((2,)),
        ],
        compiler_params=pltpu.CompilerParams(
            collective_id=2, has_side_effects=True, vmem_limit_bytes=BIG
        ),
        cost_estimate=cost(80),
        name="collect",
    )(
        normed,
        dproj,
        weight,
        mixed,
        both,
        x_rows.reshape(split),
        hidden.reshape(split),
        gain.reshape(1, -1),
        small,
    )


def rms_norm(values, gain_vec):
    return values * lax.rsqrt(jnp.mean(values * values, axis=-1, keepdims=True) + EPS) * gain_vec


def turn_tables(seq_count, head_count):
    half_dim = HEAD_SIZE // 2
    freqs = np.float32(THETA) ** (-np.arange(half_dim, dtype=np.float32) * 2.0 / HEAD_SIZE)
    angles = np.arange(seq_count, dtype=np.float32)[:, None] * freqs.astype(np.float32)[None, :]
    cosine, sine = np.cos(angles), np.sin(angles)
    return (
        jnp.asarray(np.tile(np.concatenate([cosine, cosine], axis=1), (1, head_count))),
        jnp.asarray(np.tile(np.concatenate([-sine, sine], axis=1), (1, head_count))),
    )


def swapped(values):
    return lax.ppermute(values, "core", SWAP)


def body(
    layer_in,
    seq_lengths,
    out_grad,
    norm_gain,
    mixer_weight,
    step_weight,
    state_weight,
    query_weight,
    key_value_weight,
    conv_channels,
    conv_states,
    step_bias,
    decay_log,
    skip_scale,
    group_gain,
    mamba_proj,
    attn_proj,
    ffn_gain,
    ffn_weight,
    ffn_down,
):
    core = lax.axis_index("core")
    place = lax.axis_index("tensor")
    first = core == 0
    seq_dev, rows_dev, model_dim = layer_in.shape
    groups = lax.axis_size("tensor")
    seq_total = rows_dev * groups
    half_rows = rows_dev // 2
    share = mixer_weight.shape[0]
    chans_dev = mixer_weight.shape[2]
    heads_dev = step_weight.shape[1]
    query_dev = query_weight.shape[1]
    hidden_dev = ffn_weight.shape[2]
    held = groups // 2
    step_pad = 128

    def mine(values):
        return lax.dynamic_slice_in_dim(values, core * held, held, 0)

    def other(values):
        return lax.dynamic_slice_in_dim(values, (1 - core) * held, held, 0)

    def in_order(own, others, axis):
        return jnp.where(
            first,
            jnp.concatenate([own, others], axis=axis),
            jnp.concatenate([others, own], axis=axis),
        )

    def flat(values):
        return values.transpose(1, 0, 2).reshape(values.shape[1], -1)

    spot = 2 * core + place % 2

    def positions_in(values):
        shaped = values.reshape(seq_dev, 2, half_rows, model_dim)
        keep = lax.dynamic_index_in_dim(shaped, core, 1, False)
        send = lax.dynamic_index_in_dim(shaped, 1 - core, 1, False)
        return lax.all_to_all(in_order(keep, swapped(send), 0), "tensor", 0, 0, tiled=True)

    def both_halves(own):
        both = in_order(own[:, None], swapped(own)[:, None], 1)
        return both.reshape(seq_total, model_dim)

    def positions_out(own):
        four = lax.all_to_all(own, "tensor", 0, 0, tiled=True)
        keep = lax.dynamic_slice_in_dim(four, core * seq_dev, seq_dev, 0)
        send = lax.dynamic_slice_in_dim(four, (1 - core) * seq_dev, seq_dev, 0)
        both = in_order(keep[:, None], swapped(send)[:, None], 1)
        return both.reshape(seq_dev, rows_dev, model_dim)

    def own_half(values):
        shaped = values.reshape(groups, 2, half_rows, -1)
        return lax.dynamic_index_in_dim(shaped, core, 1, False)

    def other_half(values):
        shaped = values.reshape(groups, 2, half_rows, -1)
        return lax.dynamic_index_in_dim(shaped, 1 - core, 1, False)

    out_dev = chans_dev + query_dev
    pack_two = jnp.concatenate([mamba_proj.T, attn_proj.T], axis=1)
    own_units = hidden_dev // 2
    pack_ups = jnp.concatenate([ffn_weight[:, 0], ffn_weight[:, 1]], axis=1)
    pack_downs = ffn_down.reshape(2, own_units, share).transpose(0, 2, 1)
    out_dev = chans_dev + query_dev
    pack_two = jnp.concatenate([mamba_proj.T, attn_proj.T], axis=1)
    pack_one = jnp.concatenate(
        [
            mixer_weight[:, 0],
            mixer_weight[:, 1],
            query_weight,
            jnp.pad(step_weight, ((0, 0), (0, step_pad - heads_dev))),
        ],
        axis=1,
    )
    def shared_for(at):
        pair = key_value_weight.reshape(share, 2, 2 * HEAD_SIZE)
        if not isinstance(at, int):
            pair = jnp.where(at == 0, pair, jnp.roll(pair, -HEAD_SIZE, axis=2))
            at = 0
        cols = slice(at * HEAD_SIZE, (at + 1) * HEAD_SIZE)
        return jnp.concatenate(
            [state_weight[:, 0], state_weight[:, 1], pair[:, 0, cols], pair[:, 1, cols]], axis=1
        )

    def lanes(values):
        return jnp.pad(values, (0, -values.shape[0] % 128)).reshape(-1, 128)

    small_in = jnp.concatenate(
        [
            lanes(conv_channels.reshape(-1)),
            lanes(jnp.repeat(skip_scale, HEAD_SIZE)),
            lanes(group_gain),
            lanes(step_bias),
            lanes(decay_log),
        ]
    )
    small_in = jnp.pad(small_in, ((0, -small_in.shape[0] % 8), (0, 0)))
    lengths = in_order(seq_lengths, swapped(seq_lengths), 0)
    seq_len = lengths[place]
    len_one = seq_len.reshape(1)
    valid_rows = (jnp.arange(seq_total, dtype=jnp.int32) < seq_len).astype(jnp.float32)[:, None]
    group_cols = 2 * chans_dev + query_dev + step_pad
    cosine, sine = turn_tables(seq_total, 2)
    state_taps = conv_states.reshape(KCONV, 2 * N)
    quad = lax.axis_size("plane") == 4 and groups == 4 and share == 128
    quad = quad and share == half_rows
    if quad:
        shared = jnp.stack([shared_for(0), shared_for(1)])
        (
            weight_one,
            weight_two,
            gate_up_weight,
            down_weight,
            x_low,
            normed,
            proj,
            grad_whole,
            taps,
            bias,
            decay,
            skip,
            gain,
            log_sums,
            both_low,
            state_out,
            states,
            mixed_part,
            mixed_other,
        ) = front(
            pack_one,
            pack_two,
            pack_ups,
            pack_downs,
            shared,
            layer_in,
            small_in,
            out_grad,
            state_taps,
            norm_gain.reshape(1, -1),
            len_one,
            cosine,
            sine,
        )
    else:
        x_low = both_halves(positions_in(layer_in))
        all_one = lax.all_gather(pack_one, "tensor", axis=0)
        own_one = jnp.concatenate([flat(mine(all_one)), shared_for(core)], axis=1)
        their_one = jnp.concatenate([flat(other(all_one)), shared_for(1 - core)], axis=1)
        weight_one = lax.all_gather(
            in_order(own_one, swapped(their_one), 0), "plane", axis=0, tiled=True
        )
        all_two = lax.all_gather(pack_two, "tensor", axis=0)
        weight_two = lax.all_gather(
            in_order(flat(mine(all_two)), swapped(flat(other(all_two))), 0),
            "plane",
            axis=0,
            tiled=True,
        )
        split_ups = pack_ups.reshape(share, 2, 2, own_units).transpose(2, 0, 1, 3)
        split_ups = split_ups.reshape(2, share, hidden_dev)
        rows_up, rows_down = (
            in_order(
                lax.dynamic_index_in_dim(pack, core, 0, False),
                swapped(lax.dynamic_index_in_dim(pack, 1 - core, 0, False)),
                0,
            )
            for pack in (split_ups, pack_downs)
        )
        rows_up, rows_down = (
            lax.all_gather(rows, "tensor", axis=1, tiled=True) for rows in (rows_up, rows_down)
        )
        down_weight = lax.all_gather(rows_down, "plane", axis=0, tiled=True)
        params = mine(lax.all_gather(small_in, "tensor", axis=0))
        span = chans_dev // 128

        def spread_lanes(at):
            return params[:, at : at + span].reshape(1, -1)

        taps = jnp.concatenate([spread_lanes(span * tap) for tap in range(KCONV)], axis=0)
        taps = jnp.concatenate([taps, state_taps], axis=1)
        skip, gain = spread_lanes(KCONV * span), spread_lanes((KCONV + 1) * span)
        bias, decay = params[:, (KCONV + 2) * span], params[:, (KCONV + 2) * span + 1]
        normed = low(rms_norm(wide(x_low), norm_gain))
        proj = dot(normed, weight_one)
        attn, log_sums = attention_forward(len_one, proj, cosine, sine, group_cols)
        both_low, state_out, states = mamba_forward(proj, attn, taps, bias, decay, skip, gain)
        gate_up_weight = lax.all_gather(rows_up, "plane", axis=0, tiled=True)
        grad_whole = both_halves(positions_in(out_grad))
        mixed_part = low(dot_nt(both_low, weight_two))
        mixed_other = swapped(mixed_part)

    grad_low, hidden, normed_two, act_low, gate_up_low = ffn_middle(
        len_one,
        x_low,
        mixed_part,
        mixed_other,
        ffn_gain.reshape(1, -1),
        grad_whole,
        gate_up_weight,
        down_weight,
        groups,
    )
    grad_three = ffn_gradients(grad_low, act_low, normed_two, gate_up_low, groups)
    grad_two_part = low(dot_nt(gate_up_low, gate_up_weight))
    ffn_part = low(dot_nt(act_low, down_weight))
    ffn_own = wide(own_half(ffn_part)) + wide(swapped(other_half(ffn_part)))
    out_own = own_half(valid_rows) * (own_half(hidden) + ffn_own)

    grad_hidden, grad_mixed, back, grad_ffn_gain = hidden_backward(
        hidden,
        grad_two_part,
        swapped(grad_two_part),
        grad_low,
        ffn_gain.reshape(1, -1),
        weight_two,
    )
    grad_ffn_gain = grad_ffn_gain.reshape(-1)

    def scatter(values):
        return lax.psum_scatter(values, "plane", scatter_dimension=0, tiled=True)

    def to_groups(values):
        by_part = values.reshape(2, share, held, -1).transpose(0, 2, 1, 3)
        own = lax.dynamic_index_in_dim(by_part, core, 0, False)
        theirs = swapped(lax.dynamic_index_in_dim(by_part, 1 - core, 0, False))
        whole = in_order(own, theirs, 0)
        return wide(lax.psum_scatter(whole, "tensor", scatter_dimension=0, tiled=True)[0])

    units = lax.psum_scatter(scatter(grad_three), "tensor", scatter_dimension=1, tiled=True)
    units = units.reshape(2, share, -1)
    own_part = lax.dynamic_index_in_dim(units, core, 0, True)
    their_part = swapped(lax.dynamic_index_in_dim(units, 1 - core, 0, True))
    units = wide(in_order(own_part, their_part, 0))
    sum_up = units[:, :, :hidden_dev].reshape(2, share, 2, own_units).transpose(1, 2, 0, 3)
    sum_down = units[:, :, hidden_dev:].transpose(0, 2, 1).reshape(hidden_dev, share)

    grad_q, grad_kv = attention_backward(
        len_one, proj, cosine, sine, log_sums, back, group_cols, 3
    )
    layer_out = positions_out(low(out_own))
    proj_grad, grad_taps, grad_gain, grad_skip_cols, grad_bias, grad_decay = mamba_backward(
        proj, state_out, states, back, grad_q, grad_kv, taps, bias, decay, skip, gain
    )
    edge = held * group_cols
    grad_skip = jnp.sum(grad_skip_cols.reshape(held, heads_dev, HEAD_SIZE), axis=-1)
    chan_taps = grad_taps[:, : held * chans_dev].reshape(KCONV, held, chans_dev)
    group_small = jnp.concatenate(
        [
            chan_taps.transpose(1, 0, 2).reshape(held, -1),
            grad_bias[:, :heads_dev],
            grad_decay[:, :heads_dev],
            grad_skip,
            grad_gain.reshape(held, -1),
        ],
        axis=1,
    )
    small_groups = in_order(group_small, jnp.zeros_like(group_small), 0)
    small_out = jnp.concatenate(
        [
            jnp.zeros_like(norm_gain),
            grad_ffn_gain,
            grad_taps[:, held * chans_dev :].reshape(-1),
            small_groups.reshape(-1),
        ]
    )
    if quad:
        small_size = small_out.shape[0]
        small_room = -(-small_size // 1024) * 1024
        (
            sum_mixer,
            sum_query,
            sum_step,
            shared_sum,
            small_sum,
            input_grad,
            sum_mamba,
            sum_attn,
        ) = collect(
            normed,
            proj_grad,
            weight_one,
            grad_mixed,
            both_low,
            x_low,
            grad_hidden,
            norm_gain,
            jnp.pad(small_out, (0, small_room - small_size)).reshape(-1, 128),
            (chans_dev, query_dev, group_cols),
        )
        small_sum = small_sum.reshape(-1)[:small_size]
    else:
        grad_one = low(dot_tn(normed, proj_grad))
        grad_norm_part = low(dot_nt(proj_grad, weight_one))
        grad_norm_own = wide(own_half(grad_norm_part)) + wide(swapped(other_half(grad_norm_part)))
        x_own = wide(own_half(x_low))
        r_one = lax.rsqrt(jnp.mean(x_own * x_own, axis=-1, keepdims=True) + EPS)
        scaled = grad_norm_own * norm_gain
        grad_x = low(
            own_half(grad_hidden)
            + r_one * scaled
            - x_own * (r_one**3 * jnp.mean(x_own * scaled, axis=-1, keepdims=True))
        )
        grad_norm_gain = jnp.sum(x_own * r_one * grad_norm_own, axis=(0, 1))
        small_out = small_out.at[:model_dim].set(grad_norm_gain)
        part_one = scatter(grad_one)
        both_parts = part_one[:, edge:].reshape(2, share, -1)
        own_rest = lax.dynamic_index_in_dim(both_parts, core, 0, False)
        their_rest = swapped(lax.dynamic_index_in_dim(both_parts, 1 - core, 0, False))
        shared_own = wide(own_rest[:, : 2 * N]) + wide(their_rest[:, : 2 * N])
        kv_both = in_order(own_rest[:, 2 * N :], their_rest[:, 2 * N :], 1)
        shared_low = jnp.concatenate([low(shared_own), kv_both], axis=1)
        shared_sum = jnp.sum(wide(lax.all_gather(shared_low, "tensor", axis=0)), axis=0)
        sum_one = to_groups(part_one[:, :edge])
        sum_mixer = sum_one[:, : 2 * chans_dev]
        sum_query = sum_one[:, 2 * chans_dev : 2 * chans_dev + query_dev]
        sum_step = sum_one[:, 2 * chans_dev + query_dev :]
        sum_two = to_groups(scatter(low(dot_tn(grad_mixed, both_low)))).T
        sum_mamba, sum_attn = sum_two[:chans_dev], sum_two[chans_dev:]
        input_grad = positions_out(grad_x)
        small_sum = lax.psum(small_out, ("plane", "core", "tensor"))
    kv_sum = shared_sum[:, 2 * N :].reshape(share, 2, 2, HEAD_SIZE).transpose(0, 2, 1, 3)
    group_sum = lax.dynamic_index_in_dim(
        small_sum[2 * model_dim + KCONV * 2 * N :].reshape(groups, -1), place, 0, False
    )
    pieces = []
    at = 0
    for size in (KCONV * chans_dev, heads_dev, heads_dev, heads_dev, chans_dev):
        pieces.append(group_sum[at : at + size])
        at += size

    return (
        layer_out,
        input_grad,
        small_sum[:model_dim],
        jnp.stack([sum_mixer[:, :chans_dev], sum_mixer[:, chans_dev:]], axis=1),
        sum_step[:, :heads_dev],
        jnp.stack([shared_sum[:, :N], shared_sum[:, N : 2 * N]], axis=1),
        sum_query,
        kv_sum.reshape(share, 2, 2 * HEAD_SIZE),
        pieces[0].reshape(KCONV, chans_dev),
        small_sum[2 * model_dim : 2 * model_dim + KCONV * 2 * N].reshape(KCONV, 2, N),
        pieces[1],
        pieces[2],
        pieces[3],
        pieces[4],
        sum_mamba,
        sum_attn,
        small_sum[model_dim : 2 * model_dim],
        sum_up.reshape(share, 2, hidden_dev),
        sum_down,
    )


def solution(mesh):
    rows, columns = mesh.devices.shape
    fine = Mesh(mesh.devices.reshape(rows // 2, 2, columns), ("plane", "core", "tensor"))
    dp = ("plane", "core")
    return jax.shard_map(
        body,
        mesh=fine,
        in_specs=(
            P(dp, "tensor", None),
            P(dp),
            P(dp, "tensor", None),
            P(),
            P(dp, None, "tensor"),
            P(dp, "tensor"),
            P(dp, None, None),
            P(dp, "tensor"),
            P(dp, None, None),
            P(None, "tensor"),
            P(),
            P("tensor"),
            P("tensor"),
            P("tensor"),
            P("tensor"),
            P("tensor", dp),
            P("tensor", dp),
            P(),
            P(dp, None, "tensor"),
            P("tensor", dp),
        ),
        out_specs=(
            P(dp, "tensor", None),
            P(dp, "tensor", None),
            P(),
            P(dp, None, "tensor"),
            P(dp, "tensor"),
            P(dp, None, None),
            P(dp, "tensor"),
            P(dp, None, None),
            P(None, "tensor"),
            P(),
            P("tensor"),
            P("tensor"),
            P("tensor"),
            P("tensor"),
            P("tensor", dp),
            P("tensor", dp),
            P(),
            P(dp, None, "tensor"),
            P("tensor", dp),
        ),
        check_vma=False,
    )
```
